32 devices in a mesh: dp: 8 (over z, x), seq: 4 (over y, core).
Axes of the slice: x: 2, y: 2, z: 4, core: 2. Of those that a mesh axis runs over, the one named last changes fastest.
Arguments:
- frames: bfloat16 [16, 4096, 256], P('dp', 'seq'), may hold values from -6 to 6
- time_embed: bfloat16 [16, 1024], P('dp'), may hold values from -6 to 6
- lengths: int32 [16], P('dp'), may hold values from 256 to 4096, as said below
- out_cotangent: bfloat16 [16, 2048, 256], P('dp', 'seq'), may hold values from -6 to 6
- conv_first: bfloat16 [3, 256, 256], replicated, may hold values from -0.21875 to 0.21875
- conv_second: bfloat16 [3, 256, 256], replicated, may hold values from -0.21875 to 0.21875
- conv_skip: bfloat16 [256, 256], replicated, may hold values from -0.375 to 0.375
- time_proj: bfloat16 [1024, 256], replicated, may hold values from -0.1875 to 0.1875
- w_qkv: bfloat16 [256, 384], replicated, may hold values from -0.375 to 0.375
- w_out: bfloat16 [128, 256], replicated, may hold values from -1.5 to 1.5
- ff_in: bfloat16 [256, 1024], replicated, may hold values from -0.375 to 0.375
- ff_out: bfloat16 [1024, 256], replicated, may hold values from -0.1875 to 0.1875
- conv_down: bfloat16 [3, 256, 256], replicated, may hold values from -0.21875 to 0.21875
- gains: float32 [4, 256], replicated, may hold values from 0.25 to 1.75
- shifts: float32 [11, 256], replicated, may hold values from -3 to 3
- ff_bias: float32 [1024], replicated, may hold values from -3 to 3
- snake_logs: float32 [2, 1024], replicated, may hold values from -0.7 to 0.7
Outputs:
- layer_out: bfloat16 [16, 2048, 256], P('dp', 'seq')
- grad_frames: float32 [16, 4096, 256], P('dp', 'seq')
- grad_conv_first: float32 [3, 256, 256], replicated
- grad_conv_second: float32 [3, 256, 256], replicated
- grad_conv_skip: float32 [256, 256], replicated
- grad_time_proj: float32 [1024, 256], replicated
- grad_w_qkv: float32 [256, 384], replicated
- grad_w_out: float32 [128, 256], replicated
- grad_ff_in: float32 [256, 1024], replicated
- grad_ff_out: float32 [1024, 256], replicated
- grad_conv_down: float32 [3, 256, 256], replicated
- grad_gains: float32 [4, 256], replicated
- grad_shifts: float32 [11, 256], replicated
- grad_ff_bias: float32 [1024], replicated
- grad_snake_logs: float32 [2, 1024], replicated
The draws below stay inside these ranges and needn't reach their ends.
Inputs may be any that keep to these rules, and one draw needn't show every extreme that they name: `lengths`: each aligned block of 2 utterances holds one of full length 4096.
All inputs are finite; a program needn't handle non-finite values.
Results may differ from the reference program's by a relative error of at most 0.012.
The reference program's roundings to bfloat16 on the way count: a program that leaves them out, or rounds other values in their place, can miss the bound.
Values may be sent and summed in bfloat16 or wider, within the bound.
A program may use at most 320 MiB of HBM per device.

```python
import jax
import jax.numpy as jnp
from jax import lax

C = 256
TE = 1024
FF = 1024
HEADS = 2
HEAD_DIM = 64
GROUPS = 8
UTT_DEV = 2
FRAMES = 4096
UTT = 16


def draw_lengths(key, part):
    key = jax.random.fold_in(key, 7)
    base_key, pick_key = jax.random.split(key)
    groups_count = UTT // UTT_DEV
    base_lengths = jax.random.randint(base_key, (UTT,), FRAMES // 16, FRAMES + 1)
    full_index = jax.random.randint(pick_key, (groups_count,), 0, UTT_DEV)
    chosen = (jnp.arange(UTT_DEV)[None, :] == full_index[:, None]).reshape(UTT)
    return jnp.where(chosen, FRAMES, base_lengths).astype(jnp.int32)


def steps_of(rng, extent, pieces, smallest, high):
    def one(axis_at, parts):
        heights = jax.random.uniform(jax.random.fold_in(jax.random.fold_in(rng, 6), axis_at), (parts,), jnp.float32, smallest / len(pieces), high / len(pieces))
        return jnp.repeat(jnp.exp(heights), extent[axis_at] // parts).reshape((-1,) + (1,) * (len(extent) - axis_at - 1))

    loudness = one(*pieces[0])
    for cut in pieces[1:]:
        loudness = loudness * one(*cut)
    return loudness


def scatter_about(key, extent, scale, most, cuts=(), dtype=jnp.bfloat16):
    level = steps_of(key, extent, cuts, -0.22, 0.18) if cuts else 1.0
    values = jax.random.normal(key, extent, jnp.float32) * scale * level
    return jnp.minimum(jnp.maximum(values, -most), most).astype(dtype)


def setup_inputs(seed: int = 0) -> dict:
    keys = jax.random.split(jax.random.key(seed), 18)
    frames = scatter_about(keys[0], (UTT, FRAMES, C), 1.0, 6.0, ((0, 8), (1, 4)))
    time_embed = scatter_about(keys[1], (UTT, TE), 1.0, 6.0, ((0, 8),))
    lengths = draw_lengths(jax.random.fold_in(keys[17], 71), 0)
    out_cotangent = scatter_about(keys[3], (UTT, FRAMES // 2, C), 1.0, 6.0, ((0, 8), (1, 4)))
    conv_first = scatter_about(keys[4], (3, C, C), (3 * C) ** -0.5, 0.21875)
    conv_second = scatter_about(keys[5], (3, C, C), (3 * C) ** -0.5, 0.21875)
    conv_skip = scatter_about(keys[6], (C, C), C ** -0.5, 0.375)
    time_proj = scatter_about(keys[7], (TE, C), TE ** -0.5, 0.1875)
    w_qkv = scatter_about(keys[8], (C, 3 * HEADS * HEAD_DIM), C ** -0.5, 0.375)
    w_out = scatter_about(keys[9], (HEADS * HEAD_DIM, C), (HEADS * HEAD_DIM // 8) ** -0.5, 1.5)
    ff_in = scatter_about(keys[10], (C, FF), C ** -0.5, 0.375)
    ff_out = scatter_about(keys[11], (FF, C), FF ** -0.5, 0.1875)
    conv_down = scatter_about(keys[12], (3, C, C), (3 * C) ** -0.5, 0.21875)
    gains = jnp.clip(1.0 + 0.15 * jax.random.normal(keys[13], (4, C), jnp.float32), 0.25, 1.75)
    shifts = scatter_about(keys[14], (11, C), 0.5, 3.0, (), jnp.float32)
    ff_bias = scatter_about(keys[15], (FF,), 0.5, 3.0, (), jnp.float32)
    snake_logs = jnp.clip(jax.random.uniform(keys[16], (2, FF), jnp.float32, -0.7, 0.7), -0.7, 0.7)
    return {"frames": frames, "time_embed": time_embed, "lengths": lengths, "out_cotangent": out_cotangent, "conv_first": conv_first, "conv_second": conv_second, "conv_skip": conv_skip, "time_proj": time_proj, "w_qkv": w_qkv, "w_out": w_out, "ff_in": ff_in, "ff_out": ff_out, "conv_down": conv_down, "gains": gains, "shifts": shifts, "ff_bias": ff_bias, "snake_logs": snake_logs}


@jax.custom_vjp
def low(v):
    return lax.optimization_barrier(v.astype(jnp.bfloat16)).astype(jnp.float32)

@jax.custom_vjp
def low_back(v):
    return v

def low_keep(v):
    return (low(v), None)

def low_pass(kept, grad):
    return (grad,)

def back_keep(v):
    return (v, None)

def back_low(kept, grad):
    return (low(grad),)
low.defvjp(low_keep, low_pass)
low_back.defvjp(back_keep, back_low)
norm_eps = 1e-05

def mish(values):
    return values * jnp.tanh(jax.nn.softplus(values))

def matmul(operand, matrix):
    return jnp.dot(operand, matrix, precision=lax.Precision.HIGHEST, preferred_element_type=jnp.float32)

def conv_three(values, weight):
    length = values.shape[0]
    padded = jnp.pad(values, ((1, 1), (0, 0)))
    stacked = jnp.concatenate([padded[0:length], padded[1:length + 1], padded[2:length + 2]], axis=1)
    return low_back(matmul(stacked, weight.reshape(3 * C, C)))

def group_norm(hidden, frame_mask, valid_count, gain, shift):
    length = hidden.shape[0]
    grouped = hidden.reshape(length, GROUPS, C // GROUPS)
    mask_cube = frame_mask[:, None, None]
    group_mean = lax.optimization_barrier(jnp.sum(grouped * mask_cube, axis=(0, 2))) / valid_count
    centered = grouped - group_mean[None, :, None]
    variance = lax.optimization_barrier(jnp.sum(centered * centered * mask_cube, axis=(0, 2))) / valid_count
    normed = (centered * lax.rsqrt(variance + norm_eps)[None, :, None]).reshape(length, C)
    return normed * gain + shift

def layer_norm(values, gain, shift):
    centered = values - lax.optimization_barrier(jnp.mean(values, axis=-1, keepdims=True))
    variance = lax.optimization_barrier(jnp.mean(centered * centered, axis=-1, keepdims=True))
    return centered * lax.rsqrt(variance + norm_eps) * gain + shift

def snake(values, snake_logs):
    return values + jnp.square(jnp.sin(values * jnp.exp(snake_logs[0]))) / (jnp.exp(snake_logs[1]) + 1e-09)

def utterance(frames_u, embed_u, length_u, params):
    conv_first, conv_second, conv_skip, time_proj, w_qkv, w_out, ff_in, ff_out, conv_down, gains, shifts, ff_bias, snake_logs = params
    frame_mask = (jnp.arange(FRAMES) < length_u).astype(jnp.float32)
    valid_count = length_u.astype(jnp.float32) * (C // GROUPS)
    column_mask = frame_mask[:, None]
    masked_in = frames_u * column_mask
    hidden_one = conv_three(masked_in, conv_first) + shifts[0]
    act_one = mish(group_norm(hidden_one, frame_mask, valid_count, gains[0], shifts[1])) * column_mask
    embed_act = low(mish(embed_u))
    time_shift = matmul(embed_act[None, :], time_proj) + shifts[2]
    act_in = low((act_one + time_shift) * column_mask)
    hidden_two = conv_three(act_in, conv_second) + shifts[3]
    act_two = mish(group_norm(hidden_two, frame_mask, valid_count, gains[1], shifts[4])) * column_mask
    resnet_out = act_two + low_back(matmul(masked_in, conv_skip)) + shifts[5]
    normed_one = low(layer_norm(resnet_out, gains[2], shifts[6]))
    inner_width = HEADS * HEAD_DIM
    qkv_rows = low(low_back(matmul(normed_one, w_qkv)))
    queries = qkv_rows[:, :inner_width].reshape(FRAMES, HEADS, HEAD_DIM)
    key_rows = qkv_rows[:, inner_width:2 * inner_width].reshape(FRAMES, HEADS, HEAD_DIM)
    value_rows = qkv_rows[:, 2 * inner_width:].reshape(FRAMES, HEADS, HEAD_DIM)
    raw_scores = low_back(jnp.einsum('qhd,khd->hqk', queries, key_rows, precision=lax.Precision.HIGHEST))
    scores = jnp.where(frame_mask[None, None, :] > 0, raw_scores * HEAD_DIM ** (-0.5), -1000000000.0)
    attn_probs = low(jax.nn.softmax(scores, axis=-1))
    attended = low(low_back(jnp.einsum('hqk,khd->qhd', attn_probs, value_rows, precision=lax.Precision.HIGHEST)))
    attended = attended.reshape(FRAMES, inner_width)
    resid_two = resnet_out + low_back(matmul(attended, w_out)) + shifts[7]
    normed_two = low(layer_norm(resid_two, gains[3], shifts[8]))
    ff_hidden = low_back(matmul(normed_two, ff_in)) + ff_bias
    snaked = low(snake(ff_hidden, snake_logs))
    resid_three = resid_two + low_back(matmul(snaked, ff_out)) + shifts[9]
    down_in = low(resid_three * column_mask)
    padded = jnp.pad(down_in, ((1, 1), (0, 0)))
    stacked = jnp.concatenate([padded[0:FRAMES:2], padded[1:FRAMES + 1:2], padded[2:FRAMES + 2:2]], axis=1)
    lowered = low_back(matmul(stacked, conv_down.reshape(3 * C, C))) + shifts[10]
    return lowered * frame_mask[0::2][:, None]

def reference(frames, time_embed, lengths, out_cotangent, conv_first, conv_second, conv_skip, time_proj, w_qkv, w_out, ff_in, ff_out, conv_down, gains, shifts, ff_bias, snake_logs):
    params = tuple((weight.astype(jnp.float32) for weight in (conv_first, conv_second, conv_skip, time_proj, w_qkv, w_out, ff_in, ff_out, conv_down, gains, shifts, ff_bias, snake_logs)))

    def per_utterance(totals, inputs):
        frames_u, embed_u, length_u, cotangent_u = inputs

        def forward(frames_f, params_f):
            return utterance(frames_f, embed_u, length_u, params_f)
        result, pullback = jax.vjp(forward, frames_u.astype(jnp.float32), params)
        grad_in, grad_params = pullback(cotangent_u.astype(jnp.float32))
        totals = jax.tree.map(jnp.add, totals, grad_params)
        return (totals, (result.astype(jnp.bfloat16), grad_in))
    start_totals = jax.tree.map(jnp.zeros_like, params)
    totals, (layer_out, grad_frames) = lax.scan(per_utterance, start_totals, (frames, time_embed.astype(jnp.float32), lengths, out_cotangent))
    return (layer_out, grad_frames, totals[0], totals[1], totals[2], totals[3], totals[4], totals[5], totals[6], totals[7], totals[8], totals[9], totals[10], totals[11], totals[12])
```

```python
import functools
import math

import jax
import jax.numpy as jnp
from jax import lax
from jax.experimental import pallas as pl
from jax.experimental.pallas import tpu as pltpu
from jax.sharding import PartitionSpec as P

F32, BF = jnp.float32, jnp.bfloat16
NT = (((1,), (1,)), ((), ()))
NN = (((1,), (0,)), ((), ()))
LOG2E = math.log2(math.e)


def dot(a, b, dn=NN):
    return lax.dot_general(a, b, dn, preferred_element_type=F32)


HEADS = 2
GROUPS = 8


norm_eps = 1e-05


def with_halo(x, sides, width):
    for axis, dim in sides:
        size, length = (lax.axis_size(axis), x.shape[dim])
        up = [(i, (i + 1) % size) for i in range(size - 1)]
        down = [(j, i) for i, j in up]
        last = lax.slice_in_dim(x, length - width, length, axis=dim)
        leading = lax.slice_in_dim(x, 0, width, axis=dim)
        before = lax.ppermute(last, axis, up)
        after = lax.ppermute(leading, axis, down)
        x = jnp.concatenate([before, x, after], axis=dim)
    return x


def from_behind(block, axis, distance):
    devices = range(lax.axis_size(axis))
    route = [(i - distance, i) for i in devices if i - distance in devices]
    return lax.ppermute(block, axis, route)


def mish(values):
    return values * jnp.tanh(jax.nn.softplus(values))


def project(operand, matrix):
    return lax.dot_general(
        operand, matrix, (((operand.ndim - 1,), (0,)), ((), ())), preferred_element_type=jnp.float32
    )


def project_back(grads, matrix):
    return lax.dot_general(
        grads, matrix, (((grads.ndim - 1,), (1,)), ((), ())), preferred_element_type=jnp.float32
    )


def weight_grad(operand, grads):
    flat_operand = operand.reshape(-1, operand.shape[-1])
    flat_grads = grads.reshape(-1, grads.shape[-1])
    return lax.dot_general(
        flat_operand, flat_grads, (((0,), (0,)), ((), ())), preferred_element_type=jnp.float32
    )


def conv_forward(values, weight):
    padded = with_halo(values, (("seq", 1),), 1)
    local_len = values.shape[1]
    stacked = jnp.concatenate(
        [padded[:, 0:local_len], padded[:, 1 : local_len + 1], padded[:, 2 : local_len + 2]], axis=2
    )
    return (stacked, project(stacked, weight.reshape(-1, weight.shape[2])))


def conv_backward(grads, weight):
    padded = with_halo(grads, (("seq", 1),), 1)
    local_len = grads.shape[1]
    stacked = jnp.concatenate(
        [padded[:, 2 : local_len + 2], padded[:, 1 : local_len + 1], padded[:, 0:local_len]], axis=2
    )
    flipped = jnp.transpose(weight, (0, 2, 1)).reshape(-1, weight.shape[1])
    return project(stacked, flipped)


def group_stats(hidden, frame_mask, counts):
    utt_count, frame_count, channels = hidden.shape
    grouped = hidden.reshape(utt_count, frame_count, GROUPS, channels // GROUPS)
    mask_cube = frame_mask[:, :, None, None]
    weighted = grouped * mask_cube
    group_mean = lax.psum(jnp.sum(weighted, axis=(1, 3)), "seq") / counts[:, None]
    centered = grouped - group_mean[:, None, :, None]
    variance = (
        lax.psum(jnp.sum(centered * centered * mask_cube, axis=(1, 3)), "seq") / counts[:, None]
    )
    return (group_mean, lax.rsqrt(variance + norm_eps))


def norm_mish(hidden, group_mean, inv_std, gain, shift, frame_mask):
    utt_count, frame_count, channels = hidden.shape
    grouped = hidden.reshape(utt_count, frame_count, GROUPS, channels // GROUPS)
    normed = ((grouped - group_mean[:, None, :, None]) * inv_std[:, None, :, None]).reshape(
        hidden.shape
    )
    return mish(normed * gain + shift) * frame_mask[:, :, None]


def norm_backward(grads, hidden, group_mean, inv_std, gain, shift, frame_mask, counts):

    def local_piece(hidden_v, mean_v, inv_v, gain_v, shift_v):
        return norm_mish(hidden_v, mean_v, inv_v, gain_v, shift_v, frame_mask)

    outputs, pullback = jax.vjp(local_piece, hidden, group_mean, inv_std, gain, shift)
    grad_hidden, grad_mean, grad_inv, grad_gain, grad_shift = pullback(grads)
    grad_mean, grad_inv = lax.psum((grad_mean, grad_inv), "seq")
    grad_variance = grad_inv * -0.5 * inv_std * inv_std * inv_std
    utt_count, frame_count, channels = hidden.shape
    grouped = hidden.reshape(utt_count, frame_count, GROUPS, channels // GROUPS)
    extra_grad = (
        grad_mean[:, None, :, None]
        + 2.0 * grad_variance[:, None, :, None] * (grouped - group_mean[:, None, :, None])
    ) / counts[:, None, None, None]
    grad_hidden = grad_hidden + (extra_grad * frame_mask[:, :, None, None]).reshape(hidden.shape)
    return (grad_hidden, grad_gain, grad_shift)


def layer_norm(values, gain, shift):
    centered = values - jnp.mean(values, axis=-1, keepdims=True)
    variance = jnp.mean(centered * centered, axis=-1, keepdims=True)
    return centered * lax.rsqrt(variance + norm_eps) * gain + shift


def snake(values, snake_logs):
    return values + jnp.square(jnp.sin(values * jnp.exp(snake_logs[0]))) / (
        jnp.exp(snake_logs[1]) + 1e-09
    )


def fwd_kernel(QB, CK, len_ref, q_ref, k_ref, v_ref, o_ref, qa_ref, kb, vb):
    u = pl.program_id(0)
    W = k_ref.shape[1]; F = q_ref.shape[1]
    L = len_ref[u]
    lane = lax.broadcasted_iota(jnp.int32, (1, 128), 1)
    first = lane < 64
    c = 0.125 * LOG2E
    nch = (L + CK - 1) // CK
    one = jnp.ones((), BF)
    for qi in range(F // QB):
        q = q_ref[0, qi * QB:(qi + 1) * QB, :]
        qh = [jnp.where(first, q, jnp.zeros_like(q)), jnp.where(first, jnp.zeros_like(q), q)]
        def body(j, carry):
            off = pl.multiple_of(j * CK, CK)
            k = k_ref[0, pl.ds(off, CK), :]
            v = v_ref[0, pl.ds(off, CK), :]
            vh = [jnp.where(first, v, one), jnp.where(first, one, v)]
            bias = jnp.where(off + lax.broadcasted_iota(jnp.int32, (1, CK), 1) < L, 0.0, -1e9)
            out = []
            for h in range(2):
                m, acc = carry[h]
                s = dot(qh[h], k, NT) + bias
                mn = jnp.maximum(m, jnp.max(s, axis=1, keepdims=True))
                p = jnp.exp2((s - mn) * c).astype(BF)
                al = jnp.exp2((m - mn) * c)
                acc = acc * al + dot(p, vh[h])
                out.append((mn, acc))
            return tuple(out)
        init = tuple((jnp.full((QB, 1), -1e30, F32), jnp.zeros((QB, 128), F32)) for _ in range(2))
        (m0, a0), (m1, a1) = lax.fori_loop(0, nch, body, init)
        l0 = a0[:, 64:65]; l1 = a1[:, 0:1]
        o_ref[0, qi * QB:(qi + 1) * QB, :] = jnp.where(first, a0 / l0, a1 / l1)
        for h, (m, l) in enumerate(((m0, l0), (m1, l1))):
            t = -(m + jnp.log2(l) / c)
            t1 = t.astype(BF); r = t - t1.astype(F32); t2 = r.astype(BF); r = r - t2.astype(F32); t3 = r.astype(BF)
            base = 64 * (1 - h)
            qa = jnp.where(lane == base, t1, jnp.where(lane == base + 1, t2, jnp.where(lane == base + 2, t3,
                 jnp.where(lane == base + 3, one, qh[h]))))
            qa_ref[0, h, qi * QB:(qi + 1) * QB, :] = qa

def attn_forward(lengths, q, k, v, QB=1024, CK=2048):
    U, F, _ = q.shape; W = k.shape[1]
    return pl.pallas_call(
        functools.partial(fwd_kernel, QB, CK),
        out_shape=(jax.ShapeDtypeStruct((U, F, 128), F32), jax.ShapeDtypeStruct((U, 2, F, 128), BF)),
        grid_spec=pltpu.PrefetchScalarGridSpec(num_scalar_prefetch=1, grid=(U,),
            in_specs=[pl.BlockSpec((1, F, 128), lambda u, _: (u, 0, 0)), pl.BlockSpec((1, W, 128), lambda u, _: (u, 0, 0)), pl.BlockSpec((1, W, 128), lambda u, _: (u, 0, 0))],
            out_specs=[pl.BlockSpec((1, F, 128), lambda u, _: (u, 0, 0)), pl.BlockSpec((1, 2, F, 128), lambda u, _: (u, 0, 0, 0))],
            scratch_shapes=[pltpu.VMEM((2, W, 128), BF), pltpu.VMEM((2, W, 128), BF)]),
        compiler_params=pltpu.CompilerParams(vmem_limit_bytes=56 * 2**20), name="attn_fwd",
    )(lengths, q, k, v)

def bwd_kernel(KB, len_ref, qa_ref, da_ref, k_ref, v_ref, dq_ref, dk_ref, dv_ref, dqt):
    u = pl.program_id(0)
    W = k_ref.shape[1]; F = qa_ref.shape[2]
    L = len_ref[u]
    lane = lax.broadcasted_iota(jnp.int32, (1, 128), 1)
    first = lane < 64
    c = 0.125 * LOG2E
    one = jnp.ones((), BF)
    dqt[...] = jnp.zeros_like(dqt)
    nkb = (L + KB - 1) // KB
    def body(j, _):
        off = pl.multiple_of(j * KB, KB)
        k = k_ref[0, pl.ds(off, KB), :]
        v = v_ref[0, pl.ds(off, KB), :]
        kt = k.T
        bias = jnp.where(off + lax.broadcasted_iota(jnp.int32, (KB, 1), 0) < L, 0.0, -1e9).astype(BF)
        dvs, dks = [], []
        for h in range(2):
            base = 64 * (1 - h)
            if h == 0:
                ka = jnp.where(lane < 64, k, jnp.where(lane == base + 3, bias, jnp.where(lane < base + 3, one, 0 * one)))
                va = jnp.where(lane < 64, v, jnp.where(lane < base + 3, -one, 0 * one))
            else:
                ka = jnp.where(lane >= 64, k, jnp.where(lane == base + 3, bias, jnp.where(lane < base + 3, one, 0 * one)))
                va = jnp.where(lane >= 64, v, jnp.where(lane < base + 3, -one, 0 * one))
            qa = qa_ref[0, h]
            da = da_ref[0, h]
            st = dot(ka, qa, NT)
            p = jnp.exp2(st * c)
            dp = dot(va, da, NT)
            ds = (p * dp).astype(BF)
            dvs.append(dot(p.astype(BF), da))
            dks.append(dot(ds, qa))
            dqt[h * 64:(h + 1) * 64, :] += dot(kt[h * 64:(h + 1) * 64, :], ds)
        dk_ref[0, pl.ds(off, KB), :] = (jnp.where(first, dks[0], dks[1]) * 0.125).astype(BF)
        dv_ref[0, pl.ds(off, KB), :] = jnp.where(first, dvs[0], dvs[1]).astype(BF)
        return 0
    lax.fori_loop(0, nkb, body, 0)
    def zero(j, _):
        off = pl.multiple_of(j * KB, KB)
        dk_ref[0, pl.ds(off, KB), :] = jnp.zeros((KB, 128), BF)
        dv_ref[0, pl.ds(off, KB), :] = jnp.zeros((KB, 128), BF)
        return 0
    lax.fori_loop(nkb, W // KB, zero, 0)
    dq_ref[0] = (dqt[...] * 0.125).T.astype(BF)

def attn_backward(lengths, qa, da, k, v, KB=512):
    U, _, F, _ = qa.shape; W = k.shape[1]
    return pl.pallas_call(
        functools.partial(bwd_kernel, KB),
        out_shape=(jax.ShapeDtypeStruct((U, F, 128), BF), jax.ShapeDtypeStruct((U, W, 128), BF), jax.ShapeDtypeStruct((U, W, 128), BF)),
        grid_spec=pltpu.PrefetchScalarGridSpec(num_scalar_prefetch=1, grid=(U,),
            in_specs=[pl.BlockSpec((1, 2, F, 128), lambda u, _: (u, 0, 0, 0)), pl.BlockSpec((1, 2, F, 128), lambda u, _: (u, 0, 0, 0)),
                      pl.BlockSpec((1, W, 128), lambda u, _: (u, 0, 0)), pl.BlockSpec((1, W, 128), lambda u, _: (u, 0, 0))],
            out_specs=[pl.BlockSpec((1, F, 128), lambda u, _: (u, 0, 0)), pl.BlockSpec((1, W, 128), lambda u, _: (u, 0, 0)), pl.BlockSpec((1, W, 128), lambda u, _: (u, 0, 0))],
            scratch_shapes=[pltpu.VMEM((128, F), F32)]),
        compiler_params=pltpu.CompilerParams(vmem_limit_bytes=56 * 2**20), name="attn_bwd",
    )(lengths, qa, da, k, v)


def split_bf16(t):
    t1 = t.astype(BF)
    r = t - t1.astype(F32)
    t2 = r.astype(BF)
    t3 = (r - t2.astype(F32)).astype(BF)
    return jnp.stack([t1, t2, t3], axis=-1)


def shards(
    frames,
    time_embed,
    lengths,
    out_cotangent,
    conv_first,
    conv_second,
    conv_skip,
    time_proj,
    w_qkv,
    w_out,
    ff_in,
    ff_out,
    conv_down,
    gains,
    shifts,
    ff_bias,
    snake_logs,
):
    utt_count, frame_count, channels = frames.shape
    inner_width = w_out.shape[0]
    head_dim = inner_width // HEADS
    positions = lax.axis_index("seq") * frame_count + jnp.arange(frame_count)
    frame_mask = (positions[None, :] < lengths[:, None]).astype(jnp.float32)
    counts = lengths.astype(jnp.float32) * (channels // GROUPS)
    column_mask = frame_mask[:, :, None]
    masked_in = frames * column_mask.astype(jnp.bfloat16)
    taps_one, product_one = conv_forward(masked_in, conv_first)
    hidden_one = product_one + shifts[0]
    mean_one, inv_one = group_stats(hidden_one, frame_mask, counts)
    act_one = norm_mish(hidden_one, mean_one, inv_one, gains[0], shifts[1], frame_mask)
    embed_act = mish(time_embed.astype(jnp.float32)).astype(jnp.bfloat16)
    time_shift = jnp.dot(embed_act, time_proj, preferred_element_type=jnp.float32) + shifts[2]
    act_in = ((act_one + time_shift[:, None, :]) * column_mask).astype(jnp.bfloat16)
    taps_two, product_two = conv_forward(act_in, conv_second)
    hidden_two = product_two + shifts[3]
    mean_two, inv_two = group_stats(hidden_two, frame_mask, counts)
    act_two = norm_mish(hidden_two, mean_two, inv_two, gains[1], shifts[4], frame_mask)
    resnet_out = act_two + project(masked_in, conv_skip) + shifts[5]
    normed_one = layer_norm(resnet_out, gains[2], shifts[6]).astype(jnp.bfloat16)
    qkv_rows = project(normed_one, w_qkv).astype(jnp.bfloat16)
    queries = qkv_rows[:, :, :inner_width].reshape(utt_count, frame_count, HEADS, head_dim)
    keys_all, values_all = (
        lax.all_gather(qkv_rows[:, :, inner_width : 2 * inner_width], "seq", axis=1, tiled=True),
        lax.all_gather(qkv_rows[:, :, 2 * inner_width :], "seq", axis=1, tiled=True),
    )
    attended_full, queries_aug = attn_forward(
        lengths, qkv_rows[:, :, :inner_width], keys_all, values_all
    )
    attended = attended_full.astype(BF)
    resid_two = resnet_out + project(attended, w_out) + shifts[7]
    normed_two = layer_norm(resid_two, gains[3], shifts[8]).astype(jnp.bfloat16)
    ff_hidden = project(normed_two, ff_in) + ff_bias
    snaked = snake(ff_hidden, snake_logs).astype(jnp.bfloat16)
    resid_three = resid_two + project(snaked, ff_out) + shifts[9]
    down_in = (resid_three * column_mask).astype(jnp.bfloat16)
    half_len = frame_count // 2
    before_first = from_behind(down_in[:, frame_count - 1 :], "seq", 1)
    frame_pairs = down_in.reshape(utt_count, half_len, 2, channels)
    even_rows = frame_pairs[:, :, 0]
    odd_rows = frame_pairs[:, :, 1]
    before = jnp.concatenate([before_first, odd_rows[:, : half_len - 1]], axis=1)
    taps_down = jnp.concatenate([before, even_rows, odd_rows], axis=2)
    half_mask = frame_mask[:, 0::2][:, :, None]
    lowered = project(taps_down, conv_down.reshape(-1, channels)) + shifts[10]
    layer_out = (lowered * half_mask).astype(jnp.bfloat16)
    grad_lowered = out_cotangent.astype(jnp.float32) * half_mask
    grad_shift_down = jnp.sum(grad_lowered, axis=(0, 1))
    grad_low = grad_lowered.astype(jnp.bfloat16)
    grad_conv_down = weight_grad(taps_down, grad_low).reshape(3, channels, channels)
    grad_taps = project_back(grad_low, conv_down.reshape(-1, channels))
    grad_before = grad_taps[:, :, :channels]
    grad_evens = grad_taps[:, :, channels : 2 * channels]
    grad_odds = grad_taps[:, :, 2 * channels :]
    from_next = from_behind(grad_before[:, 0:1], "seq", -1)
    grad_odds = grad_odds + jnp.concatenate([grad_before[:, 1:], from_next], axis=1)
    grad_down_in = jnp.stack([grad_evens, grad_odds], axis=2).reshape(
        utt_count, frame_count, channels
    )
    grad_three = grad_down_in * column_mask
    grad_shift_ff = jnp.sum(grad_three, axis=(0, 1))
    grad_ff_low = grad_three.astype(jnp.bfloat16)
    grad_ff_out = weight_grad(snaked, grad_ff_low)
    grad_snaked = project_back(grad_ff_low, ff_out)
    outputs, snake_pull = jax.vjp(snake, ff_hidden, snake_logs)
    grad_hidden, grad_snake_logs = snake_pull(grad_snaked)
    grad_ff_bias = jnp.sum(grad_hidden, axis=(0, 1))
    grad_hidden_low = grad_hidden.astype(jnp.bfloat16)
    grad_ff_in = weight_grad(normed_two, grad_hidden_low)
    grad_normed_two = project_back(grad_hidden_low, ff_in)
    outputs, norm_pull_two = jax.vjp(layer_norm, resid_two, gains[3], shifts[8])
    grad_resid_norm, grad_gain_three, grad_shift_three = norm_pull_two(grad_normed_two)
    grad_two = grad_three + grad_resid_norm
    grad_shift_attn = jnp.sum(grad_two, axis=(0, 1))
    grad_attn_low = grad_two.astype(jnp.bfloat16)
    grad_w_out = weight_grad(attended, grad_attn_low)
    grad_attended = project_back(grad_attn_low, w_out).astype(jnp.bfloat16)
    row_terms = jnp.sum(
        (grad_attended.astype(F32) * attended_full).reshape(utt_count, frame_count, HEADS, head_dim),
        axis=-1,
    )
    pieces = split_bf16(row_terms)
    blank = jnp.zeros((utt_count, frame_count, head_dim - 3), BF)
    grad_aug = jnp.stack(
        [
            jnp.concatenate([grad_attended[:, :, :head_dim], pieces[:, :, 0], blank], axis=-1),
            jnp.concatenate([pieces[:, :, 1], blank, grad_attended[:, :, head_dim:]], axis=-1),
        ],
        axis=1,
    )
    grad_queries, key_terms, value_terms = attn_backward(
        lengths, queries_aug, grad_aug, keys_all, values_all
    )
    grad_keys, grad_values = (
        lax.psum_scatter(key_terms, "seq", scatter_dimension=1, tiled=True),
        lax.psum_scatter(value_terms, "seq", scatter_dimension=1, tiled=True),
    )
    grad_qkv = jnp.concatenate(
        [grad_queries, grad_keys, grad_values], axis=2
    )
    grad_w_qkv = weight_grad(normed_one, grad_qkv)
    grad_normed_one = project_back(grad_qkv, w_qkv)
    outputs, norm_pull_one = jax.vjp(layer_norm, resnet_out, gains[2], shifts[6])
    grad_resid_one, grad_gain_two, grad_shift_two = norm_pull_one(grad_normed_one)
    grad_one = grad_two + grad_resid_one
    upper_gains = jnp.stack([grad_gain_two, grad_gain_three])
    upper_shifts = jnp.stack(
        [grad_shift_two, grad_shift_attn, grad_shift_three, grad_shift_ff, grad_shift_down]
    )
    upper_sums = (
        grad_conv_down,
        grad_w_qkv,
        grad_w_out,
        grad_ff_in,
        grad_ff_out,
        grad_ff_bias,
        grad_snake_logs,
        upper_gains,
        upper_shifts,
    )
    grad_shift_skip = jnp.sum(grad_one, axis=(0, 1))
    grad_skip_low = grad_one.astype(jnp.bfloat16)
    grad_conv_skip = weight_grad(masked_in, grad_skip_low)
    grad_masked = project_back(grad_skip_low, conv_skip)
    grad_hidden_two, grad_gain_norm_two, grad_shift_norm_two = norm_backward(
        grad_one, hidden_two, mean_two, inv_two, gains[1], shifts[4], frame_mask, counts
    )
    grad_shift_conv_two = jnp.sum(grad_hidden_two, axis=(0, 1))
    grad_two_low = grad_hidden_two.astype(jnp.bfloat16)
    grad_conv_second = weight_grad(taps_two, grad_two_low).reshape(3, channels, channels)
    grad_act_in = conv_backward(grad_two_low, conv_second) * column_mask
    grad_time = jnp.sum(grad_act_in, axis=1)
    grad_shift_time = jnp.sum(grad_time, axis=0)
    grad_time_proj = jnp.sum(
        embed_act.astype(jnp.float32)[:, :, None] * grad_time[:, None, :], axis=0
    )
    grad_hidden_one, grad_gain_norm_one, grad_shift_norm_one = norm_backward(
        grad_act_in, hidden_one, mean_one, inv_one, gains[0], shifts[1], frame_mask, counts
    )
    grad_shift_conv_one = jnp.sum(grad_hidden_one, axis=(0, 1))
    grad_one_low = grad_hidden_one.astype(jnp.bfloat16)
    grad_conv_first = weight_grad(taps_one, grad_one_low).reshape(3, channels, channels)
    grad_masked = grad_masked + conv_backward(grad_one_low, conv_first)
    grad_frames = grad_masked * column_mask
    lower_gains = jnp.stack([grad_gain_norm_one, grad_gain_norm_two])
    lower_shifts = jnp.stack(
        [
            grad_shift_conv_one,
            grad_shift_norm_one,
            grad_shift_time,
            grad_shift_conv_two,
            grad_shift_norm_two,
            grad_shift_skip,
        ]
    )
    summed = lax.psum(
        (
            grad_conv_first,
            grad_conv_second,
            grad_conv_skip,
            grad_time_proj,
            lower_gains,
            lower_shifts,
            upper_sums[0],
            upper_sums[1],
            upper_sums[2],
            upper_sums[3],
            upper_sums[4],
            upper_sums[5],
            upper_sums[6],
            upper_sums[7],
            upper_sums[8],
        ),
        ("dp", "seq"),
    )
    lower_sums = summed[:6]
    upper_sums = summed[6:]
    grad_gains = jnp.concatenate([lower_sums[4], upper_sums[7]], axis=0)
    grad_shifts = jnp.concatenate([lower_sums[5], upper_sums[8]], axis=0)
    return (
        layer_out,
        grad_frames,
        lower_sums[0],
        lower_sums[1],
        lower_sums[2],
        lower_sums[3],
        upper_sums[1],
        upper_sums[2],
        upper_sums[3],
        upper_sums[4],
        upper_sums[0],
        grad_gains,
        grad_shifts,
        upper_sums[5],
        upper_sums[6],
    )


def solution(mesh):
    in_specs = (
        P("dp", "seq", None),
        P("dp", None),
        P("dp"),
        P("dp", "seq", None),
        P(),
        P(),
        P(),
        P(),
        P(),
        P(),
        P(),
        P(),
        P(),
        P(),
        P(),
        P(),
        P(),
    )
    out_specs = (
        P("dp", "seq", None),
        P("dp", "seq", None),
        P(),
        P(),
        P(),
        P(),
        P(),
        P(),
        P(),
        P(),
        P(),
        P(),
        P(),
        P(),
        P(),
    )
    return jax.shard_map(shards, mesh=mesh, in_specs=in_specs, out_specs=out_specs, check_vma=False)
```

```python
import functools
import math

import jax
import jax.numpy as jnp
from jax import lax
from jax.experimental import pallas as pl
from jax.experimental.pallas import tpu as pltpu
from jax.sharding import PartitionSpec as P

F32, BF = jnp.float32, jnp.bfloat16
NT = (((1,), (1,)), ((), ()))
NN = (((1,), (0,)), ((), ()))
LOG2E = math.log2(math.e)
MESH = pl.DeviceIdType.MESH


def dot(a, b, dn=NN):
    return lax.dot_general(a, b, dn, preferred_element_type=F32)


HEADS = 2
GROUPS = 8


norm_eps = 1e-05


def with_halo(x, sides, width):
    for axis, dim in sides:
        size, length = (lax.axis_size(axis), x.shape[dim])
        up = [(i, (i + 1) % size) for i in range(size - 1)]
        down = [(j, i) for i, j in up]
        last = lax.slice_in_dim(x, length - width, length, axis=dim)
        leading = lax.slice_in_dim(x, 0, width, axis=dim)
        before = lax.ppermute(last, axis, up)
        after = lax.ppermute(leading, axis, down)
        x = jnp.concatenate([before, x, after], axis=dim)
    return x


def from_behind(block, axis, distance):
    devices = range(lax.axis_size(axis))
    route = [(i - distance, i) for i in devices if i - distance in devices]
    return lax.ppermute(block, axis, route)


def mish(values):
    return values * jnp.tanh(jax.nn.softplus(values))


def project(operand, matrix):
    return lax.dot_general(
        operand, matrix, (((operand.ndim - 1,), (0,)), ((), ())), preferred_element_type=jnp.float32
    )


def project_back(grads, matrix):
    return lax.dot_general(
        grads, matrix, (((grads.ndim - 1,), (1,)), ((), ())), preferred_element_type=jnp.float32
    )


def weight_grad(operand, grads):
    flat_operand = operand.reshape(-1, operand.shape[-1])
    flat_grads = grads.reshape(-1, grads.shape[-1])
    return lax.dot_general(
        flat_operand, flat_grads, (((0,), (0,)), ((), ())), preferred_element_type=jnp.float32
    )


def conv_forward(values, weight):
    padded = with_halo(values, (("seq", 1),), 1)
    local_len = values.shape[1]
    stacked = jnp.concatenate(
        [padded[:, 0:local_len], padded[:, 1 : local_len + 1], padded[:, 2 : local_len + 2]], axis=2
    )
    return (stacked, project(stacked, weight.reshape(-1, weight.shape[2])))


def conv_backward(grads, weight):
    padded = with_halo(grads, (("seq", 1),), 1)
    local_len = grads.shape[1]
    stacked = jnp.concatenate(
        [padded[:, 2 : local_len + 2], padded[:, 1 : local_len + 1], padded[:, 0:local_len]], axis=2
    )
    flipped = jnp.transpose(weight, (0, 2, 1)).reshape(-1, weight.shape[1])
    return project(stacked, flipped)


def group_stats(hidden, frame_mask, counts):
    utt_count, frame_count, channels = hidden.shape
    grouped = hidden.reshape(utt_count, frame_count, GROUPS, channels // GROUPS)
    mask_cube = frame_mask[:, :, None, None]
    weighted = grouped * mask_cube
    group_mean = lax.psum(jnp.sum(weighted, axis=(1, 3)), "seq") / counts[:, None]
    centered = grouped - group_mean[:, None, :, None]
    variance = (
        lax.psum(jnp.sum(centered * centered * mask_cube, axis=(1, 3)), "seq") / counts[:, None]
    )
    return (group_mean, lax.rsqrt(variance + norm_eps))


def norm_mish(hidden, group_mean, inv_std, gain, shift, frame_mask):
    utt_count, frame_count, channels = hidden.shape
    grouped = hidden.reshape(utt_count, frame_count, GROUPS, channels // GROUPS)
    normed = ((grouped - group_mean[:, None, :, None]) * inv_std[:, None, :, None]).reshape(
        hidden.shape
    )
    return mish(normed * gain + shift) * frame_mask[:, :, None]


def norm_backward(grads, hidden, group_mean, inv_std, gain, shift, frame_mask, counts):

    def local_piece(hidden_v, mean_v, inv_v, gain_v, shift_v):
        return norm_mish(hidden_v, mean_v, inv_v, gain_v, shift_v, frame_mask)

    outputs, pullback = jax.vjp(local_piece, hidden, group_mean, inv_std, gain, shift)
    grad_hidden, grad_mean, grad_inv, grad_gain, grad_shift = pullback(grads)
    grad_mean, grad_inv = lax.psum((grad_mean, grad_inv), "seq")
    grad_variance = grad_inv * -0.5 * inv_std * inv_std * inv_std
    utt_count, frame_count, channels = hidden.shape
    grouped = hidden.reshape(utt_count, frame_count, GROUPS, channels // GROUPS)
    extra_grad = (
        grad_mean[:, None, :, None]
        + 2.0 * grad_variance[:, None, :, None] * (grouped - group_mean[:, None, :, None])
    ) / counts[:, None, None, None]
    grad_hidden = grad_hidden + (extra_grad * frame_mask[:, :, None, None]).reshape(hidden.shape)
    return (grad_hidden, grad_gain, grad_shift)


def layer_norm(values, gain, shift):
    centered = values - jnp.mean(values, axis=-1, keepdims=True)
    variance = jnp.mean(centered * centered, axis=-1, keepdims=True)
    return centered * lax.rsqrt(variance + norm_eps) * gain + shift


def snake(values, snake_logs):
    return values + jnp.square(jnp.sin(values * jnp.exp(snake_logs[0]))) / (
        jnp.exp(snake_logs[1]) + 1e-09
    )


def fwd_kernel(QB, CK, len_ref, q_ref, k_ref, v_ref, o_ref, qa_ref, kb, vb):
    u = pl.program_id(0)
    W = k_ref.shape[1]; F = q_ref.shape[1]
    L = len_ref[u]
    lane = lax.broadcasted_iota(jnp.int32, (1, 128), 1)
    first = lane < 64
    c = 0.125 * LOG2E
    nch = (L + CK - 1) // CK
    one = jnp.ones((), BF)
    for qi in range(F // QB):
        q = q_ref[0, qi * QB:(qi + 1) * QB, :]
        qh = [jnp.where(first, q, jnp.zeros_like(q)), jnp.where(first, jnp.zeros_like(q), q)]
        def body(j, carry):
            off = pl.multiple_of(j * CK, CK)
            k = k_ref[0, pl.ds(off, CK), :]
            v = v_ref[0, pl.ds(off, CK), :]
            vh = [jnp.where(first, v, one), jnp.where(first, one, v)]
            bias = jnp.where(off + lax.broadcasted_iota(jnp.int32, (1, CK), 1) < L, 0.0, -1e9)
            out = []
            for h in range(2):
                m, acc = carry[h]
                s = dot(qh[h], k, NT) + bias
                mn = jnp.maximum(m, jnp.max(s, axis=1, keepdims=True))
                p = jnp.exp2((s - mn) * c).astype(BF)
                al = jnp.exp2((m - mn) * c)
                acc = acc * al + dot(p, vh[h])
                out.append((mn, acc))
            return tuple(out)
        init = tuple((jnp.full((QB, 1), -1e30, F32), jnp.zeros((QB, 128), F32)) for _ in range(2))
        (m0, a0), (m1, a1) = lax.fori_loop(0, nch, body, init)
        l0 = a0[:, 64:65]; l1 = a1[:, 0:1]
        o_ref[0, qi * QB:(qi + 1) * QB, :] = jnp.where(first, a0 / l0, a1 / l1)
        for h, (m, l) in enumerate(((m0, l0), (m1, l1))):
            t = -(m + jnp.log2(l) / c)
            t1 = t.astype(BF); r = t - t1.astype(F32); t2 = r.astype(BF); r = r - t2.astype(F32); t3 = r.astype(BF)
            base = 64 * (1 - h)
            qa = jnp.where(lane == base, t1, jnp.where(lane == base + 1, t2, jnp.where(lane == base + 2, t3,
                 jnp.where(lane == base + 3, one, qh[h]))))
            qa_ref[0, h, qi * QB:(qi + 1) * QB, :] = qa

def attn_forward(lengths, q, k, v, QB=1024, CK=2048):
    U, F, _ = q.shape; W = k.shape[1]
    return pl.pallas_call(
        functools.partial(fwd_kernel, QB, CK),
        out_shape=(jax.ShapeDtypeStruct((U, F, 128), F32), jax.ShapeDtypeStruct((U, 2, F, 128), BF)),
        grid_spec=pltpu.PrefetchScalarGridSpec(num_scalar_prefetch=1, grid=(U,),
            in_specs=[pl.BlockSpec((1, F, 128), lambda u, _: (u, 0, 0)), pl.BlockSpec((1, W, 128), lambda u, _: (u, 0, 0)), pl.BlockSpec((1, W, 128), lambda u, _: (u, 0, 0))],
            out_specs=[pl.BlockSpec((1, F, 128), lambda u, _: (u, 0, 0)), pl.BlockSpec((1, 2, F, 128), lambda u, _: (u, 0, 0, 0))],
            scratch_shapes=[pltpu.VMEM((2, W, 128), BF), pltpu.VMEM((2, W, 128), BF)]),
        compiler_params=pltpu.CompilerParams(vmem_limit_bytes=56 * 2**20), name="attn_fwd",
    )(lengths, q, k, v)

def bwd_kernel(KB, len_ref, qa_ref, da_ref, k_ref, v_ref, dq_ref, dk_ref, dv_ref, dqt):
    u = pl.program_id(0)
    W = k_ref.shape[1]; F = qa_ref.shape[2]
    L = len_ref[u]
    lane = lax.broadcasted_iota(jnp.int32, (1, 128), 1)
    first = lane < 64
    c = 0.125 * LOG2E
    one = jnp.ones((), BF)
    dqt[...] = jnp.zeros_like(dqt)
    nkb = (L + KB - 1) // KB
    def body(j, _):
        off = pl.multiple_of(j * KB, KB)
        k = k_ref[0, pl.ds(off, KB), :]
        v = v_ref[0, pl.ds(off, KB), :]
        kt = k.T
        bias = jnp.where(off + lax.broadcasted_iota(jnp.int32, (KB, 1), 0) < L, 0.0, -1e9).astype(BF)
        dvs, dks = [], []
        for h in range(2):
            base = 64 * (1 - h)
            if h == 0:
                ka = jnp.where(lane < 64, k, jnp.where(lane == base + 3, bias, jnp.where(lane < base + 3, one, 0 * one)))
                va = jnp.where(lane < 64, v, jnp.where(lane < base + 3, -one, 0 * one))
            else:
                ka = jnp.where(lane >= 64, k, jnp.where(lane == base + 3, bias, jnp.where(lane < base + 3, one, 0 * one)))
                va = jnp.where(lane >= 64, v, jnp.where(lane < base + 3, -one, 0 * one))
            qa = qa_ref[0, h]
            da = da_ref[0, h]
            st = dot(ka, qa, NT)
            p = jnp.exp2(st * c)
            dp = dot(va, da, NT)
            ds = (p * dp).astype(BF)
            dvs.append(dot(p.astype(BF), da))
            dks.append(dot(ds, qa))
            dqt[h * 64:(h + 1) * 64, :] += dot(kt[h * 64:(h + 1) * 64, :], ds)
        dk_ref[0, pl.ds(off, KB), :] = (jnp.where(first, dks[0], dks[1]) * 0.125).astype(BF)
        dv_ref[0, pl.ds(off, KB), :] = jnp.where(first, dvs[0], dvs[1]).astype(BF)
        return 0
    lax.fori_loop(0, nkb, body, 0)
    def zero(j, _):
        off = pl.multiple_of(j * KB, KB)
        dk_ref[0, pl.ds(off, KB), :] = jnp.zeros((KB, 128), BF)
        dv_ref[0, pl.ds(off, KB), :] = jnp.zeros((KB, 128), BF)
        return 0
    lax.fori_loop(nkb, W // KB, zero, 0)
    dq_ref[0] = (dqt[...] * 0.125).T.astype(BF)

def attn_backward(lengths, qa, da, k, v, KB=512):
    U, _, F, _ = qa.shape; W = k.shape[1]
    return pl.pallas_call(
        functools.partial(bwd_kernel, KB),
        out_shape=(jax.ShapeDtypeStruct((U, F, 128), BF), jax.ShapeDtypeStruct((U, W, 128), BF), jax.ShapeDtypeStruct((U, W, 128), BF)),
        grid_spec=pltpu.PrefetchScalarGridSpec(num_scalar_prefetch=1, grid=(U,),
            in_specs=[pl.BlockSpec((1, 2, F, 128), lambda u, _: (u, 0, 0, 0)), pl.BlockSpec((1, 2, F, 128), lambda u, _: (u, 0, 0, 0)),
                      pl.BlockSpec((1, W, 128), lambda u, _: (u, 0, 0)), pl.BlockSpec((1, W, 128), lambda u, _: (u, 0, 0))],
            out_specs=[pl.BlockSpec((1, F, 128), lambda u, _: (u, 0, 0)), pl.BlockSpec((1, W, 128), lambda u, _: (u, 0, 0)), pl.BlockSpec((1, W, 128), lambda u, _: (u, 0, 0))],
            scratch_shapes=[pltpu.VMEM((128, F), F32)]),
        compiler_params=pltpu.CompilerParams(vmem_limit_bytes=56 * 2**20), name="attn_bwd",
    )(lengths, qa, da, k, v)


def split_bf16(t):
    t1 = t.astype(BF)
    r = t - t1.astype(F32)
    t2 = r.astype(BF)
    t3 = (r - t2.astype(F32)).astype(BF)
    return jnp.stack([t1, t2, t3], axis=-1)


def butterfly(axes):
    hops = []
    for axis, size in axes:
        place = lax.axis_index(axis)
        bit = 1
        while bit < size:
            up = (place // bit) % 2
            hops.append((axis, place + bit - 2 * bit * up, up))
            bit *= 2
    return hops


def orders(count):
    plain = list(range(count))
    if count < 5:
        return [plain] * 3
    tail = plain[4:]
    return [plain, [0, 2, 3, 1] + tail, [0, 3, 1, 2] + tail]


def greet(hops):
    barrier = pltpu.get_barrier_semaphore()
    for axis, partner, _ in hops:
        pl.semaphore_signal(barrier, inc=1, device_id={axis: partner}, device_id_type=MESH)
    pl.semaphore_wait(barrier, len(hops))


def reduce_kernel(axes, count, refs_n, *refs):
    ins, small_in = refs[:refs_n], refs[refs_n]
    outs, small_out = refs[refs_n + 1 : 2 * refs_n + 1], refs[2 * refs_n + 1]
    total, sent, got, whole, small_got, sems, small_sems = refs[2 * refs_n + 2 :]
    hops = butterfly(axes)
    greet(hops)
    rows_all = total.shape[0]
    part = rows_all // 3
    plans = orders(count)

    def copy(src, dst, hop, send, recv):
        axis, partner, _ = hops[hop]
        return pltpu.make_async_remote_copy(
            src, dst, send, recv, device_id={axis: partner}, device_id_type=MESH
        )

    row = 0
    for ref in ins:
        rows, columns = ref.shape
        for column in range(0, columns, 128):
            total[pl.ds(row, rows), :] = ref[:, column : column + 128]
            row += rows
    lows = [None] * 3
    small_out[...] = small_in[...]
    for phase in range(count):
        length = part >> (phase + 1)
        copies = []
        for p in range(3):
            hop = plans[p][phase]
            up = hops[hop][2]
            start = p * part if phase == 0 else lows[p]
            keep = pl.multiple_of(start + up * length, 16)
            give = pl.multiple_of(start + (1 - up) * length, 16)
            lows[p] = keep
            at = p * part + part - (part >> phase)
            slot = pl.ds(at, length)
            sent[slot, :] = total[pl.ds(give, length), :].astype(BF)
            sem = p * count + phase
            go = copy(sent.at[slot], got.at[slot], hop, sems.at[0, sem], sems.at[1, sem])
            go.start()
            copies.append((go, slot, keep))
        small = copy(
            small_out, small_got.at[phase], phase, small_sems.at[0, phase], small_sems.at[1, phase]
        )
        small.start()
        for go, slot, keep in copies:
            go.wait()
            total[pl.ds(keep, length), :] += got[slot, :].astype(F32)
        small.wait()
        small_out[...] += small_got[phase]
    length = part >> count
    for p in range(3):
        whole[pl.ds(lows[p], length), :] = total[pl.ds(lows[p], length), :].astype(BF)
    for phase in range(count - 1, -1, -1):
        length = part >> (phase + 1)
        copies = []
        for p in range(3):
            hop = plans[p][phase]
            up = hops[hop][2]
            here = pl.ds(lows[p], length)
            sem = (3 + p) * count + phase
            go = copy(whole.at[here], whole.at[here], hop, sems.at[0, sem], sems.at[1, sem])
            go.start()
            copies.append(go)
            lows[p] = pl.multiple_of(lows[p] - up * length, 16)
        for go in copies:
            go.wait()
    row = 0
    for ref in outs:
        rows, columns = ref.shape
        for column in range(0, columns, 128):
            ref[:, column : column + 128] = whole[pl.ds(row, rows), :].astype(F32)
            row += rows


def reduce_all(mats, small, axes):
    count = sum(size.bit_length() - 1 for _, size in axes)
    rows = sum(m.shape[0] * m.shape[1] // 128 for m in mats)
    unit = 3 * 16 << count
    padded = -(-rows // unit) * unit
    vmem = pl.BlockSpec(memory_space=pltpu.VMEM)
    out = pl.pallas_call(
        functools.partial(reduce_kernel, axes, count, len(mats)),
        out_shape=tuple(jax.ShapeDtypeStruct(m.shape, F32) for m in [*mats, small]),
        in_specs=[vmem] * (len(mats) + 1),
        out_specs=[vmem] * (len(mats) + 1),
        scratch_shapes=[
            pltpu.VMEM((padded, 128), F32),
            pltpu.VMEM((padded, 128), BF),
            pltpu.VMEM((padded, 128), BF),
            pltpu.VMEM((padded, 128), BF),
            pltpu.VMEM((count, *small.shape), F32),
            pltpu.SemaphoreType.DMA((2, 6 * count)),
            pltpu.SemaphoreType.DMA((2, count)),
        ],
        compiler_params=pltpu.CompilerParams(
            collective_id=0, has_side_effects=True, vmem_limit_bytes=58 * 2**20
        ),
        name="reduce_weights",
    )(*mats, small)
    return out[:-1], out[-1]


def shards(
    frames,
    time_embed,
    lengths,
    out_cotangent,
    conv_first,
    conv_second,
    conv_skip,
    time_proj,
    w_qkv,
    w_out,
    ff_in,
    ff_out,
    conv_down,
    gains,
    shifts,
    ff_bias,
    snake_logs,
):
    utt_count, frame_count, channels = frames.shape
    inner_width = w_out.shape[0]
    head_dim = inner_width // HEADS
    positions = lax.axis_index("seq") * frame_count + jnp.arange(frame_count)
    frame_mask = (positions[None, :] < lengths[:, None]).astype(jnp.float32)
    counts = lengths.astype(jnp.float32) * (channels // GROUPS)
    column_mask = frame_mask[:, :, None]
    masked_in = frames * column_mask.astype(jnp.bfloat16)
    taps_one, product_one = conv_forward(masked_in, conv_first)
    hidden_one = product_one + shifts[0]
    mean_one, inv_one = group_stats(hidden_one, frame_mask, counts)
    act_one = norm_mish(hidden_one, mean_one, inv_one, gains[0], shifts[1], frame_mask)
    embed_act = mish(time_embed.astype(jnp.float32)).astype(jnp.bfloat16)
    time_shift = jnp.dot(embed_act, time_proj, preferred_element_type=jnp.float32) + shifts[2]
    act_in = ((act_one + time_shift[:, None, :]) * column_mask).astype(jnp.bfloat16)
    taps_two, product_two = conv_forward(act_in, conv_second)
    hidden_two = product_two + shifts[3]
    mean_two, inv_two = group_stats(hidden_two, frame_mask, counts)
    act_two = norm_mish(hidden_two, mean_two, inv_two, gains[1], shifts[4], frame_mask)
    resnet_out = act_two + project(masked_in, conv_skip) + shifts[5]
    normed_one = layer_norm(resnet_out, gains[2], shifts[6]).astype(jnp.bfloat16)
    qkv_rows = project(normed_one, w_qkv).astype(jnp.bfloat16)
    queries = qkv_rows[:, :, :inner_width].reshape(utt_count, frame_count, HEADS, head_dim)
    keys_all, values_all = (
        lax.all_gather(qkv_rows[:, :, inner_width : 2 * inner_width], "seq", axis=1, tiled=True),
        lax.all_gather(qkv_rows[:, :, 2 * inner_width :], "seq", axis=1, tiled=True),
    )
    attended_full, queries_aug = attn_forward(
        lengths, qkv_rows[:, :, :inner_width], keys_all, values_all
    )
    attended = attended_full.astype(BF)
    resid_two = resnet_out + project(attended, w_out) + shifts[7]
    normed_two = layer_norm(resid_two, gains[3], shifts[8]).astype(jnp.bfloat16)
    ff_hidden = project(normed_two, ff_in) + ff_bias
    snaked = snake(ff_hidden, snake_logs).astype(jnp.bfloat16)
    resid_three = resid_two + project(snaked, ff_out) + shifts[9]
    down_in = (resid_three * column_mask).astype(jnp.bfloat16)
    half_len = frame_count // 2
    before_first = from_behind(down_in[:, frame_count - 1 :], "seq", 1)
    frame_pairs = down_in.reshape(utt_count, half_len, 2, channels)
    even_rows = frame_pairs[:, :, 0]
    odd_rows = frame_pairs[:, :, 1]
    before = jnp.concatenate([before_first, odd_rows[:, : half_len - 1]], axis=1)
    taps_down = jnp.concatenate([before, even_rows, odd_rows], axis=2)
    half_mask = frame_mask[:, 0::2][:, :, None]
    lowered = project(taps_down, conv_down.reshape(-1, channels)) + shifts[10]
    layer_out = (lowered * half_mask).astype(jnp.bfloat16)
    grad_lowered = out_cotangent.astype(jnp.float32) * half_mask
    grad_shift_down = jnp.sum(grad_lowered, axis=(0, 1))
    grad_low = grad_lowered.astype(jnp.bfloat16)
    grad_conv_down = weight_grad(taps_down, grad_low).reshape(3, channels, channels)
    grad_taps = project_back(grad_low, conv_down.reshape(-1, channels))
    grad_before = grad_taps[:, :, :channels]
    grad_evens = grad_taps[:, :, channels : 2 * channels]
    grad_odds = grad_taps[:, :, 2 * channels :]
    from_next = from_behind(grad_before[:, 0:1], "seq", -1)
    grad_odds = grad_odds + jnp.concatenate([grad_before[:, 1:], from_next], axis=1)
    grad_down_in = jnp.stack([grad_evens, grad_odds], axis=2).reshape(
        utt_count, frame_count, channels
    )
    grad_three = grad_down_in * column_mask
    grad_shift_ff = jnp.sum(grad_three, axis=(0, 1))
    grad_ff_low = grad_three.astype(jnp.bfloat16)
    grad_ff_out = weight_grad(snaked, grad_ff_low)
    grad_snaked = project_back(grad_ff_low, ff_out)
    outputs, snake_pull = jax.vjp(snake, ff_hidden, snake_logs)
    grad_hidden, grad_snake_logs = snake_pull(grad_snaked)
    grad_ff_bias = jnp.sum(grad_hidden, axis=(0, 1))
    grad_hidden_low = grad_hidden.astype(jnp.bfloat16)
    grad_ff_in = weight_grad(normed_two, grad_hidden_low)
    grad_normed_two = project_back(grad_hidden_low, ff_in)
    outputs, norm_pull_two = jax.vjp(layer_norm, resid_two, gains[3], shifts[8])
    grad_resid_norm, grad_gain_three, grad_shift_three = norm_pull_two(grad_normed_two)
    grad_two = grad_three + grad_resid_norm
    grad_shift_attn = jnp.sum(grad_two, axis=(0, 1))
    grad_attn_low = grad_two.astype(jnp.bfloat16)
    grad_w_out = weight_grad(attended, grad_attn_low)
    grad_attended = project_back(grad_attn_low, w_out).astype(jnp.bfloat16)
    row_terms = jnp.sum(
        (grad_attended.astype(F32) * attended_full).reshape(utt_count, frame_count, HEADS, head_dim),
        axis=-1,
    )
    pieces = split_bf16(row_terms)
    blank = jnp.zeros((utt_count, frame_count, head_dim - 3), BF)
    grad_aug = jnp.stack(
        [
            jnp.concatenate([grad_attended[:, :, :head_dim], pieces[:, :, 0], blank], axis=-1),
            jnp.concatenate([pieces[:, :, 1], blank, grad_attended[:, :, head_dim:]], axis=-1),
        ],
        axis=1,
    )
    grad_queries, key_terms, value_terms = attn_backward(
        lengths, queries_aug, grad_aug, keys_all, values_all
    )
    grad_keys, grad_values = (
        lax.psum_scatter(key_terms, "seq", scatter_dimension=1, tiled=True),
        lax.psum_scatter(value_terms, "seq", scatter_dimension=1, tiled=True),
    )
    grad_qkv = jnp.concatenate(
        [grad_queries, grad_keys, grad_values], axis=2
    )
    grad_w_qkv = weight_grad(normed_one, grad_qkv)
    grad_normed_one = project_back(grad_qkv, w_qkv)
    outputs, norm_pull_one = jax.vjp(layer_norm, resnet_out, gains[2], shifts[6])
    grad_resid_one, grad_gain_two, grad_shift_two = norm_pull_one(grad_normed_one)
    grad_one = grad_two + grad_resid_one
    upper_gains = jnp.stack([grad_gain_two, grad_gain_three])
    upper_shifts = jnp.stack(
        [grad_shift_two, grad_shift_attn, grad_shift_three, grad_shift_ff, grad_shift_down]
    )
    upper_sums = (
        grad_conv_down,
        grad_w_qkv,
        grad_w_out,
        grad_ff_in,
        grad_ff_out,
        grad_ff_bias,
        grad_snake_logs,
        upper_gains,
        upper_shifts,
    )
    grad_shift_skip = jnp.sum(grad_one, axis=(0, 1))
    grad_skip_low = grad_one.astype(jnp.bfloat16)
    grad_conv_skip = weight_grad(masked_in, grad_skip_low)
    grad_masked = project_back(grad_skip_low, conv_skip)
    grad_hidden_two, grad_gain_norm_two, grad_shift_norm_two = norm_backward(
        grad_one, hidden_two, mean_two, inv_two, gains[1], shifts[4], frame_mask, counts
    )
    grad_shift_conv_two = jnp.sum(grad_hidden_two, axis=(0, 1))
    grad_two_low = grad_hidden_two.astype(jnp.bfloat16)
    grad_conv_second = weight_grad(taps_two, grad_two_low).reshape(3, channels, channels)
    grad_act_in = conv_backward(grad_two_low, conv_second) * column_mask
    grad_time = jnp.sum(grad_act_in, axis=1)
    grad_shift_time = jnp.sum(grad_time, axis=0)
    grad_time_proj = jnp.sum(
        embed_act.astype(jnp.float32)[:, :, None] * grad_time[:, None, :], axis=0
    )
    grad_hidden_one, grad_gain_norm_one, grad_shift_norm_one = norm_backward(
        grad_act_in, hidden_one, mean_one, inv_one, gains[0], shifts[1], frame_mask, counts
    )
    grad_shift_conv_one = jnp.sum(grad_hidden_one, axis=(0, 1))
    grad_one_low = grad_hidden_one.astype(jnp.bfloat16)
    grad_conv_first = weight_grad(taps_one, grad_one_low).reshape(3, channels, channels)
    grad_masked = grad_masked + conv_backward(grad_one_low, conv_first)
    grad_frames = grad_masked * column_mask
    lower_gains = jnp.stack([grad_gain_norm_one, grad_gain_norm_two])
    lower_shifts = jnp.stack(
        [
            grad_shift_conv_one,
            grad_shift_norm_one,
            grad_shift_time,
            grad_shift_conv_two,
            grad_shift_norm_two,
            grad_shift_skip,
        ]
    )
    axes = (("seq", lax.axis_size("seq")), ("dp", lax.axis_size("dp")))
    small = jnp.concatenate(
        [
            *lower_gains,
            *upper_sums[7],
            *lower_shifts,
            *upper_sums[8],
            upper_sums[5],
            *upper_sums[6],
            jnp.zeros((5 * channels,), F32),
        ]
    ).reshape(-1, channels)
    mats = [
        grad_conv_first.reshape(-1, channels),
        grad_conv_second.reshape(-1, channels),
        grad_conv_skip,
        grad_time_proj,
        grad_w_qkv,
        grad_w_out,
        grad_ff_in,
        grad_ff_out,
        grad_conv_down.reshape(-1, channels),
    ]
    summed, small = reduce_all(mats, small, axes)
    hidden = grad_ff_bias.shape[0]
    grad_gains, grad_shifts = small[:4], small[4:15]
    flat = small[15:].reshape(-1)
    lower_sums = (
        summed[0].reshape(conv_first.shape),
        summed[1].reshape(conv_second.shape),
        summed[2],
        summed[3],
    )
    upper_sums = (
        summed[8].reshape(conv_down.shape),
        summed[4],
        summed[5],
        summed[6],
        summed[7],
        flat[:hidden],
        flat[hidden : 3 * hidden].reshape(2, hidden),
    )
    return (
        layer_out,
        grad_frames,
        lower_sums[0],
        lower_sums[1],
        lower_sums[2],
        lower_sums[3],
        upper_sums[1],
        upper_sums[2],
        upper_sums[3],
        upper_sums[4],
        upper_sums[0],
        grad_gains,
        grad_shifts,
        upper_sums[5],
        upper_sums[6],
    )


def solution(mesh):
    in_specs = (
        P("dp", "seq", None),
        P("dp", None),
        P("dp"),
        P("dp", "seq", None),
        P(),
        P(),
        P(),
        P(),
        P(),
        P(),
        P(),
        P(),
        P(),
        P(),
        P(),
        P(),
        P(),
    )
    out_specs = (
        P("dp", "seq", None),
        P("dp", "seq", None),
        P(),
        P(),
        P(),
        P(),
        P(),
        P(),
        P(),
        P(),
        P(),
        P(),
        P(),
        P(),
        P(),
    )
    return jax.shard_map(shards, mesh=mesh, in_specs=in_specs, out_specs=out_specs, check_vma=False)
```

```python
import functools
import math

import jax
import jax.numpy as jnp
from jax import lax
from jax.experimental import pallas as pl
from jax.experimental.pallas import tpu as pltpu
from jax.sharding import PartitionSpec as P

F32, BF = jnp.float32, jnp.bfloat16
NT = (((1,), (1,)), ((), ()))
NN = (((1,), (0,)), ((), ()))
TN = (((0,), (0,)), ((), ()))
LOG2E = math.log2(math.e)
MESH = pl.DeviceIdType.MESH


def dot(a, b, dn=NN):
    return lax.dot_general(a, b, dn, preferred_element_type=F32)


HEADS = 2
GROUPS = 8


norm_eps = 1e-05


def with_halo(x, sides, width):
    for axis, dim in sides:
        size, length = (lax.axis_size(axis), x.shape[dim])
        up = [(i, (i + 1) % size) for i in range(size - 1)]
        down = [(j, i) for i, j in up]
        last = lax.slice_in_dim(x, length - width, length, axis=dim)
        leading = lax.slice_in_dim(x, 0, width, axis=dim)
        before = lax.ppermute(last, axis, up)
        after = lax.ppermute(leading, axis, down)
        x = jnp.concatenate([before, x, after], axis=dim)
    return x


def from_behind(block, axis, distance):
    devices = range(lax.axis_size(axis))
    route = [(i - distance, i) for i in devices if i - distance in devices]
    return lax.ppermute(block, axis, route)


def mish(values):
    return values * jnp.tanh(jax.nn.softplus(values))


def project(operand, matrix):
    return lax.dot_general(
        operand, matrix, (((operand.ndim - 1,), (0,)), ((), ())), preferred_element_type=jnp.float32
    )


def project_back(grads, matrix):
    return lax.dot_general(
        grads, matrix, (((grads.ndim - 1,), (1,)), ((), ())), preferred_element_type=jnp.float32
    )


def weight_grad(operand, grads):
    flat_operand = operand.reshape(-1, operand.shape[-1])
    flat_grads = grads.reshape(-1, grads.shape[-1])
    return lax.dot_general(
        flat_operand, flat_grads, (((0,), (0,)), ((), ())), preferred_element_type=jnp.float32
    )


def conv_forward(values, weight):
    padded = with_halo(values, (("seq", 1),), 1)
    local_len = values.shape[1]
    stacked = jnp.concatenate(
        [padded[:, 0:local_len], padded[:, 1 : local_len + 1], padded[:, 2 : local_len + 2]], axis=2
    )
    return (stacked, project(stacked, weight.reshape(-1, weight.shape[2])))


def conv_backward(grads, weight):
    padded = with_halo(grads, (("seq", 1),), 1)
    local_len = grads.shape[1]
    stacked = jnp.concatenate(
        [padded[:, 2 : local_len + 2], padded[:, 1 : local_len + 1], padded[:, 0:local_len]], axis=2
    )
    flipped = jnp.transpose(weight, (0, 2, 1)).reshape(-1, weight.shape[1])
    return project(stacked, flipped)


def group_stats(hidden, frame_mask, counts):
    utt_count, frame_count, channels = hidden.shape
    grouped = hidden.reshape(utt_count, frame_count, GROUPS, channels // GROUPS)
    mask_cube = frame_mask[:, :, None, None]
    weighted = grouped * mask_cube
    group_mean = lax.psum(jnp.sum(weighted, axis=(1, 3)), "seq") / counts[:, None]
    centered = grouped - group_mean[:, None, :, None]
    variance = (
        lax.psum(jnp.sum(centered * centered * mask_cube, axis=(1, 3)), "seq") / counts[:, None]
    )
    return (group_mean, lax.rsqrt(variance + norm_eps))


def norm_mish(hidden, group_mean, inv_std, gain, shift, frame_mask):
    utt_count, frame_count, channels = hidden.shape
    grouped = hidden.reshape(utt_count, frame_count, GROUPS, channels // GROUPS)
    normed = ((grouped - group_mean[:, None, :, None]) * inv_std[:, None, :, None]).reshape(
        hidden.shape
    )
    return mish(normed * gain + shift) * frame_mask[:, :, None]


def norm_backward(grads, hidden, group_mean, inv_std, gain, shift, frame_mask, counts):

    def local_piece(hidden_v, mean_v, inv_v, gain_v, shift_v):
        return norm_mish(hidden_v, mean_v, inv_v, gain_v, shift_v, frame_mask)

    outputs, pullback = jax.vjp(local_piece, hidden, group_mean, inv_std, gain, shift)
    grad_hidden, grad_mean, grad_inv, grad_gain, grad_shift = pullback(grads)
    grad_mean, grad_inv = lax.psum((grad_mean, grad_inv), "seq")
    grad_variance = grad_inv * -0.5 * inv_std * inv_std * inv_std
    utt_count, frame_count, channels = hidden.shape
    grouped = hidden.reshape(utt_count, frame_count, GROUPS, channels // GROUPS)
    extra_grad = (
        grad_mean[:, None, :, None]
        + 2.0 * grad_variance[:, None, :, None] * (grouped - group_mean[:, None, :, None])
    ) / counts[:, None, None, None]
    grad_hidden = grad_hidden + (extra_grad * frame_mask[:, :, None, None]).reshape(hidden.shape)
    return (grad_hidden, grad_gain, grad_shift)


def layer_norm(values, gain, shift):
    centered = values - jnp.mean(values, axis=-1, keepdims=True)
    variance = jnp.mean(centered * centered, axis=-1, keepdims=True)
    return centered * lax.rsqrt(variance + norm_eps) * gain + shift


SIN_PI = (3.141592580060032, -5.167706879868365, 2.55003139258664, -0.598045264752551, 0.0772203056339658)
COS_PI = (0.9999999534804945, -4.934792860766467, 4.05841196261883, -1.3318805129033002, 0.21969758323424166)


def horner(coefficients, x):
    value = coefficients[-1]
    for coefficient in coefficients[-2::-1]:
        value = value * x + coefficient
    return value


def sin_cos_half_turns(turns):
    part = turns - jnp.round(turns)
    square = part * part
    return part * horner(SIN_PI, square), horner(COS_PI, square)


def row_sum(x):
    return jnp.sum(x, axis=0, keepdims=True)


def lane_mean(x):
    return jnp.mean(x, axis=1, keepdims=True)


def tn(a, b):
    return lax.dot_general(a, b, TN, preferred_element_type=F32)


def middle_kernel(
    RB,
    FC,
    len_ref,
    att_ref,
    res_ref,
    cot_ref,
    next_ref,
    w_out,
    ff_in,
    ff_out,
    conv_down,
    gains,
    shifts,
    ff_bias,
    snake_logs,
    out_ref,
    gtwo_ref,
    aug_ref,
    last_ref,
    gw_out,
    gff_in,
    gff_out,
    gdown,
    gsmall,
    gff_small,
    pairs,
    before_last,
    acc_out,
):
    u, i = pl.program_id(0), pl.program_id(1)
    U, nb = pl.num_programs(0), pl.num_programs(1)
    half = RB // 2
    frames = nb * RB
    length = len_ref[u]
    base = lax.axis_index("seq") * frames
    at = base + i * RB

    @pl.when((u == 0) & (i == 0))
    def _():
        for ref in (gw_out, gff_in, gdown, gsmall, gff_small, acc_out):
            ref[...] = jnp.zeros_like(ref)

    def column_mask(start, rows, step):
        places = start + step * lax.broadcasted_iota(jnp.int32, (rows, 1), 0)
        return jnp.where(places < length, 1.0, 0.0)

    mask = column_mask(at, RB, 1)
    half_mask = column_mask(at, half, 2)
    low_f32 = cot_ref[0, pl.ds(pl.multiple_of(i * half, half), half), :].astype(F32) * half_mask
    gsmall[4:5, :] += row_sum(low_f32)
    low = low_f32.astype(BF)
    follow = jnp.minimum(i * half + half, frames // 2 - 16)
    inner = cot_ref[0, pl.ds(pl.multiple_of(follow, 16), 16), :].astype(F32)[0:1]
    outer = next_ref[0].astype(F32)[0:1]
    after = jnp.where(i == nb - 1, outer, inner) * jnp.where(at + RB < length, 1.0, 0.0)
    row_at = lax.broadcasted_iota(jnp.int32, (half, 1), 0)
    low_next = jnp.where(row_at == half - 1, after, pltpu.roll(low_f32, half - 1, 0)).astype(BF)
    even_grads = dot(low, conv_down[1], NT)
    odd_grads = dot(low, conv_down[2], NT) + dot(low_next, conv_down[0], NT)
    for lanes in (0, 128):
        pairs[lanes // 128, pl.ds(0, half, stride=2), :] = even_grads[:, lanes : lanes + 128]
        pairs[lanes // 128, pl.ds(1, half, stride=2), :] = odd_grads[:, lanes : lanes + 128]
    grad_three = jnp.concatenate([pairs[0], pairs[1]], axis=1) * mask
    gsmall[3:4, :] += row_sum(grad_three)
    grad_low = grad_three.astype(BF)
    attended = att_ref[0]
    att_low = attended.astype(BF)
    resid_two = res_ref[0] + dot(att_low, w_out[...]) + shifts[7:8, :]
    centered = resid_two - lane_mean(resid_two)
    inv = lax.rsqrt(lane_mean(centered * centered) + norm_eps)
    hat = centered * inv
    normed = (hat * gains[3:4, :] + shifts[8:9, :]).astype(BF)
    freq = jnp.exp(snake_logs[0:1, :])
    spread = jnp.exp(snake_logs[1:2, :])
    size = 1.0 / (spread + 1e-09)
    turn = freq * (1.0 / math.pi)
    resid_three = resid_two + shifts[9:10, :]
    grad_normed = jnp.zeros_like(resid_two)
    for c in range(0, ff_bias.shape[1], FC):
        cols = slice(c, c + FC)
        hidden = dot(normed, ff_in[:, cols]) + ff_bias[:, cols]
        sine, cosine = sin_cos_half_turns(hidden * turn[:, cols])
        square = sine * sine
        snaked = (hidden + square * size[:, cols]).astype(BF)
        resid_three = resid_three + dot(snaked, ff_out[cols, :])
        acc_out[:, cols] += tn(grad_low, snaked)
        grad_snaked = dot(grad_low, ff_out[cols, :], NT)
        cross = grad_snaked * (sine * cosine)
        grad_hidden = grad_snaked + cross * (2.0 * size * freq)[:, cols]
        gff_small[0:1, cols] += row_sum(grad_hidden)
        gff_small[1:2, cols] += row_sum(cross * hidden)
        gff_small[2:3, cols] += row_sum(grad_snaked * square)
        hidden_low = grad_hidden.astype(BF)
        gff_in[:, cols] += tn(normed, hidden_low)
        grad_normed = grad_normed + dot(hidden_low, ff_in[:, cols], NT)
    down = (resid_three * mask).astype(BF)
    down_f32 = down.astype(F32)
    for lanes in (0, 128):
        pairs[lanes // 128] = down_f32[:, lanes : lanes + 128]
    even = jnp.concatenate([pairs[j, pl.ds(0, half, stride=2), :] for j in range(2)], axis=1)
    odd = jnp.concatenate([pairs[j, pl.ds(1, half, stride=2), :] for j in range(2)], axis=1)
    first = jnp.where(i == 0, 0.0, before_last[0:1, :])
    before = jnp.where(row_at == 0, first, pltpu.roll(odd, 1, 0)).astype(BF)
    before_last[0:1, :] = odd[half - 1 : half, :]
    last_ref[0] = down[RB - 16 :, :]
    even, odd = even.astype(BF), odd.astype(BF)
    lowered = dot(before, conv_down[0]) + dot(even, conv_down[1]) + dot(odd, conv_down[2])
    out_ref[0] = ((lowered + shifts[10:11, :]) * half_mask).astype(BF)
    gdown[0] += tn(before, low)
    gdown[1] += tn(even, low)
    gdown[2] += tn(odd, low)
    gsmall[0:1, :] += row_sum(grad_normed * hat)
    gsmall[2:3, :] += row_sum(grad_normed)
    grad_hat = grad_normed * gains[3:4, :]
    grad_two = grad_three + inv * (
        grad_hat - lane_mean(grad_hat) - hat * lane_mean(grad_hat * hat)
    )
    gtwo_ref[0] = grad_two
    gsmall[1:2, :] += row_sum(grad_two)
    two_low = grad_two.astype(BF)
    gw_out[...] += tn(att_low, two_low)
    grad_att = dot(two_low, w_out[...], NT).astype(BF)
    terms = grad_att.astype(F32) * attended
    lane = lax.broadcasted_iota(jnp.int32, (1, 128), 1)
    zero = jnp.zeros((), F32)
    for h in range(2):
        mine = (lane >= 64 * h) & (lane < 64 * h + 64)
        term = jnp.sum(jnp.where(mine, terms, zero), axis=1, keepdims=True)
        aug_ref[0, h] = with_pieces(jnp.where(mine, grad_att, jnp.zeros((), BF)), term, lane, h)

    @pl.when((u == U - 1) & (i == nb - 1))
    def _():
        gff_out[...] = acc_out[...].T
        gff_small[1:2, :] = gff_small[1:2, :] * (2.0 * size * freq)
        gff_small[2:3, :] = gff_small[2:3, :] * (-(size * size) * spread)


def with_pieces(block, value, lane, h):
    base = 64 * (1 - h)
    for j in range(3):
        piece = value.astype(BF)
        value = value - piece.astype(F32)
        block = jnp.where(lane == base + j, piece, block)
    return block


def middle(lengths, attended, resnet_out, cotangent, next_rows, w_out, ff_in, ff_out, conv_down, gains, shifts, ff_bias, snake_logs, RB=512, FC=256):
    U, F, C = resnet_out.shape
    inner = attended.shape[2]
    FF = ff_bias.shape[0]
    whole = lambda shape: pl.BlockSpec(shape, lambda u, i, _: (0,) * len(shape))
    rows = lambda n, c: pl.BlockSpec((1, n, c), lambda u, i, _: (u, i, 0))
    per_utt = lambda n, c: pl.BlockSpec((1, n, c), lambda u, i, _: (u, 0, 0))
    sums = ((inner, C), (C, FF), (FF, C), (3, C, C), (8, C), (8, FF))
    return pl.pallas_call(
        functools.partial(middle_kernel, RB, FC),
        out_shape=(
            jax.ShapeDtypeStruct((U, F // 2, C), BF),
            jax.ShapeDtypeStruct((U, F, C), F32),
            jax.ShapeDtypeStruct((U, 2, F, inner), BF),
            jax.ShapeDtypeStruct((U, 16, C), BF),
            *(jax.ShapeDtypeStruct(shape, F32) for shape in sums),
        ),
        grid_spec=pltpu.PrefetchScalarGridSpec(
            num_scalar_prefetch=1,
            grid=(U, F // RB),
            in_specs=[
                rows(RB, inner),
                rows(RB, C),
                per_utt(F // 2, C),
                per_utt(16, C),
                whole((inner, C)),
                whole((C, FF)),
                whole((FF, C)),
                whole((3, C, C)),
                whole(gains.shape),
                whole(shifts.shape),
                whole((1, FF)),
                whole((2, FF)),
            ],
            out_specs=[
                rows(RB // 2, C),
                rows(RB, C),
                pl.BlockSpec((1, 2, RB, inner), lambda u, i, _: (u, 0, i, 0)),
                per_utt(16, C),
                *(whole(shape) for shape in sums),
            ],
            scratch_shapes=[
                pltpu.VMEM((2, RB, 128), F32),
                pltpu.VMEM((8, C), F32),
                pltpu.VMEM((C, FF), F32),
            ],
        ),
        compiler_params=pltpu.CompilerParams(vmem_limit_bytes=56 * 2**20),
        name="middle",
    )(lengths, attended, resnet_out, cotangent, next_rows, w_out, ff_in, ff_out, conv_down, gains, shifts, ff_bias.reshape(1, -1), snake_logs)


def butterfly(axes):
    hops = []
    for axis, size in axes:
        place = lax.axis_index(axis)
        bit = 1
        while bit < size:
            up = (place // bit) % 2
            hops.append((axis, place + bit - 2 * bit * up, up))
            bit *= 2
    return hops


def orders(count):
    plain = list(range(count))
    if count < 5:
        return [plain] * 3
    tail = plain[4:]
    return [plain, [0, 2, 3, 1] + tail, [0, 3, 1, 2] + tail]


def greet(hops):
    barrier = pltpu.get_barrier_semaphore()
    for axis, partner, _ in hops:
        pl.semaphore_signal(barrier, inc=1, device_id={axis: partner}, device_id_type=MESH)
    pl.semaphore_wait(barrier, len(hops))


def reduce_kernel(axes, count, refs_n, *refs):
    ins, small_in = refs[:refs_n], refs[refs_n]
    outs, small_out = refs[refs_n + 1 : 2 * refs_n + 1], refs[2 * refs_n + 1]
    total, sent, got, whole, small_got, sems, small_sems = refs[2 * refs_n + 2 :]
    hops = butterfly(axes)
    greet(hops)
    rows_all = total.shape[0]
    part = rows_all // 3
    plans = orders(count)

    def copy(src, dst, hop, send, recv):
        axis, partner, _ = hops[hop]
        return pltpu.make_async_remote_copy(
            src, dst, send, recv, device_id={axis: partner}, device_id_type=MESH
        )

    row = 0
    for ref in ins:
        rows, columns = ref.shape
        for column in range(0, columns, 128):
            total[pl.ds(row, rows), :] = ref[:, column : column + 128]
            row += rows
    lows = [None] * 3
    small_out[...] = small_in[...]
    for phase in range(count):
        length = part >> (phase + 1)
        copies = []
        for p in range(3):
            hop = plans[p][phase]
            up = hops[hop][2]
            start = p * part if phase == 0 else lows[p]
            keep = pl.multiple_of(start + up * length, 16)
            give = pl.multiple_of(start + (1 - up) * length, 16)
            lows[p] = keep
            at = p * part + part - (part >> phase)
            slot = pl.ds(at, length)
            sent[slot, :] = total[pl.ds(give, length), :].astype(BF)
            sem = p * count + phase
            go = copy(sent.at[slot], got.at[slot], hop, sems.at[0, sem], sems.at[1, sem])
            go.start()
            copies.append((go, slot, keep))
        small = copy(
            small_out, small_got.at[phase], phase, small_sems.at[0, phase], small_sems.at[1, phase]
        )
        small.start()
        for go, slot, keep in copies:
            go.wait()
            total[pl.ds(keep, length), :] += got[slot, :].astype(F32)
        small.wait()
        small_out[...] += small_got[phase]
    length = part >> count
    for p in range(3):
        whole[pl.ds(lows[p], length), :] = total[pl.ds(lows[p], length), :].astype(BF)
    for phase in range(count - 1, -1, -1):
        length = part >> (phase + 1)
        copies = []
        for p in range(3):
            hop = plans[p][phase]
            up = hops[hop][2]
            here = pl.ds(lows[p], length)
            sem = (3 + p) * count + phase
            go = copy(whole.at[here], whole.at[here], hop, sems.at[0, sem], sems.at[1, sem])
            go.start()
            copies.append(go)
            lows[p] = pl.multiple_of(lows[p] - up * length, 16)
        for go in copies:
            go.wait()
    row = 0
    for ref in outs:
        rows, columns = ref.shape
        for column in range(0, columns, 128):
            ref[:, column : column + 128] = whole[pl.ds(row, rows), :].astype(F32)
            row += rows


def reduce_all(mats, small, axes):
    count = sum(size.bit_length() - 1 for _, size in axes)
    rows = sum(m.shape[0] * m.shape[1] // 128 for m in mats)
    unit = 3 * 16 << count
    padded = -(-rows // unit) * unit
    vmem = pl.BlockSpec(memory_space=pltpu.VMEM)
    out = pl.pallas_call(
        functools.partial(reduce_kernel, axes, count, len(mats)),
        out_shape=tuple(jax.ShapeDtypeStruct(m.shape, F32) for m in [*mats, small]),
        in_specs=[vmem] * (len(mats) + 1),
        out_specs=[vmem] * (len(mats) + 1),
        scratch_shapes=[
            pltpu.VMEM((padded, 128), F32),
            pltpu.VMEM((padded, 128), BF),
            pltpu.VMEM((padded, 128), BF),
            pltpu.VMEM((padded, 128), BF),
            pltpu.VMEM((count, *small.shape), F32),
            pltpu.SemaphoreType.DMA((2, 6 * count)),
            pltpu.SemaphoreType.DMA((2, count)),
        ],
        compiler_params=pltpu.CompilerParams(
            collective_id=0, has_side_effects=True, vmem_limit_bytes=58 * 2**20
        ),
        name="reduce_weights",
    )(*mats, small)
    return out[:-1], out[-1]


SCALE2 = 0.125 * LOG2E


def head_lanes(lane, h):
    return (lane >= 64 * h) & (lane < 64 * h + 64)


def greet_seq(me):
    barrier = pltpu.get_barrier_semaphore()
    for flip in (1, 2):
        pl.semaphore_signal(barrier, inc=1, device_id={"seq": flipped(me, flip)}, device_id_type=MESH)
    pl.semaphore_wait(barrier, 2)


def flipped(place, bit):
    return place + bit - 2 * bit * ((place // bit) % 2)


def to_peer(src, dst, sems, place, peer):
    return pltpu.make_async_remote_copy(
        src, dst, sems.at[(0, *place)], sems.at[(1, *place)], device_id={"seq": peer}, device_id_type=MESH
    )


def forward_kernel(len_ref, q_ref, kv_ref, o_ref, qa_ref, all_ref, top, acc, sems):
    U, F, _ = q_ref.shape
    me = lax.axis_index("seq")
    near, far = flipped(me, 1), flipped(me, 2)
    lane = lax.broadcasted_iota(jnp.int32, (1, 128), 1)
    one, zero = jnp.ones((), BF), jnp.zeros((), BF)
    greet_seq(me)

    def hop(kind, u):
        if kind == 0:
            return to_peer(kv_ref.at[u], all_ref.at[1, u], sems, (kind, u), near)
        if kind == 1:
            return to_peer(kv_ref.at[u], all_ref.at[2, u], sems, (kind, u), far)
        return to_peer(all_ref.at[2, u], all_ref.at[3, u], sems, (kind, u), near)

    hop(1, 0).start()
    hop(0, 0).start()
    hop(0, 1).start()
    all_ref[0] = kv_ref[...]
    top[...] = jnp.full(top.shape, -1e30, F32)
    acc[...] = jnp.zeros(acc.shape, F32)

    def step(i, _):
        late = i // 4
        r = (1 - late) * (i // 2) + late * (2 + i % 2)
        u = (1 - late) * (i % 2) + late * ((i - 4) // 2)

        @pl.when(i == 2)
        def _():
            hop(0, 0).wait_recv()

        @pl.when(i == 3)
        def _():
            hop(1, 0).wait_send()
            hop(1, 1).start()
            hop(0, 1).wait_recv()

        @pl.when(i == 4)
        def _():
            hop(1, 0).wait_recv()
            hop(2, 0).start()

        @pl.when(i == 5)
        def _():
            hop(2, 0).wait_recv()

        @pl.when(i == 6)
        def _():
            hop(1, 1).wait_recv()
            hop(2, 1).start()

        @pl.when(i == 7)
        def _():
            hop(2, 1).wait_recv()

        block = xor4(me, r)
        spot = block * F + lax.broadcasted_iota(jnp.int32, (1, F), 1)
        bias = jnp.where(spot < len_ref[u], 0.0, -1e9)
        q = q_ref[u]
        k = all_ref[r, u, :, 0:128]
        v = all_ref[r, u, :, 128:256]
        for h in range(2):
            mine = head_lanes(lane, h)
            s = dot(jnp.where(mine, q, zero), k, NT) + bias
            old = top[u, h, :, 0:1]
            new = jnp.maximum(old, jnp.max(s, axis=1, keepdims=True))
            p = jnp.exp2((s - new) * SCALE2).astype(BF)
            acc[u, h] = acc[u, h] * jnp.exp2((old - new) * SCALE2) + dot(p, jnp.where(mine, v, one))
            top[u, h, :, 0:1] = new
        return 0

    lax.fori_loop(0, 8, step, 0)
    for u in range(U):
        outs = []
        for h in range(2):
            mine = head_lanes(lane, h)
            sums = acc[u, h]
            total = sums[:, 64 * (1 - h) : 64 * (1 - h) + 1]
            outs.append(sums / total)
            log_total = top[u, h, :, 0:1] + jnp.log2(total) / SCALE2
            aug = jnp.where(mine, q_ref[u], jnp.where(lane == 64 * (1 - h) + 3, one, zero))
            qa_ref[u, h] = with_pieces(aug, -log_total, lane, h)
        o_ref[u] = jnp.where(head_lanes(lane, 0), outs[0], outs[1])
    for u in range(U):
        hop(0, u).wait_send()
        hop(2, u).wait_send()
    hop(1, 1).wait_send()


def xor4(place, r):
    low = (place % 2 + r % 2) % 2
    high = (place // 2 + r // 2) % 2
    return 2 * high + low


def attend(lengths, q, kv):
    U, F, _ = q.shape
    vmem = pl.BlockSpec(memory_space=pltpu.VMEM)
    return pl.pallas_call(
        forward_kernel,
        out_shape=(
            jax.ShapeDtypeStruct((U, F, 128), F32),
            jax.ShapeDtypeStruct((U, 2, F, 128), BF),
            jax.ShapeDtypeStruct((4, U, F, 256), BF),
        ),
        in_specs=[pl.BlockSpec(memory_space=pltpu.SMEM), vmem, vmem],
        out_specs=[vmem] * 3,
        scratch_shapes=[
            pltpu.VMEM((U, 2, F, 128), F32),
            pltpu.VMEM((U, 2, F, 128), F32),
            pltpu.SemaphoreType.DMA((2, 3, U)),
        ],
        compiler_params=pltpu.CompilerParams(
            collective_id=1, has_side_effects=True, vmem_limit_bytes=56 * 2**20
        ),
        name="attend",
    )(lengths, q, kv)


def backward_kernel(KB, len_ref, qa_ref, da_ref, all_ref, grad_ref, dqt, part, sent, got, sems):
    U, _, F, _ = qa_ref.shape
    me = lax.axis_index("seq")
    near, far = flipped(me, 1), flipped(me, 2)
    lane = lax.broadcasted_iota(jnp.int32, (1, 128), 1)
    one, zero = jnp.ones((), BF), jnp.zeros((), BF)
    greet_seq(me)
    dqt[...] = jnp.zeros(dqt.shape, F32)

    def hop(kind, u):
        peer = far if kind == 1 else near
        return to_peer(sent.at[kind, u], got.at[kind, u], sems, (kind, u), peer)

    def step(i, _):
        late = i // 4
        r = (1 - late) * (3 - i % 2) + late * (1 - (i - 4) // 2)
        u = (1 - late) * ((i // 2) % 2) + late * (i % 2)
        block = xor4(me, r)

        def tile(j, _):
            off = pl.multiple_of(j * KB, KB)
            here = pl.ds(off, KB)
            k = all_ref[r, u, here, 0:128]
            v = all_ref[r, u, here, 128:256]
            kt = k.T
            spot = block * F + off + lax.broadcasted_iota(jnp.int32, (KB, 1), 0)
            bias = jnp.where(spot < len_ref[u], 0.0, -1e9).astype(BF)
            dks, dvs = [], []
            for h in range(2):
                mine = head_lanes(lane, h)
                base = 64 * (1 - h)
                extra = (lane >= base) & (lane < base + 3)
                ka = jnp.where(mine, k, jnp.where(extra, one, jnp.where(lane == base + 3, bias, zero)))
                va = jnp.where(mine, v, jnp.where(extra, -one, zero))
                qa = qa_ref[u, h]
                da = da_ref[u, h]
                p = jnp.exp2(dot(ka, qa, NT) * SCALE2)
                ds = (p * dot(va, da, NT)).astype(BF)
                dvs.append(dot(p.astype(BF), da))
                dks.append(dot(ds, qa))
                rows = slice(64 * h, 64 * h + 64)
                dqt[u, rows, :] += dot(kt[rows, :], ds)
            part[here, 0:128] = jnp.where(head_lanes(lane, 0), dks[0], dks[1]) * 0.125
            part[here, 128:256] = jnp.where(head_lanes(lane, 0), dvs[0], dvs[1])
            return 0

        lax.fori_loop(0, F // KB, tile, 0)

        @pl.when(r == 3)
        def _():
            sent[0, u] = part[...].astype(BF)
            hop(0, u).start()

        @pl.when(r == 2)
        def _():
            hop(0, u).wait_recv()
            sent[1, u] = (part[...] + got[0, u].astype(F32)).astype(BF)
            hop(1, u).start()

        @pl.when(r == 1)
        def _():
            sent[2, u] = part[...].astype(BF)
            hop(2, u).start()

        @pl.when(r == 0)
        def _():
            hop(1, u).wait_recv()
            hop(2, u).wait_recv()
            whole = part[...] + got[1, u].astype(F32) + got[2, u].astype(F32)
            grad_ref[u, :, 128:384] = whole.astype(BF)
            grad_ref[u, :, 0:128] = (dqt[u] * 0.125).T.astype(BF)

        return 0

    lax.fori_loop(0, 8, step, 0)
    for kind in range(3):
        for u in range(U):
            hop(kind, u).wait_send()


def attend_back(lengths, qa, da, kv_all, KB=512):
    U, _, F, _ = qa.shape
    vmem = pl.BlockSpec(memory_space=pltpu.VMEM)
    return pl.pallas_call(
        functools.partial(backward_kernel, KB),
        out_shape=jax.ShapeDtypeStruct((U, F, 384), BF),
        in_specs=[pl.BlockSpec(memory_space=pltpu.SMEM), vmem, vmem, vmem],
        out_specs=vmem,
        scratch_shapes=[
            pltpu.VMEM((U, 128, F), F32),
            pltpu.VMEM((F, 256), F32),
            pltpu.VMEM((3, U, F, 256), BF),
            pltpu.VMEM((3, U, F, 256), BF),
            pltpu.SemaphoreType.DMA((2, 3, U)),
        ],
        compiler_params=pltpu.CompilerParams(
            collective_id=2, has_side_effects=True, vmem_limit_bytes=56 * 2**20
        ),
        name="attend_back",
    )(lengths, qa, da, kv_all)


def shards(
    frames,
    time_embed,
    lengths,
    out_cotangent,
    conv_first,
    conv_second,
    conv_skip,
    time_proj,
    w_qkv,
    w_out,
    ff_in,
    ff_out,
    conv_down,
    gains,
    shifts,
    ff_bias,
    snake_logs,
):
    utt_count, frame_count, channels = frames.shape
    inner_width = w_out.shape[0]
    positions = lax.axis_index("seq") * frame_count + jnp.arange(frame_count)
    frame_mask = (positions[None, :] < lengths[:, None]).astype(jnp.float32)
    counts = lengths.astype(jnp.float32) * (channels // GROUPS)
    column_mask = frame_mask[:, :, None]
    masked_in = frames * column_mask.astype(jnp.bfloat16)
    taps_one, product_one = conv_forward(masked_in, conv_first)
    hidden_one = product_one + shifts[0]
    mean_one, inv_one = group_stats(hidden_one, frame_mask, counts)
    act_one = norm_mish(hidden_one, mean_one, inv_one, gains[0], shifts[1], frame_mask)
    embed_act = mish(time_embed.astype(jnp.float32)).astype(jnp.bfloat16)
    time_shift = jnp.dot(embed_act, time_proj, preferred_element_type=jnp.float32) + shifts[2]
    act_in = ((act_one + time_shift[:, None, :]) * column_mask).astype(jnp.bfloat16)
    taps_two, product_two = conv_forward(act_in, conv_second)
    hidden_two = product_two + shifts[3]
    mean_two, inv_two = group_stats(hidden_two, frame_mask, counts)
    act_two = norm_mish(hidden_two, mean_two, inv_two, gains[1], shifts[4], frame_mask)
    resnet_out = act_two + project(masked_in, conv_skip) + shifts[5]
    normed_one = layer_norm(resnet_out, gains[2], shifts[6]).astype(jnp.bfloat16)
    qkv_rows = project(normed_one, w_qkv).astype(jnp.bfloat16)
    attended_full, queries_aug, kv_all = attend(
        lengths, qkv_rows[:, :, :inner_width], qkv_rows[:, :, inner_width:]
    )
    next_rows = from_behind(out_cotangent[:, 0:16], "seq", -1)
    (
        layer_out,
        grad_two,
        grad_aug,
        last_rows,
        grad_w_out,
        grad_ff_in,
        grad_ff_out,
        grad_conv_down,
        mid_small,
        ff_small,
    ) = middle(
        lengths,
        attended_full,
        resnet_out,
        out_cotangent,
        next_rows,
        w_out,
        ff_in,
        ff_out,
        conv_down,
        gains,
        shifts,
        ff_bias,
        snake_logs,
    )
    before_first = from_behind(last_rows, "seq", 1)[:, 15:16]
    half_mask = frame_mask[:, 0:1][:, :, None]
    first_low = out_cotangent[:, 0:1].astype(F32) * half_mask
    first_out = layer_out[:, 0:1].astype(F32) + project(before_first, conv_down[0]) * half_mask
    layer_out = layer_out.at[:, 0:1].set(first_out.astype(BF))
    grad_conv_down = grad_conv_down.at[0].add(weight_grad(before_first, first_low.astype(BF)))
    grad_gain_three, grad_shift_attn, grad_shift_three, grad_shift_ff, grad_shift_down = mid_small[:5]
    grad_ff_bias, grad_snake_logs = ff_small[0], ff_small[1:3]
    grad_qkv = attend_back(lengths, queries_aug, grad_aug, kv_all)
    grad_w_qkv = weight_grad(normed_one, grad_qkv)
    grad_normed_one = project_back(grad_qkv, w_qkv)
    outputs, norm_pull_one = jax.vjp(layer_norm, resnet_out, gains[2], shifts[6])
    grad_resid_one, grad_gain_two, grad_shift_two = norm_pull_one(grad_normed_one)
    grad_one = grad_two + grad_resid_one
    upper_gains = jnp.stack([grad_gain_two, grad_gain_three])
    upper_shifts = jnp.stack(
        [grad_shift_two, grad_shift_attn, grad_shift_three, grad_shift_ff, grad_shift_down]
    )
    upper_sums = (
        grad_conv_down,
        grad_w_qkv,
        grad_w_out,
        grad_ff_in,
        grad_ff_out,
        grad_ff_bias,
        grad_snake_logs,
        upper_gains,
        upper_shifts,
    )
    grad_shift_skip = jnp.sum(grad_one, axis=(0, 1))
    grad_skip_low = grad_one.astype(jnp.bfloat16)
    grad_conv_skip = weight_grad(masked_in, grad_skip_low)
    grad_masked = project_back(grad_skip_low, conv_skip)
    grad_hidden_two, grad_gain_norm_two, grad_shift_norm_two = norm_backward(
        grad_one, hidden_two, mean_two, inv_two, gains[1], shifts[4], frame_mask, counts
    )
    grad_shift_conv_two = jnp.sum(grad_hidden_two, axis=(0, 1))
    grad_two_low = grad_hidden_two.astype(jnp.bfloat16)
    grad_conv_second = weight_grad(taps_two, grad_two_low).reshape(3, channels, channels)
    grad_act_in = conv_backward(grad_two_low, conv_second) * column_mask
    grad_time = jnp.sum(grad_act_in, axis=1)
    grad_shift_time = jnp.sum(grad_time, axis=0)
    grad_time_proj = jnp.sum(
        embed_act.astype(jnp.float32)[:, :, None] * grad_time[:, None, :], axis=0
    )
    grad_hidden_one, grad_gain_norm_one, grad_shift_norm_one = norm_backward(
        grad_act_in, hidden_one, mean_one, inv_one, gains[0], shifts[1], frame_mask, counts
    )
    grad_shift_conv_one = jnp.sum(grad_hidden_one, axis=(0, 1))
    grad_one_low = grad_hidden_one.astype(jnp.bfloat16)
    grad_conv_first = weight_grad(taps_one, grad_one_low).reshape(3, channels, channels)
    grad_masked = grad_masked + conv_backward(grad_one_low, conv_first)
    grad_frames = grad_masked * column_mask
    lower_gains = jnp.stack([grad_gain_norm_one, grad_gain_norm_two])
    lower_shifts = jnp.stack(
        [
            grad_shift_conv_one,
            grad_shift_norm_one,
            grad_shift_time,
            grad_shift_conv_two,
            grad_shift_norm_two,
            grad_shift_skip,
        ]
    )
    axes = (("seq", lax.axis_size("seq")), ("dp", lax.axis_size("dp")))
    small = jnp.concatenate(
        [
            *lower_gains,
            *upper_sums[7],
            *lower_shifts,
            *upper_sums[8],
            upper_sums[5],
            *upper_sums[6],
            jnp.zeros((5 * channels,), F32),
        ]
    ).reshape(-1, channels)
    mats = [
        grad_conv_first.reshape(-1, channels),
        grad_conv_second.reshape(-1, channels),
        grad_conv_skip,
        grad_time_proj,
        grad_w_qkv,
        grad_w_out,
        grad_ff_in,
        grad_ff_out,
        grad_conv_down.reshape(-1, channels),
    ]
    summed, small = reduce_all(mats, small, axes)
    hidden = grad_ff_bias.shape[0]
    grad_gains, grad_shifts = small[:4], small[4:15]
    flat = small[15:].reshape(-1)
    lower_sums = (
        summed[0].reshape(conv_first.shape),
        summed[1].reshape(conv_second.shape),
        summed[2],
        summed[3],
    )
    upper_sums = (
        summed[8].reshape(conv_down.shape),
        summed[4],
        summed[5],
        summed[6],
        summed[7],
        flat[:hidden],
        flat[hidden : 3 * hidden].reshape(2, hidden),
    )
    return (
        layer_out,
        grad_frames,
        lower_sums[0],
        lower_sums[1],
        lower_sums[2],
        lower_sums[3],
        upper_sums[1],
        upper_sums[2],
        upper_sums[3],
        upper_sums[4],
        upper_sums[0],
        grad_gains,
        grad_shifts,
        upper_sums[5],
        upper_sums[6],
    )


def solution(mesh):
    in_specs = (
        P("dp", "seq", None),
        P("dp", None),
        P("dp"),
        P("dp", "seq", None),
        P(),
        P(),
        P(),
        P(),
        P(),
        P(),
        P(),
        P(),
        P(),
        P(),
        P(),
        P(),
        P(),
    )
    out_specs = (
        P("dp", "seq", None),
        P("dp", "seq", None),
        P(),
        P(),
        P(),
        P(),
        P(),
        P(),
        P(),
        P(),
        P(),
        P(),
        P(),
        P(),
        P(),
    )
    return jax.shard_map(shards, mesh=mesh, in_specs=in_specs, out_specs=out_specs, check_vma=False)
```

```python
import functools
import math

import jax
import jax.numpy as jnp
from jax import lax
from jax.experimental import pallas as pl
from jax.experimental.pallas import tpu as pltpu
from jax.sharding import PartitionSpec as P

F32, BF = jnp.float32, jnp.bfloat16
NT = (((1,), (1,)), ((), ()))
NN = (((1,), (0,)), ((), ()))
TN = (((0,), (0,)), ((), ()))
MESH = pl.DeviceIdType.MESH
EDGE = 16


def dot(a, b, dn=NN):
    return lax.dot_general(a, b, dn, preferred_element_type=F32)


HEADS = 2
GROUPS = 8


norm_eps = 1e-05


def from_behind(block, axis, distance):
    devices = range(lax.axis_size(axis))
    route = [(i - distance, i) for i in devices if i - distance in devices]
    return lax.ppermute(block, axis, route)


def project(operand, matrix):
    return lax.dot_general(
        operand, matrix, (((operand.ndim - 1,), (0,)), ((), ())), preferred_element_type=jnp.float32
    )


def weight_grad(operand, grads):
    flat_operand = operand.reshape(-1, operand.shape[-1])
    flat_grads = grads.reshape(-1, grads.shape[-1])
    return lax.dot_general(
        flat_operand, flat_grads, (((0,), (0,)), ((), ())), preferred_element_type=jnp.float32
    )


SIN_PI = (3.141592580060032, -5.167706879868365, 2.55003139258664, -0.598045264752551, 0.0772203056339658)
COS_PI = (0.9999999534804945, -4.934792860766467, 4.05841196261883, -1.3318805129033002, 0.21969758323424166)


def horner(coefficients, x):
    value = coefficients[-1]
    for coefficient in coefficients[-2::-1]:
        value = value * x + coefficient
    return value


def sin_cos_half_turns(turns):
    part = turns - jnp.round(turns)
    square = part * part
    return part * horner(SIN_PI, square), horner(COS_PI, square)


def row_sum(x):
    return jnp.sum(x, axis=0, keepdims=True)


def lane_mean(x):
    return jnp.mean(x, axis=1, keepdims=True)


def tn(a, b):
    return lax.dot_general(a, b, TN, preferred_element_type=F32)


def middle_kernel(
    RB,
    FC,
    len_ref,
    att_ref,
    res_ref,
    cot_ref,
    next_ref,
    w_out,
    ff_in,
    ff_out,
    conv_down,
    gains,
    shifts,
    ff_bias,
    snake_logs,
    out_ref,
    gtwo_ref,
    aug_ref,
    last_ref,
    gw_out,
    gff_in,
    gff_out,
    gdown,
    gsmall,
    gff_small,
    pairs,
    before_last,
    acc_out,
):
    u, i = pl.program_id(0), pl.program_id(1)
    U, nb = pl.num_programs(0), pl.num_programs(1)
    half = RB // 2
    frames = nb * RB
    length = len_ref[u]
    base = lax.axis_index("seq") * frames
    at = base + i * RB

    @pl.when((u == 0) & (i == 0))
    def _():
        for ref in (gw_out, gff_in, gdown, gsmall, gff_small, acc_out):
            ref[...] = jnp.zeros_like(ref)

    def column_mask(start, rows, step):
        places = start + step * lax.broadcasted_iota(jnp.int32, (rows, 1), 0)
        return jnp.where(places < length, 1.0, 0.0)

    mask = column_mask(at, RB, 1)
    half_mask = column_mask(at, half, 2)
    low_f32 = cot_ref[0, pl.ds(pl.multiple_of(i * half, half), half), :].astype(F32) * half_mask
    gsmall[4:5, :] += row_sum(low_f32)
    low = low_f32.astype(BF)
    follow = jnp.minimum(i * half + half, frames // 2 - 16)
    inner = cot_ref[0, pl.ds(pl.multiple_of(follow, 16), 16), :].astype(F32)[0:1]
    outer = next_ref[0].astype(F32)[0:1]
    after = jnp.where(i == nb - 1, outer, inner) * jnp.where(at + RB < length, 1.0, 0.0)
    row_at = lax.broadcasted_iota(jnp.int32, (half, 1), 0)
    low_next = jnp.where(row_at == half - 1, after, pltpu.roll(low_f32, half - 1, 0)).astype(BF)
    even_grads = dot(low, conv_down[1], NT)
    odd_grads = dot(low, conv_down[2], NT) + dot(low_next, conv_down[0], NT)
    for lanes in (0, 128):
        pairs[lanes // 128, pl.ds(0, half, stride=2), :] = even_grads[:, lanes : lanes + 128]
        pairs[lanes // 128, pl.ds(1, half, stride=2), :] = odd_grads[:, lanes : lanes + 128]
    grad_three = jnp.concatenate([pairs[0], pairs[1]], axis=1) * mask
    gsmall[3:4, :] += row_sum(grad_three)
    grad_low = grad_three.astype(BF)
    attended = att_ref[0]
    att_low = attended.astype(BF)
    resid_two = res_ref[0] + dot(att_low, w_out[...]) + shifts[7:8, :]
    centered = resid_two - lane_mean(resid_two)
    inv = lax.rsqrt(lane_mean(centered * centered) + norm_eps)
    hat = centered * inv
    normed = (hat * gains[3:4, :] + shifts[8:9, :]).astype(BF)
    freq = jnp.exp(snake_logs[0:1, :])
    spread = jnp.exp(snake_logs[1:2, :])
    size = 1.0 / (spread + 1e-09)
    turn = freq * (1.0 / math.pi)
    resid_three = resid_two + shifts[9:10, :]
    grad_normed = jnp.zeros_like(resid_two)
    for c in range(0, ff_bias.shape[1], FC):
        cols = slice(c, c + FC)
        hidden = dot(normed, ff_in[:, cols]) + ff_bias[:, cols]
        sine, cosine = sin_cos_half_turns(hidden * turn[:, cols])
        square = sine * sine
        snaked = (hidden + square * size[:, cols]).astype(BF)
        resid_three = resid_three + dot(snaked, ff_out[cols, :])
        acc_out[:, cols] += tn(grad_low, snaked)
        grad_snaked = dot(grad_low, ff_out[cols, :], NT)
        cross = grad_snaked * (sine * cosine)
        grad_hidden = grad_snaked + cross * (2.0 * size * freq)[:, cols]
        gff_small[0:1, cols] += row_sum(grad_hidden)
        gff_small[1:2, cols] += row_sum(cross * hidden)
        gff_small[2:3, cols] += row_sum(grad_snaked * square)
        hidden_low = grad_hidden.astype(BF)
        gff_in[:, cols] += tn(normed, hidden_low)
        grad_normed = grad_normed + dot(hidden_low, ff_in[:, cols], NT)
    down = (resid_three * mask).astype(BF)
    down_f32 = down.astype(F32)
    for lanes in (0, 128):
        pairs[lanes // 128] = down_f32[:, lanes : lanes + 128]
    even = jnp.concatenate([pairs[j, pl.ds(0, half, stride=2), :] for j in range(2)], axis=1)
    odd = jnp.concatenate([pairs[j, pl.ds(1, half, stride=2), :] for j in range(2)], axis=1)
    first = jnp.where(i == 0, 0.0, before_last[0:1, :])
    before = jnp.where(row_at == 0, first, pltpu.roll(odd, 1, 0)).astype(BF)
    before_last[0:1, :] = odd[half - 1 : half, :]
    last_ref[0] = down[RB - 16 :, :]
    even, odd = even.astype(BF), odd.astype(BF)
    lowered = dot(before, conv_down[0]) + dot(even, conv_down[1]) + dot(odd, conv_down[2])
    out_ref[0] = ((lowered + shifts[10:11, :]) * half_mask).astype(BF)
    gdown[0] += tn(before, low)
    gdown[1] += tn(even, low)
    gdown[2] += tn(odd, low)
    gsmall[0:1, :] += row_sum(grad_normed * hat)
    gsmall[2:3, :] += row_sum(grad_normed)
    grad_hat = grad_normed * gains[3:4, :]
    grad_two = grad_three + inv * (
        grad_hat - lane_mean(grad_hat) - hat * lane_mean(grad_hat * hat)
    )
    gtwo_ref[0] = grad_two
    gsmall[1:2, :] += row_sum(grad_two)
    two_low = grad_two.astype(BF)
    gw_out[...] += tn(att_low, two_low)
    grad_att = dot(two_low, w_out[...], NT).astype(BF)
    terms = grad_att.astype(F32) * attended
    lane = lax.broadcasted_iota(jnp.int32, (1, 128), 1)
    zero = jnp.zeros((), F32)
    for h in range(2):
        mine = (lane >= 64 * h) & (lane < 64 * h + 64)
        term = jnp.sum(jnp.where(mine, terms, zero), axis=1, keepdims=True)
        aug_ref[0, h] = with_pieces(jnp.where(mine, grad_att, jnp.zeros((), BF)), term, lane, h)

    @pl.when((u == U - 1) & (i == nb - 1))
    def _():
        gff_out[...] = acc_out[...].T
        gff_small[1:2, :] = gff_small[1:2, :] * (2.0 * size * freq)
        gff_small[2:3, :] = gff_small[2:3, :] * (-(size * size) * spread)


def with_pieces(block, value, lane, h):
    base = 64 * (1 - h)
    for j in range(3):
        piece = value.astype(BF)
        value = value - piece.astype(F32)
        block = jnp.where(lane == base + j, piece, block)
    return block


def middle(lengths, attended, resnet_out, cotangent, next_rows, w_out, ff_in, ff_out, conv_down, gains, shifts, ff_bias, snake_logs, RB=512, FC=256):
    U, F, C = resnet_out.shape
    inner = attended.shape[2]
    FF = ff_bias.shape[0]
    whole = lambda shape: pl.BlockSpec(shape, lambda u, i, _: (0,) * len(shape))
    rows = lambda n, c: pl.BlockSpec((1, n, c), lambda u, i, _: (u, i, 0))
    per_utt = lambda n, c: pl.BlockSpec((1, n, c), lambda u, i, _: (u, 0, 0))
    sums = ((inner, C), (C, FF), (FF, C), (3, C, C), (8, C), (8, FF))
    return pl.pallas_call(
        functools.partial(middle_kernel, RB, FC),
        out_shape=(
            jax.ShapeDtypeStruct((U, F // 2, C), BF),
            jax.ShapeDtypeStruct((U, F, C), F32),
            jax.ShapeDtypeStruct((U, 2, F, inner), BF),
            jax.ShapeDtypeStruct((U, 16, C), BF),
            *(jax.ShapeDtypeStruct(shape, F32) for shape in sums),
        ),
        grid_spec=pltpu.PrefetchScalarGridSpec(
            num_scalar_prefetch=1,
            grid=(U, F // RB),
            in_specs=[
                rows(RB, inner),
                rows(RB, C),
                per_utt(F // 2, C),
                per_utt(16, C),
                whole((inner, C)),
                whole((C, FF)),
                whole((FF, C)),
                whole((3, C, C)),
                whole(gains.shape),
                whole(shifts.shape),
                whole((1, FF)),
                whole((2, FF)),
            ],
            out_specs=[
                rows(RB // 2, C),
                rows(RB, C),
                pl.BlockSpec((1, 2, RB, inner), lambda u, i, _: (u, 0, i, 0)),
                per_utt(16, C),
                *(whole(shape) for shape in sums),
            ],
            scratch_shapes=[
                pltpu.VMEM((2, RB, 128), F32),
                pltpu.VMEM((8, C), F32),
                pltpu.VMEM((C, FF), F32),
            ],
        ),
        compiler_params=pltpu.CompilerParams(vmem_limit_bytes=56 * 2**20),
        name="middle",
    )(lengths, attended, resnet_out, cotangent, next_rows, w_out, ff_in, ff_out, conv_down, gains, shifts, ff_bias.reshape(1, -1), snake_logs)


def butterfly(axes):
    hops = []
    for axis, size in axes:
        place = lax.axis_index(axis)
        bit = 1
        while bit < size:
            up = (place // bit) % 2
            hops.append((axis, place + bit - 2 * bit * up, up))
            bit *= 2
    return hops


def bits_of(axes):
    return sum(size.bit_length() - 1 for _, size in axes)


def stages_of(axes):
    stages = []
    for axis, size in axes:
        stride = 1
        while stride < size:
            radix = min(2 if axis == "seq" else 8, size // stride)
            place = lax.axis_index(axis)
            digit = (place // stride) % radix
            peers = [place + ((digit + m) % radix - digit) * stride for m in range(1, radix)]
            stages.append((axis, radix, digit, peers))
            stride *= radix
    return stages


def padded_rows(rows, axes):
    unit = EDGE << bits_of(axes)
    return -(-rows // unit) * unit


def packed_rows(mats):
    return sum(m.shape[0] * m.shape[1] // 128 for m in mats)


def greet_stages(stages, extra=()):
    barrier = pltpu.get_barrier_semaphore()
    met = [(axis, peer) for axis, _, _, peers in stages for peer in peers] + list(extra)
    for axis, peer in met:
        pl.semaphore_signal(barrier, inc=1, device_id={axis: peer}, device_id_type=MESH)
    pl.semaphore_wait(barrier, len(met))


def hop_copy(hop, src, dst, sems, place):
    axis, partner, _ = hop
    return pltpu.make_async_remote_copy(
        src, dst, sems.at[(0, *place)], sems.at[(1, *place)], device_id={axis: partner}, device_id_type=MESH
    )


def pack(total, mats):
    row = 0
    for ref in mats:
        rows, columns = ref.shape
        for column in range(0, columns, 128):
            total[pl.ds(row, rows), :] = ref[:, column : column + 128]
            row += rows
    if row < total.shape[0]:
        total[pl.ds(row, total.shape[0] - row), :] = jnp.zeros((total.shape[0] - row, 128), F32)


def shares_of(stages, rows):
    low, length, shares = 0, rows, []
    for _, radix, digit, _ in stages:
        shares.append((low, length, length // radix))
        length //= radix
        low = pl.multiple_of(low + digit * length, EDGE)
    return shares, low


def halving_steps(stages, total, sent, got, ends, sems):
    rows = total.shape[0]
    shares, _ = shares_of(stages, rows)

    def copies(s):
        axis, radix, _, peers = stages[s]
        _, before, length = shares[s]
        for m, peer in enumerate(peers):
            slot = pl.ds(rows - before + m * length, length)
            yield m, slot, hop_copy((axis, peer, 0), sent.at[slot], got.at[slot], sems, (s, m))

    def run(k):
        if k > 0:
            _, radix, digit, _ = stages[k - 1]
            low, _, length = shares[k - 1]
            here = pl.ds(pl.multiple_of(low + digit * length, EDGE), length)
            value = total[here, :]
            for _, slot, copy in copies(k - 1):
                copy.wait()
                value = value + got[slot, :].astype(F32)
            if k < len(stages):
                total[here, :] = value
            else:
                ends[...] = value.astype(BF)
        if k < len(stages):
            _, radix, digit, _ = stages[k]
            low, _, length = shares[k]
            for m, slot, copy in copies(k):
                give = pl.multiple_of(low + (digit + m + 1) % radix * length, EDGE)
                sent[slot, :] = total[pl.ds(give, length), :].astype(BF)
                copy.start()

    return run


def doubling_steps(stages, ends, whole, sems):
    count = len(stages)
    shares, own = shares_of(stages, whole.shape[0])

    def copies(s):
        axis, _, digit, peers = stages[s]
        low, _, length = shares[s]
        here = pl.ds(pl.multiple_of(low + digit * length, EDGE), length)
        for m, peer in enumerate(peers):
            yield hop_copy((axis, peer, 0), whole.at[here], whole.at[here], sems, (s, m))

    def run(k):
        if k == 0:
            whole[pl.ds(own, ends.shape[0]), :] = ends[...]
        if k > 0:
            for copy in copies(count - k):
                copy.wait()
        if k < count:
            for copy in copies(count - 1 - k):
                copy.start()

    return run


def sum_steps(stages, total, sent, got, ends, whole, sems, more_sems):
    count = len(stages)
    halving = halving_steps(stages, total, sent, got, ends, sems)
    doubling = doubling_steps(stages, ends, whole, more_sems)

    def run(k):
        if k <= count:
            halving(k)
        if k >= count:
            doubling(k - count)

    return run


def small_steps(hops, mine, got, sems):
    def run(k):
        if 0 < k <= len(hops):
            hop_copy(hops[k - 1], mine, got.at[k - 1], sems, (k - 1,)).wait()
            mine[...] += got[k - 1]
        if k < len(hops):
            hop_copy(hops[k], mine, got.at[k], sems, (k,)).start()

    return run


def stage_count(axes):
    return sum(-(-(size.bit_length() - 1) // (1 if axis == "seq" else 3)) for axis, size in axes)


def halving_scratch(rows, axes):
    return [
        pltpu.VMEM((rows, 128), F32),
        pltpu.VMEM((rows, 128), BF),
        pltpu.VMEM((rows, 128), BF),
        pltpu.SemaphoreType.DMA((2, stage_count(axes), 7)),
    ]


def sum_scratch(rows, axes):
    total, sent, got, sems = halving_scratch(rows, axes)
    return [total, sent, got, pltpu.VMEM((rows >> bits_of(axes), 128), BF), sems, sems]


def finish_kernel(up, mid, late, last, small_up, small_late, *outs):
    (
        first, second, skip, time_out, qkv, w_out, ff_in, ff_out, down, gains, shifts, bias, logs
    ) = outs

    def unpack(packed, refs):
        row = 0
        for ref in refs:
            flat = ref.reshape(-1, ref.shape[-1]) if len(ref.shape) == 3 else ref
            rows, columns = flat.shape
            for column in range(0, columns, 128):
                flat[:, column : column + 128] = packed[pl.ds(row, rows), :].astype(F32)
                row += rows

    unpack(up, [w_out, ff_in, ff_out, down])
    unpack(mid, [skip, qkv])
    unpack(late, [second])
    unpack(last, [first])
    C = skip.shape[0]
    wide = bias.shape[1] // C
    utts = small_late.shape[0] - 16
    gains[0:3, :] = small_late[8:11, :]
    gains[3:4, :] = small_up[0:1, :]
    shifts[0:7, :] = small_late[0:7, :]
    shifts[7:11, :] = small_up[1:5, :]
    blocks = [small_up[8 * (j + 1) : 8 * (j + 2), :] for j in range(wide)]
    embed = [small_up[8 * (wide + 1) + utts * j : 8 * (wide + 1) + utts * (j + 1), :] for j in range(time_out.shape[0] // C)]
    for j in range(wide):
        bias[:, j * C : (j + 1) * C] = blocks[j][0:1]
        logs[:, j * C : (j + 1) * C] = blocks[j][1:3]
    grads = small_late[16:, :]
    for j, part in enumerate(embed):
        time_out[j * C : (j + 1) * C, :] = lax.dot_general(
            part, grads, TN, precision=lax.Precision.HIGHEST, preferred_element_type=F32
        )


def finish(up, mid, late, last, small_up, small_late, shapes):
    vmem = pl.BlockSpec(memory_space=pltpu.VMEM)
    return pl.pallas_call(
        finish_kernel,
        out_shape=tuple(jax.ShapeDtypeStruct(shape, F32) for shape in shapes),
        in_specs=[vmem] * 6,
        out_specs=[vmem] * len(shapes),
        compiler_params=pltpu.CompilerParams(vmem_limit_bytes=56 * 2**20),
        name="finish",
    )(up, mid, late, last, small_up, small_late)


SCALE = 0.125


def head_lanes(lane, h):
    return (lane >= 64 * h) & (lane < 64 * h + 64)


def greet_seq(me):
    barrier = pltpu.get_barrier_semaphore()
    for flip in (1, 2):
        pl.semaphore_signal(barrier, inc=1, device_id={"seq": flipped(me, flip)}, device_id_type=MESH)
    pl.semaphore_wait(barrier, 2)


def flipped(place, bit):
    return place + bit - 2 * bit * ((place // bit) % 2)


def to_peer(src, dst, sems, place, peer):
    return pltpu.make_async_remote_copy(
        src, dst, sems.at[(0, *place)], sems.at[(1, *place)], device_id={"seq": peer}, device_id_type=MESH
    )


def forward_kernel(
    len_ref,
    q_ref,
    kv_ref,
    o_ref,
    qa_ref,
    all_ref,
    top,
    acc,
    held_one,
    held_two,
    tops_one,
    tops_two,
    sems,
):
    U, F, _ = q_ref.shape
    me = lax.axis_index("seq")
    near, far = flipped(me, 1), flipped(me, 2)
    lane = lax.broadcasted_iota(jnp.int32, (1, 128), 1)
    one, zero = jnp.ones((), BF), jnp.zeros((), BF)
    greet_seq(me)

    def hop(kind, u):
        if kind == 0:
            return to_peer(kv_ref.at[u], all_ref.at[1, u], sems, (kind, u), near)
        if kind == 1:
            return to_peer(kv_ref.at[u], all_ref.at[2, u], sems, (kind, u), far)
        return to_peer(all_ref.at[2, u], all_ref.at[3, u], sems, (kind, u), near)

    hop(1, 0).start()
    hop(1, 1).start()
    hop(0, 0).start()
    hop(0, 1).start()
    all_ref[0] = kv_ref[...]
    top[...] = jnp.full(top.shape, -1e30, F32)
    for u in range(U):
        for h in range(2):
            other = jnp.where(lane == 64 * (1 - h) + 3, one, zero)
            qa_ref[u, h] = jnp.where(head_lanes(lane, h), q_ref[u] * SCALE, other)
    acc[...] = jnp.zeros(acc.shape, F32)

    def block_of(t):
        late = t // 4
        r = (1 - late) * (t // 2) + late * (2 + t % 2)
        return r, (1 - late) * (t % 2) + late * ((t - 4) // 2)

    def arrive(t):
        @pl.when(t == 2)
        def _():
            hop(0, 0).wait_recv()

        @pl.when(t == 3)
        def _():
            hop(0, 1).wait_recv()

        @pl.when(t == 4)
        def _():
            hop(1, 0).wait()
            hop(2, 0).start()

        @pl.when(t == 5)
        def _():
            hop(2, 0).wait_recv()

        @pl.when(t == 6)
        def _():
            hop(1, 1).wait()
            hop(2, 1).start()

        @pl.when(t == 7)
        def _():
            hop(2, 1).wait_recv()

    def scores(t, held, tops):
        r, u = block_of(t)
        k = all_ref[r, u, :, 0:128]
        spot = xor4(me, r) * F + lax.broadcasted_iota(jnp.int32, (F, 1), 0)
        bias = jnp.where(spot < len_ref[u], 0.0, -1e9).astype(BF)
        for h in range(2):
            ka = jnp.where(head_lanes(lane, h), k, jnp.where(lane == 64 * (1 - h) + 3, bias, zero))
            s = dot(ka, qa_ref[u, h], NT)
            held[h] = s
            tops[h, 0:1, :] = jnp.max(s, axis=0, keepdims=True)

    def weigh(t, held, tops):
        r, u = block_of(t)
        vt = all_ref[r, u, :, 128:256].T
        ones = jnp.ones((EDGE, F), BF)
        for h in range(2):
            old = top[u, h, 0:1, :]
            new = jnp.maximum(old, tops[h, 0:1, :])
            p = jnp.exp(held[h] - new).astype(BF)
            va = jnp.concatenate([vt[64 * h : 64 * h + 64], ones], axis=0)
            acc[u, h] = acc[u, h] * jnp.exp(old - new) + dot(va, p)
            top[u, h, 0:1, :] = new

    scores(0, held_one, tops_one)

    def two_steps(n, _):
        t = 2 * n
        arrive(t + 1)
        scores(t + 1, held_two, tops_two)
        weigh(t, held_one, tops_one)
        arrive(t + 2)
        scores(t + 2, held_one, tops_one)
        weigh(t + 1, held_two, tops_two)
        return 0

    lax.fori_loop(0, 3, two_steps, 0)
    arrive(7)
    scores(7, held_two, tops_two)
    weigh(6, held_one, tops_one)
    weigh(7, held_two, tops_two)
    for u in range(U):
        outs, logs = [], []
        for h in range(2):
            total = acc[u, h, 64:65, :]
            outs.append(acc[u, h, 0:64, :] / total)
            logs.append(top[u, h, 0:1, :] + jnp.log(total))
        o_ref[u] = jnp.concatenate(outs, axis=0).T
        columns = jnp.concatenate([*logs, jnp.zeros((6, F), F32)], axis=0).T
        for h in range(2):
            qa_ref[u, h] = with_pieces(qa_ref[u, h], -columns[:, h : h + 1], lane, h)
    for u in range(U):
        hop(0, u).wait_send()
        hop(2, u).wait_send()


def xor4(place, r):
    low = (place % 2 + r % 2) % 2
    high = (place // 2 + r // 2) % 2
    return 2 * high + low


def attend(lengths, q, kv):
    U, F, _ = q.shape
    vmem = pl.BlockSpec(memory_space=pltpu.VMEM)
    return pl.pallas_call(
        forward_kernel,
        out_shape=(
            jax.ShapeDtypeStruct((U, F, 128), F32),
            jax.ShapeDtypeStruct((U, 2, F, 128), BF),
            jax.ShapeDtypeStruct((4, U, F, 256), BF),
        ),
        in_specs=[pl.BlockSpec(memory_space=pltpu.SMEM), vmem, vmem],
        out_specs=[vmem] * 3,
        scratch_shapes=[
            pltpu.VMEM((U, 2, 8, F), F32),
            pltpu.VMEM((U, 2, 64 + EDGE, F), F32),
            pltpu.VMEM((2, F, F), F32),
            pltpu.VMEM((2, F, F), F32),
            pltpu.VMEM((2, 8, F), F32),
            pltpu.VMEM((2, 8, F), F32),
            pltpu.SemaphoreType.DMA((2, 3, U)),
        ],
        compiler_params=pltpu.CompilerParams(
            collective_id=1, has_side_effects=True, vmem_limit_bytes=56 * 2**20
        ),
        name="attend",
    )(lengths, q, kv)


def backward_kernel(
    KB, axes, len_ref, qa_ref, da_ref, all_ref, mid_small, ff_small, embed_ref, *refs
):
    mats, refs = refs[:4], refs[4:]
    grad_ref, ends, small, dqt, part, sent, got, sems, small_got, small_sems = refs[:10]
    total, sum_sent, sum_got, sum_sems = refs[10:]
    U, _, F, _ = qa_ref.shape
    C = mid_small.shape[1]
    me = lax.axis_index("seq")
    near, far = flipped(me, 1), flipped(me, 2)
    lane = lax.broadcasted_iota(jnp.int32, (1, 128), 1)
    one, zero = jnp.ones((), BF), jnp.zeros((), BF)
    hops, stages = butterfly(axes), stages_of(axes)
    greet_stages(stages)
    pack(total, mats)
    small[...] = jnp.zeros(small.shape, F32)
    small[0:8, :] = mid_small[...]
    wide = ff_small.shape[1] // C
    for j in range(wide):
        small[8 * (j + 1) : 8 * (j + 2), :] = ff_small[:, j * C : (j + 1) * C]
    utts = U * dict(axes)["dp"]
    embed = embed_ref[...].astype(F32)
    first = jnp.where(me == 0, 1.0, 0.0)
    for j in range(embed.shape[1] // C):
        for u in range(U):
            row = 8 * (wide + 1) + j * utts + lax.axis_index("dp") * U + u
            small[pl.ds(row, 1), :] = embed[u : u + 1, j * C : (j + 1) * C] * first
    run_sum = halving_steps(stages, total, sum_sent, sum_got, ends, sum_sems)
    run_small = small_steps(hops, small, small_got, small_sems)
    dqt[...] = jnp.zeros(dqt.shape, F32)

    def hop(kind, u):
        peer = far if kind == 1 else near
        return to_peer(sent.at[kind, u], got.at[kind, u], sems, (kind, u), peer)

    tiles = F // KB
    run_sum(0)
    run_small(0)

    def tile(t, _):
        i, j = t // tiles, t % tiles
        late = i // 4
        r = (1 - late) * (3 - i % 2) + late * (1 - (i - 4) // 2)
        u = (1 - late) * ((i // 2) % 2) + late * (i % 2)
        block = xor4(me, r)
        off = pl.multiple_of(j * KB, KB)
        here = pl.ds(off, KB)
        k = all_ref[r, u, here, 0:128]
        v = all_ref[r, u, here, 128:256]
        kt = k.T
        spot = block * F + off + lax.broadcasted_iota(jnp.int32, (KB, 1), 0)
        bias = jnp.where(spot < len_ref[u], 0.0, -1e9).astype(BF)
        dks, dvs = [], []
        for h in range(2):
            mine = head_lanes(lane, h)
            base = 64 * (1 - h)
            extra = (lane >= base) & (lane < base + 3)
            ka = jnp.where(mine, k, jnp.where(extra, one, jnp.where(lane == base + 3, bias, zero)))
            va = jnp.where(mine, v, jnp.where(extra, -one, zero))
            qa = qa_ref[u, h]
            da = da_ref[u, h]
            p = jnp.exp(dot(ka, qa, NT))
            ds = (p * dot(va, da, NT)).astype(BF)
            dvs.append(dot(p.astype(BF), da))
            dks.append(dot(ds, qa))
            rows = slice(64 * h, 64 * h + 64)
            dqt[u, rows, :] += dot(kt[rows, :], ds)
        part[here, 0:128] = jnp.where(head_lanes(lane, 0), dks[0], dks[1])
        part[here, 128:256] = jnp.where(head_lanes(lane, 0), dvs[0], dvs[1])
        done = j == tiles - 1

        @pl.when(done & (r == 3))
        def _():
            sent[0, u] = part[...].astype(BF)
            hop(0, u).start()

        @pl.when(done & (r == 2))
        def _():
            hop(0, u).wait_recv()
            sent[1, u] = (part[...] + got[0, u].astype(F32)).astype(BF)
            hop(1, u).start()

        @pl.when(done & (r == 1))
        def _():
            sent[2, u] = part[...].astype(BF)
            hop(2, u).start()

        @pl.when(done & (r == 0))
        def _():
            hop(1, u).wait_recv()
            hop(2, u).wait_recv()
            both = part[...] + got[1, u].astype(F32) + got[2, u].astype(F32)
            grad_ref[u, :, 128:384] = both.astype(BF)
            grad_ref[u, :, 0:128] = (dqt[u] * SCALE).T.astype(BF)

        for slot in range(8 * tiles):
            sums = [n for n in range(1, len(stages) + 1) if sum_slot(n, len(stages), 8 * tiles) == slot]
            smalls = [n for n in range(1, len(hops) + 1) if sum_slot(n, len(hops), 8 * tiles) == slot]
            if sums or smalls:

                @pl.when(t == slot)
                def _(sums=sums, smalls=smalls):
                    for n in sums:
                        run_sum(n)
                    for n in smalls:
                        run_small(n)

        return 0

    lax.fori_loop(0, 8 * tiles, tile, 0)
    for kind in range(3):
        for u in range(U):
            hop(kind, u).wait_send()


def sum_slot(step, count, slots):
    if step == 1:
        return 0
    return slots // 4 + (step - 2) * (slots // 2) // (count - 1)


def attend_back(lengths, qa, da, kv_all, mid_small, ff_small, embed, mats, axes, KB=512):
    U, _, F, _ = qa.shape
    C = mid_small.shape[1]
    count = bits_of(axes)
    rows = padded_rows(packed_rows(mats), axes)
    utts = U * dict(axes)["dp"]
    small_rows = 8 + 8 * (ff_small.shape[1] // C) + utts * (embed.shape[1] // C)
    vmem = pl.BlockSpec(memory_space=pltpu.VMEM)
    return pl.pallas_call(
        functools.partial(backward_kernel, KB, axes),
        out_shape=(
            jax.ShapeDtypeStruct((U, F, 384), BF),
            jax.ShapeDtypeStruct((rows >> count, 128), BF),
            jax.ShapeDtypeStruct((small_rows, C), F32),
        ),
        in_specs=[pl.BlockSpec(memory_space=pltpu.SMEM)] + [vmem] * (6 + len(mats)),
        out_specs=[vmem] * 3,
        scratch_shapes=[
            pltpu.VMEM((U, 128, F), F32),
            pltpu.VMEM((F, 256), F32),
            pltpu.VMEM((3, U, F, 256), BF),
            pltpu.VMEM((3, U, F, 256), BF),
            pltpu.SemaphoreType.DMA((2, 3, U)),
            pltpu.VMEM((count, small_rows, C), F32),
            pltpu.SemaphoreType.DMA((2, count)),
            *halving_scratch(rows, axes),
        ],
        compiler_params=pltpu.CompilerParams(
            collective_id=2, has_side_effects=True, vmem_limit_bytes=60 * 2**20
        ),
        name="attend_back",
    )(lengths, qa, da, kv_all, mid_small, ff_small, embed, *mats)


def frame_mask_of(start, rows, length):
    spot = start + lax.broadcasted_iota(jnp.int32, (rows, 1), 0)
    return jnp.where((spot >= 0) & (spot < length), 1.0, 0.0)


def taps_of(x):
    wide = x.astype(F32)
    rows = x.shape[0]
    return jnp.concatenate(
        [pltpu.roll(wide, 1, 0).astype(BF), x, pltpu.roll(wide, rows - 1, 0).astype(BF)], axis=1
    )


def group_sums(rows):
    C = rows.shape[1]
    width = C // GROUPS
    one = lax.broadcasted_iota(jnp.int32, (C, C), 0) // width
    two = lax.broadcasted_iota(jnp.int32, (C, C), 1) // width
    same = jnp.where(one == two, 1.0, 0.0)
    return lax.dot_general(
        rows, same, NN, precision=lax.Precision.HIGHEST, preferred_element_type=F32
    )


def mish_parts(v):
    e = jnp.exp(jnp.minimum(v, 20.0))
    w = e * (e + 2.0)
    r = 1.0 / (w + 2.0)
    return e, w, r


def greet_all(me):
    barrier = pltpu.get_barrier_semaphore()
    for flip in (1, 2, 3):
        pl.semaphore_signal(barrier, inc=1, device_id={"seq": xor4(me, flip)}, device_id_type=MESH)
    pl.semaphore_wait(barrier, 3)


def share(mine, got, sems, u, me):
    return [
        pltpu.make_async_remote_copy(
            mine.at[u],
            got.at[j, u],
            sems.at[0, j, u],
            sems.at[1, j, u],
            device_id={"seq": xor4(me, j + 1)},
            device_id_type=MESH,
        )
        for j in range(3)
    ]


def resnet_kernel(
    len_ref,
    frames,
    embed,
    cotangent,
    conv_first,
    conv_second,
    conv_skip,
    time_proj,
    w_qkv,
    gains,
    shifts,
    x_ref,
    h1_ref,
    act_ref,
    h2_ref,
    res_ref,
    q_ref,
    kv_ref,
    stat_ref,
    embed_ref,
    next_ref,
    lead,
    stat_one,
    got_one,
    stat_two,
    got_two,
    halo_sems,
    sems_one,
    sems_two,
):
    U, F, C = frames.shape
    rows = F + 2 * EDGE
    own = pl.ds(EDGE, F)
    me = lax.axis_index("seq")
    count = lax.axis_size("seq")
    after, behind = lax.rem(me + 1, count), lax.rem(me + count - 1, count)
    start = me * F
    greet_all(me)
    for ref in (stat_one, stat_two, stat_ref):
        ref[...] = jnp.zeros_like(ref)

    def halo(src, dst, kind, peer):
        return pltpu.make_async_remote_copy(
            src, dst, halo_sems.at[0, kind], halo_sems.at[1, kind], device_id={"seq": peer}, device_id_type=MESH
        )

    halos = [
        halo(frames.at[:, pl.ds(F - EDGE, EDGE)], lead.at[0], 0, after),
        halo(frames.at[:, pl.ds(0, EDGE)], lead.at[1], 1, behind),
        halo(cotangent.at[:, pl.ds(0, EDGE)], next_ref, 2, behind),
    ]
    for copy in halos:
        copy.start()
    active = embed[...].astype(F32)
    e, w, r = mish_parts(active)
    active = (active * w * r).astype(BF)
    embed_ref[...] = active
    time_shift = dot(active, time_proj[...]) + shifts[2:3, :]
    first_taps = conv_first[...].reshape(3 * C, C)
    second_taps = conv_second[...].reshape(3 * C, C)

    def masked(block, at, u):
        return (block.astype(F32) * frame_mask_of(at, block.shape[0], len_ref[u])).astype(BF)

    for u in range(U):
        x_ref[u, own, :] = masked(frames[u], start, u)
    for copy in halos[:2]:
        copy.wait_recv()
    for u in range(U):
        x_ref[u, 0:EDGE, :] = masked(lead[0, u], start - EDGE, u)
        x_ref[u, F + EDGE :, :] = masked(lead[1, u], start + F, u)

    def valid(i, u):
        return jnp.clip(len_ref[u] - i * F, 0, F).astype(F32)

    def local_stats(hidden, stat, got, sems, u):
        mask = frame_mask_of(start, F, len_ref[u])
        inside = hidden[EDGE : EDGE + F]
        many = jnp.maximum(valid(me, u) * (C // GROUPS), 1.0)
        mean = group_sums(row_sum(inside * mask)) / many
        centered = (inside - mean) * mask
        stat[u, 0:1, :] = mean
        stat[u, 1:2, :] = group_sums(row_sum(centered * centered))
        for copy in share(stat, got, sems, u, me):
            copy.start()

    def whole_stats(stat, got, sems, u):
        for copy in share(stat, got, sems, u, me):
            copy.wait()
        total = len_ref[u].astype(F32)
        parts = [(valid(me, u), stat[u])]
        for j in range(3):
            parts.append((valid(xor4(me, j + 1), u), got[j, u]))
        mean = sum(n * p[0:1] for n, p in parts) / total
        squares = sum(p[1:2] + (n * (C // GROUPS)) * jnp.square(p[0:1] - mean) for n, p in parts)
        inv = lax.rsqrt(squares / (total * (C // GROUPS)) + norm_eps)
        return mean, inv

    def activate(hidden, mean, inv, gain, shift):
        v = (hidden - mean) * inv * gain + shift
        e, w, r = mish_parts(v)
        return v * w * r

    for u in range(U):
        hidden = dot(taps_of(x_ref[u]), first_taps) + shifts[0:1, :]
        h1_ref[u] = hidden
        local_stats(hidden, stat_one, got_one, sems_one, u)
    for u in range(U):
        mean, inv = whole_stats(stat_one, got_one, sems_one, u)
        stat_ref[u, 0:1, :] = mean
        stat_ref[u, 1:2, :] = inv
        mask = frame_mask_of(start - EDGE, rows, len_ref[u])
        act = activate(h1_ref[u], mean, inv, gains[0:1, :], shifts[1:2, :])
        act_in = ((act + time_shift[u : u + 1]) * mask).astype(BF)
        act_ref[u] = act_in
        hidden = dot(taps_of(act_in), second_taps) + shifts[3:4, :]
        h2_ref[u] = hidden
        local_stats(hidden, stat_two, got_two, sems_two, u)
    for u in range(U):
        mean, inv = whole_stats(stat_two, got_two, sems_two, u)
        stat_ref[u, 2:3, :] = mean
        stat_ref[u, 3:4, :] = inv
        mask = frame_mask_of(start, F, len_ref[u])
        act = activate(h2_ref[u, own, :], mean, inv, gains[1:2, :], shifts[4:5, :]) * mask
        res = act + dot(x_ref[u, own, :], conv_skip[...]) + shifts[5:6, :]
        res_ref[u] = res
        centered = res - lane_mean(res)
        hat = centered * lax.rsqrt(lane_mean(centered * centered) + norm_eps)
        normed = (hat * gains[2:3, :] + shifts[6:7, :]).astype(BF)
        qkv = dot(normed, w_qkv[...]).astype(BF)
        q_ref[u] = qkv[:, 0:128]
        kv_ref[u] = qkv[:, 128:384]
    for copy in halos:
        copy.wait_send()
    halos[2].wait_recv()


def resnet(lengths, frames, embed, cotangent, conv_first, conv_second, conv_skip, time_proj, w_qkv, gains, shifts):
    U, F, C = frames.shape
    rows = F + 2 * EDGE
    vmem = pl.BlockSpec(memory_space=pltpu.VMEM)
    stat = pltpu.VMEM((U, 8, C), F32)
    got = pltpu.VMEM((3, U, 8, C), F32)
    return pl.pallas_call(
        resnet_kernel,
        out_shape=(
            jax.ShapeDtypeStruct((U, rows, C), BF),
            jax.ShapeDtypeStruct((U, rows, C), F32),
            jax.ShapeDtypeStruct((U, rows, C), BF),
            jax.ShapeDtypeStruct((U, rows, C), F32),
            jax.ShapeDtypeStruct((U, F, C), F32),
            jax.ShapeDtypeStruct((U, F, 128), BF),
            jax.ShapeDtypeStruct((U, F, 256), BF),
            jax.ShapeDtypeStruct((U, 8, C), F32),
            jax.ShapeDtypeStruct(embed.shape, BF),
            jax.ShapeDtypeStruct((U, EDGE, C), BF),
        ),
        in_specs=[pl.BlockSpec(memory_space=pltpu.SMEM), vmem, vmem, pl.BlockSpec(memory_space=pl.ANY)] + [vmem] * 7,
        out_specs=[vmem] * 10,
        scratch_shapes=[
            pltpu.VMEM((2, U, EDGE, C), BF),
            stat,
            got,
            stat,
            got,
            pltpu.SemaphoreType.DMA((2, 3)),
            pltpu.SemaphoreType.DMA((2, 3, U)),
            pltpu.SemaphoreType.DMA((2, 3, U)),
        ],
        compiler_params=pltpu.CompilerParams(
            collective_id=3, has_side_effects=True, vmem_limit_bytes=56 * 2**20
        ),
        name="resnet",
    )(lengths, frames, embed, cotangent, conv_first, conv_second, conv_skip, time_proj, w_qkv, gains, shifts)


def resnet_back_kernel(
    axes,
    len_ref,
    gqkv_ref,
    gtwo_ref,
    res_ref,
    x_ref,
    h1_ref,
    act_ref,
    h2_ref,
    stat_ref,
    conv_first,
    conv_second,
    conv_skip,
    w_qkv,
    gains,
    shifts,
    up_ends,
    gframes,
    up,
    mid,
    late,
    last,
    gsmall,
    gfirst,
    gsecond,
    gskip,
    gw_qkv,
    lows,
    edges,
    gone,
    gmasked,
    sum_two,
    got_two,
    sum_one,
    got_one,
    halo_sems,
    sems_two,
    sems_one,
    small_got,
    small_sems,
    *sum_refs,
):
    U, F, C = gtwo_ref.shape
    rows = F + 2 * EDGE
    own = pl.ds(EDGE, F)
    inner = slice(EDGE, EDGE + F)
    me = lax.axis_index("seq")
    count = lax.axis_size("seq")
    after, behind = lax.rem(me + 1, count), lax.rem(me + count - 1, count)
    start = me * F
    hops, stages = butterfly(axes), stages_of(axes)
    greet_stages(stages, [("seq", xor4(me, 3))])
    run_up = doubling_steps(stages, up_ends, up, sum_refs[0])
    run_mid = sum_steps(stages, *sum_refs[1:5], mid, *sum_refs[5:7])
    run_late = sum_steps(stages, *sum_refs[7:11], late, *sum_refs[11:13])
    run_last = sum_steps(stages, *sum_refs[13:17], last, *sum_refs[17:19])
    run_small = small_steps(hops, gsmall, small_got, small_sems)
    for ref in (gsmall, sum_two, sum_one):
        ref[...] = jnp.zeros_like(ref)

    run_up(0)

    def halo(kind, u):
        spot = pl.ds(F, EDGE) if kind == 0 else pl.ds(EDGE, EDGE)
        return pltpu.make_async_remote_copy(
            gone.at[u, spot],
            edges.at[kind, u],
            halo_sems.at[0, kind, u],
            halo_sems.at[1, kind, u],
            device_id={"seq": after if kind == 0 else behind},
            device_id_type=MESH,
        )

    for u in range(U):
        res = res_ref[u]
        centered = res - lane_mean(res)
        inv = lax.rsqrt(lane_mean(centered * centered) + norm_eps)
        hat = centered * inv
        normed = (hat * gains[2:3, :] + shifts[6:7, :]).astype(BF)
        gqkv = gqkv_ref[u]
        part = tn(normed, gqkv)
        gw_qkv[...] = part if u == 0 else gw_qkv[...] + part
        grad = dot(gqkv, w_qkv[...], NT)
        gsmall[10:11, :] += row_sum(grad * hat)
        gsmall[6:7, :] += row_sum(grad)
        grad = grad * gains[2:3, :]
        grad = gtwo_ref[u] + inv * (grad - lane_mean(grad) - hat * lane_mean(grad * hat))
        gone[u, own, :] = grad
        for kind in range(2):
            halo(kind, u).start()
        gsmall[5:6, :] += row_sum(grad)
        low = grad.astype(BF)
        part = tn(x_ref[u, own, :], low)
        gskip[...] = part if u == 0 else gskip[...] + part
        gmasked[u] = dot(low, conv_skip[...], NT)
    pack(sum_refs[1], [gskip, gw_qkv])
    run_mid(0)

    def norm_terms(grad, hidden, u, at):
        mean, inv = stat_ref[u, 2 * at : 2 * at + 1, :], stat_ref[u, 2 * at + 1 : 2 * at + 2, :]
        gain, shift = gains[at : at + 1, :], shifts[1 + 3 * at : 2 + 3 * at, :]
        hat = (hidden - mean) * inv
        v = hat * gain + shift
        e, w, r = mish_parts(v)
        slope = w * r + v * (4.0 * e * (1.0 + e)) * (r * r)
        return hat, grad * slope, inv, gain

    def local_sums(hat, grad, gain, sums, got, sems, u, at):
        hat, grad = hat[inner], grad[inner]
        gsmall[8 + at : 9 + at, :] += row_sum(grad * hat)
        gsmall[1 + 3 * at : 2 + 3 * at, :] += row_sum(grad)
        grad = grad * gain
        both = jnp.concatenate([row_sum(grad), row_sum(grad * hat)], axis=0)
        sums[u, 0:2, :] = group_sums(both)
        for copy in share(sums, got, sems, u, me):
            copy.start()

    def whole_sums(sums, got, sems, u):
        for copy in share(sums, got, sems, u, me):
            copy.wait()
        return (sums[u] + got[0, u]) + (got[1, u] + got[2, u])

    def hidden_grad(hat, grad, inv, gain, total, u, mask):
        many = len_ref[u].astype(F32) * (C // GROUPS)
        return inv * (grad * gain - mask * ((total[0:1] + hat * total[1:2]) / many))

    def back_taps(grad, weight):
        wide = grad.astype(F32)
        many = grad.shape[0]
        later = pltpu.roll(wide, many - 1, 0).astype(BF)
        earlier = pltpu.roll(wide, 1, 0).astype(BF)
        return dot(later, weight[0], NT) + dot(grad, weight[1], NT) + dot(earlier, weight[2], NT)

    def wide_mask(u):
        return frame_mask_of(start - EDGE, rows, len_ref[u])

    for u in range(U):
        for kind in range(2):
            halo(kind, u).wait()
        gone[u, 0:EDGE, :] = edges[0, u]
        gone[u, F + EDGE :, :] = edges[1, u]
        hat, grad, inv, gain = norm_terms(gone[u] * wide_mask(u), h2_ref[u], u, 1)
        gone[u] = grad
        local_sums(hat, grad, gain, sum_two, got_two, sems_two, u, 1)
    run_mid(1)
    for u in range(U):
        total = whole_sums(sum_two, got_two, sems_two, u)
        mask = wide_mask(u)
        inv, gain = stat_ref[u, 3:4, :], gains[1:2, :]
        hat = (h2_ref[u] - stat_ref[u, 2:3, :]) * inv
        grad = hidden_grad(hat, gone[u], inv, gain, total, u, mask)
        gsmall[3:4, :] += row_sum(grad[inner])
        low = grad.astype(BF)
        part = tn(taps_of(act_ref[u])[inner], low[inner])
        gsecond[...] = part if u == 0 else gsecond[...] + part
        grad = back_taps(low, conv_second) * mask
        by_time = row_sum(grad[inner])
        gsmall[2:3, :] += by_time
        gsmall[pl.ds(16 + lax.axis_index("dp") * U + u, 1), :] = by_time
        hat, grad, inv, gain = norm_terms(grad, h1_ref[u], u, 0)
        gone[u] = grad
        local_sums(hat, grad, gain, sum_one, got_one, sems_one, u, 0)
        if u == U - 1:
            run_mid(2)
    pack(sum_refs[7], [gsecond])
    run_late(0)
    for u in range(U):
        total = whole_sums(sum_one, got_one, sems_one, u)
        mask = wide_mask(u)
        inv, gain = stat_ref[u, 1:2, :], gains[0:1, :]
        hat = (h1_ref[u] - stat_ref[u, 0:1, :]) * inv
        grad = hidden_grad(hat, gone[u], inv, gain, total, u, mask)
        gsmall[0:1, :] += row_sum(grad[inner])
        low = grad.astype(BF)
        lows[u] = low
        part = tn(taps_of(x_ref[u])[inner], low[inner])
        gfirst[...] = part if u == 0 else gfirst[...] + part
        if u == U - 1:
            run_late(1)
            run_mid(3)
    pack(sum_refs[13], [gfirst])
    steps = 2 * len(stages)
    for n in range(max(steps, len(hops)) + 1):
        for run, ahead, final in (
            (run_last, 0, steps),
            (run_late, 2, steps),
            (run_mid, 4, steps),
            (run_small, 0, len(hops)),
        ):
            if ahead + n <= final:
                run(ahead + n)
        for k in range(1, len(stages) + 1):
            if n == min(2 * k, steps):
                run_up(k)
        if n < U:
            grad = back_taps(lows[n], conv_first)[inner] + gmasked[n]
            gframes[n] = grad * frame_mask_of(start, F, len_ref[n])


def resnet_back(lengths, gqkv, gtwo, res, x, h1, act, h2, stat, conv_first, conv_second, conv_skip, w_qkv, gains, shifts, up_ends, axes):
    U, F, C = gtwo.shape
    count = bits_of(axes)
    shapes = [(3 * C, C), (3 * C, C), (C, C), w_qkv.shape]
    mats = [jax.ShapeDtypeStruct(shape, F32) for shape in shapes]
    up_rows = up_ends.shape[0] << count
    row_counts = [padded_rows(packed_rows(some), axes) for some in (mats[2:], mats[1:2], mats[:1])]
    small_rows = 16 + U * dict(axes)["dp"]
    rows = F + 2 * EDGE
    vmem = pl.BlockSpec(memory_space=pltpu.VMEM)
    sums = pltpu.VMEM((U, 8, C), F32)
    got = pltpu.VMEM((3, U, 8, C), F32)
    return pl.pallas_call(
        functools.partial(resnet_back_kernel, axes),
        out_shape=(
            jax.ShapeDtypeStruct((U, F, C), F32),
            *(jax.ShapeDtypeStruct((many, 128), BF) for many in [up_rows, *row_counts]),
            jax.ShapeDtypeStruct((small_rows, C), F32),
        ),
        in_specs=[pl.BlockSpec(memory_space=pltpu.SMEM)] + [vmem] * 15,
        out_specs=[vmem] * 6,
        scratch_shapes=[
            *(pltpu.VMEM(shape, F32) for shape in shapes),
            pltpu.VMEM((U, rows, C), BF),
            pltpu.VMEM((2, U, EDGE, C), F32),
            pltpu.VMEM((U, rows, C), F32),
            pltpu.VMEM((U, F, C), F32),
            sums,
            got,
            sums,
            got,
            pltpu.SemaphoreType.DMA((2, 2, U)),
            pltpu.SemaphoreType.DMA((2, 3, U)),
            pltpu.SemaphoreType.DMA((2, 3, U)),
            pltpu.VMEM((count, small_rows, C), F32),
            pltpu.SemaphoreType.DMA((2, count)),
            pltpu.SemaphoreType.DMA((2, stage_count(axes), 7)),
            *(ref for many in row_counts for ref in sum_scratch(many, axes)),
        ],
        compiler_params=pltpu.CompilerParams(
            collective_id=4, has_side_effects=True, vmem_limit_bytes=60 * 2**20
        ),
        name="resnet_back",
    )(lengths, gqkv, gtwo, res, x, h1, act, h2, stat, conv_first, conv_second, conv_skip, w_qkv, gains, shifts, up_ends)


def shards(
    frames,
    time_embed,
    lengths,
    out_cotangent,
    conv_first,
    conv_second,
    conv_skip,
    time_proj,
    w_qkv,
    w_out,
    ff_in,
    ff_out,
    conv_down,
    gains,
    shifts,
    ff_bias,
    snake_logs,
):
    channels = frames.shape[2]
    (
        masked_in,
        hidden_one,
        act_in,
        hidden_two,
        resnet_out,
        queries,
        keys_values,
        stats,
        embed_act,
        next_rows,
    ) = resnet(
        lengths,
        frames,
        time_embed,
        out_cotangent,
        conv_first,
        conv_second,
        conv_skip,
        time_proj,
        w_qkv,
        gains,
        shifts,
    )
    attended_full, queries_aug, kv_all = attend(lengths, queries, keys_values)
    (
        layer_out,
        grad_two,
        grad_aug,
        last_rows,
        grad_w_out,
        grad_ff_in,
        grad_ff_out,
        grad_conv_down,
        mid_small,
        ff_small,
    ) = middle(
        lengths,
        attended_full,
        resnet_out,
        out_cotangent,
        next_rows,
        w_out,
        ff_in,
        ff_out,
        conv_down,
        gains,
        shifts,
        ff_bias,
        snake_logs,
    )
    before_first = from_behind(last_rows, "seq", 1)[:, 15:16]
    start = lax.axis_index("seq") * frames.shape[1]
    half_mask = (start < lengths).astype(F32)[:, None, None]
    first_low = out_cotangent[:, 0:1].astype(F32) * half_mask
    first_out = layer_out[:, 0:1].astype(F32) + project(before_first, conv_down[0]) * half_mask
    layer_out = layer_out.at[:, 0:1].set(first_out.astype(BF))
    grad_conv_down = grad_conv_down.at[0].add(weight_grad(before_first, first_low.astype(BF)))
    axes = (("seq", lax.axis_size("seq")), ("dp", lax.axis_size("dp")))
    grad_qkv, up_ends, small_up = attend_back(
        lengths,
        queries_aug,
        grad_aug,
        kv_all,
        mid_small,
        ff_small,
        embed_act,
        [grad_w_out, grad_ff_in, grad_ff_out, grad_conv_down.reshape(-1, channels)],
        axes,
    )
    grad_frames, up, mid, late, last, small_late = resnet_back(
        lengths,
        grad_qkv,
        grad_two,
        resnet_out,
        masked_in,
        hidden_one,
        act_in,
        hidden_two,
        stats,
        conv_first,
        conv_second,
        conv_skip,
        w_qkv,
        gains,
        shifts,
        up_ends,
        axes,
    )
    weights = (
        conv_first,
        conv_second,
        conv_skip,
        time_proj,
        w_qkv,
        w_out,
        ff_in,
        ff_out,
        conv_down,
        gains,
        shifts,
        ff_bias.reshape(1, -1),
        snake_logs,
    )
    grads = finish(up, mid, late, last, small_up, small_late, [w.shape for w in weights])
    return (layer_out, grad_frames, *grads[:11], grads[11].reshape(-1), grads[12])


def solution(mesh):
    in_specs = (
        P("dp", "seq", None),
        P("dp", None),
        P("dp"),
        P("dp", "seq", None),
        P(),
        P(),
        P(),
        P(),
        P(),
        P(),
        P(),
        P(),
        P(),
        P(),
        P(),
        P(),
        P(),
    )
    out_specs = (
        P("dp", "seq", None),
        P("dp", "seq", None),
        P(),
        P(),
        P(),
        P(),
        P(),
        P(),
        P(),
        P(),
        P(),
        P(),
        P(),
        P(),
        P(),
    )
    return jax.shard_map(shards, mesh=mesh, in_specs=in_specs, out_specs=out_specs, check_vma=False)
```

```python
import functools
import math

import jax
import jax.numpy as jnp
from jax import lax
from jax.experimental import pallas as pl
from jax.experimental.pallas import tpu as pltpu
from jax.sharding import PartitionSpec as P

F32, BF = jnp.float32, jnp.bfloat16
NT = (((1,), (1,)), ((), ()))
NN = (((1,), (0,)), ((), ()))
TN = (((0,), (0,)), ((), ()))
MESH = pl.DeviceIdType.MESH
EDGE = 16


def dot(a, b, dn=NN):
    return lax.dot_general(a, b, dn, preferred_element_type=F32)


HEADS = 2
GROUPS = 8


norm_eps = 1e-05


SIN_PI = (3.141592580060032, -5.167706879868365, 2.55003139258664, -0.598045264752551, 0.0772203056339658)
COS_PI = (0.9999999534804945, -4.934792860766467, 4.05841196261883, -1.3318805129033002, 0.21969758323424166)


def horner(coefficients, x):
    value = coefficients[-1]
    for coefficient in coefficients[-2::-1]:
        value = value * x + coefficient
    return value


def sin_cos_half_turns(turns):
    part = turns - jnp.round(turns)
    square = part * part
    return part * horner(SIN_PI, square), horner(COS_PI, square)


def row_sum(x):
    return jnp.sum(x, axis=0, keepdims=True)


def lane_mean(x):
    return jnp.mean(x, axis=1, keepdims=True)


def tn(a, b):
    return lax.dot_general(a, b, TN, preferred_element_type=F32)


def middle_kernel(
    RB,
    FC,
    len_ref,
    att_ref,
    res_ref,
    cot_ref,
    next_ref,
    w_out,
    ff_in,
    ff_out,
    conv_down,
    gains,
    shifts,
    ff_bias,
    snake_logs,
    out_ref,
    gtwo_ref,
    aug_ref,
    row_ref,
    tail_ref,
    gw_out,
    gff_in,
    gff_out,
    gdown,
    gsmall,
    gff_small,
    pairs,
    before_last,
    acc_out,
):
    u, i = pl.program_id(0), pl.program_id(1)
    U, nb = pl.num_programs(0), pl.num_programs(1)
    half = RB // 2
    frames = nb * RB
    length = len_ref[u]
    base = lax.axis_index("seq") * frames
    at = base + i * RB

    @pl.when((u == 0) & (i == 0))
    def _():
        for ref in (gw_out, gff_in, gdown, gsmall, gff_small, acc_out):
            ref[...] = jnp.zeros_like(ref)

    def column_mask(start, rows, step):
        places = start + step * lax.broadcasted_iota(jnp.int32, (rows, 1), 0)
        return jnp.where(places < length, 1.0, 0.0)

    mask = column_mask(at, RB, 1)
    half_mask = column_mask(at, half, 2)
    low_f32 = cot_ref[0, pl.ds(pl.multiple_of(i * half, half), half), :].astype(F32) * half_mask
    gsmall[4:5, :] += row_sum(low_f32)
    low = low_f32.astype(BF)
    follow = jnp.minimum(i * half + half, frames // 2 - 16)
    inner = cot_ref[0, pl.ds(pl.multiple_of(follow, 16), 16), :].astype(F32)[0:1]
    outer = next_ref[0].astype(F32)[0:1]
    after = jnp.where(i == nb - 1, outer, inner) * jnp.where(at + RB < length, 1.0, 0.0)
    row_at = lax.broadcasted_iota(jnp.int32, (half, 1), 0)
    low_next = jnp.where(row_at == half - 1, after, pltpu.roll(low_f32, half - 1, 0)).astype(BF)
    even_grads = dot(low, conv_down[1], NT)
    odd_grads = dot(low, conv_down[2], NT) + dot(low_next, conv_down[0], NT)
    for lanes in (0, 128):
        pairs[lanes // 128, pl.ds(0, half, stride=2), :] = even_grads[:, lanes : lanes + 128]
        pairs[lanes // 128, pl.ds(1, half, stride=2), :] = odd_grads[:, lanes : lanes + 128]
    grad_three = jnp.concatenate([pairs[0], pairs[1]], axis=1) * mask
    gsmall[3:4, :] += row_sum(grad_three)
    grad_low = grad_three.astype(BF)
    attended = att_ref[0]
    att_low = attended.astype(BF)
    resid_two = res_ref[0] + dot(att_low, w_out[...]) + shifts[7:8, :]
    centered = resid_two - lane_mean(resid_two)
    inv = lax.rsqrt(lane_mean(centered * centered) + norm_eps)
    hat = centered * inv
    normed = (hat * gains[3:4, :] + shifts[8:9, :]).astype(BF)
    freq = jnp.exp(snake_logs[0:1, :])
    spread = jnp.exp(snake_logs[1:2, :])
    size = 1.0 / (spread + 1e-09)
    turn = freq * (1.0 / math.pi)
    resid_three = resid_two + shifts[9:10, :]
    grad_normed = jnp.zeros_like(resid_two)
    for c in range(0, ff_bias.shape[1], FC):
        cols = slice(c, c + FC)
        hidden = dot(normed, ff_in[:, cols]) + ff_bias[:, cols]
        sine, cosine = sin_cos_half_turns(hidden * turn[:, cols])
        square = sine * sine
        snaked = (hidden + square * size[:, cols]).astype(BF)
        resid_three = resid_three + dot(snaked, ff_out[cols, :])
        acc_out[:, cols] += tn(grad_low, snaked)
        grad_snaked = dot(grad_low, ff_out[cols, :], NT)
        cross = grad_snaked * (sine * cosine)
        grad_hidden = grad_snaked + cross * (2.0 * size * freq)[:, cols]
        gff_small[0:1, cols] += row_sum(grad_hidden)
        gff_small[1:2, cols] += row_sum(cross * hidden)
        gff_small[2:3, cols] += row_sum(grad_snaked * square)
        hidden_low = grad_hidden.astype(BF)
        gff_in[:, cols] += tn(normed, hidden_low)
        grad_normed = grad_normed + dot(hidden_low, ff_in[:, cols], NT)
    down = (resid_three * mask).astype(BF)
    down_f32 = down.astype(F32)
    for lanes in (0, 128):
        pairs[lanes // 128] = down_f32[:, lanes : lanes + 128]
    even = jnp.concatenate([pairs[j, pl.ds(0, half, stride=2), :] for j in range(2)], axis=1)
    odd = jnp.concatenate([pairs[j, pl.ds(1, half, stride=2), :] for j in range(2)], axis=1)
    first = jnp.where(i == 0, 0.0, before_last[0:1, :])
    before = jnp.where(row_at == 0, first, pltpu.roll(odd, 1, 0)).astype(BF)
    before_last[0:1, :] = odd[half - 1 : half, :]
    tail_ref[0] = dot(down[RB - 16 :, :], conv_down[0])[8:16]
    even, odd = even.astype(BF), odd.astype(BF)
    lowered = dot(before, conv_down[0]) + dot(even, conv_down[1]) + dot(odd, conv_down[2])
    lowered = lowered + shifts[10:11, :]

    @pl.when(i == 0)
    def _():
        row_ref[0] = lowered[0:8]

    out_ref[0] = (lowered * half_mask).astype(BF)
    gdown[0] += tn(odd, low_next)
    gdown[1] += tn(even, low)
    gdown[2] += tn(odd, low)
    gsmall[0:1, :] += row_sum(grad_normed * hat)
    gsmall[2:3, :] += row_sum(grad_normed)
    grad_hat = grad_normed * gains[3:4, :]
    grad_two = grad_three + inv * (
        grad_hat - lane_mean(grad_hat) - hat * lane_mean(grad_hat * hat)
    )
    gtwo_ref[0] = grad_two
    gsmall[1:2, :] += row_sum(grad_two)
    two_low = grad_two.astype(BF)
    gw_out[...] += tn(att_low, two_low)
    grad_att = dot(two_low, w_out[...], NT).astype(BF)
    terms = grad_att.astype(F32) * attended
    lane = lax.broadcasted_iota(jnp.int32, (1, 128), 1)
    zero = jnp.zeros((), F32)
    for h in range(2):
        mine = (lane >= 64 * h) & (lane < 64 * h + 64)
        term = jnp.sum(jnp.where(mine, terms, zero), axis=1, keepdims=True)
        aug_ref[0, h] = with_pieces(jnp.where(mine, grad_att, jnp.zeros((), BF)), term, lane, h)

    @pl.when((u == U - 1) & (i == nb - 1))
    def _():
        gff_out[...] = acc_out[...].T
        gff_small[1:2, :] = gff_small[1:2, :] * (2.0 * size * freq)
        gff_small[2:3, :] = gff_small[2:3, :] * (-(size * size) * spread)


def with_pieces(block, value, lane, h):
    base = 64 * (1 - h)
    for j in range(3):
        piece = value.astype(BF)
        value = value - piece.astype(F32)
        block = jnp.where(lane == base + j, piece, block)
    return block


def middle(lengths, attended, resnet_out, cotangent, next_rows, w_out, ff_in, ff_out, conv_down, gains, shifts, ff_bias, snake_logs, FC=256):
    U, F, C = resnet_out.shape
    RB = min(F, 1024)
    inner = attended.shape[2]
    FF = ff_bias.shape[0]
    whole = lambda shape: pl.BlockSpec(shape, lambda u, i, _: (0,) * len(shape))
    rows = lambda n, c: pl.BlockSpec((1, n, c), lambda u, i, _: (u, i, 0))
    per_utt = lambda n, c: pl.BlockSpec((1, n, c), lambda u, i, _: (u, 0, 0))
    sums = ((inner, C), (C, FF), (FF, C), (3, C, C), (8, C), (8, FF))
    return pl.pallas_call(
        functools.partial(middle_kernel, RB, FC),
        out_shape=(
            jax.ShapeDtypeStruct((U, F // 2, C), BF),
            jax.ShapeDtypeStruct((U, F, C), F32),
            jax.ShapeDtypeStruct((U, 2, F, inner), BF),
            jax.ShapeDtypeStruct((U, 8, C), F32),
            jax.ShapeDtypeStruct((U, 8, C), F32),
            *(jax.ShapeDtypeStruct(shape, F32) for shape in sums),
        ),
        grid_spec=pltpu.PrefetchScalarGridSpec(
            num_scalar_prefetch=1,
            grid=(U, F // RB),
            in_specs=[
                rows(RB, inner),
                rows(RB, C),
                per_utt(F // 2, C),
                per_utt(16, C),
                whole((inner, C)),
                whole((C, FF)),
                whole((FF, C)),
                whole((3, C, C)),
                whole(gains.shape),
                whole(shifts.shape),
                whole((1, FF)),
                whole((2, FF)),
            ],
            out_specs=[
                rows(RB // 2, C),
                rows(RB, C),
                pl.BlockSpec((1, 2, RB, inner), lambda u, i, _: (u, 0, i, 0)),
                per_utt(8, C),
                per_utt(8, C),
                *(whole(shape) for shape in sums),
            ],
            scratch_shapes=[
                pltpu.VMEM((2, RB, 128), F32),
                pltpu.VMEM((8, C), F32),
                pltpu.VMEM((C, FF), F32),
            ],
        ),
        compiler_params=pltpu.CompilerParams(vmem_limit_bytes=56 * 2**20),
        name="middle",
    )(lengths, attended, resnet_out, cotangent, next_rows, w_out, ff_in, ff_out, conv_down, gains, shifts, ff_bias.reshape(1, -1), snake_logs)


def butterfly(axes):
    hops = []
    for axis, size in axes:
        place = lax.axis_index(axis)
        bit = 1
        while bit < size:
            up = (place // bit) % 2
            hops.append((axis, place + bit - 2 * bit * up, up))
            bit *= 2
    return hops


def bits_of(axes):
    return sum(size.bit_length() - 1 for _, size in axes)


def stages_of(axes):
    stages = []
    for axis, size in axes:
        stride = 1
        while stride < size:
            radix = min(2 if axis == "seq" else 8, size // stride)
            place = lax.axis_index(axis)
            digit = (place // stride) % radix
            peers = [place + ((digit + m) % radix - digit) * stride for m in range(1, radix)]
            stages.append((axis, radix, digit, peers))
            stride *= radix
    return stages


def padded_rows(rows, axes):
    unit = EDGE << bits_of(axes)
    return -(-rows // unit) * unit


def packed_rows(mats):
    return sum(m.shape[0] * m.shape[1] // 128 for m in mats)


def greet_stages(stages, extra=()):
    barrier = pltpu.get_barrier_semaphore()
    met = [(axis, peer) for axis, _, _, peers in stages for peer in peers] + list(extra)
    for axis, peer in met:
        pl.semaphore_signal(barrier, inc=1, device_id={axis: peer}, device_id_type=MESH)
    pl.semaphore_wait(barrier, len(met))


def hop_copy(hop, src, dst, sems, place):
    axis, partner, _ = hop
    return pltpu.make_async_remote_copy(
        src, dst, sems.at[(0, *place)], sems.at[(1, *place)], device_id={axis: partner}, device_id_type=MESH
    )


def pack(total, mats):
    row = 0
    for ref in mats:
        rows, columns = ref.shape
        for column in range(0, columns, 128):
            total[pl.ds(row, rows), :] = ref[:, column : column + 128]
            row += rows
    if row < total.shape[0]:
        total[pl.ds(row, total.shape[0] - row), :] = jnp.zeros((total.shape[0] - row, 128), F32)


def shares_of(stages, rows):
    low, length, shares = 0, rows, []
    for _, radix, digit, _ in stages:
        shares.append((low, length, length // radix))
        length //= radix
        low = pl.multiple_of(low + digit * length, EDGE)
    return shares, low


def halving_steps(stages, total, sent, got, ends, sems):
    rows = total.shape[0]
    shares, _ = shares_of(stages, rows)

    def copies(s):
        axis, radix, _, peers = stages[s]
        _, before, length = shares[s]
        for m, peer in enumerate(peers):
            slot = pl.ds(rows - before + m * length, length)
            yield m, slot, hop_copy((axis, peer, 0), sent.at[slot], got.at[slot], sems, (s, m))

    def run(k):
        if k > 0:
            _, radix, digit, _ = stages[k - 1]
            low, _, length = shares[k - 1]
            here = pl.ds(pl.multiple_of(low + digit * length, EDGE), length)
            value = total[here, :]
            for _, slot, copy in copies(k - 1):
                copy.wait()
                value = value + got[slot, :].astype(F32)
            if k < len(stages):
                total[here, :] = value
            else:
                ends[...] = value.astype(BF)
        if k < len(stages):
            _, radix, digit, _ = stages[k]
            low, _, length = shares[k]
            for m, slot, copy in copies(k):
                give = pl.multiple_of(low + (digit + m + 1) % radix * length, EDGE)
                sent[slot, :] = total[pl.ds(give, length), :].astype(BF)
                copy.start()

    return run


def doubling_steps(stages, ends, whole, sems):
    count = len(stages)
    shares, own = shares_of(stages, whole.shape[0])

    def copies(s):
        axis, _, digit, peers = stages[s]
        low, _, length = shares[s]
        here = pl.ds(pl.multiple_of(low + digit * length, EDGE), length)
        for m, peer in enumerate(peers):
            yield hop_copy((axis, peer, 0), whole.at[here], whole.at[here], sems, (s, m))

    def run(k):
        if k == 0:
            whole[pl.ds(own, ends.shape[0]), :] = ends[...]
        if k > 0:
            for copy in copies(count - k):
                copy.wait()
        if k < count:
            for copy in copies(count - 1 - k):
                copy.start()

    return run


def sum_steps(stages, total, sent, got, ends, whole, sems, more_sems):
    count = len(stages)
    halving = halving_steps(stages, total, sent, got, ends, sems)
    doubling = doubling_steps(stages, ends, whole, more_sems)

    def run(k):
        if k <= count:
            halving(k)
        if k >= count:
            doubling(k - count)

    return run


def small_steps(hops, mine, got, sems):
    def run(k):
        if 0 < k <= len(hops):
            hop_copy(hops[k - 1], mine, got.at[k - 1], sems, (k - 1,)).wait()
            mine[...] += got[k - 1]
        if k < len(hops):
            hop_copy(hops[k], mine, got.at[k], sems, (k,)).start()

    return run


def stage_count(axes):
    return sum(-(-(size.bit_length() - 1) // (1 if axis == "seq" else 3)) for axis, size in axes)


def halving_scratch(rows, axes):
    return [
        pltpu.VMEM((rows, 128), F32),
        pltpu.VMEM((rows, 128), BF),
        pltpu.VMEM((rows, 128), BF),
        pltpu.SemaphoreType.DMA((2, stage_count(axes), 7)),
    ]


def sum_scratch(rows, axes):
    total, sent, got, sems = halving_scratch(rows, axes)
    return [total, sent, got, pltpu.VMEM((rows >> bits_of(axes), 128), BF), sems, sems]


def finish_kernel(len_ref, rows, tails, layer, up, mid, late, last, small_up, small_late, *refs):
    *outs, patched, edge, sems = refs
    U = rows.shape[0]
    fetch = pltpu.make_async_copy(layer.at[:, pl.ds(0, EDGE)], edge, sems.at[0])
    fetch.start()
    (
        first, second, skip, time_out, qkv, w_out, ff_in, ff_out, down, gains, shifts, bias, logs
    ) = outs

    def unpack(packed, refs):
        row = 0
        for ref in refs:
            flat = ref.reshape(-1, ref.shape[-1]) if len(ref.shape) == 3 else ref
            rows, columns = flat.shape
            for column in range(0, columns, 128):
                flat[:, column : column + 128] = packed[pl.ds(row, rows), :].astype(F32)
                row += rows

    fetch.wait()
    me = lax.axis_index("seq")
    frames = 2 * layer.shape[1]
    is_first = lax.broadcasted_iota(jnp.int32, (EDGE, 1), 0) == 0
    for u in range(U):
        value = rows[u, 0:1] + jnp.where(me > 0, tails[u, 7:8], 0.0)
        value = value * jnp.where(me * frames < len_ref[u], 1.0, 0.0)
        edge[u] = jnp.where(is_first, value, edge[u].astype(F32)).astype(BF)
    store = pltpu.make_async_copy(edge, patched.at[:, pl.ds(0, EDGE)], sems.at[1])
    store.start()
    unpack(up, [w_out, ff_in, ff_out, down])
    unpack(mid, [skip, qkv])
    unpack(late, [second])
    unpack(last, [first])
    C = skip.shape[0]
    wide = bias.shape[1] // C
    utts = small_late.shape[0] - 16
    gains[0:3, :] = small_late[8:11, :]
    gains[3:4, :] = small_up[0:1, :]
    shifts[0:7, :] = small_late[0:7, :]
    shifts[7:11, :] = small_up[1:5, :]
    blocks = [small_up[8 * (j + 1) : 8 * (j + 2), :] for j in range(wide)]
    embed = [small_up[8 * (wide + 1) + utts * j : 8 * (wide + 1) + utts * (j + 1), :] for j in range(time_out.shape[0] // C)]
    for j in range(wide):
        bias[:, j * C : (j + 1) * C] = blocks[j][0:1]
        logs[:, j * C : (j + 1) * C] = blocks[j][1:3]
    grads = small_late[16:, :]
    for j, part in enumerate(embed):
        time_out[j * C : (j + 1) * C, :] = lax.dot_general(
            part, grads, TN, precision=lax.Precision.HIGHEST, preferred_element_type=F32
        )
    store.wait()


def finish(lengths, rows, tails, layer, up, mid, late, last, small_up, small_late, shapes):
    vmem = pl.BlockSpec(memory_space=pltpu.VMEM)
    anywhere = pl.BlockSpec(memory_space=pl.ANY)
    return pl.pallas_call(
        finish_kernel,
        out_shape=(
            *(jax.ShapeDtypeStruct(shape, F32) for shape in shapes),
            jax.ShapeDtypeStruct(layer.shape, BF),
        ),
        in_specs=[pl.BlockSpec(memory_space=pltpu.SMEM), vmem, vmem, anywhere] + [vmem] * 6,
        out_specs=[vmem] * len(shapes) + [anywhere],
        scratch_shapes=[
            pltpu.VMEM((rows.shape[0], EDGE, rows.shape[2]), BF),
            pltpu.SemaphoreType.DMA((2,)),
        ],
        input_output_aliases={3: len(shapes)},
        compiler_params=pltpu.CompilerParams(vmem_limit_bytes=56 * 2**20),
        name="finish",
    )(lengths, rows, tails, layer, up, mid, late, last, small_up, small_late)


SCALE = 0.125


def head_lanes(lane, h):
    return (lane >= 64 * h) & (lane < 64 * h + 64)


def greet_seq(me):
    barrier = pltpu.get_barrier_semaphore()
    for flip in (1, 2):
        pl.semaphore_signal(barrier, inc=1, device_id={"seq": flipped(me, flip)}, device_id_type=MESH)
    pl.semaphore_wait(barrier, 2)


def flipped(place, bit):
    return place + bit - 2 * bit * ((place // bit) % 2)


def to_peer(src, dst, sems, place, peer):
    return pltpu.make_async_remote_copy(
        src, dst, sems.at[(0, *place)], sems.at[(1, *place)], device_id={"seq": peer}, device_id_type=MESH
    )


def xor4(place, r):
    low = (place % 2 + r % 2) % 2
    high = (place // 2 + r // 2) % 2
    return 2 * high + low


def backward_kernel(
    KB, axes, len_ref, qa_ref, da_ref, all_ref, mid_small, ff_small, embed_ref, tail_ref, *refs
):
    mats, refs = refs[:4], refs[4:]
    grad_ref, ends, small, tail_got, dqt, part, sent, got, sems, small_got, small_sems, tail_sems = refs[:12]
    total, sum_sent, sum_got, sum_sems = refs[12:]
    U, _, F, _ = qa_ref.shape
    C = mid_small.shape[1]
    me = lax.axis_index("seq")
    near, far = flipped(me, 1), flipped(me, 2)
    lane = lax.broadcasted_iota(jnp.int32, (1, 128), 1)
    one, zero = jnp.ones((), BF), jnp.zeros((), BF)
    hops, stages = butterfly(axes), stages_of(axes)
    greet_stages(stages, [("seq", xor4(me, 3))])
    tails = pltpu.make_async_remote_copy(
        tail_ref,
        tail_got,
        tail_sems.at[0],
        tail_sems.at[1],
        device_id={"seq": lax.rem(me + 1, lax.axis_size("seq"))},
        device_id_type=MESH,
    )
    tails.start()
    pack(total, mats)
    small[...] = jnp.zeros(small.shape, F32)
    small[0:8, :] = mid_small[...]
    wide = ff_small.shape[1] // C
    for j in range(wide):
        small[8 * (j + 1) : 8 * (j + 2), :] = ff_small[:, j * C : (j + 1) * C]
    utts = U * dict(axes)["dp"]
    embed = embed_ref[...].astype(F32)
    first = jnp.where(me == 0, 1.0, 0.0)
    for j in range(embed.shape[1] // C):
        for u in range(U):
            row = 8 * (wide + 1) + j * utts + lax.axis_index("dp") * U + u
            small[pl.ds(row, 1), :] = embed[u : u + 1, j * C : (j + 1) * C] * first
    run_sum = halving_steps(stages, total, sum_sent, sum_got, ends, sum_sems)
    run_small = small_steps(hops, small, small_got, small_sems)
    dqt[...] = jnp.zeros(dqt.shape, F32)

    def hop(kind, u):
        peer = far if kind == 1 else near
        return to_peer(sent.at[kind, u], got.at[kind, u], sems, (kind, u), peer)

    tiles = F // KB
    run_sum(0)
    run_small(0)

    def tile(t, _):
        i, j = t // tiles, t % tiles
        late = i // 4
        r = (1 - late) * (3 - i % 2) + late * (1 - (i - 4) // 2)
        u = (1 - late) * ((i // 2) % 2) + late * (i % 2)
        block = xor4(me, r)
        off = pl.multiple_of(j * KB, KB)
        here = pl.ds(off, KB)
        k = all_ref[r, u, here, 0:128]
        v = all_ref[r, u, here, 128:256]
        kt = k.T
        spot = block * F + off + lax.broadcasted_iota(jnp.int32, (KB, 1), 0)
        bias = jnp.where(spot < len_ref[u], 0.0, -1e9).astype(BF)
        dks, dvs = [], []
        for h in range(2):
            mine = head_lanes(lane, h)
            base = 64 * (1 - h)
            extra = (lane >= base) & (lane < base + 3)
            ka = jnp.where(mine, k, jnp.where(extra, one, jnp.where(lane == base + 3, bias, zero)))
            va = jnp.where(mine, v, jnp.where(extra, -one, zero))
            qa = qa_ref[u, h]
            da = da_ref[u, h]
            p = jnp.exp(dot(ka, qa, NT))
            ds = (p * dot(va, da, NT)).astype(BF)
            dvs.append(dot(p.astype(BF), da))
            dks.append(dot(ds, qa))
            rows = slice(64 * h, 64 * h + 64)
            dqt[u, rows, :] += dot(kt[rows, :], ds)
        part[here, 0:128] = jnp.where(head_lanes(lane, 0), dks[0], dks[1])
        part[here, 128:256] = jnp.where(head_lanes(lane, 0), dvs[0], dvs[1])
        done = j == tiles - 1

        @pl.when(done & (r == 3))
        def _():
            sent[0, u] = part[...].astype(BF)
            hop(0, u).start()

        @pl.when(done & (r == 2))
        def _():
            hop(0, u).wait_recv()
            sent[1, u] = (part[...] + got[0, u].astype(F32)).astype(BF)
            hop(1, u).start()

        @pl.when(done & (r == 1))
        def _():
            sent[2, u] = part[...].astype(BF)
            hop(2, u).start()

        @pl.when(done & (r == 0))
        def _():
            hop(1, u).wait_recv()
            hop(2, u).wait_recv()
            both = part[...] + got[1, u].astype(F32) + got[2, u].astype(F32)
            grad_ref[u, :, 128:384] = both.astype(BF)
            grad_ref[u, :, 0:128] = (dqt[u] * SCALE).T.astype(BF)

        for slot in range(8 * tiles):
            sums = [n for n in range(1, len(stages) + 1) if sum_slot(n, len(stages), 8 * tiles) == slot]
            smalls = [n for n in range(1, len(hops) + 1) if sum_slot(n, len(hops), 8 * tiles) == slot]
            if sums or smalls:

                @pl.when(t == slot)
                def _(sums=sums, smalls=smalls):
                    for n in sums:
                        run_sum(n)
                    for n in smalls:
                        run_small(n)

        return 0

    lax.fori_loop(0, 8 * tiles, tile, 0)
    tails.wait()
    for kind in range(3):
        for u in range(U):
            hop(kind, u).wait_send()


def sum_slot(step, count, slots):
    if step == 1:
        return 0
    return slots // 4 + (step - 2) * (slots // 2) // (count - 1)


def attend_back(lengths, qa, da, kv_all, mid_small, ff_small, embed, tails, mats, axes):
    U, _, F, _ = qa.shape
    C = mid_small.shape[1]
    count = bits_of(axes)
    rows = padded_rows(packed_rows(mats), axes)
    KB = min(F, 1024)
    utts = U * dict(axes)["dp"]
    small_rows = 8 + 8 * (ff_small.shape[1] // C) + utts * (embed.shape[1] // C)
    vmem = pl.BlockSpec(memory_space=pltpu.VMEM)
    return pl.pallas_call(
        functools.partial(backward_kernel, KB, axes),
        out_shape=(
            jax.ShapeDtypeStruct((U, F, 384), BF),
            jax.ShapeDtypeStruct((rows >> count, 128), BF),
            jax.ShapeDtypeStruct((small_rows, C), F32),
            jax.ShapeDtypeStruct(tails.shape, F32),
        ),
        in_specs=[pl.BlockSpec(memory_space=pltpu.SMEM)] + [vmem] * (7 + len(mats)),
        out_specs=[vmem] * 4,
        scratch_shapes=[
            pltpu.VMEM((U, 128, F), F32),
            pltpu.VMEM((F, 256), F32),
            pltpu.VMEM((3, U, F, 256), BF),
            pltpu.VMEM((3, U, F, 256), BF),
            pltpu.SemaphoreType.DMA((2, 3, U)),
            pltpu.VMEM((count, small_rows, C), F32),
            pltpu.SemaphoreType.DMA((2, count)),
            pltpu.SemaphoreType.DMA((2,)),
            *halving_scratch(rows, axes),
        ],
        compiler_params=pltpu.CompilerParams(
            collective_id=2, has_side_effects=True, vmem_limit_bytes=60 * 2**20
        ),
        name="attend_back",
    )(lengths, qa, da, kv_all, mid_small, ff_small, embed, tails, *mats)


def frame_mask_of(start, rows, length):
    spot = start + lax.broadcasted_iota(jnp.int32, (rows, 1), 0)
    return jnp.where((spot >= 0) & (spot < length), 1.0, 0.0)


def taps_of(x):
    wide = x.astype(F32)
    rows = x.shape[0]
    return jnp.concatenate(
        [pltpu.roll(wide, 1, 0).astype(BF), x, pltpu.roll(wide, rows - 1, 0).astype(BF)], axis=1
    )


def group_sums(rows):
    C = rows.shape[1]
    width = C // GROUPS
    one = lax.broadcasted_iota(jnp.int32, (C, C), 0) // width
    two = lax.broadcasted_iota(jnp.int32, (C, C), 1) // width
    same = jnp.where(one == two, 1.0, 0.0)
    return lax.dot_general(
        rows, same, NN, precision=lax.Precision.HIGHEST, preferred_element_type=F32
    )


def mish_parts(v):
    e = jnp.exp(jnp.minimum(v, 20.0))
    w = e * (e + 2.0)
    r = 1.0 / (w + 2.0)
    return e, w, r


def greet_all(me):
    barrier = pltpu.get_barrier_semaphore()
    for flip in (1, 2, 3):
        pl.semaphore_signal(barrier, inc=1, device_id={"seq": xor4(me, flip)}, device_id_type=MESH)
    pl.semaphore_wait(barrier, 3)


def share(mine, got, sems, u, me):
    return [
        pltpu.make_async_remote_copy(
            mine.at[u],
            got.at[j, u],
            sems.at[0, j, u],
            sems.at[1, j, u],
            device_id={"seq": xor4(me, j + 1)},
            device_id_type=MESH,
        )
        for j in range(3)
    ]


def front_kernel(
    len_ref,
    frames,
    embed,
    cotangent,
    conv_first,
    conv_second,
    conv_skip,
    time_proj,
    w_qkv,
    gains,
    shifts,
    x_out,
    h1_out,
    act_out,
    h2_out,
    res_out,
    all_out,
    o_ref,
    qa_ref,
    stat_ref,
    embed_ref,
    next_ref,
    x_ref,
    h1_ref,
    act_ref,
    h2_ref,
    res_ref,
    all_ref,
    lead,
    stat_one,
    got_one,
    stat_two,
    got_two,
    top,
    acc,
    held_one,
    held_two,
    tops_one,
    tops_two,
    halo_sems,
    sems_one,
    sems_two,
    kv_sems,
    keep_sems,
    block_sems,
):
    U, F, C = frames.shape
    rows = F + 2 * EDGE
    own = pl.ds(EDGE, F)
    me = lax.axis_index("seq")
    count = lax.axis_size("seq")
    after, behind = lax.rem(me + 1, count), lax.rem(me + count - 1, count)
    start = me * F
    near, far = flipped(me, 1), flipped(me, 2)
    lane = lax.broadcasted_iota(jnp.int32, (1, 128), 1)
    one, zero = jnp.ones((), BF), jnp.zeros((), BF)
    greet_all(me)
    made = (x_ref, h1_ref, act_ref, h2_ref, res_ref)
    kept = (x_out, h1_out, act_out, h2_out, res_out)

    def keep(name):
        return pltpu.make_async_copy(made[name], kept[name], keep_sems.at[name])

    def keep_block(r, u):
        return pltpu.make_async_copy(all_ref.at[r, u], all_out.at[r, u], block_sems.at[r, u])

    def hop(kind, u):
        if kind == 0:
            return to_peer(all_ref.at[0, u], all_ref.at[1, u], kv_sems, (kind, u), near)
        if kind == 1:
            return to_peer(all_ref.at[0, u], all_ref.at[2, u], kv_sems, (kind, u), far)
        return to_peer(all_ref.at[2, u], all_ref.at[3, u], kv_sems, (kind, u), near)

    for ref in (stat_one, stat_two, stat_ref):
        ref[...] = jnp.zeros_like(ref)

    def halo(src, dst, kind, peer):
        return pltpu.make_async_remote_copy(
            src, dst, halo_sems.at[0, kind], halo_sems.at[1, kind], device_id={"seq": peer}, device_id_type=MESH
        )

    halos = [
        halo(frames.at[:, pl.ds(F - EDGE, EDGE)], lead.at[0], 0, after),
        halo(frames.at[:, pl.ds(0, EDGE)], lead.at[1], 1, behind),
        halo(cotangent.at[:, pl.ds(0, EDGE)], next_ref, 2, behind),
    ]
    for copy in halos:
        copy.start()
    active = embed[...].astype(F32)
    e, w, r = mish_parts(active)
    active = (active * w * r).astype(BF)
    embed_ref[...] = active
    time_shift = dot(active, time_proj[...]) + shifts[2:3, :]
    first_taps = conv_first[...].reshape(3 * C, C)
    second_taps = conv_second[...].reshape(3 * C, C)

    def masked(block, at, u):
        return (block.astype(F32) * frame_mask_of(at, block.shape[0], len_ref[u])).astype(BF)

    for u in range(U):
        x_ref[u, own, :] = masked(frames[u], start, u)
    for copy in halos[:2]:
        copy.wait_recv()
    for u in range(U):
        x_ref[u, 0:EDGE, :] = masked(lead[0, u], start - EDGE, u)
        x_ref[u, F + EDGE :, :] = masked(lead[1, u], start + F, u)
    keep(0).start()

    def valid(i, u):
        return jnp.clip(len_ref[u] - i * F, 0, F).astype(F32)

    def local_stats(hidden, stat, got, sems, u):
        mask = frame_mask_of(start, F, len_ref[u])
        inside = hidden[EDGE : EDGE + F]
        many = jnp.maximum(valid(me, u) * (C // GROUPS), 1.0)
        mean = group_sums(row_sum(inside * mask)) / many
        centered = (inside - mean) * mask
        stat[u, 0:1, :] = mean
        stat[u, 1:2, :] = group_sums(row_sum(centered * centered))
        for copy in share(stat, got, sems, u, me):
            copy.start()

    def whole_stats(stat, got, sems, u):
        for copy in share(stat, got, sems, u, me):
            copy.wait()
        total = len_ref[u].astype(F32)
        parts = [(valid(me, u), stat[u])]
        for j in range(3):
            parts.append((valid(xor4(me, j + 1), u), got[j, u]))
        mean = sum(n * p[0:1] for n, p in parts) / total
        squares = sum(p[1:2] + (n * (C // GROUPS)) * jnp.square(p[0:1] - mean) for n, p in parts)
        inv = lax.rsqrt(squares / (total * (C // GROUPS)) + norm_eps)
        return mean, inv

    def activate(hidden, mean, inv, gain, shift):
        v = (hidden - mean) * inv * gain + shift
        e, w, r = mish_parts(v)
        return v * w * r

    for u in range(U):
        hidden = dot(taps_of(x_ref[u]), first_taps) + shifts[0:1, :]
        h1_ref[u] = hidden
        local_stats(hidden, stat_one, got_one, sems_one, u)
    keep(1).start()
    for u in range(U):
        mean, inv = whole_stats(stat_one, got_one, sems_one, u)
        stat_ref[u, 0:1, :] = mean
        stat_ref[u, 1:2, :] = inv
        mask = frame_mask_of(start - EDGE, rows, len_ref[u])
        act = activate(h1_ref[u], mean, inv, gains[0:1, :], shifts[1:2, :])
        act_in = ((act + time_shift[u : u + 1]) * mask).astype(BF)
        act_ref[u] = act_in
        hidden = dot(taps_of(act_in), second_taps) + shifts[3:4, :]
        h2_ref[u] = hidden
        local_stats(hidden, stat_two, got_two, sems_two, u)
    keep(2).start()
    keep(3).start()
    for u in range(U):
        mean, inv = whole_stats(stat_two, got_two, sems_two, u)
        stat_ref[u, 2:3, :] = mean
        stat_ref[u, 3:4, :] = inv
        mask = frame_mask_of(start, F, len_ref[u])
        act = activate(h2_ref[u, own, :], mean, inv, gains[1:2, :], shifts[4:5, :]) * mask
        res = act + dot(x_ref[u, own, :], conv_skip[...]) + shifts[5:6, :]
        res_ref[u] = res
        centered = res - lane_mean(res)
        hat = centered * lax.rsqrt(lane_mean(centered * centered) + norm_eps)
        normed = (hat * gains[2:3, :] + shifts[6:7, :]).astype(BF)
        qkv = dot(normed, w_qkv[...]).astype(BF)
        all_ref[0, u] = qkv[:, 128:384]
        hop(1, u).start()
        hop(0, u).start()
        keep_block(0, u).start()
        for h in range(2):
            other = jnp.where(lane == 64 * (1 - h) + 3, one, zero)
            qa_ref[u, h] = jnp.where(head_lanes(lane, h), qkv[:, 0:128] * SCALE, other)
    keep(4).start()
    top[...] = jnp.full(top.shape, -1e30, F32)
    acc[...] = jnp.zeros(acc.shape, F32)

    def block_of(t):
        late = t // 4
        r = (1 - late) * (t // 2) + late * (2 + t % 2)
        return r, (1 - late) * (t % 2) + late * ((t - 4) // 2)

    def arrive(t):
        @pl.when(t == 2)
        def _():
            hop(0, 0).wait_recv()
            keep_block(1, 0).start()

        @pl.when(t == 3)
        def _():
            hop(0, 1).wait_recv()
            keep_block(1, 1).start()

        @pl.when(t == 4)
        def _():
            hop(1, 0).wait()
            hop(2, 0).start()
            keep_block(2, 0).start()

        @pl.when(t == 5)
        def _():
            hop(2, 0).wait_recv()
            keep_block(3, 0).start()

        @pl.when(t == 6)
        def _():
            hop(1, 1).wait()
            hop(2, 1).start()
            keep_block(2, 1).start()

        @pl.when(t == 7)
        def _():
            hop(2, 1).wait_recv()
            keep_block(3, 1).start()

    def scores(t, held, tops):
        r, u = block_of(t)
        k = all_ref[r, u, :, 0:128]
        spot = xor4(me, r) * F + lax.broadcasted_iota(jnp.int32, (F, 1), 0)
        bias = jnp.where(spot < len_ref[u], 0.0, -1e9).astype(BF)
        for h in range(2):
            ka = jnp.where(head_lanes(lane, h), k, jnp.where(lane == 64 * (1 - h) + 3, bias, zero))
            s = dot(ka, qa_ref[u, h], NT)
            held[h] = s
            tops[h, 0:1, :] = jnp.max(s, axis=0, keepdims=True)

    def weigh(t, held, tops):
        r, u = block_of(t)
        vt = all_ref[r, u, :, 128:256].T
        ones = jnp.ones((EDGE, F), BF)
        for h in range(2):
            old = top[u, h, 0:1, :]
            new = jnp.maximum(old, tops[h, 0:1, :])
            p = jnp.exp(held[h] - new).astype(BF)
            va = jnp.concatenate([vt[64 * h : 64 * h + 64], ones], axis=0)
            acc[u, h] = acc[u, h] * jnp.exp(old - new) + dot(va, p)
            top[u, h, 0:1, :] = new

    scores(0, held_one, tops_one)

    def two_steps(n, _):
        t = 2 * n
        arrive(t + 1)
        scores(t + 1, held_two, tops_two)
        weigh(t, held_one, tops_one)
        arrive(t + 2)
        scores(t + 2, held_one, tops_one)
        weigh(t + 1, held_two, tops_two)
        return 0

    lax.fori_loop(0, 3, two_steps, 0)
    arrive(7)
    scores(7, held_two, tops_two)
    weigh(6, held_one, tops_one)
    weigh(7, held_two, tops_two)
    for u in range(U):
        outs, logs = [], []
        for h in range(2):
            total = acc[u, h, 64:65, :]
            outs.append(acc[u, h, 0:64, :] / total)
            logs.append(top[u, h, 0:1, :] + jnp.log(total))
        o_ref[u] = jnp.concatenate(outs, axis=0).T
        columns = jnp.concatenate([*logs, jnp.zeros((6, F), F32)], axis=0).T
        for h in range(2):
            qa_ref[u, h] = with_pieces(qa_ref[u, h], -columns[:, h : h + 1], lane, h)
    for u in range(U):
        hop(0, u).wait_send()
        hop(2, u).wait_send()
        for r in range(4):
            keep_block(r, u).wait()
    for name in range(5):
        keep(name).wait()
    for copy in halos:
        copy.wait_send()
    halos[2].wait_recv()


def front(lengths, frames, embed, cotangent, conv_first, conv_second, conv_skip, time_proj, w_qkv, gains, shifts):
    U, F, C = frames.shape
    rows = F + 2 * EDGE
    vmem = pl.BlockSpec(memory_space=pltpu.VMEM)
    stat = pltpu.VMEM((U, 8, C), F32)
    got = pltpu.VMEM((3, U, 8, C), F32)
    return pl.pallas_call(
        front_kernel,
        out_shape=(
            jax.ShapeDtypeStruct((U, rows, C), BF),
            jax.ShapeDtypeStruct((U, rows, C), F32),
            jax.ShapeDtypeStruct((U, rows, C), BF),
            jax.ShapeDtypeStruct((U, rows, C), F32),
            jax.ShapeDtypeStruct((U, F, C), F32),
            jax.ShapeDtypeStruct((4, U, F, 256), BF),
            jax.ShapeDtypeStruct((U, F, 128), F32),
            jax.ShapeDtypeStruct((U, 2, F, 128), BF),
            jax.ShapeDtypeStruct((U, 8, C), F32),
            jax.ShapeDtypeStruct(embed.shape, BF),
            jax.ShapeDtypeStruct((U, EDGE, C), BF),
        ),
        in_specs=[pl.BlockSpec(memory_space=pltpu.SMEM), vmem, vmem, pl.BlockSpec(memory_space=pl.ANY)] + [vmem] * 7,
        out_specs=[pl.BlockSpec(memory_space=pl.ANY)] * 6 + [vmem] * 5,
        scratch_shapes=[
            pltpu.VMEM((U, rows, C), BF),
            pltpu.VMEM((U, rows, C), F32),
            pltpu.VMEM((U, rows, C), BF),
            pltpu.VMEM((U, rows, C), F32),
            pltpu.VMEM((U, F, C), F32),
            pltpu.VMEM((4, U, F, 256), BF),
            pltpu.VMEM((2, U, EDGE, C), BF),
            stat,
            got,
            stat,
            got,
            pltpu.VMEM((U, 2, 8, F), F32),
            pltpu.VMEM((U, 2, 64 + EDGE, F), F32),
            pltpu.VMEM((2, F, F), F32),
            pltpu.VMEM((2, F, F), F32),
            pltpu.VMEM((2, 8, F), F32),
            pltpu.VMEM((2, 8, F), F32),
            pltpu.SemaphoreType.DMA((2, 3)),
            pltpu.SemaphoreType.DMA((2, 3, U)),
            pltpu.SemaphoreType.DMA((2, 3, U)),
            pltpu.SemaphoreType.DMA((2, 3, U)),
            pltpu.SemaphoreType.DMA((5,)),
            pltpu.SemaphoreType.DMA((4, U)),
        ],
        compiler_params=pltpu.CompilerParams(
            collective_id=1, has_side_effects=True, vmem_limit_bytes=60 * 2**20
        ),
        name="front",
    )(lengths, frames, embed, cotangent, conv_first, conv_second, conv_skip, time_proj, w_qkv, gains, shifts)


def resnet_back_kernel(
    axes,
    len_ref,
    gqkv_ref,
    gtwo_ref,
    res_ref,
    x_ref,
    h1_ref,
    act_ref,
    h2_ref,
    stat_ref,
    conv_first,
    conv_second,
    conv_skip,
    w_qkv,
    gains,
    shifts,
    up_ends,
    gframes,
    up,
    mid,
    late,
    last,
    gsmall,
    gfirst,
    gsecond,
    gskip,
    gw_qkv,
    lows,
    edges,
    gone,
    gmasked,
    sum_two,
    got_two,
    sum_one,
    got_one,
    halo_sems,
    sems_two,
    sems_one,
    small_got,
    small_sems,
    *sum_refs,
):
    U, F, C = gtwo_ref.shape
    rows = F + 2 * EDGE
    own = pl.ds(EDGE, F)
    inner = slice(EDGE, EDGE + F)
    me = lax.axis_index("seq")
    count = lax.axis_size("seq")
    after, behind = lax.rem(me + 1, count), lax.rem(me + count - 1, count)
    start = me * F
    hops, stages = butterfly(axes), stages_of(axes)
    greet_stages(stages, [("seq", xor4(me, 3))])
    run_up = doubling_steps(stages, up_ends, up, sum_refs[0])
    run_mid = sum_steps(stages, *sum_refs[1:5], mid, *sum_refs[5:7])
    run_late = sum_steps(stages, *sum_refs[7:11], late, *sum_refs[11:13])
    run_last = sum_steps(stages, *sum_refs[13:17], last, *sum_refs[17:19])
    run_small = small_steps(hops, gsmall, small_got, small_sems)
    for ref in (gsmall, sum_two, sum_one):
        ref[...] = jnp.zeros_like(ref)

    run_up(0)

    def halo(kind, u):
        spot = pl.ds(F, EDGE) if kind == 0 else pl.ds(EDGE, EDGE)
        return pltpu.make_async_remote_copy(
            gone.at[u, spot],
            edges.at[kind, u],
            halo_sems.at[0, kind, u],
            halo_sems.at[1, kind, u],
            device_id={"seq": after if kind == 0 else behind},
            device_id_type=MESH,
        )

    for u in range(U):
        res = res_ref[u]
        centered = res - lane_mean(res)
        inv = lax.rsqrt(lane_mean(centered * centered) + norm_eps)
        hat = centered * inv
        normed = (hat * gains[2:3, :] + shifts[6:7, :]).astype(BF)
        gqkv = gqkv_ref[u]
        part = tn(normed, gqkv)
        gw_qkv[...] = part if u == 0 else gw_qkv[...] + part
        grad = dot(gqkv, w_qkv[...], NT)
        gsmall[10:11, :] += row_sum(grad * hat)
        gsmall[6:7, :] += row_sum(grad)
        grad = grad * gains[2:3, :]
        grad = gtwo_ref[u] + inv * (grad - lane_mean(grad) - hat * lane_mean(grad * hat))
        gone[u, own, :] = grad
        for kind in range(2):
            halo(kind, u).start()
        gsmall[5:6, :] += row_sum(grad)
        low = grad.astype(BF)
        part = tn(x_ref[u, own, :], low)
        gskip[...] = part if u == 0 else gskip[...] + part
        gmasked[u] = dot(low, conv_skip[...], NT)
    pack(sum_refs[1], [gskip, gw_qkv])
    run_mid(0)

    def norm_terms(grad, hidden, u, at):
        mean, inv = stat_ref[u, 2 * at : 2 * at + 1, :], stat_ref[u, 2 * at + 1 : 2 * at + 2, :]
        gain, shift = gains[at : at + 1, :], shifts[1 + 3 * at : 2 + 3 * at, :]
        hat = (hidden - mean) * inv
        v = hat * gain + shift
        e, w, r = mish_parts(v)
        slope = w * r + v * (4.0 * e * (1.0 + e)) * (r * r)
        return hat, grad * slope, inv, gain

    def local_sums(hat, grad, gain, sums, got, sems, u, at):
        hat, grad = hat[inner], grad[inner]
        gsmall[8 + at : 9 + at, :] += row_sum(grad * hat)
        gsmall[1 + 3 * at : 2 + 3 * at, :] += row_sum(grad)
        grad = grad * gain
        both = jnp.concatenate([row_sum(grad), row_sum(grad * hat)], axis=0)
        sums[u, 0:2, :] = group_sums(both)
        for copy in share(sums, got, sems, u, me):
            copy.start()

    def whole_sums(sums, got, sems, u):
        for copy in share(sums, got, sems, u, me):
            copy.wait()
        return (sums[u] + got[0, u]) + (got[1, u] + got[2, u])

    def hidden_grad(hat, grad, inv, gain, total, u, mask):
        many = len_ref[u].astype(F32) * (C // GROUPS)
        return inv * (grad * gain - mask * ((total[0:1] + hat * total[1:2]) / many))

    def back_taps(grad, weight):
        wide = grad.astype(F32)
        many = grad.shape[0]
        later = pltpu.roll(wide, many - 1, 0).astype(BF)
        earlier = pltpu.roll(wide, 1, 0).astype(BF)
        return dot(later, weight[0], NT) + dot(grad, weight[1], NT) + dot(earlier, weight[2], NT)

    def wide_mask(u):
        return frame_mask_of(start - EDGE, rows, len_ref[u])

    for u in range(U):
        for kind in range(2):
            halo(kind, u).wait()
        gone[u, 0:EDGE, :] = edges[0, u]
        gone[u, F + EDGE :, :] = edges[1, u]
        hat, grad, inv, gain = norm_terms(gone[u] * wide_mask(u), h2_ref[u], u, 1)
        gone[u] = grad
        local_sums(hat, grad, gain, sum_two, got_two, sems_two, u, 1)
    run_mid(1)
    for u in range(U):
        total = whole_sums(sum_two, got_two, sems_two, u)
        mask = wide_mask(u)
        inv, gain = stat_ref[u, 3:4, :], gains[1:2, :]
        hat = (h2_ref[u] - stat_ref[u, 2:3, :]) * inv
        grad = hidden_grad(hat, gone[u], inv, gain, total, u, mask)
        gsmall[3:4, :] += row_sum(grad[inner])
        low = grad.astype(BF)
        part = tn(taps_of(act_ref[u])[inner], low[inner])
        gsecond[...] = part if u == 0 else gsecond[...] + part
        grad = back_taps(low, conv_second) * mask
        by_time = row_sum(grad[inner])
        gsmall[2:3, :] += by_time
        gsmall[pl.ds(16 + lax.axis_index("dp") * U + u, 1), :] = by_time
        hat, grad, inv, gain = norm_terms(grad, h1_ref[u], u, 0)
        gone[u] = grad
        local_sums(hat, grad, gain, sum_one, got_one, sems_one, u, 0)
        if u == U - 1:
            run_mid(2)
    pack(sum_refs[7], [gsecond])
    run_late(0)
    for u in range(U):
        total = whole_sums(sum_one, got_one, sems_one, u)
        mask = wide_mask(u)
        inv, gain = stat_ref[u, 1:2, :], gains[0:1, :]
        hat = (h1_ref[u] - stat_ref[u, 0:1, :]) * inv
        grad = hidden_grad(hat, gone[u], inv, gain, total, u, mask)
        gsmall[0:1, :] += row_sum(grad[inner])
        low = grad.astype(BF)
        lows[u] = low
        part = tn(taps_of(x_ref[u])[inner], low[inner])
        gfirst[...] = part if u == 0 else gfirst[...] + part
        if u == U - 1:
            run_late(1)
            run_mid(3)
    pack(sum_refs[13], [gfirst])
    steps = 2 * len(stages)
    for n in range(max(steps, len(hops)) + 1):
        for run, ahead, final in (
            (run_last, 0, steps),
            (run_late, 2, steps),
            (run_mid, 4, steps),
            (run_small, 0, len(hops)),
        ):
            if ahead + n <= final:
                run(ahead + n)
        for k in range(1, len(stages) + 1):
            if n == min(2 * k, steps):
                run_up(k)
        if n < U:
            grad = back_taps(lows[n], conv_first)[inner] + gmasked[n]
            gframes[n] = grad * frame_mask_of(start, F, len_ref[n])


def resnet_back(lengths, gqkv, gtwo, res, x, h1, act, h2, stat, conv_first, conv_second, conv_skip, w_qkv, gains, shifts, up_ends, axes):
    U, F, C = gtwo.shape
    count = bits_of(axes)
    shapes = [(3 * C, C), (3 * C, C), (C, C), w_qkv.shape]
    mats = [jax.ShapeDtypeStruct(shape, F32) for shape in shapes]
    up_rows = up_ends.shape[0] << count
    row_counts = [padded_rows(packed_rows(some), axes) for some in (mats[2:], mats[1:2], mats[:1])]
    small_rows = 16 + U * dict(axes)["dp"]
    rows = F + 2 * EDGE
    vmem = pl.BlockSpec(memory_space=pltpu.VMEM)
    sums = pltpu.VMEM((U, 8, C), F32)
    got = pltpu.VMEM((3, U, 8, C), F32)
    return pl.pallas_call(
        functools.partial(resnet_back_kernel, axes),
        out_shape=(
            jax.ShapeDtypeStruct((U, F, C), F32),
            *(jax.ShapeDtypeStruct((many, 128), BF) for many in [up_rows, *row_counts]),
            jax.ShapeDtypeStruct((small_rows, C), F32),
        ),
        in_specs=[pl.BlockSpec(memory_space=pltpu.SMEM)] + [vmem] * 15,
        out_specs=[vmem] * 6,
        scratch_shapes=[
            *(pltpu.VMEM(shape, F32) for shape in shapes),
            pltpu.VMEM((U, rows, C), BF),
            pltpu.VMEM((2, U, EDGE, C), F32),
            pltpu.VMEM((U, rows, C), F32),
            pltpu.VMEM((U, F, C), F32),
            sums,
            got,
            sums,
            got,
            pltpu.SemaphoreType.DMA((2, 2, U)),
            pltpu.SemaphoreType.DMA((2, 3, U)),
            pltpu.SemaphoreType.DMA((2, 3, U)),
            pltpu.VMEM((count, small_rows, C), F32),
            pltpu.SemaphoreType.DMA((2, count)),
            pltpu.SemaphoreType.DMA((2, stage_count(axes), 7)),
            *(ref for many in row_counts for ref in sum_scratch(many, axes)),
        ],
        compiler_params=pltpu.CompilerParams(
            collective_id=4, has_side_effects=True, vmem_limit_bytes=60 * 2**20
        ),
        name="resnet_back",
    )(lengths, gqkv, gtwo, res, x, h1, act, h2, stat, conv_first, conv_second, conv_skip, w_qkv, gains, shifts, up_ends)


def shards(
    frames,
    time_embed,
    lengths,
    out_cotangent,
    conv_first,
    conv_second,
    conv_skip,
    time_proj,
    w_qkv,
    w_out,
    ff_in,
    ff_out,
    conv_down,
    gains,
    shifts,
    ff_bias,
    snake_logs,
):
    channels = frames.shape[2]
    (
        masked_in,
        hidden_one,
        act_in,
        hidden_two,
        resnet_out,
        kv_all,
        attended_full,
        queries_aug,
        stats,
        embed_act,
        next_rows,
    ) = front(
        lengths,
        frames,
        time_embed,
        out_cotangent,
        conv_first,
        conv_second,
        conv_skip,
        time_proj,
        w_qkv,
        gains,
        shifts,
    )
    (
        layer_out,
        grad_two,
        grad_aug,
        first_rows,
        tail_rows,
        grad_w_out,
        grad_ff_in,
        grad_ff_out,
        grad_conv_down,
        mid_small,
        ff_small,
    ) = middle(
        lengths,
        attended_full,
        resnet_out,
        out_cotangent,
        next_rows,
        w_out,
        ff_in,
        ff_out,
        conv_down,
        gains,
        shifts,
        ff_bias,
        snake_logs,
    )
    axes = (("seq", lax.axis_size("seq")), ("dp", lax.axis_size("dp")))
    grad_qkv, up_ends, small_up, tail_rows = attend_back(
        lengths,
        queries_aug,
        grad_aug,
        kv_all,
        mid_small,
        ff_small,
        embed_act,
        tail_rows,
        [grad_w_out, grad_ff_in, grad_ff_out, grad_conv_down.reshape(-1, channels)],
        axes,
    )
    grad_frames, up, mid, late, last, small_late = resnet_back(
        lengths,
        grad_qkv,
        grad_two,
        resnet_out,
        masked_in,
        hidden_one,
        act_in,
        hidden_two,
        stats,
        conv_first,
        conv_second,
        conv_skip,
        w_qkv,
        gains,
        shifts,
        up_ends,
        axes,
    )
    weights = (
        conv_first,
        conv_second,
        conv_skip,
        time_proj,
        w_qkv,
        w_out,
        ff_in,
        ff_out,
        conv_down,
        gains,
        shifts,
        ff_bias.reshape(1, -1),
        snake_logs,
    )
    grads = finish(
        lengths,
        first_rows,
        tail_rows,
        layer_out,
        up,
        mid,
        late,
        last,
        small_up,
        small_late,
        [w.shape for w in weights],
    )
    return (grads[13], grad_frames, *grads[:11], grads[11].reshape(-1), grads[12])


def solution(mesh):
    in_specs = (
        P("dp", "seq", None),
        P("dp", None),
        P("dp"),
        P("dp", "seq", None),
        P(),
        P(),
        P(),
        P(),
        P(),
        P(),
        P(),
        P(),
        P(),
        P(),
        P(),
        P(),
        P(),
    )
    out_specs = (
        P("dp", "seq", None),
        P("dp", "seq", None),
        P(),
        P(),
        P(),
        P(),
        P(),
        P(),
        P(),
        P(),
        P(),
        P(),
        P(),
        P(),
        P(),
    )
    return jax.shard_map(shards, mesh=mesh, in_specs=in_specs, out_specs=out_specs, check_vma=False)
```

```python
import functools
import math

import jax
import jax.numpy as jnp
from jax import lax
from jax.experimental import pallas as pl
from jax.experimental.pallas import tpu as pltpu
from jax.sharding import PartitionSpec as P

F32, BF = jnp.float32, jnp.bfloat16
NT = (((1,), (1,)), ((), ()))
NN = (((1,), (0,)), ((), ()))
TN = (((0,), (0,)), ((), ()))
MESH = pl.DeviceIdType.MESH
EDGE = 16


def dot(a, b, dn=NN):
    return lax.dot_general(a, b, dn, preferred_element_type=F32)


HEADS = 2
GROUPS = 8


norm_eps = 1e-05


SIN_PI = (3.141592580060032, -5.167706879868365, 2.55003139258664, -0.598045264752551, 0.0772203056339658)
COS_PI = (0.9999999534804945, -4.934792860766467, 4.05841196261883, -1.3318805129033002, 0.21969758323424166)


def horner(coefficients, x):
    value = coefficients[-1]
    for coefficient in coefficients[-2::-1]:
        value = value * x + coefficient
    return value


def sin_cos_half_turns(turns):
    part = turns - jnp.round(turns)
    square = part * part
    return part * horner(SIN_PI, square), horner(COS_PI, square)


def row_sum(x):
    return jnp.sum(x, axis=0, keepdims=True)


def lane_mean(x):
    return jnp.mean(x, axis=1, keepdims=True)


def tn(a, b):
    return lax.dot_general(a, b, TN, preferred_element_type=F32)


def middle_kernel(
    RB,
    FC,
    len_ref,
    att_ref,
    res_ref,
    cot_ref,
    next_ref,
    w_out,
    ff_in,
    ff_out,
    conv_down,
    gains,
    shifts,
    ff_bias,
    snake_logs,
    out_ref,
    gtwo_ref,
    aug_ref,
    row_ref,
    tail_ref,
    gw_out,
    gff_in,
    gff_out,
    gdown,
    gsmall,
    gff_small,
    pairs,
    before_last,
    acc_out,
):
    u, i = pl.program_id(0), pl.program_id(1)
    U, nb = pl.num_programs(0), pl.num_programs(1)
    half = RB // 2
    frames = nb * RB
    length = len_ref[u]
    base = lax.axis_index("seq") * frames
    at = base + i * RB

    @pl.when((u == 0) & (i == 0))
    def _():
        for ref in (gw_out, gff_in, gdown, gsmall, gff_small, acc_out):
            ref[...] = jnp.zeros_like(ref)

    def column_mask(start, rows, step):
        places = start + step * lax.broadcasted_iota(jnp.int32, (rows, 1), 0)
        return jnp.where(places < length, 1.0, 0.0)

    mask = column_mask(at, RB, 1)
    half_mask = column_mask(at, half, 2)
    low_f32 = cot_ref[0, pl.ds(pl.multiple_of(i * half, half), half), :].astype(F32) * half_mask
    gsmall[4:5, :] += row_sum(low_f32)
    low = low_f32.astype(BF)
    follow = jnp.minimum(i * half + half, frames // 2 - 16)
    inner = cot_ref[0, pl.ds(pl.multiple_of(follow, 16), 16), :].astype(F32)[0:1]
    outer = next_ref[0].astype(F32)[0:1]
    after = jnp.where(i == nb - 1, outer, inner) * jnp.where(at + RB < length, 1.0, 0.0)
    row_at = lax.broadcasted_iota(jnp.int32, (half, 1), 0)
    low_next = jnp.where(row_at == half - 1, after, pltpu.roll(low_f32, half - 1, 0)).astype(BF)
    even_grads = dot(low, conv_down[1], NT)
    odd_grads = dot(low, conv_down[2], NT) + dot(low_next, conv_down[0], NT)
    for lanes in (0, 128):
        pairs[lanes // 128, pl.ds(0, half, stride=2), :] = even_grads[:, lanes : lanes + 128]
        pairs[lanes // 128, pl.ds(1, half, stride=2), :] = odd_grads[:, lanes : lanes + 128]
    grad_three = jnp.concatenate([pairs[0], pairs[1]], axis=1) * mask
    gsmall[3:4, :] += row_sum(grad_three)
    grad_low = grad_three.astype(BF)
    attended = att_ref[0]
    att_low = attended.astype(BF)
    resid_two = res_ref[0] + dot(att_low, w_out[...]) + shifts[7:8, :]
    centered = resid_two - lane_mean(resid_two)
    inv = lax.rsqrt(lane_mean(centered * centered) + norm_eps)
    hat = centered * inv
    normed = (hat * gains[3:4, :] + shifts[8:9, :]).astype(BF)
    freq = jnp.exp(snake_logs[0:1, :])
    spread = jnp.exp(snake_logs[1:2, :])
    size = 1.0 / (spread + 1e-09)
    turn = freq * (1.0 / math.pi)
    resid_three = resid_two + shifts[9:10, :]
    grad_normed = jnp.zeros_like(resid_two)
    for c in range(0, ff_bias.shape[1], FC):
        cols = slice(c, c + FC)
        hidden = dot(normed, ff_in[:, cols]) + ff_bias[:, cols]
        sine, cosine = sin_cos_half_turns(hidden * turn[:, cols])
        square = sine * sine
        snaked = (hidden + square * size[:, cols]).astype(BF)
        resid_three = resid_three + dot(snaked, ff_out[cols, :])
        acc_out[:, cols] += tn(grad_low, snaked)
        grad_snaked = dot(grad_low, ff_out[cols, :], NT)
        cross = grad_snaked * (sine * cosine)
        grad_hidden = grad_snaked + cross * (2.0 * size * freq)[:, cols]
        gff_small[0:1, cols] += row_sum(grad_hidden)
        gff_small[1:2, cols] += row_sum(cross * hidden)
        gff_small[2:3, cols] += row_sum(grad_snaked * square)
        hidden_low = grad_hidden.astype(BF)
        gff_in[:, cols] += tn(normed, hidden_low)
        grad_normed = grad_normed + dot(hidden_low, ff_in[:, cols], NT)
    down = (resid_three * mask).astype(BF)
    down_f32 = down.astype(F32)
    for lanes in (0, 128):
        pairs[lanes // 128] = down_f32[:, lanes : lanes + 128]
    even = jnp.concatenate([pairs[j, pl.ds(0, half, stride=2), :] for j in range(2)], axis=1)
    odd = jnp.concatenate([pairs[j, pl.ds(1, half, stride=2), :] for j in range(2)], axis=1)
    first = jnp.where(i == 0, 0.0, before_last[0:1, :])
    before = jnp.where(row_at == 0, first, pltpu.roll(odd, 1, 0)).astype(BF)
    before_last[0:1, :] = odd[half - 1 : half, :]
    tail_ref[0] = dot(down[RB - 16 :, :], conv_down[0])[8:16]
    even, odd = even.astype(BF), odd.astype(BF)
    lowered = dot(before, conv_down[0]) + dot(even, conv_down[1]) + dot(odd, conv_down[2])
    lowered = lowered + shifts[10:11, :]

    @pl.when(i == 0)
    def _():
        row_ref[0] = lowered[0:8]

    out_ref[0] = (lowered * half_mask).astype(BF)
    gdown[0] += tn(odd, low_next)
    gdown[1] += tn(even, low)
    gdown[2] += tn(odd, low)
    gsmall[0:1, :] += row_sum(grad_normed * hat)
    gsmall[2:3, :] += row_sum(grad_normed)
    grad_hat = grad_normed * gains[3:4, :]
    grad_two = grad_three + inv * (
        grad_hat - lane_mean(grad_hat) - hat * lane_mean(grad_hat * hat)
    )
    gtwo_ref[0] = grad_two
    gsmall[1:2, :] += row_sum(grad_two)
    two_low = grad_two.astype(BF)
    gw_out[...] += tn(att_low, two_low)
    grad_att = dot(two_low, w_out[...], NT).astype(BF)
    terms = grad_att.astype(F32) * attended
    lane = lax.broadcasted_iota(jnp.int32, (1, 128), 1)
    zero = jnp.zeros((), F32)
    for h in range(2):
        mine = (lane >= 64 * h) & (lane < 64 * h + 64)
        term = jnp.sum(jnp.where(mine, terms, zero), axis=1, keepdims=True)
        aug_ref[0, h] = with_pieces(jnp.where(mine, grad_att, jnp.zeros((), BF)), term, lane, h)

    @pl.when((u == U - 1) & (i == nb - 1))
    def _():
        gff_out[...] = acc_out[...].T
        gff_small[1:2, :] = gff_small[1:2, :] * (2.0 * size * freq)
        gff_small[2:3, :] = gff_small[2:3, :] * (-(size * size) * spread)


def with_pieces(block, value, lane, h):
    base = 64 * (1 - h)
    for j in range(3):
        piece = value.astype(BF)
        value = value - piece.astype(F32)
        block = jnp.where(lane == base + j, piece, block)
    return block


def middle(lengths, attended, resnet_out, cotangent, next_rows, w_out, ff_in, ff_out, conv_down, gains, shifts, ff_bias, snake_logs, FC=256):
    U, F, C = resnet_out.shape
    RB = min(F, 1024)
    inner = attended.shape[2]
    FF = ff_bias.shape[0]
    whole = lambda shape: pl.BlockSpec(shape, lambda u, i, _: (0,) * len(shape))
    rows = lambda n, c: pl.BlockSpec((1, n, c), lambda u, i, _: (u, i, 0))
    per_utt = lambda n, c: pl.BlockSpec((1, n, c), lambda u, i, _: (u, 0, 0))
    sums = ((inner, C), (C, FF), (FF, C), (3, C, C), (8, C), (8, FF))
    return pl.pallas_call(
        functools.partial(middle_kernel, RB, FC),
        out_shape=(
            jax.ShapeDtypeStruct((U, F // 2, C), BF),
            jax.ShapeDtypeStruct((U, F, C), F32),
            jax.ShapeDtypeStruct((U, 2, F, inner), BF),
            jax.ShapeDtypeStruct((U, 8, C), F32),
            jax.ShapeDtypeStruct((U, 8, C), F32),
            *(jax.ShapeDtypeStruct(shape, F32) for shape in sums),
        ),
        grid_spec=pltpu.PrefetchScalarGridSpec(
            num_scalar_prefetch=1,
            grid=(U, F // RB),
            in_specs=[
                rows(RB, inner),
                rows(RB, C),
                per_utt(F // 2, C),
                per_utt(16, C),
                whole((inner, C)),
                whole((C, FF)),
                whole((FF, C)),
                whole((3, C, C)),
                whole(gains.shape),
                whole(shifts.shape),
                whole((1, FF)),
                whole((2, FF)),
            ],
            out_specs=[
                rows(RB // 2, C),
                rows(RB, C),
                pl.BlockSpec((1, 2, RB, inner), lambda u, i, _: (u, 0, i, 0)),
                per_utt(8, C),
                per_utt(8, C),
                *(whole(shape) for shape in sums),
            ],
            scratch_shapes=[
                pltpu.VMEM((2, RB, 128), F32),
                pltpu.VMEM((8, C), F32),
                pltpu.VMEM((C, FF), F32),
            ],
        ),
        compiler_params=pltpu.CompilerParams(vmem_limit_bytes=56 * 2**20),
        name="middle",
    )(lengths, attended, resnet_out, cotangent, next_rows, w_out, ff_in, ff_out, conv_down, gains, shifts, ff_bias.reshape(1, -1), snake_logs)


def butterfly(axes):
    hops = []
    for axis, size in axes:
        place = lax.axis_index(axis)
        bit = 1
        while bit < size:
            up = (place // bit) % 2
            hops.append((axis, place + bit - 2 * bit * up, up))
            bit *= 2
    return hops


def bits_of(axes):
    return sum(size.bit_length() - 1 for _, size in axes)


def radices(axis, size, fine):
    while size > 1:
        radix = min(2 if axis == "seq" else 8, size)
        if fine and axis == "dp":
            radix = 2 if fine == 1 else min(4, size)
            fine = 2
        yield radix
        size //= radix


def stages_of(axes, fine=0):
    stages = []
    for axis, size in axes:
        stride = 1
        for radix in radices(axis, size, fine):
            place = lax.axis_index(axis)
            digit = (place // stride) % radix
            peers = [place + ((digit + m) % radix - digit) * stride for m in range(1, radix)]
            stages.append((axis, radix, digit, peers))
            stride *= radix
    return [stages[0], *stages[2:], stages[1]] if fine else stages


def padded_rows(rows, axes):
    unit = EDGE << bits_of(axes)
    return -(-rows // unit) * unit


def packed_rows(mats):
    return sum(m.shape[0] * m.shape[1] // 128 for m in mats)


def greet_stages(stages, extra=()):
    barrier = pltpu.get_barrier_semaphore()
    met = [(axis, peer) for axis, _, _, peers in stages for peer in peers] + list(extra)
    for axis, peer in met:
        pl.semaphore_signal(barrier, inc=1, device_id={axis: peer}, device_id_type=MESH)
    pl.semaphore_wait(barrier, len(met))


def hop_copy(hop, src, dst, sems, place):
    axis, partner, _ = hop
    return pltpu.make_async_remote_copy(
        src, dst, sems.at[(0, *place)], sems.at[(1, *place)], device_id={axis: partner}, device_id_type=MESH
    )


def pack(total, mats):
    row = 0
    for ref in mats:
        rows, columns = ref.shape
        for column in range(0, columns, 128):
            total[pl.ds(row, rows), :] = ref[:, column : column + 128]
            row += rows
    if row < total.shape[0]:
        total[pl.ds(row, total.shape[0] - row), :] = jnp.zeros((total.shape[0] - row, 128), F32)


def shares_of(stages, rows):
    low, length, shares = 0, rows, []
    for _, radix, digit, _ in stages:
        shares.append((low, length, length // radix))
        length //= radix
        low = pl.multiple_of(low + digit * length, EDGE)
    return shares, low


def halving_steps(stages, total, sent, got, ends, sems):
    rows = total.shape[0]
    shares, _ = shares_of(stages, rows)

    def copies(s):
        axis, radix, _, peers = stages[s]
        _, before, length = shares[s]
        for m, peer in enumerate(peers):
            slot = pl.ds(rows - before + m * length, length)
            yield m, slot, hop_copy((axis, peer, 0), sent.at[slot], got.at[slot], sems, (s, m))

    def run(k):
        if k > 0:
            _, radix, digit, _ = stages[k - 1]
            low, _, length = shares[k - 1]
            here = pl.ds(pl.multiple_of(low + digit * length, EDGE), length)
            value = total[here, :]
            for _, slot, copy in copies(k - 1):
                copy.wait()
                value = value + got[slot, :].astype(F32)
            if k < len(stages):
                total[here, :] = value
            else:
                ends[...] = value.astype(BF)
        if k < len(stages):
            _, radix, digit, _ = stages[k]
            low, _, length = shares[k]
            for m, slot, copy in copies(k):
                give = pl.multiple_of(low + (digit + m + 1) % radix * length, EDGE)
                sent[slot, :] = total[pl.ds(give, length), :].astype(BF)
                copy.start()

    return run


def doubling_steps(stages, ends, whole, sems):
    count = len(stages)
    shares, own = shares_of(stages, whole.shape[0])

    def copies(s):
        axis, _, digit, peers = stages[s]
        low, _, length = shares[s]
        here = pl.ds(pl.multiple_of(low + digit * length, EDGE), length)
        for m, peer in enumerate(peers):
            yield hop_copy((axis, peer, 0), whole.at[here], whole.at[here], sems, (s, m))

    def run(k):
        if k == 0:
            whole[pl.ds(own, ends.shape[0]), :] = ends[...]
        if k > 0:
            for copy in copies(count - k):
                copy.wait()
        if k < count:
            for copy in copies(count - 1 - k):
                copy.start()

    return run


def sum_steps(stages, total, sent, got, ends, whole, sems, more_sems):
    count = len(stages)
    halving = halving_steps(stages, total, sent, got, ends, sems)
    doubling = doubling_steps(stages, ends, whole, more_sems)

    def run(k):
        if k <= count:
            halving(k)
        if k >= count:
            doubling(k - count)

    return run


def small_steps(hops, mine, got, sems):
    def run(k):
        if 0 < k <= len(hops):
            hop_copy(hops[k - 1], mine, got.at[k - 1], sems, (k - 1,)).wait()
            mine[...] += got[k - 1]
        if k < len(hops):
            hop_copy(hops[k], mine, got.at[k], sems, (k,)).start()

    return run


def stage_count(axes, fine):
    return sum(len(list(radices(axis, size, fine))) for axis, size in axes)


def halving_scratch(rows, axes, fine):
    return [
        pltpu.VMEM((rows, 128), F32),
        pltpu.VMEM((rows, 128), BF),
        pltpu.VMEM((rows, 128), BF),
        pltpu.SemaphoreType.DMA((2, stage_count(axes, fine), 7)),
    ]


def sum_scratch(rows, axes):
    total, sent, got, sems = halving_scratch(rows, axes, 0)
    return [total, sent, got, pltpu.VMEM((rows >> bits_of(axes), 128), BF), sems, sems]


def finish_kernel(len_ref, rows, tails, layer, up, mid, late, last, small_up, small_late, *refs):
    outs, patched, edge, sems = refs[:13], refs[13], refs[14], refs[15]
    big, big_sems = refs[16:25], refs[25]
    U = rows.shape[0]
    fetch = pltpu.make_async_copy(layer.at[:, pl.ds(0, EDGE)], edge, sems.at[0])
    fetch.start()
    (
        first, second, skip, time_out, qkv, w_out, ff_in, ff_out, down, gains, shifts, bias, logs
    ) = (*big, *outs[9:])

    def send(n):
        return pltpu.make_async_copy(big[n], outs[n], big_sems.at[n])

    def unpack(packed, refs):
        row = 0
        for ref in refs:
            flat = ref.reshape(-1, ref.shape[-1]) if len(ref.shape) == 3 else ref
            rows, columns = flat.shape
            for column in range(0, columns, 128):
                flat[:, column : column + 128] = packed[pl.ds(row, rows), :].astype(F32)
                row += rows

    unpack(up, [w_out, ff_in, ff_out, down])
    for n in range(5, 9):
        send(n).start()
    unpack(mid, [skip, qkv])
    unpack(late, [second])
    unpack(last, [first])
    for n in (0, 1, 2, 4):
        send(n).start()
    C = skip.shape[0]
    wide = bias.shape[1] // C
    utts = small_late.shape[0] - 16
    gains[0:3, :] = small_late[8:11, :]
    gains[3:4, :] = small_up[0:1, :]
    shifts[0:7, :] = small_late[0:7, :]
    shifts[7:11, :] = small_up[1:5, :]
    blocks = [small_up[8 * (j + 1) : 8 * (j + 2), :] for j in range(wide)]
    base = packed_rows([w_out, ff_in, ff_out, down.reshape(-1, C)])
    embed = [up[pl.ds(base + utts * j, utts), :].astype(F32) for j in range(time_out.shape[0] // 128)]
    for j in range(wide):
        bias[:, j * C : (j + 1) * C] = blocks[j][0:1]
        logs[:, j * C : (j + 1) * C] = blocks[j][1:3]
    grads = small_late[16:, :]
    for j, part in enumerate(embed):
        time_out[j * 128 : (j + 1) * 128, :] = lax.dot_general(
            part, grads, TN, precision=lax.Precision.HIGHEST, preferred_element_type=F32
        )
    send(3).start()
    fetch.wait()
    me = lax.axis_index("seq")
    frames = 2 * layer.shape[1]
    is_first = lax.broadcasted_iota(jnp.int32, (EDGE, 1), 0) == 0
    for u in range(U):
        value = rows[u, 0:1] + jnp.where(me > 0, tails[u, 7:8], 0.0)
        value = value * jnp.where(me * frames < len_ref[u], 1.0, 0.0)
        edge[u] = jnp.where(is_first, value, edge[u].astype(F32)).astype(BF)
    store = pltpu.make_async_copy(edge, patched.at[:, pl.ds(0, EDGE)], sems.at[1])
    store.start()
    for n in range(9):
        send(n).wait()
    store.wait()


def finish(lengths, rows, tails, layer, up, mid, late, last, small_up, small_late, shapes):
    vmem = pl.BlockSpec(memory_space=pltpu.VMEM)
    anywhere = pl.BlockSpec(memory_space=pl.ANY)
    return pl.pallas_call(
        finish_kernel,
        out_shape=(
            *(jax.ShapeDtypeStruct(shape, F32) for shape in shapes),
            jax.ShapeDtypeStruct(layer.shape, BF),
        ),
        in_specs=[pl.BlockSpec(memory_space=pltpu.SMEM), vmem, vmem, anywhere] + [vmem] * 6,
        out_specs=[anywhere] * 9 + [vmem] * 4 + [anywhere],
        scratch_shapes=[
            pltpu.VMEM((rows.shape[0], EDGE, rows.shape[2]), BF),
            pltpu.SemaphoreType.DMA((2,)),
            *(pltpu.VMEM(shape, F32) for shape in shapes[:9]),
            pltpu.SemaphoreType.DMA((9,)),
        ],
        input_output_aliases={3: len(shapes)},
        compiler_params=pltpu.CompilerParams(vmem_limit_bytes=56 * 2**20),
        name="finish",
    )(lengths, rows, tails, layer, up, mid, late, last, small_up, small_late)


SCALE = 0.125


def head_lanes(lane, h):
    return (lane >= 64 * h) & (lane < 64 * h + 64)


def greet_seq(me):
    barrier = pltpu.get_barrier_semaphore()
    for flip in (1, 2):
        pl.semaphore_signal(barrier, inc=1, device_id={"seq": flipped(me, flip)}, device_id_type=MESH)
    pl.semaphore_wait(barrier, 2)


def flipped(place, bit):
    return place + bit - 2 * bit * ((place // bit) % 2)


def to_peer(src, dst, sems, place, peer):
    return pltpu.make_async_remote_copy(
        src, dst, sems.at[(0, *place)], sems.at[(1, *place)], device_id={"seq": peer}, device_id_type=MESH
    )


def xor4(place, r):
    low = (place % 2 + r % 2) % 2
    high = (place // 2 + r // 2) % 2
    return 2 * high + low


def backward_kernel(
    axes, qa_ref, da_ref, all_in, probs_ref, factors, mid_small, ff_small, embed_ref, tail_ref, *refs
):
    mats_in, refs = refs[:4], refs[4:]
    grad_ref, ends, small, tail_got, dqt, part, sent, got, sems, small_got, small_sems, tail_sems = refs[:12]
    probs, probs_sems, total, sum_sent, sum_got, sum_sems, all_ref = refs[12:19]
    block_sems, mat_sems, mats = refs[19], refs[20], refs[21:]
    U, _, F, _ = qa_ref.shape
    C = mid_small.shape[1]
    me = lax.axis_index("seq")
    near, far = flipped(me, 1), flipped(me, 2)
    lane = lax.broadcasted_iota(jnp.int32, (1, 128), 1)
    one, zero = jnp.ones((), BF), jnp.zeros((), BF)
    hops, stages = butterfly(axes), stages_of(axes)
    greet_stages(stages, [("seq", xor4(me, 3))])
    tails = pltpu.make_async_remote_copy(
        tail_ref,
        tail_got,
        tail_sems.at[0],
        tail_sems.at[1],
        device_id={"seq": lax.rem(me + 1, lax.axis_size("seq"))},
        device_id_type=MESH,
    )
    tails.start()
    small[...] = jnp.zeros(small.shape, F32)
    small[0:8, :] = mid_small[...]
    wide = ff_small.shape[1] // C
    for j in range(wide):
        small[8 * (j + 1) : 8 * (j + 2), :] = ff_small[:, j * C : (j + 1) * C]

    def bring_mat(n):
        return pltpu.make_async_copy(mats_in[n], mats[n], mat_sems.at[n])

    def fill():
        for n in range(len(mats)):
            bring_mat(n).wait()
        pack(total, mats)
        embed = embed_ref[...].astype(F32) * jnp.where(me == 0, 1.0, 0.0)
        base = packed_rows(mats)
        for j in range(embed.shape[1] // 128):
            for u in range(U):
                row = base + j * U * dict(axes)["dp"] + lax.axis_index("dp") * U + u
                total[pl.ds(row, 1), :] = embed[u : u + 1, j * 128 : (j + 1) * 128]

    fine = stages_of(axes, 1)
    run_sum = halving_steps(fine, total, sum_sent, sum_got, ends, sum_sems)
    run_small = small_steps(hops, small, small_got, small_sems)
    dqt[...] = jnp.zeros(dqt.shape, F32)

    def hop(kind, u):
        peer = far if kind == 1 else near
        return to_peer(sent.at[kind, u], got.at[kind, u], sems, (kind, u), peer)

    def block_of(t):
        late = t // 4
        r = (1 - late) * (3 - t % 2) + late * (1 - (t - 4) // 2)
        return r, (1 - late) * ((t // 2) % 2) + late * (t % 2)

    def fetch(t):
        r, u = block_of(t)
        return pltpu.make_async_copy(probs_ref.at[r, u], probs.at[t % 2], probs_sems.at[t % 2])

    def bring(t):
        r, u = block_of(t)
        return pltpu.make_async_copy(all_in.at[r, u], all_ref.at[r, u], block_sems.at[t])

    bring(0).start()
    fetch(0).start()
    for t in range(1, 8):
        bring(t).start()
    for n in range(len(mats)):
        bring_mat(n).start()
    run_small(0)

    def step(t, _):
        r, u = block_of(t)

        @pl.when(t < 7)
        def _():
            fetch(t + 1).start()

        bring(t).wait()
        fetch(t).wait()
        v = all_ref[r, u, :, 128:256]
        kt = all_ref[r, u, :, 0:128].T
        dks, dvs = [], []
        for h in range(2):
            base = 64 * (1 - h)
            extra = (lane >= base) & (lane < base + 3)
            va = jnp.where(head_lanes(lane, h), v, jnp.where(extra, -one, zero))
            qa = qa_ref[u, h]
            da = da_ref[u, h]
            p = probs[t % 2, h].astype(F32) * factors[r, u, h : h + 1, :]
            ds = (p * dot(va, da, NT)).astype(BF)
            dvs.append(dot(p.astype(BF), da))
            dks.append(dot(ds, qa))
            rows = slice(64 * h, 64 * h + 64)
            dqt[u, rows, :] += dot(kt[rows, :], ds)
        part[:, 0:128] = jnp.where(head_lanes(lane, 0), dks[0], dks[1])
        part[:, 128:256] = jnp.where(head_lanes(lane, 0), dvs[0], dvs[1])

        @pl.when(r == 3)
        def _():
            sent[0, u] = part[...].astype(BF)
            hop(0, u).start()

        @pl.when(r == 2)
        def _():
            hop(0, u).wait_recv()
            sent[1, u] = (part[...] + got[0, u].astype(F32)).astype(BF)
            hop(1, u).start()

        @pl.when(r == 1)
        def _():
            sent[2, u] = part[...].astype(BF)
            hop(2, u).start()

        @pl.when(r == 0)
        def _():
            hop(1, u).wait_recv()
            hop(2, u).wait_recv()
            both = part[...] + got[1, u].astype(F32) + got[2, u].astype(F32)
            grad_ref[u, :, 128:384] = both.astype(BF)
            grad_ref[u, :, 0:128] = (dqt[u] * SCALE).T.astype(BF)

        for slot in range(8):
            sums = [n for n in range(len(fine) + 1) if sum_slot(n, len(fine) + 1, 8) == slot]
            smalls = [n for n in range(1, len(hops) + 1) if sum_slot(n - 1, len(hops), 8) == slot]
            if sums or smalls:

                @pl.when(t == slot)
                def _(sums=sums, smalls=smalls):
                    for n in sums:
                        if n == 0:
                            fill()
                        run_sum(n)
                    for n in smalls:
                        run_small(n)

        return 0

    lax.fori_loop(0, 8, step, 0)
    tails.wait()
    for kind in range(3):
        for u in range(U):
            hop(kind, u).wait_send()


def sum_slot(step, count, slots):
    return -(-step * (slots - 1) // (count - 1))


def attend_back(qa, da, kv_all, probs, factors, mid_small, ff_small, embed, tails, mats, axes):
    U, _, F, _ = qa.shape
    C = mid_small.shape[1]
    count = bits_of(axes)
    embed_rows = U * dict(axes)["dp"] * embed.shape[1] // 128
    rows = padded_rows(packed_rows(mats) + embed_rows, axes)
    small_rows = 8 + 8 * (ff_small.shape[1] // C)
    vmem = pl.BlockSpec(memory_space=pltpu.VMEM)
    anywhere = pl.BlockSpec(memory_space=pl.ANY)
    return pl.pallas_call(
        functools.partial(backward_kernel, axes),
        out_shape=(
            jax.ShapeDtypeStruct((U, F, 384), BF),
            jax.ShapeDtypeStruct((rows >> count, 128), BF),
            jax.ShapeDtypeStruct((small_rows, C), F32),
            jax.ShapeDtypeStruct(tails.shape, F32),
        ),
        in_specs=[vmem, vmem, anywhere, anywhere] + [vmem] * 5 + [anywhere] * len(mats),
        out_specs=[vmem] * 4,
        scratch_shapes=[
            pltpu.VMEM((U, 128, F), F32),
            pltpu.VMEM((F, 256), F32),
            pltpu.VMEM((3, U, F, 256), BF),
            pltpu.VMEM((3, U, F, 256), BF),
            pltpu.SemaphoreType.DMA((2, 3, U)),
            pltpu.VMEM((count, small_rows, C), F32),
            pltpu.SemaphoreType.DMA((2, count)),
            pltpu.SemaphoreType.DMA((2,)),
            pltpu.VMEM((2, 2, F, F), BF),
            pltpu.SemaphoreType.DMA((2,)),
            *halving_scratch(rows, axes, 1),
            pltpu.VMEM(kv_all.shape, BF),
            pltpu.SemaphoreType.DMA((8,)),
            pltpu.SemaphoreType.DMA((len(mats),)),
            *(pltpu.VMEM(m.shape, F32) for m in mats),
        ],
        compiler_params=pltpu.CompilerParams(
            collective_id=2, has_side_effects=True, vmem_limit_bytes=60 * 2**20
        ),
        name="attend_back",
    )(qa, da, kv_all, probs, factors, mid_small, ff_small, embed, tails, *mats)


def frame_mask_of(start, rows, length):
    spot = start + lax.broadcasted_iota(jnp.int32, (rows, 1), 0)
    return jnp.where((spot >= 0) & (spot < length), 1.0, 0.0)


def taps_of(x):
    wide = x.astype(F32)
    rows = x.shape[0]
    return jnp.concatenate(
        [pltpu.roll(wide, 1, 0).astype(BF), x, pltpu.roll(wide, rows - 1, 0).astype(BF)], axis=1
    )


def group_sums(rows):
    C = rows.shape[1]
    width = C // GROUPS
    one = lax.broadcasted_iota(jnp.int32, (C, C), 0) // width
    two = lax.broadcasted_iota(jnp.int32, (C, C), 1) // width
    same = jnp.where(one == two, 1.0, 0.0)
    return lax.dot_general(
        rows, same, NN, precision=lax.Precision.HIGHEST, preferred_element_type=F32
    )


def mish_parts(v):
    e = jnp.exp(jnp.minimum(v, 20.0))
    w = e * (e + 2.0)
    r = 1.0 / (w + 2.0)
    return e, w, r


def greet_all(me):
    barrier = pltpu.get_barrier_semaphore()
    for flip in (1, 2, 3):
        pl.semaphore_signal(barrier, inc=1, device_id={"seq": xor4(me, flip)}, device_id_type=MESH)
    pl.semaphore_wait(barrier, 3)


def share(mine, got, sems, u, me):
    return [
        pltpu.make_async_remote_copy(
            mine.at[u],
            got.at[j, u],
            sems.at[0, j, u],
            sems.at[1, j, u],
            device_id={"seq": xor4(me, j + 1)},
            device_id_type=MESH,
        )
        for j in range(3)
    ]


def front_kernel(
    len_ref,
    frames,
    embed,
    cotangent,
    conv_first,
    conv_second,
    conv_skip,
    time_proj,
    w_qkv,
    gains,
    shifts,
    x_out,
    h1_out,
    act_out,
    h2_out,
    res_out,
    all_out,
    probs_out,
    o_ref,
    qa_ref,
    stat_ref,
    embed_ref,
    next_ref,
    factors,
    x_ref,
    h1_ref,
    act_ref,
    h2_ref,
    res_ref,
    all_ref,
    lead,
    stat_one,
    got_one,
    stat_two,
    got_two,
    top,
    acc,
    held_one,
    held_two,
    tops_one,
    tops_two,
    probs,
    tops_used,
    halo_sems,
    sems_one,
    sems_two,
    kv_sems,
    keep_sems,
    block_sems,
    probs_sems,
):
    U, F, C = frames.shape
    rows = F + 2 * EDGE
    own = pl.ds(EDGE, F)
    me = lax.axis_index("seq")
    count = lax.axis_size("seq")
    after, behind = lax.rem(me + 1, count), lax.rem(me + count - 1, count)
    start = me * F
    near, far = flipped(me, 1), flipped(me, 2)
    lane = lax.broadcasted_iota(jnp.int32, (1, 128), 1)
    one, zero = jnp.ones((), BF), jnp.zeros((), BF)
    greet_all(me)
    made = (x_ref, h1_ref, act_ref, h2_ref, res_ref)
    kept = (x_out, h1_out, act_out, h2_out, res_out)

    def keep(name):
        return pltpu.make_async_copy(made[name], kept[name], keep_sems.at[name])

    def keep_block(r, u):
        return pltpu.make_async_copy(all_ref.at[r, u], all_out.at[r, u], block_sems.at[r, u])

    def hop(kind, u):
        if kind == 0:
            return to_peer(all_ref.at[0, u], all_ref.at[1, u], kv_sems, (kind, u), near)
        if kind == 1:
            return to_peer(all_ref.at[0, u], all_ref.at[2, u], kv_sems, (kind, u), far)
        return to_peer(all_ref.at[2, u], all_ref.at[3, u], kv_sems, (kind, u), near)

    for ref in (stat_one, stat_two, stat_ref):
        ref[...] = jnp.zeros_like(ref)

    def halo(src, dst, kind, peer):
        return pltpu.make_async_remote_copy(
            src, dst, halo_sems.at[0, kind], halo_sems.at[1, kind], device_id={"seq": peer}, device_id_type=MESH
        )

    halos = [
        halo(frames.at[:, pl.ds(F - EDGE, EDGE)], lead.at[0], 0, after),
        halo(frames.at[:, pl.ds(0, EDGE)], lead.at[1], 1, behind),
        halo(cotangent.at[:, pl.ds(0, EDGE)], next_ref, 2, behind),
    ]
    for copy in halos:
        copy.start()
    active = embed[...].astype(F32)
    e, w, r = mish_parts(active)
    active = (active * w * r).astype(BF)
    embed_ref[...] = active
    time_shift = dot(active, time_proj[...]) + shifts[2:3, :]
    first_taps = conv_first[...].reshape(3 * C, C)
    second_taps = conv_second[...].reshape(3 * C, C)

    def masked(block, at, u):
        return (block.astype(F32) * frame_mask_of(at, block.shape[0], len_ref[u])).astype(BF)

    for u in range(U):
        x_ref[u, own, :] = masked(frames[u], start, u)
    for copy in halos[:2]:
        copy.wait_recv()
    for u in range(U):
        x_ref[u, 0:EDGE, :] = masked(lead[0, u], start - EDGE, u)
        x_ref[u, F + EDGE :, :] = masked(lead[1, u], start + F, u)
    keep(0).start()

    def valid(i, u):
        return jnp.clip(len_ref[u] - i * F, 0, F).astype(F32)

    def local_stats(hidden, stat, got, sems, u):
        mask = frame_mask_of(start, F, len_ref[u])
        inside = hidden[EDGE : EDGE + F]
        many = jnp.maximum(valid(me, u) * (C // GROUPS), 1.0)
        mean = group_sums(row_sum(inside * mask)) / many
        centered = (inside - mean) * mask
        stat[u, 0:1, :] = mean
        stat[u, 1:2, :] = group_sums(row_sum(centered * centered))
        for copy in share(stat, got, sems, u, me):
            copy.start()

    def whole_stats(stat, got, sems, u):
        for copy in share(stat, got, sems, u, me):
            copy.wait()
        total = len_ref[u].astype(F32)
        parts = [(valid(me, u), stat[u])]
        for j in range(3):
            parts.append((valid(xor4(me, j + 1), u), got[j, u]))
        mean = sum(n * p[0:1] for n, p in parts) / total
        squares = sum(p[1:2] + (n * (C // GROUPS)) * jnp.square(p[0:1] - mean) for n, p in parts)
        inv = lax.rsqrt(squares / (total * (C // GROUPS)) + norm_eps)
        return mean, inv

    def activate(hidden, mean, inv, gain, shift):
        v = (hidden - mean) * inv * gain + shift
        e, w, r = mish_parts(v)
        return v * w * r

    for u in range(U):
        hidden = dot(taps_of(x_ref[u]), first_taps) + shifts[0:1, :]
        h1_ref[u] = hidden
        local_stats(hidden, stat_one, got_one, sems_one, u)
    keep(1).start()
    for u in range(U):
        mean, inv = whole_stats(stat_one, got_one, sems_one, u)
        stat_ref[u, 0:1, :] = mean
        stat_ref[u, 1:2, :] = inv
        mask = frame_mask_of(start - EDGE, rows, len_ref[u])
        act = activate(h1_ref[u], mean, inv, gains[0:1, :], shifts[1:2, :])
        act_in = ((act + time_shift[u : u + 1]) * mask).astype(BF)
        act_ref[u] = act_in
        hidden = dot(taps_of(act_in), second_taps) + shifts[3:4, :]
        h2_ref[u] = hidden
        local_stats(hidden, stat_two, got_two, sems_two, u)
    keep(2).start()
    keep(3).start()
    for u in range(U):
        mean, inv = whole_stats(stat_two, got_two, sems_two, u)
        stat_ref[u, 2:3, :] = mean
        stat_ref[u, 3:4, :] = inv
        mask = frame_mask_of(start, F, len_ref[u])
        act = activate(h2_ref[u, own, :], mean, inv, gains[1:2, :], shifts[4:5, :]) * mask
        res = act + dot(x_ref[u, own, :], conv_skip[...]) + shifts[5:6, :]
        res_ref[u] = res
        centered = res - lane_mean(res)
        hat = centered * lax.rsqrt(lane_mean(centered * centered) + norm_eps)
        normed = (hat * gains[2:3, :] + shifts[6:7, :]).astype(BF)
        qkv = dot(normed, w_qkv[...]).astype(BF)
        all_ref[0, u] = qkv[:, 128:384]
        hop(1, u).start()
        hop(0, u).start()
        keep_block(0, u).start()
        for h in range(2):
            other = jnp.where(lane == 64 * (1 - h) + 3, one, zero)
            qa_ref[u, h] = jnp.where(head_lanes(lane, h), qkv[:, 0:128] * SCALE, other)
    keep(4).start()
    top[...] = jnp.full(top.shape, -1e30, F32)
    factors[...] = jnp.zeros(factors.shape, F32)
    acc[...] = jnp.zeros(acc.shape, F32)

    def block_of(t):
        late = t // 4
        r = (1 - late) * (t // 2) + late * (2 + t % 2)
        return r, (1 - late) * (t % 2) + late * ((t - 4) // 2)

    def keep_probs(t):
        r, u = block_of(t)
        return pltpu.make_async_copy(probs.at[t % 2], probs_out.at[r, u], probs_sems.at[t % 2])

    def arrive(t):
        @pl.when(t >= 3)
        def _():
            keep_probs(t - 3).wait()

        @pl.when(t >= 2)
        def _():
            keep_probs(t - 2).start()

        @pl.when(t == 2)
        def _():
            hop(0, 0).wait_recv()
            keep_block(1, 0).start()

        @pl.when(t == 3)
        def _():
            hop(0, 1).wait_recv()
            keep_block(1, 1).start()

        @pl.when(t == 4)
        def _():
            hop(1, 0).wait()
            hop(2, 0).start()
            keep_block(2, 0).start()

        @pl.when(t == 5)
        def _():
            hop(2, 0).wait_recv()
            keep_block(3, 0).start()

        @pl.when(t == 6)
        def _():
            hop(1, 1).wait()
            hop(2, 1).start()
            keep_block(2, 1).start()

        @pl.when(t == 7)
        def _():
            hop(2, 1).wait_recv()
            keep_block(3, 1).start()

    def scores(t, held, tops):
        r, u = block_of(t)
        k = all_ref[r, u, :, 0:128]
        spot = xor4(me, r) * F + lax.broadcasted_iota(jnp.int32, (F, 1), 0)
        bias = jnp.where(spot < len_ref[u], 0.0, -1e9).astype(BF)
        for h in range(2):
            ka = jnp.where(head_lanes(lane, h), k, jnp.where(lane == 64 * (1 - h) + 3, bias, zero))
            s = dot(ka, qa_ref[u, h], NT)
            held[h] = s
            tops[h, 0:1, :] = jnp.max(s, axis=0, keepdims=True)

    def weigh(t, slot, held, tops):
        r, u = block_of(t)
        vt = all_ref[r, u, :, 128:256].T
        ones = jnp.ones((EDGE, F), BF)
        for h in range(2):
            old = top[u, h, 0:1, :]
            new = jnp.maximum(old, tops[h, 0:1, :])
            p = jnp.exp(held[h] - new).astype(BF)
            probs[slot, h] = p
            tops_used[r, u, h : h + 1, :] = new
            va = jnp.concatenate([vt[64 * h : 64 * h + 64], ones], axis=0)
            acc[u, h] = acc[u, h] * jnp.exp(old - new) + dot(va, p)
            top[u, h, 0:1, :] = new

    scores(0, held_one, tops_one)

    def two_steps(n, _):
        t = 2 * n
        arrive(t + 1)
        scores(t + 1, held_two, tops_two)
        weigh(t, 0, held_one, tops_one)
        arrive(t + 2)
        scores(t + 2, held_one, tops_one)
        weigh(t + 1, 1, held_two, tops_two)
        return 0

    lax.fori_loop(0, 3, two_steps, 0)
    arrive(7)
    scores(7, held_two, tops_two)
    weigh(6, 0, held_one, tops_one)
    keep_probs(5).wait()
    keep_probs(6).start()
    weigh(7, 1, held_two, tops_two)
    keep_probs(7).start()
    for u in range(U):
        outs, logs = [], []
        for h in range(2):
            total = acc[u, h, 64:65, :]
            outs.append(acc[u, h, 0:64, :] / total)
            logs.append(top[u, h, 0:1, :] + jnp.log(total))
        o_ref[u] = jnp.concatenate(outs, axis=0).T
        for r in range(4):
            for h in range(2):
                factors[r, u, h : h + 1, :] = jnp.exp(tops_used[r, u, h : h + 1, :] - logs[h])
    for u in range(U):
        hop(0, u).wait_send()
        hop(2, u).wait_send()
        for r in range(4):
            keep_block(r, u).wait()
    for name in range(5):
        keep(name).wait()
    keep_probs(6).wait()
    keep_probs(7).wait()
    for copy in halos:
        copy.wait_send()
    halos[2].wait_recv()


def front(lengths, frames, embed, cotangent, conv_first, conv_second, conv_skip, time_proj, w_qkv, gains, shifts):
    U, F, C = frames.shape
    rows = F + 2 * EDGE
    vmem = pl.BlockSpec(memory_space=pltpu.VMEM)
    stat = pltpu.VMEM((U, 8, C), F32)
    got = pltpu.VMEM((3, U, 8, C), F32)
    return pl.pallas_call(
        front_kernel,
        out_shape=(
            jax.ShapeDtypeStruct((U, rows, C), BF),
            jax.ShapeDtypeStruct((U, rows, C), F32),
            jax.ShapeDtypeStruct((U, rows, C), BF),
            jax.ShapeDtypeStruct((U, rows, C), F32),
            jax.ShapeDtypeStruct((U, F, C), F32),
            jax.ShapeDtypeStruct((4, U, F, 256), BF),
            jax.ShapeDtypeStruct((4, U, 2, F, F), BF),
            jax.ShapeDtypeStruct((U, F, 128), F32),
            jax.ShapeDtypeStruct((U, 2, F, 128), BF),
            jax.ShapeDtypeStruct((U, 8, C), F32),
            jax.ShapeDtypeStruct(embed.shape, BF),
            jax.ShapeDtypeStruct((U, EDGE, C), BF),
            jax.ShapeDtypeStruct((4, U, 8, F), F32),
        ),
        in_specs=[pl.BlockSpec(memory_space=pltpu.SMEM), vmem, vmem, pl.BlockSpec(memory_space=pl.ANY)] + [vmem] * 7,
        out_specs=[pl.BlockSpec(memory_space=pl.ANY)] * 7 + [vmem] * 6,
        scratch_shapes=[
            pltpu.VMEM((U, rows, C), BF),
            pltpu.VMEM((U, rows, C), F32),
            pltpu.VMEM((U, rows, C), BF),
            pltpu.VMEM((U, rows, C), F32),
            pltpu.VMEM((U, F, C), F32),
            pltpu.VMEM((4, U, F, 256), BF),
            pltpu.VMEM((2, U, EDGE, C), BF),
            stat,
            got,
            stat,
            got,
            pltpu.VMEM((U, 2, 8, F), F32),
            pltpu.VMEM((U, 2, 64 + EDGE, F), F32),
            pltpu.VMEM((2, F, F), F32),
            pltpu.VMEM((2, F, F), F32),
            pltpu.VMEM((2, 8, F), F32),
            pltpu.VMEM((2, 8, F), F32),
            pltpu.VMEM((2, 2, F, F), BF),
            pltpu.VMEM((4, U, 8, F), F32),
            pltpu.SemaphoreType.DMA((2, 3)),
            pltpu.SemaphoreType.DMA((2, 3, U)),
            pltpu.SemaphoreType.DMA((2, 3, U)),
            pltpu.SemaphoreType.DMA((2, 3, U)),
            pltpu.SemaphoreType.DMA((5,)),
            pltpu.SemaphoreType.DMA((4, U)),
            pltpu.SemaphoreType.DMA((2,)),
        ],
        compiler_params=pltpu.CompilerParams(
            collective_id=1, has_side_effects=True, vmem_limit_bytes=62 * 2**20
        ),
        name="front",
    )(lengths, frames, embed, cotangent, conv_first, conv_second, conv_skip, time_proj, w_qkv, gains, shifts)


def resnet_back_kernel(
    axes,
    len_ref,
    gqkv_in,
    gtwo_in,
    res_in,
    x_in,
    h1_in,
    act_in,
    h2_in,
    stat_ref,
    conv_first,
    conv_second,
    conv_skip,
    w_qkv,
    gains,
    shifts,
    up_ends,
    gframes,
    up,
    mid,
    late,
    last,
    gsmall,
    gfirst,
    gsecond,
    gskip,
    gw_qkv,
    lows,
    gqkv_ref,
    gtwo_ref,
    res_ref,
    x_ref,
    h1_ref,
    act_ref,
    h2_ref,
    load_sems,
    edges,
    gone,
    gmasked,
    sum_two,
    got_two,
    sum_one,
    got_one,
    halo_sems,
    sems_two,
    sems_one,
    small_got,
    small_sems,
    *sum_refs,
):
    U, F, C = gtwo_ref.shape
    given = (gqkv_in, res_in, gtwo_in, x_in, h2_in, act_in, h1_in)
    held = (gqkv_ref, res_ref, gtwo_ref, x_ref, h2_ref, act_ref, h1_ref)

    def load(name, u):
        return pltpu.make_async_copy(given[name].at[u], held[name].at[u], load_sems.at[name, u])

    for names in ((0, 1, 2, 3), (4, 5, 6)):
        for u in range(U):
            for name in names:
                load(name, u).start()
    rows = F + 2 * EDGE
    own = pl.ds(EDGE, F)
    inner = slice(EDGE, EDGE + F)
    me = lax.axis_index("seq")
    count = lax.axis_size("seq")
    after, behind = lax.rem(me + 1, count), lax.rem(me + count - 1, count)
    start = me * F
    hops, stages = butterfly(axes), stages_of(axes)
    greet_stages(stages, [("seq", xor4(me, 3))])
    fine = stages_of(axes, 1)
    run_up = doubling_steps(fine, up_ends, up, sum_refs[0])
    run_mid = sum_steps(stages, *sum_refs[1:5], mid, *sum_refs[5:7])
    run_late = sum_steps(stages, *sum_refs[7:11], late, *sum_refs[11:13])
    run_last = sum_steps(stages, *sum_refs[13:17], last, *sum_refs[17:19])
    run_small = small_steps(hops, gsmall, small_got, small_sems)
    for ref in (gsmall, sum_two, sum_one):
        ref[...] = jnp.zeros_like(ref)

    run_up(0)

    def halo(kind, u):
        spot = pl.ds(F, EDGE) if kind == 0 else pl.ds(EDGE, EDGE)
        return pltpu.make_async_remote_copy(
            gone.at[u, spot],
            edges.at[kind, u],
            halo_sems.at[0, kind, u],
            halo_sems.at[1, kind, u],
            device_id={"seq": after if kind == 0 else behind},
            device_id_type=MESH,
        )

    for u in range(U):
        for name in range(4):
            load(name, u).wait()
        res = res_ref[u]
        centered = res - lane_mean(res)
        inv = lax.rsqrt(lane_mean(centered * centered) + norm_eps)
        hat = centered * inv
        normed = (hat * gains[2:3, :] + shifts[6:7, :]).astype(BF)
        gqkv = gqkv_ref[u]
        part = tn(normed, gqkv)
        gw_qkv[...] = part if u == 0 else gw_qkv[...] + part
        grad = dot(gqkv, w_qkv[...], NT)
        gsmall[10:11, :] += row_sum(grad * hat)
        gsmall[6:7, :] += row_sum(grad)
        grad = grad * gains[2:3, :]
        grad = gtwo_ref[u] + inv * (grad - lane_mean(grad) - hat * lane_mean(grad * hat))
        gone[u, own, :] = grad
        for kind in range(2):
            halo(kind, u).start()
        gsmall[5:6, :] += row_sum(grad)
        low = grad.astype(BF)
        part = tn(x_ref[u, own, :], low)
        gskip[...] = part if u == 0 else gskip[...] + part
        gmasked[u] = dot(low, conv_skip[...], NT)
        if u == 0:
            run_up(1)

    def norm_terms(grad, hidden, u, at):
        mean, inv = stat_ref[u, 2 * at : 2 * at + 1, :], stat_ref[u, 2 * at + 1 : 2 * at + 2, :]
        gain, shift = gains[at : at + 1, :], shifts[1 + 3 * at : 2 + 3 * at, :]
        hat = (hidden - mean) * inv
        v = hat * gain + shift
        e, w, r = mish_parts(v)
        slope = w * r + v * (4.0 * e * (1.0 + e)) * (r * r)
        return hat, grad * slope, inv, gain

    def local_sums(hat, grad, gain, sums, got, sems, u, at):
        hat, grad = hat[inner], grad[inner]
        gsmall[8 + at : 9 + at, :] += row_sum(grad * hat)
        gsmall[1 + 3 * at : 2 + 3 * at, :] += row_sum(grad)
        grad = grad * gain
        both = jnp.concatenate([row_sum(grad), row_sum(grad * hat)], axis=0)
        sums[u, 0:2, :] = group_sums(both)
        for copy in share(sums, got, sems, u, me):
            copy.start()

    def whole_sums(sums, got, sems, u):
        for copy in share(sums, got, sems, u, me):
            copy.wait()
        return (sums[u] + got[0, u]) + (got[1, u] + got[2, u])

    def hidden_grad(hat, grad, inv, gain, total, u, mask):
        many = len_ref[u].astype(F32) * (C // GROUPS)
        return inv * (grad * gain - mask * ((total[0:1] + hat * total[1:2]) / many))

    def back_taps(grad, weight):
        wide = grad.astype(F32)
        many = grad.shape[0]
        later = pltpu.roll(wide, many - 1, 0).astype(BF)
        earlier = pltpu.roll(wide, 1, 0).astype(BF)
        return dot(later, weight[0], NT) + dot(grad, weight[1], NT) + dot(earlier, weight[2], NT)

    def wide_mask(u):
        return frame_mask_of(start - EDGE, rows, len_ref[u])

    for u in range(U):
        for kind in range(2):
            halo(kind, u).wait()
        load(4, u).wait()
        gone[u, 0:EDGE, :] = edges[0, u]
        gone[u, F + EDGE :, :] = edges[1, u]
        hat, grad, inv, gain = norm_terms(gone[u] * wide_mask(u), h2_ref[u], u, 1)
        gone[u] = grad
        local_sums(hat, grad, gain, sum_two, got_two, sems_two, u, 1)
    for u in range(U):
        load(5, u).wait()
        load(6, u).wait()
        total = whole_sums(sum_two, got_two, sems_two, u)
        mask = wide_mask(u)
        inv, gain = stat_ref[u, 3:4, :], gains[1:2, :]
        hat = (h2_ref[u] - stat_ref[u, 2:3, :]) * inv
        grad = hidden_grad(hat, gone[u], inv, gain, total, u, mask)
        gsmall[3:4, :] += row_sum(grad[inner])
        low = grad.astype(BF)
        part = tn(taps_of(act_ref[u])[inner], low[inner])
        gsecond[...] = part if u == 0 else gsecond[...] + part
        grad = back_taps(low, conv_second) * mask
        by_time = row_sum(grad[inner])
        gsmall[2:3, :] += by_time
        gsmall[pl.ds(16 + lax.axis_index("dp") * U + u, 1), :] = by_time
        hat, grad, inv, gain = norm_terms(grad, h1_ref[u], u, 0)
        gone[u] = grad
        local_sums(hat, grad, gain, sum_one, got_one, sems_one, u, 0)
        if u == 0:
            run_up(2)
        else:
            pack(sum_refs[1], [gskip, gw_qkv])
            run_mid(0)
    pack(sum_refs[7], [gsecond])
    run_late(0)
    for u in range(U):
        total = whole_sums(sum_one, got_one, sems_one, u)
        mask = wide_mask(u)
        inv, gain = stat_ref[u, 1:2, :], gains[0:1, :]
        hat = (h1_ref[u] - stat_ref[u, 0:1, :]) * inv
        grad = hidden_grad(hat, gone[u], inv, gain, total, u, mask)
        gsmall[0:1, :] += row_sum(grad[inner])
        low = grad.astype(BF)
        lows[u] = low
        part = tn(taps_of(x_ref[u])[inner], low[inner])
        gfirst[...] = part if u == 0 else gfirst[...] + part
        if u == U - 1:
            run_late(1)
            run_mid(1)
    pack(sum_refs[13], [gfirst])
    steps = 2 * len(stages)
    for n in range(max(steps, len(hops)) + 1):
        for run, ahead, final in (
            (run_last, 0, steps),
            (run_late, 2, steps),
            (run_mid, 2, steps),
            (run_small, 0, len(hops)),
        ):
            if ahead + n <= final:
                run(ahead + n)
        if 0 <= n - 2 <= len(fine) - 3:
            run_up(n + 1)
        if n < U:
            grad = back_taps(lows[n], conv_first)[inner] + gmasked[n]
            gframes[n] = grad * frame_mask_of(start, F, len_ref[n])


def resnet_back(lengths, gqkv, gtwo, res, x, h1, act, h2, stat, conv_first, conv_second, conv_skip, w_qkv, gains, shifts, up_ends, axes):
    U, F, C = gtwo.shape
    count = bits_of(axes)
    shapes = [(3 * C, C), (3 * C, C), (C, C), w_qkv.shape]
    mats = [jax.ShapeDtypeStruct(shape, F32) for shape in shapes]
    up_rows = up_ends.shape[0] << count
    row_counts = [padded_rows(packed_rows(some), axes) for some in (mats[2:], mats[1:2], mats[:1])]
    small_rows = 16 + U * dict(axes)["dp"]
    rows = F + 2 * EDGE
    vmem = pl.BlockSpec(memory_space=pltpu.VMEM)
    sums = pltpu.VMEM((U, 8, C), F32)
    got = pltpu.VMEM((3, U, 8, C), F32)
    return pl.pallas_call(
        functools.partial(resnet_back_kernel, axes),
        out_shape=(
            jax.ShapeDtypeStruct((U, F, C), F32),
            *(jax.ShapeDtypeStruct((many, 128), BF) for many in [up_rows, *row_counts]),
            jax.ShapeDtypeStruct((small_rows, C), F32),
        ),
        in_specs=[pl.BlockSpec(memory_space=pltpu.SMEM)]
        + [pl.BlockSpec(memory_space=pl.ANY)] * 7
        + [vmem] * 8,
        out_specs=[vmem] * 6,
        scratch_shapes=[
            *(pltpu.VMEM(shape, F32) for shape in shapes),
            pltpu.VMEM((U, rows, C), BF),
            *(pltpu.VMEM(x.shape, x.dtype) for x in (gqkv, gtwo, res, x, h1, act, h2)),
            pltpu.SemaphoreType.DMA((7, U)),
            pltpu.VMEM((2, U, EDGE, C), F32),
            pltpu.VMEM((U, rows, C), F32),
            pltpu.VMEM((U, F, C), F32),
            sums,
            got,
            sums,
            got,
            pltpu.SemaphoreType.DMA((2, 2, U)),
            pltpu.SemaphoreType.DMA((2, 3, U)),
            pltpu.SemaphoreType.DMA((2, 3, U)),
            pltpu.VMEM((count, small_rows, C), F32),
            pltpu.SemaphoreType.DMA((2, count)),
            pltpu.SemaphoreType.DMA((2, stage_count(axes, 1), 7)),
            *(ref for many in row_counts for ref in sum_scratch(many, axes)),
        ],
        compiler_params=pltpu.CompilerParams(
            collective_id=4, has_side_effects=True, vmem_limit_bytes=60 * 2**20
        ),
        name="resnet_back",
    )(lengths, gqkv, gtwo, res, x, h1, act, h2, stat, conv_first, conv_second, conv_skip, w_qkv, gains, shifts, up_ends)


def shards(
    frames,
    time_embed,
    lengths,
    out_cotangent,
    conv_first,
    conv_second,
    conv_skip,
    time_proj,
    w_qkv,
    w_out,
    ff_in,
    ff_out,
    conv_down,
    gains,
    shifts,
    ff_bias,
    snake_logs,
):
    channels = frames.shape[2]
    (
        masked_in,
        hidden_one,
        act_in,
        hidden_two,
        resnet_out,
        kv_all,
        probs,
        attended_full,
        queries_aug,
        stats,
        embed_act,
        next_rows,
        factors,
    ) = front(
        lengths,
        frames,
        time_embed,
        out_cotangent,
        conv_first,
        conv_second,
        conv_skip,
        time_proj,
        w_qkv,
        gains,
        shifts,
    )
    (
        layer_out,
        grad_two,
        grad_aug,
        first_rows,
        tail_rows,
        grad_w_out,
        grad_ff_in,
        grad_ff_out,
        grad_conv_down,
        mid_small,
        ff_small,
    ) = middle(
        lengths,
        attended_full,
        resnet_out,
        out_cotangent,
        next_rows,
        w_out,
        ff_in,
        ff_out,
        conv_down,
        gains,
        shifts,
        ff_bias,
        snake_logs,
    )
    axes = (("seq", lax.axis_size("seq")), ("dp", lax.axis_size("dp")))
    grad_qkv, up_ends, small_up, tail_rows = attend_back(
        queries_aug,
        grad_aug,
        kv_all,
        probs,
        factors,
        mid_small,
        ff_small,
        embed_act,
        tail_rows,
        [grad_w_out, grad_ff_in, grad_ff_out, grad_conv_down.reshape(-1, channels)],
        axes,
    )
    grad_frames, up, mid, late, last, small_late = resnet_back(
        lengths,
        grad_qkv,
        grad_two,
        resnet_out,
        masked_in,
        hidden_one,
        act_in,
        hidden_two,
        stats,
        conv_first,
        conv_second,
        conv_skip,
        w_qkv,
        gains,
        shifts,
        up_ends,
        axes,
    )
    weights = (
        conv_first,
        conv_second,
        conv_skip,
        time_proj,
        w_qkv,
        w_out,
        ff_in,
        ff_out,
        conv_down,
        gains,
        shifts,
        ff_bias.reshape(1, -1),
        snake_logs,
    )
    grads = finish(
        lengths,
        first_rows,
        tail_rows,
        layer_out,
        up,
        mid,
        late,
        last,
        small_up,
        small_late,
        [w.shape for w in weights],
    )
    return (grads[13], grad_frames, *grads[:11], grads[11].reshape(-1), grads[12])


def solution(mesh):
    in_specs = (
        P("dp", "seq", None),
        P("dp", None),
        P("dp"),
        P("dp", "seq", None),
        P(),
        P(),
        P(),
        P(),
        P(),
        P(),
        P(),
        P(),
        P(),
        P(),
        P(),
        P(),
        P(),
    )
    out_specs = (
        P("dp", "seq", None),
        P("dp", "seq", None),
        P(),
        P(),
        P(),
        P(),
        P(),
        P(),
        P(),
        P(),
        P(),
        P(),
        P(),
        P(),
        P(),
    )
    return jax.shard_map(shards, mesh=mesh, in_specs=in_specs, out_specs=out_specs, check_vma=False)
```

```python
import functools
import math

import jax
import jax.numpy as jnp
from jax import lax
from jax.experimental import pallas as pl
from jax.experimental.pallas import tpu as pltpu
from jax.sharding import PartitionSpec as P

F32, BF = jnp.float32, jnp.bfloat16
NT = (((1,), (1,)), ((), ()))
NN = (((1,), (0,)), ((), ()))
TN = (((0,), (0,)), ((), ()))
MESH = pl.DeviceIdType.MESH
EDGE = 16


def dot(a, b, dn=NN):
    return lax.dot_general(a, b, dn, preferred_element_type=F32)


HEADS = 2
GROUPS = 8


norm_eps = 1e-05


SIN_PI = (3.141592580060032, -5.167706879868365, 2.55003139258664, -0.598045264752551, 0.0772203056339658)
COS_PI = (0.9999999534804945, -4.934792860766467, 4.05841196261883, -1.3318805129033002, 0.21969758323424166)


def horner(coefficients, x):
    value = coefficients[-1]
    for coefficient in coefficients[-2::-1]:
        value = value * x + coefficient
    return value


def sin_cos_half_turns(turns):
    part = turns - jnp.round(turns)
    square = part * part
    return part * horner(SIN_PI, square), horner(COS_PI, square)


def row_sum(x):
    return jnp.sum(x, axis=0, keepdims=True)


def lane_mean(x):
    return jnp.mean(x, axis=1, keepdims=True)


def tn(a, b):
    return lax.dot_general(a, b, TN, preferred_element_type=F32)


def middle_kernel(
    RB,
    FC,
    len_ref,
    att_ref,
    res_ref,
    cot_ref,
    next_ref,
    w_out,
    ff_in,
    ff_out,
    conv_down,
    gains,
    shifts,
    ff_bias,
    snake_logs,
    out_ref,
    gtwo_ref,
    aug_ref,
    row_ref,
    tail_ref,
    gw_out,
    gff_in,
    gff_out,
    gdown,
    gsmall,
    gff_small,
    pairs,
    before_last,
    acc_out,
):
    u, i = pl.program_id(0), pl.program_id(1)
    U, nb = pl.num_programs(0), pl.num_programs(1)
    half = RB // 2
    frames = nb * RB
    length = len_ref[u]
    base = lax.axis_index("seq") * frames
    at = base + i * RB

    @pl.when((u == 0) & (i == 0))
    def _():
        for ref in (gw_out, gff_in, gdown, gsmall, gff_small, acc_out):
            ref[...] = jnp.zeros_like(ref)

    def column_mask(start, rows, step):
        places = start + step * lax.broadcasted_iota(jnp.int32, (rows, 1), 0)
        return jnp.where(places < length, 1.0, 0.0)

    mask = column_mask(at, RB, 1)
    half_mask = column_mask(at, half, 2)
    low_f32 = cot_ref[0, pl.ds(pl.multiple_of(i * half, half), half), :].astype(F32) * half_mask
    gsmall[4:5, :] += row_sum(low_f32)
    low = low_f32.astype(BF)
    follow = jnp.minimum(i * half + half, frames // 2 - 16)
    inner = cot_ref[0, pl.ds(pl.multiple_of(follow, 16), 16), :].astype(F32)[0:1]
    outer = next_ref[0].astype(F32)[0:1]
    after = jnp.where(i == nb - 1, outer, inner) * jnp.where(at + RB < length, 1.0, 0.0)
    row_at = lax.broadcasted_iota(jnp.int32, (half, 1), 0)
    low_next = jnp.where(row_at == half - 1, after, pltpu.roll(low_f32, half - 1, 0)).astype(BF)
    even_grads = dot(low, conv_down[1], NT)
    odd_grads = dot(low, conv_down[2], NT) + dot(low_next, conv_down[0], NT)
    for lanes in (0, 128):
        pairs[lanes // 128, pl.ds(0, half, stride=2), :] = even_grads[:, lanes : lanes + 128]
        pairs[lanes // 128, pl.ds(1, half, stride=2), :] = odd_grads[:, lanes : lanes + 128]
    grad_three = jnp.concatenate([pairs[0], pairs[1]], axis=1) * mask
    gsmall[3:4, :] += row_sum(grad_three)
    grad_low = grad_three.astype(BF)
    attended = att_ref[0]
    att_low = attended.astype(BF)
    resid_two = res_ref[0] + dot(att_low, w_out[...]) + shifts[7:8, :]
    centered = resid_two - lane_mean(resid_two)
    inv = lax.rsqrt(lane_mean(centered * centered) + norm_eps)
    hat = centered * inv
    normed = (hat * gains[3:4, :] + shifts[8:9, :]).astype(BF)
    freq = jnp.exp(snake_logs[0:1, :])
    spread = jnp.exp(snake_logs[1:2, :])
    size = 1.0 / (spread + 1e-09)
    turn = freq * (1.0 / math.pi)
    resid_three = resid_two + shifts[9:10, :]
    grad_normed = jnp.zeros_like(resid_two)
    for c in range(0, ff_bias.shape[1], FC):
        cols = slice(c, c + FC)
        hidden = dot(normed, ff_in[:, cols]) + ff_bias[:, cols]
        sine, cosine = sin_cos_half_turns(hidden * turn[:, cols])
        square = sine * sine
        snaked = (hidden + square * size[:, cols]).astype(BF)
        resid_three = resid_three + dot(snaked, ff_out[cols, :])
        acc_out[:, cols] += tn(grad_low, snaked)
        grad_snaked = dot(grad_low, ff_out[cols, :], NT)
        cross = grad_snaked * (sine * cosine)
        grad_hidden = grad_snaked + cross * (2.0 * size * freq)[:, cols]
        gff_small[0:1, cols] += row_sum(grad_hidden)
        gff_small[1:2, cols] += row_sum(cross * hidden)
        gff_small[2:3, cols] += row_sum(grad_snaked * square)
        hidden_low = grad_hidden.astype(BF)
        gff_in[:, cols] += tn(normed, hidden_low)
        grad_normed = grad_normed + dot(hidden_low, ff_in[:, cols], NT)
    down = (resid_three * mask).astype(BF)
    down_f32 = down.astype(F32)
    for lanes in (0, 128):
        pairs[lanes // 128] = down_f32[:, lanes : lanes + 128]
    even = jnp.concatenate([pairs[j, pl.ds(0, half, stride=2), :] for j in range(2)], axis=1)
    odd = jnp.concatenate([pairs[j, pl.ds(1, half, stride=2), :] for j in range(2)], axis=1)
    first = jnp.where(i == 0, 0.0, before_last[0:1, :])
    before = jnp.where(row_at == 0, first, pltpu.roll(odd, 1, 0)).astype(BF)
    before_last[0:1, :] = odd[half - 1 : half, :]
    tail_ref[0] = dot(down[RB - 16 :, :], conv_down[0])[8:16]
    even, odd = even.astype(BF), odd.astype(BF)
    lowered = dot(before, conv_down[0]) + dot(even, conv_down[1]) + dot(odd, conv_down[2])
    lowered = lowered + shifts[10:11, :]

    @pl.when(i == 0)
    def _():
        row_ref[0] = lowered[0:8]

    out_ref[0] = (lowered * half_mask).astype(BF)
    gdown[0] += tn(odd, low_next)
    gdown[1] += tn(even, low)
    gdown[2] += tn(odd, low)
    gsmall[0:1, :] += row_sum(grad_normed * hat)
    gsmall[2:3, :] += row_sum(grad_normed)
    grad_hat = grad_normed * gains[3:4, :]
    grad_two = grad_three + inv * (
        grad_hat - lane_mean(grad_hat) - hat * lane_mean(grad_hat * hat)
    )
    gtwo_ref[0] = grad_two
    gsmall[1:2, :] += row_sum(grad_two)
    two_low = grad_two.astype(BF)
    gw_out[...] += tn(att_low, two_low)
    grad_att = dot(two_low, w_out[...], NT).astype(BF)
    terms = grad_att.astype(F32) * attended
    lane = lax.broadcasted_iota(jnp.int32, (1, 128), 1)
    zero = jnp.zeros((), F32)
    for h in range(2):
        mine = (lane >= 64 * h) & (lane < 64 * h + 64)
        term = jnp.sum(jnp.where(mine, terms, zero), axis=1, keepdims=True)
        aug_ref[0, h] = with_pieces(jnp.where(mine, grad_att, jnp.zeros((), BF)), term, lane, h)

    @pl.when((u == U - 1) & (i == nb - 1))
    def _():
        gff_out[...] = acc_out[...].T
        gff_small[1:2, :] = gff_small[1:2, :] * (2.0 * size * freq)
        gff_small[2:3, :] = gff_small[2:3, :] * (-(size * size) * spread)


def with_pieces(block, value, lane, h):
    base = 64 * (1 - h)
    for j in range(3):
        piece = value.astype(BF)
        value = value - piece.astype(F32)
        block = jnp.where(lane == base + j, piece, block)
    return block


def middle(lengths, attended, resnet_out, cotangent, next_rows, w_out, ff_in, ff_out, conv_down, gains, shifts, ff_bias, snake_logs, FC=256):
    U, F, C = resnet_out.shape
    RB = min(F, 1024)
    inner = attended.shape[2]
    FF = ff_bias.shape[0]
    whole = lambda shape: pl.BlockSpec(shape, lambda u, i, _: (0,) * len(shape))
    rows = lambda n, c: pl.BlockSpec((1, n, c), lambda u, i, _: (u, i, 0))
    per_utt = lambda n, c: pl.BlockSpec((1, n, c), lambda u, i, _: (u, 0, 0))
    sums = ((inner, C), (C, FF), (FF, C), (3, C, C), (8, C), (8, FF))
    return pl.pallas_call(
        functools.partial(middle_kernel, RB, FC),
        out_shape=(
            jax.ShapeDtypeStruct((U, F // 2, C), BF),
            jax.ShapeDtypeStruct((U, F, C), F32),
            jax.ShapeDtypeStruct((U, 2, F, inner), BF),
            jax.ShapeDtypeStruct((U, 8, C), F32),
            jax.ShapeDtypeStruct((U, 8, C), F32),
            *(jax.ShapeDtypeStruct(shape, F32) for shape in sums),
        ),
        grid_spec=pltpu.PrefetchScalarGridSpec(
            num_scalar_prefetch=1,
            grid=(U, F // RB),
            in_specs=[
                rows(RB, inner),
                rows(RB, C),
                per_utt(F // 2, C),
                per_utt(16, C),
                whole((inner, C)),
                whole((C, FF)),
                whole((FF, C)),
                whole((3, C, C)),
                whole(gains.shape),
                whole(shifts.shape),
                whole((1, FF)),
                whole((2, FF)),
            ],
            out_specs=[
                rows(RB // 2, C),
                rows(RB, C),
                pl.BlockSpec((1, 2, RB, inner), lambda u, i, _: (u, 0, i, 0)),
                per_utt(8, C),
                per_utt(8, C),
                *(whole(shape) for shape in sums),
            ],
            scratch_shapes=[
                pltpu.VMEM((2, RB, 128), F32),
                pltpu.VMEM((8, C), F32),
                pltpu.VMEM((C, FF), F32),
            ],
        ),
        compiler_params=pltpu.CompilerParams(vmem_limit_bytes=56 * 2**20),
        name="middle",
    )(lengths, attended, resnet_out, cotangent, next_rows, w_out, ff_in, ff_out, conv_down, gains, shifts, ff_bias.reshape(1, -1), snake_logs)


def butterfly(axes):
    hops = []
    for axis, size in axes:
        place = lax.axis_index(axis)
        bit = 1
        while bit < size:
            up = (place // bit) % 2
            hops.append((axis, place + bit - 2 * bit * up, up))
            bit *= 2
    return hops


def bits_of(axes):
    return sum(size.bit_length() - 1 for _, size in axes)


def radices(axis, size, fine):
    while size > 1:
        radix = min(2 if axis == "seq" else 8, size)
        if fine and axis == "dp":
            radix = 2 if fine == 1 else min(4, size)
            fine = 2
        yield radix
        size //= radix


def stages_of(axes, fine=0):
    stages = []
    for axis, size in axes:
        stride = 1
        for radix in radices(axis, size, fine):
            place = lax.axis_index(axis)
            digit = (place // stride) % radix
            peers = [place + ((digit + m) % radix - digit) * stride for m in range(1, radix)]
            stages.append((axis, radix, digit, peers))
            stride *= radix
    return [stages[0], *stages[2:], stages[1]] if fine else stages


def padded_rows(rows, axes):
    unit = EDGE << bits_of(axes)
    return -(-rows // unit) * unit


def packed_rows(mats):
    return sum(m.shape[0] * m.shape[1] // 128 for m in mats)


def greet_stages(stages, extra=()):
    barrier = pltpu.get_barrier_semaphore()
    met = [(axis, peer) for axis, _, _, peers in stages for peer in peers] + list(extra)
    for axis, peer in met:
        pl.semaphore_signal(barrier, inc=1, device_id={axis: peer}, device_id_type=MESH)
    pl.semaphore_wait(barrier, len(met))


def hop_copy(hop, src, dst, sems, place):
    axis, partner, _ = hop
    return pltpu.make_async_remote_copy(
        src, dst, sems.at[(0, *place)], sems.at[(1, *place)], device_id={axis: partner}, device_id_type=MESH
    )


def pack(total, mats):
    row = 0
    for ref in mats:
        rows, columns = ref.shape
        for column in range(0, columns, 128):
            total[pl.ds(row, rows), :] = ref[:, column : column + 128]
            row += rows
    if row < total.shape[0]:
        total[pl.ds(row, total.shape[0] - row), :] = jnp.zeros((total.shape[0] - row, 128), F32)


def shares_of(stages, rows):
    low, length, shares = 0, rows, []
    for _, radix, digit, _ in stages:
        shares.append((low, length, length // radix))
        length //= radix
        low = pl.multiple_of(low + digit * length, EDGE)
    return shares, low


def halving_steps(stages, total, sent, got, ends, sems):
    rows = total.shape[0]
    shares, _ = shares_of(stages, rows)

    def copies(s):
        axis, radix, _, peers = stages[s]
        _, before, length = shares[s]
        for m, peer in enumerate(peers):
            slot = pl.ds(rows - before + m * length, length)
            yield m, slot, hop_copy((axis, peer, 0), sent.at[slot], got.at[slot], sems, (s, m))

    def run(k):
        if k > 0:
            _, radix, digit, _ = stages[k - 1]
            low, _, length = shares[k - 1]
            here = pl.ds(pl.multiple_of(low + digit * length, EDGE), length)
            value = total[here, :]
            for _, slot, copy in copies(k - 1):
                copy.wait()
                value = value + got[slot, :].astype(F32)
            if k < len(stages):
                total[here, :] = value
            else:
                ends[...] = value.astype(BF)
        if k < len(stages):
            _, radix, digit, _ = stages[k]
            low, _, length = shares[k]
            for m, slot, copy in copies(k):
                give = pl.multiple_of(low + (digit + m + 1) % radix * length, EDGE)
                sent[slot, :] = total[pl.ds(give, length), :].astype(BF)
                copy.start()

    return run


def doubling_steps(stages, ends, whole, sems):
    count = len(stages)
    shares, own = shares_of(stages, whole.shape[0])

    def copies(s):
        axis, _, digit, peers = stages[s]
        low, _, length = shares[s]
        here = pl.ds(pl.multiple_of(low + digit * length, EDGE), length)
        for m, peer in enumerate(peers):
            yield hop_copy((axis, peer, 0), whole.at[here], whole.at[here], sems, (s, m))

    def run(k):
        if k == 0:
            whole[pl.ds(own, ends.shape[0]), :] = ends[...]
        if k > 0:
            for copy in copies(count - k):
                copy.wait()
        if k < count:
            for copy in copies(count - 1 - k):
                copy.start()

    return run


def sum_steps(stages, total, sent, got, ends, whole, sems, more_sems):
    count = len(stages)
    halving = halving_steps(stages, total, sent, got, ends, sems)
    doubling = doubling_steps(stages, ends, whole, more_sems)

    def run(k):
        if k <= count:
            halving(k)
        if k >= count:
            doubling(k - count)

    return run


def small_steps(hops, mine, got, sems):
    def run(k):
        if 0 < k <= len(hops):
            hop_copy(hops[k - 1], mine, got.at[k - 1], sems, (k - 1,)).wait()
            mine[...] += got[k - 1]
        if k < len(hops):
            hop_copy(hops[k], mine, got.at[k], sems, (k,)).start()

    return run


def stage_count(axes, fine):
    return sum(len(list(radices(axis, size, fine))) for axis, size in axes)


def halving_scratch(rows, axes, fine):
    return [
        pltpu.VMEM((rows, 128), F32),
        pltpu.VMEM((rows, 128), BF),
        pltpu.VMEM((rows, 128), BF),
        pltpu.SemaphoreType.DMA((2, stage_count(axes, fine), 7)),
    ]


def sum_scratch(rows, axes):
    total, sent, got, sems = halving_scratch(rows, axes, 0)
    return [total, sent, got, pltpu.VMEM((rows >> bits_of(axes), 128), BF), sems, sems]


def finish_kernel(len_ref, rows, tails, layer, up, mid, late, last, small_up, small_late, *refs):
    outs, patched, edge, sems = refs[:13], refs[13], refs[14], refs[15]
    big, big_sems = refs[16:25], refs[25]
    U = rows.shape[0]
    fetch = pltpu.make_async_copy(layer.at[:, pl.ds(0, EDGE)], edge, sems.at[0])
    fetch.start()
    (
        first, second, skip, time_out, qkv, w_out, ff_in, ff_out, down, gains, shifts, bias, logs
    ) = (*big, *outs[9:])

    def send(n):
        return pltpu.make_async_copy(big[n], outs[n], big_sems.at[n])

    def unpack(packed, refs):
        row = 0
        for ref in refs:
            flat = ref.reshape(-1, ref.shape[-1]) if len(ref.shape) == 3 else ref
            rows, columns = flat.shape
            for column in range(0, columns, 128):
                flat[:, column : column + 128] = packed[pl.ds(row, rows), :].astype(F32)
                row += rows

    unpack(up, [w_out, ff_in, ff_out, down])
    for n in range(5, 9):
        send(n).start()
    unpack(mid, [skip, qkv])
    unpack(late, [second])
    unpack(last, [first])
    for n in (0, 1, 2, 4):
        send(n).start()
    C = skip.shape[0]
    wide = bias.shape[1] // C
    utts = small_late.shape[0] - 16
    gains[0:3, :] = small_late[8:11, :]
    gains[3:4, :] = small_up[0:1, :]
    shifts[0:7, :] = small_late[0:7, :]
    shifts[7:11, :] = small_up[1:5, :]
    blocks = [small_up[8 * (j + 1) : 8 * (j + 2), :] for j in range(wide)]
    base = packed_rows([w_out, ff_in, ff_out, down.reshape(-1, C)])
    embed = [up[pl.ds(base + utts * j, utts), :].astype(F32) for j in range(time_out.shape[0] // 128)]
    for j in range(wide):
        bias[:, j * C : (j + 1) * C] = blocks[j][0:1]
        logs[:, j * C : (j + 1) * C] = blocks[j][1:3]
    grads = small_late[16:, :]
    for j, part in enumerate(embed):
        time_out[j * 128 : (j + 1) * 128, :] = lax.dot_general(
            part, grads, TN, precision=lax.Precision.HIGHEST, preferred_element_type=F32
        )
    send(3).start()
    fetch.wait()
    me = lax.axis_index("seq")
    frames = 2 * layer.shape[1]
    is_first = lax.broadcasted_iota(jnp.int32, (EDGE, 1), 0) == 0
    for u in range(U):
        value = rows[u, 0:1] + jnp.where(me > 0, tails[u, 7:8], 0.0)
        value = value * jnp.where(me * frames < len_ref[u], 1.0, 0.0)
        edge[u] = jnp.where(is_first, value, edge[u].astype(F32)).astype(BF)
    store = pltpu.make_async_copy(edge, patched.at[:, pl.ds(0, EDGE)], sems.at[1])
    store.start()
    for n in range(9):
        send(n).wait()
    store.wait()


def finish(lengths, rows, tails, layer, up, mid, late, last, small_up, small_late, shapes):
    vmem = pl.BlockSpec(memory_space=pltpu.VMEM)
    anywhere = pl.BlockSpec(memory_space=pl.ANY)
    return pl.pallas_call(
        finish_kernel,
        out_shape=(
            *(jax.ShapeDtypeStruct(shape, F32) for shape in shapes),
            jax.ShapeDtypeStruct(layer.shape, BF),
        ),
        in_specs=[pl.BlockSpec(memory_space=pltpu.SMEM), vmem, vmem, anywhere] + [vmem] * 6,
        out_specs=[anywhere] * 9 + [vmem] * 4 + [anywhere],
        scratch_shapes=[
            pltpu.VMEM((rows.shape[0], EDGE, rows.shape[2]), BF),
            pltpu.SemaphoreType.DMA((2,)),
            *(pltpu.VMEM(shape, F32) for shape in shapes[:9]),
            pltpu.SemaphoreType.DMA((9,)),
        ],
        input_output_aliases={3: len(shapes)},
        compiler_params=pltpu.CompilerParams(vmem_limit_bytes=56 * 2**20),
        name="finish",
    )(lengths, rows, tails, layer, up, mid, late, last, small_up, small_late)


SCALE = 0.125


def head_lanes(lane, h):
    return (lane >= 64 * h) & (lane < 64 * h + 64)


def greet_seq(me):
    barrier = pltpu.get_barrier_semaphore()
    for flip in (1, 2):
        pl.semaphore_signal(barrier, inc=1, device_id={"seq": flipped(me, flip)}, device_id_type=MESH)
    pl.semaphore_wait(barrier, 2)


def flipped(place, bit):
    return place + bit - 2 * bit * ((place // bit) % 2)


def to_peer(src, dst, sems, place, peer):
    return pltpu.make_async_remote_copy(
        src, dst, sems.at[(0, *place)], sems.at[(1, *place)], device_id={"seq": peer}, device_id_type=MESH
    )


def xor4(place, r):
    low = (place % 2 + r % 2) % 2
    high = (place // 2 + r // 2) % 2
    return 2 * high + low


def backward_kernel(
    axes, qa_ref, da_ref, all_in, probs_ref, factors, mid_small, ff_small, embed_ref, tail_ref, *refs
):
    mats_in, refs = refs[:4], refs[4:]
    grad_ref, ends, small, tail_got, dqt, part, sent, got, sems, small_got, small_sems, tail_sems = refs[:12]
    probs, probs_sems, total, sum_sent, sum_got, sum_sems, all_ref = refs[12:19]
    block_sems, mat_sems, mats = refs[19], refs[20], refs[21:]
    U, _, F, _ = qa_ref.shape
    C = mid_small.shape[1]
    me = lax.axis_index("seq")
    near, far = flipped(me, 1), flipped(me, 2)
    lane = lax.broadcasted_iota(jnp.int32, (1, 128), 1)
    one, zero = jnp.ones((), BF), jnp.zeros((), BF)
    hops, stages = butterfly(axes), stages_of(axes)
    greet_stages(stages, [("seq", xor4(me, 3))])
    tails = pltpu.make_async_remote_copy(
        tail_ref,
        tail_got,
        tail_sems.at[0],
        tail_sems.at[1],
        device_id={"seq": lax.rem(me + 1, lax.axis_size("seq"))},
        device_id_type=MESH,
    )
    tails.start()
    small[...] = jnp.zeros(small.shape, F32)
    small[0:8, :] = mid_small[...]
    wide = ff_small.shape[1] // C
    for j in range(wide):
        small[8 * (j + 1) : 8 * (j + 2), :] = ff_small[:, j * C : (j + 1) * C]

    def bring_mat(n):
        return pltpu.make_async_copy(mats_in[n], mats[n], mat_sems.at[n])

    def fill():
        for n in range(len(mats)):
            bring_mat(n).wait()
        pack(total, mats)
        embed = embed_ref[...].astype(F32) * jnp.where(me == 0, 1.0, 0.0)
        base = packed_rows(mats)
        for j in range(embed.shape[1] // 128):
            for u in range(U):
                row = base + j * U * dict(axes)["dp"] + lax.axis_index("dp") * U + u
                total[pl.ds(row, 1), :] = embed[u : u + 1, j * 128 : (j + 1) * 128]

    fine = stages_of(axes, 1)
    run_sum = halving_steps(fine, total, sum_sent, sum_got, ends, sum_sems)
    run_small = small_steps(hops, small, small_got, small_sems)
    dqt[...] = jnp.zeros(dqt.shape, F32)

    def hop(kind, u):
        peer = far if kind == 1 else near
        return to_peer(sent.at[kind, u], got.at[kind, u], sems, (kind, u), peer)

    def block_of(t):
        late = t // 4
        r = (1 - late) * (3 - t % 2) + late * (1 - (t - 4) // 2)
        return r, (1 - late) * ((t // 2) % 2) + late * (t % 2)

    def fetch(t):
        r, u = block_of(t)
        return pltpu.make_async_copy(probs_ref.at[r, u], probs.at[t % 2], probs_sems.at[t % 2])

    def bring(t):
        r, u = block_of(t)
        return pltpu.make_async_copy(all_in.at[r, u], all_ref.at[r, u], block_sems.at[t])

    bring(0).start()
    fetch(0).start()
    for t in range(1, 8):
        bring(t).start()
    for n in range(len(mats)):
        bring_mat(n).start()
    run_small(0)

    def step(t, _):
        r, u = block_of(t)

        @pl.when(t < 7)
        def _():
            fetch(t + 1).start()

        bring(t).wait()
        fetch(t).wait()
        v = all_ref[r, u, :, 128:256]
        kt = all_ref[r, u, :, 0:128].T
        dks, dvs = [], []
        for h in range(2):
            base = 64 * (1 - h)
            extra = (lane >= base) & (lane < base + 3)
            va = jnp.where(head_lanes(lane, h), v, jnp.where(extra, -one, zero))
            qa = qa_ref[u, h]
            da = da_ref[u, h]
            p = jnp.concatenate(
                [
                    probs[t % 2, h, pl.ds(row * F // 2, F // 2), :].astype(F32)
                    * factors[r, u, 2 * h + row : 2 * h + row + 1, :]
                    for row in range(2)
                ],
                axis=0,
            )
            ds = (p * dot(va, da, NT)).astype(BF)
            dvs.append(dot(p.astype(BF), da))
            dks.append(dot(ds, qa))
            rows = slice(64 * h, 64 * h + 64)
            dqt[u, rows, :] += dot(kt[rows, :], ds)
        part[:, 0:128] = jnp.where(head_lanes(lane, 0), dks[0], dks[1])
        part[:, 128:256] = jnp.where(head_lanes(lane, 0), dvs[0], dvs[1])

        @pl.when(r == 3)
        def _():
            sent[0, u] = part[...].astype(BF)
            hop(0, u).start()

        @pl.when(r == 2)
        def _():
            hop(0, u).wait_recv()
            sent[1, u] = (part[...] + got[0, u].astype(F32)).astype(BF)
            hop(1, u).start()

        @pl.when(r == 1)
        def _():
            sent[2, u] = part[...].astype(BF)
            hop(2, u).start()

        @pl.when(r == 0)
        def _():
            hop(1, u).wait_recv()
            hop(2, u).wait_recv()
            both = part[...] + got[1, u].astype(F32) + got[2, u].astype(F32)
            grad_ref[u, :, 128:384] = both.astype(BF)
            grad_ref[u, :, 0:128] = (dqt[u] * SCALE).T.astype(BF)

        for slot in range(8):
            sums = [n for n in range(len(fine) + 1) if sum_slot(n, len(fine) + 1, 8) == slot]
            smalls = [n for n in range(1, len(hops) + 1) if sum_slot(n - 1, len(hops), 8) == slot]
            if sums or smalls:

                @pl.when(t == slot)
                def _(sums=sums, smalls=smalls):
                    for n in sums:
                        if n == 0:
                            fill()
                        run_sum(n)
                    for n in smalls:
                        run_small(n)

        return 0

    lax.fori_loop(0, 8, step, 0)
    tails.wait()
    for kind in range(3):
        for u in range(U):
            hop(kind, u).wait_send()


def sum_slot(step, count, slots):
    return -(-step * (slots - 1) // (count - 1))


def attend_back(qa, da, kv_all, probs, factors, mid_small, ff_small, embed, tails, mats, axes):
    U, _, F, _ = qa.shape
    C = mid_small.shape[1]
    count = bits_of(axes)
    embed_rows = U * dict(axes)["dp"] * embed.shape[1] // 128
    rows = padded_rows(packed_rows(mats) + embed_rows, axes)
    small_rows = 8 + 8 * (ff_small.shape[1] // C)
    vmem = pl.BlockSpec(memory_space=pltpu.VMEM)
    anywhere = pl.BlockSpec(memory_space=pl.ANY)
    return pl.pallas_call(
        functools.partial(backward_kernel, axes),
        out_shape=(
            jax.ShapeDtypeStruct((U, F, 384), BF),
            jax.ShapeDtypeStruct((rows >> count, 128), BF),
            jax.ShapeDtypeStruct((small_rows, C), F32),
            jax.ShapeDtypeStruct(tails.shape, F32),
        ),
        in_specs=[vmem, vmem, anywhere, anywhere] + [vmem] * 5 + [anywhere] * len(mats),
        out_specs=[vmem] * 4,
        scratch_shapes=[
            pltpu.VMEM((U, 128, F), F32),
            pltpu.VMEM((F, 256), F32),
            pltpu.VMEM((3, U, F, 256), BF),
            pltpu.VMEM((3, U, F, 256), BF),
            pltpu.SemaphoreType.DMA((2, 3, U)),
            pltpu.VMEM((count, small_rows, C), F32),
            pltpu.SemaphoreType.DMA((2, count)),
            pltpu.SemaphoreType.DMA((2,)),
            pltpu.VMEM((2, 2, F, F), BF),
            pltpu.SemaphoreType.DMA((2,)),
            *halving_scratch(rows, axes, 1),
            pltpu.VMEM(kv_all.shape, BF),
            pltpu.SemaphoreType.DMA((8,)),
            pltpu.SemaphoreType.DMA((len(mats),)),
            *(pltpu.VMEM(m.shape, F32) for m in mats),
        ],
        compiler_params=pltpu.CompilerParams(
            collective_id=2, has_side_effects=True, vmem_limit_bytes=60 * 2**20
        ),
        name="attend_back",
    )(qa, da, kv_all, probs, factors, mid_small, ff_small, embed, tails, *mats)


def frame_mask_of(start, rows, length):
    spot = start + lax.broadcasted_iota(jnp.int32, (rows, 1), 0)
    return jnp.where((spot >= 0) & (spot < length), 1.0, 0.0)


def taps_of(x):
    wide = x.astype(F32)
    rows = x.shape[0]
    return jnp.concatenate(
        [pltpu.roll(wide, 1, 0).astype(BF), x, pltpu.roll(wide, rows - 1, 0).astype(BF)], axis=1
    )


def group_sums(rows):
    C = rows.shape[1]
    width = C // GROUPS
    one = lax.broadcasted_iota(jnp.int32, (C, C), 0) // width
    two = lax.broadcasted_iota(jnp.int32, (C, C), 1) // width
    same = jnp.where(one == two, 1.0, 0.0)
    return lax.dot_general(
        rows, same, NN, precision=lax.Precision.HIGHEST, preferred_element_type=F32
    )


def mish_parts(v):
    e = jnp.exp(jnp.minimum(v, 20.0))
    w = e * (e + 2.0)
    r = 1.0 / (w + 2.0)
    return e, w, r


def greet_all(me):
    barrier = pltpu.get_barrier_semaphore()
    for flip in (1, 2, 3):
        pl.semaphore_signal(barrier, inc=1, device_id={"seq": xor4(me, flip)}, device_id_type=MESH)
    pl.semaphore_wait(barrier, 3)


def share(mine, got, sems, u, me):
    return [
        pltpu.make_async_remote_copy(
            mine.at[u],
            got.at[j, u],
            sems.at[0, j, u],
            sems.at[1, j, u],
            device_id={"seq": xor4(me, j + 1)},
            device_id_type=MESH,
        )
        for j in range(3)
    ]


def front_kernel(
    len_ref,
    frames,
    embed,
    cotangent,
    conv_first,
    conv_second,
    conv_skip,
    time_proj,
    w_qkv,
    gains,
    shifts,
    x_out,
    h1_out,
    act_out,
    h2_out,
    res_out,
    all_out,
    probs_out,
    o_ref,
    qa_ref,
    stat_ref,
    embed_ref,
    next_ref,
    factors,
    x_ref,
    h1_ref,
    act_ref,
    h2_ref,
    res_ref,
    all_ref,
    lead,
    stat_one,
    got_one,
    stat_two,
    got_two,
    top,
    acc,
    held_one,
    held_two,
    tops_one,
    tops_two,
    probs,
    tops_used,
    time_rows,
    halo_sems,
    sems_one,
    sems_two,
    kv_sems,
    keep_sems,
    block_sems,
    probs_sems,
):
    U, F, C = frames.shape
    rows = F + 2 * EDGE
    own = pl.ds(EDGE, F)
    me = lax.axis_index("seq")
    count = lax.axis_size("seq")
    after, behind = lax.rem(me + 1, count), lax.rem(me + count - 1, count)
    start = me * F
    near, far = flipped(me, 1), flipped(me, 2)
    lane = lax.broadcasted_iota(jnp.int32, (1, 128), 1)
    one, zero = jnp.ones((), BF), jnp.zeros((), BF)
    greet_all(me)
    made = (x_ref, h1_ref, act_ref, h2_ref, res_ref)
    kept = (x_out, h1_out, act_out, h2_out, res_out)

    def keep(name):
        return pltpu.make_async_copy(made[name], kept[name], keep_sems.at[name])

    def keep_block(r, u):
        return pltpu.make_async_copy(all_ref.at[r, u], all_out.at[r, u], block_sems.at[r, u])

    half = F // 2

    def hop(kind, u, part=None):
        rows = slice(None) if part is None else pl.ds(part * half, half)
        source, slot, peer = ((0, 1, near), (0, 2, far), (2, 3, near))[kind]
        place = (kind, u if part is None else u + part)
        return to_peer(all_ref.at[source, u, rows], all_ref.at[slot, u, rows], kv_sems, place, peer)

    def halo(src, dst, kind, peer):
        return pltpu.make_async_remote_copy(
            src, dst, halo_sems.at[0, kind], halo_sems.at[1, kind], device_id={"seq": peer}, device_id_type=MESH
        )

    halos = [
        halo(frames.at[:, pl.ds(F - EDGE, EDGE)], lead.at[0], 0, after),
        halo(frames.at[:, pl.ds(0, EDGE)], lead.at[1], 1, behind),
        halo(cotangent.at[:, pl.ds(0, EDGE)], next_ref, 2, behind),
    ]
    for copy in halos:
        copy.start()
    active = embed[...].astype(F32)
    e, w, r = mish_parts(active)
    active = (active * w * r).astype(BF)
    embed_ref[...] = active
    time_rows[0:U, :] = dot(active, time_proj[...]) + shifts[2:3, :]
    first_taps = conv_first[...].reshape(3 * C, C)
    second_taps = conv_second[...].reshape(3 * C, C)

    def masked(block, at, u):
        return (block.astype(F32) * frame_mask_of(at, block.shape[0], len_ref[u])).astype(BF)

    for u in range(U):
        x_ref[u, own, :] = masked(frames[u], start, u)
    for copy in halos[:2]:
        copy.wait_recv()
    for u in range(U):
        x_ref[u, 0:EDGE, :] = masked(lead[0, u], start - EDGE, u)
        x_ref[u, F + EDGE :, :] = masked(lead[1, u], start + F, u)
    keep(0).start()

    def valid(i, u):
        return jnp.clip(len_ref[u] - i * F, 0, F).astype(F32)

    def local_stats(hidden, stat, got, sems, u):
        mask = frame_mask_of(start, F, len_ref[u])
        inside = hidden[EDGE : EDGE + F]
        many = jnp.maximum(valid(me, u) * (C // GROUPS), 1.0)
        mean = group_sums(row_sum(inside * mask)) / many
        centered = (inside - mean) * mask
        stat[u, 0:1, :] = mean
        stat[u, 1:2, :] = group_sums(row_sum(centered * centered))
        for copy in share(stat, got, sems, u, me):
            copy.start()

    def whole_stats(stat, got, sems, u):
        for copy in share(stat, got, sems, u, me):
            copy.wait()
        total = len_ref[u].astype(F32)
        parts = [(valid(me, u), stat[u])]
        for j in range(3):
            parts.append((valid(xor4(me, j + 1), u), got[j, u]))
        mean = sum(n * p[0:1] for n, p in parts) / total
        squares = sum(p[1:2] + (n * (C // GROUPS)) * jnp.square(p[0:1] - mean) for n, p in parts)
        inv = lax.rsqrt(squares / (total * (C // GROUPS)) + norm_eps)
        return mean, inv

    def activate(hidden, mean, inv, gain, shift):
        v = (hidden - mean) * inv * gain + shift
        e, w, r = mish_parts(v)
        return v * w * r

    def first_conv(u, _):
        hidden = dot(taps_of(x_ref[u]), first_taps) + shifts[0:1, :]
        h1_ref[u] = hidden
        local_stats(hidden, stat_one, got_one, sems_one, u)
        return 0

    lax.fori_loop(0, U, first_conv, 0)
    keep(1).start()

    def second_conv(u, _):
        mean, inv = whole_stats(stat_one, got_one, sems_one, u)
        stat_ref[u, 0:1, :] = mean
        stat_ref[u, 1:2, :] = inv
        mask = frame_mask_of(start - EDGE, rows, len_ref[u])
        act = activate(h1_ref[u], mean, inv, gains[0:1, :], shifts[1:2, :])
        act_in = ((act + time_rows[pl.ds(u, 1), :]) * mask).astype(BF)
        act_ref[u] = act_in
        hidden = dot(taps_of(act_in), second_taps) + shifts[3:4, :]
        h2_ref[u] = hidden
        local_stats(hidden, stat_two, got_two, sems_two, u)
        return 0

    lax.fori_loop(0, U, second_conv, 0)
    keep(2).start()
    keep(3).start()

    def to_qkv(u, _):
        mean, inv = whole_stats(stat_two, got_two, sems_two, u)
        stat_ref[u, 2:3, :] = mean
        stat_ref[u, 3:4, :] = inv
        mask = frame_mask_of(start, F, len_ref[u])
        act = activate(h2_ref[u, own, :], mean, inv, gains[1:2, :], shifts[4:5, :]) * mask
        res = act + dot(x_ref[u, own, :], conv_skip[...]) + shifts[5:6, :]
        res_ref[u] = res
        centered = res - lane_mean(res)
        hat = centered * lax.rsqrt(lane_mean(centered * centered) + norm_eps)
        normed = (hat * gains[2:3, :] + shifts[6:7, :]).astype(BF)
        qkv = dot(normed, w_qkv[...]).astype(BF)
        all_ref[0, u] = qkv[:, 128:384]

        @pl.when(u < U - 1)
        def _():
            hop(1, u).start()

        @pl.when(u == U - 1)
        def _():
            for part in (0, 1):
                hop(1, U - 1, part).start()

        hop(0, u).start()
        keep_block(0, u).start()
        for h in range(2):
            other = jnp.where(lane == 64 * (1 - h) + 3, one, zero)
            qa_ref[u, h] = jnp.where(head_lanes(lane, h), qkv[:, 0:128] * SCALE, other)
        return 0

    lax.fori_loop(0, U, to_qkv, 0)
    keep(4).start()
    top[...] = jnp.full(top.shape, -1e30, F32)
    factors[...] = jnp.zeros(factors.shape, F32)
    acc[...] = jnp.zeros(acc.shape, F32)

    def block_of(t):
        late = t // 4
        r = (1 - late) * (t // 2) + late * (2 + t % 2)
        return r, (1 - late) * (t % 2) + late * ((t - 4) // 2)

    def keep_probs(t):
        r, u = block_of(t)
        return pltpu.make_async_copy(probs.at[t % 2], probs_out.at[r, u], probs_sems.at[t % 2])

    def arrive(t):
        @pl.when(t >= 3)
        def _():
            keep_probs(t - 3).wait()

        @pl.when(t >= 2)
        def _():
            keep_probs(t - 2).start()

        @pl.when(t == 2)
        def _():
            hop(0, 0).wait_recv()
            keep_block(1, 0).start()

        @pl.when(t == 3)
        def _():
            hop(0, 1).wait_recv()
            keep_block(1, 1).start()

        @pl.when(t == 4)
        def _():
            hop(1, 0).wait()
            hop(2, 0).start()
            keep_block(2, 0).start()

        @pl.when(t == 5)
        def _():
            hop(2, 0).wait_recv()
            keep_block(3, 0).start()

    def scores(t, held, tops, part=None):
        r, u = block_of(t)
        first, count = (0, F) if part is None else (part * half, half)
        k = all_ref[r, u, pl.ds(first, count), 0:128]
        spot = xor4(me, r) * F + first + lax.broadcasted_iota(jnp.int32, (count, 1), 0)
        bias = jnp.where(spot < len_ref[u], 0.0, -1e9).astype(BF)
        for h in range(2):
            ka = jnp.where(head_lanes(lane, h), k, jnp.where(lane == 64 * (1 - h) + 3, bias, zero))
            s = dot(ka, qa_ref[u, h], NT)
            held[h, 0:count] = s
            tops[h, 0:1, :] = jnp.max(s, axis=0, keepdims=True)

    def weigh(t, slot, held, tops, part=None):
        r, u = block_of(t)
        first, count = (0, F) if part is None else (part * half, half)
        vt = all_ref[r, u, pl.ds(first, count), 128:256].T
        ones = jnp.ones((EDGE, count), BF)
        for h in range(2):
            old = top[u, h, 0:1, :]
            new = jnp.maximum(old, tops[h, 0:1, :])
            p = jnp.exp(held[h, 0:count] - new).astype(BF)
            probs[slot, h, pl.ds(first, count), :] = p
            for row in (0, 1) if part is None else (part,):
                tops_used[r, u, 2 * h + row : 2 * h + row + 1, :] = new
            va = jnp.concatenate([vt[64 * h : 64 * h + 64], ones], axis=0)
            acc[u, h] = acc[u, h] * jnp.exp(old - new) + dot(va, p)
            top[u, h, 0:1, :] = new

    scores(0, held_one, tops_one)

    def two_steps(n, _):
        t = 2 * n
        arrive(t + 1)
        scores(t + 1, held_two, tops_two)
        weigh(t, 0, held_one, tops_one)
        arrive(t + 2)
        scores(t + 2, held_one, tops_one)
        weigh(t + 1, 1, held_two, tops_two)
        return 0

    lax.fori_loop(0, 2, two_steps, 0)
    arrive(5)
    scores(5, held_two, tops_two)
    weigh(4, 0, held_one, tops_one)
    keep_probs(3).wait()
    keep_probs(4).start()
    for part in (0, 1):
        hop(1, 1, part).wait()
        hop(2, 1, part).start()
        scores(6, held_one, tops_one, part)
        if part == 0:
            weigh(5, 1, held_two, tops_two)
            keep_probs(4).wait()
            keep_probs(5).start()
        else:
            keep_block(2, 1).start()
            weigh(7, 1, held_two, tops_two, 0)
        hop(2, 1, part).wait_recv()
        scores(7, held_two, tops_two, part)
        weigh(6, 0, held_one, tops_one, part)
        if part == 0:
            keep_probs(5).wait()
    keep_block(3, 1).start()
    keep_probs(6).start()
    weigh(7, 1, held_two, tops_two, 1)
    keep_probs(7).start()
    for u in range(U):
        outs, logs = [], []
        for h in range(2):
            total = acc[u, h, 64:65, :]
            outs.append(acc[u, h, 0:64, :] / total)
            logs.append(top[u, h, 0:1, :] + jnp.log(total))
        o_ref[u] = jnp.concatenate(outs, axis=0).T
        for r in range(4):
            for row in range(4):
                used = tops_used[r, u, row : row + 1, :]
                factors[r, u, row : row + 1, :] = jnp.exp(used - logs[row // 2])
    for u in range(U):
        hop(0, u).wait_send()
        for part in (None,) if u < U - 1 else (0, 1):
            hop(2, u, part).wait_send()
        for r in range(4):
            keep_block(r, u).wait()
    for name in range(5):
        keep(name).wait()
    keep_probs(6).wait()
    keep_probs(7).wait()
    for copy in halos:
        copy.wait_send()
    halos[2].wait_recv()


def front(lengths, frames, embed, cotangent, conv_first, conv_second, conv_skip, time_proj, w_qkv, gains, shifts):
    U, F, C = frames.shape
    rows = F + 2 * EDGE
    vmem = pl.BlockSpec(memory_space=pltpu.VMEM)
    stat = pltpu.VMEM((U, 8, C), F32)
    got = pltpu.VMEM((3, U, 8, C), F32)
    return pl.pallas_call(
        front_kernel,
        out_shape=(
            jax.ShapeDtypeStruct((U, rows, C), BF),
            jax.ShapeDtypeStruct((U, rows, C), F32),
            jax.ShapeDtypeStruct((U, rows, C), BF),
            jax.ShapeDtypeStruct((U, rows, C), F32),
            jax.ShapeDtypeStruct((U, F, C), F32),
            jax.ShapeDtypeStruct((4, U, F, 256), BF),
            jax.ShapeDtypeStruct((4, U, 2, F, F), BF),
            jax.ShapeDtypeStruct((U, F, 128), F32),
            jax.ShapeDtypeStruct((U, 2, F, 128), BF),
            jax.ShapeDtypeStruct((U, 8, C), F32),
            jax.ShapeDtypeStruct(embed.shape, BF),
            jax.ShapeDtypeStruct((U, EDGE, C), BF),
            jax.ShapeDtypeStruct((4, U, 8, F), F32),
        ),
        in_specs=[pl.BlockSpec(memory_space=pltpu.SMEM), vmem, vmem, pl.BlockSpec(memory_space=pl.ANY)] + [vmem] * 7,
        out_specs=[pl.BlockSpec(memory_space=pl.ANY)] * 7 + [vmem] * 6,
        scratch_shapes=[
            pltpu.VMEM((U, rows, C), BF),
            pltpu.VMEM((U, rows, C), F32),
            pltpu.VMEM((U, rows, C), BF),
            pltpu.VMEM((U, rows, C), F32),
            pltpu.VMEM((U, F, C), F32),
            pltpu.VMEM((4, U, F, 256), BF),
            pltpu.VMEM((2, U, EDGE, C), BF),
            stat,
            got,
            stat,
            got,
            pltpu.VMEM((U, 2, 8, F), F32),
            pltpu.VMEM((U, 2, 64 + EDGE, F), F32),
            pltpu.VMEM((2, F, F), F32),
            pltpu.VMEM((2, F, F), F32),
            pltpu.VMEM((2, 8, F), F32),
            pltpu.VMEM((2, 8, F), F32),
            pltpu.VMEM((2, 2, F, F), BF),
            pltpu.VMEM((4, U, 8, F), F32),
            pltpu.VMEM((8, C), F32),
            pltpu.SemaphoreType.DMA((2, 3)),
            pltpu.SemaphoreType.DMA((2, 3, U)),
            pltpu.SemaphoreType.DMA((2, 3, U)),
            pltpu.SemaphoreType.DMA((2, 3, U + 1)),
            pltpu.SemaphoreType.DMA((5,)),
            pltpu.SemaphoreType.DMA((4, U)),
            pltpu.SemaphoreType.DMA((2,)),
        ],
        compiler_params=pltpu.CompilerParams(
            collective_id=1, has_side_effects=True, vmem_limit_bytes=62 * 2**20
        ),
        name="front",
    )(lengths, frames, embed, cotangent, conv_first, conv_second, conv_skip, time_proj, w_qkv, gains, shifts)


def resnet_back_kernel(
    axes,
    len_ref,
    gqkv_in,
    gtwo_in,
    res_in,
    x_in,
    h1_in,
    act_in,
    h2_in,
    stat_ref,
    conv_first,
    conv_second,
    conv_skip,
    w_qkv,
    gains,
    shifts,
    up_ends,
    gframes,
    up,
    mid,
    late,
    last,
    gsmall,
    gfirst,
    gsecond,
    gskip,
    gw_qkv,
    lows,
    gqkv_ref,
    gtwo_ref,
    res_ref,
    x_ref,
    h1_ref,
    act_ref,
    h2_ref,
    load_sems,
    edges,
    gone,
    gmasked,
    sum_two,
    got_two,
    sum_one,
    got_one,
    halo_sems,
    sems_two,
    sems_one,
    small_got,
    small_sems,
    *sum_refs,
):
    U, F, C = gtwo_ref.shape
    given = (gqkv_in, res_in, gtwo_in, x_in, h2_in, act_in, h1_in)
    held = (gqkv_ref, res_ref, gtwo_ref, x_ref, h2_ref, act_ref, h1_ref)

    def load(name, u):
        return pltpu.make_async_copy(given[name].at[u], held[name].at[u], load_sems.at[name, u])

    for names in ((0, 1, 2, 3), (4, 5, 6)):
        for u in range(U):
            for name in names:
                load(name, u).start()
    rows = F + 2 * EDGE
    own = pl.ds(EDGE, F)
    inner = slice(EDGE, EDGE + F)
    me = lax.axis_index("seq")
    count = lax.axis_size("seq")
    after, behind = lax.rem(me + 1, count), lax.rem(me + count - 1, count)
    start = me * F
    hops, stages = butterfly(axes), stages_of(axes)
    greet_stages(stages, [("seq", xor4(me, 3))])
    fine = stages_of(axes, 1)
    run_up = doubling_steps(fine, up_ends, up, sum_refs[0])
    run_mid = sum_steps(stages, *sum_refs[1:5], mid, *sum_refs[5:7])
    run_late = sum_steps(stages, *sum_refs[7:11], late, *sum_refs[11:13])
    run_last = sum_steps(stages, *sum_refs[13:17], last, *sum_refs[17:19])
    run_small = small_steps(hops, gsmall, small_got, small_sems)
    for ref in (gsmall, sum_two, sum_one, gfirst, gsecond, gskip, gw_qkv):
        ref[...] = jnp.zeros_like(ref)

    run_up(0)

    def halo(kind, u):
        spot = pl.ds(F, EDGE) if kind == 0 else pl.ds(EDGE, EDGE)
        return pltpu.make_async_remote_copy(
            gone.at[u, spot],
            edges.at[kind, u],
            halo_sems.at[0, kind, u],
            halo_sems.at[1, kind, u],
            device_id={"seq": after if kind == 0 else behind},
            device_id_type=MESH,
        )

    def through_qkv(u, _):
        for name in range(4):
            load(name, u).wait()
        res = res_ref[u]
        centered = res - lane_mean(res)
        inv = lax.rsqrt(lane_mean(centered * centered) + norm_eps)
        hat = centered * inv
        normed = (hat * gains[2:3, :] + shifts[6:7, :]).astype(BF)
        gqkv = gqkv_ref[u]
        gw_qkv[...] += tn(normed, gqkv)
        grad = dot(gqkv, w_qkv[...], NT)
        gsmall[10:11, :] += row_sum(grad * hat)
        gsmall[6:7, :] += row_sum(grad)
        grad = grad * gains[2:3, :]
        grad = gtwo_ref[u] + inv * (grad - lane_mean(grad) - hat * lane_mean(grad * hat))
        gone[u, own, :] = grad
        for kind in range(2):
            halo(kind, u).start()
        gsmall[5:6, :] += row_sum(grad)
        low = grad.astype(BF)
        gskip[...] += tn(x_ref[u, own, :], low)
        gmasked[u] = dot(low, conv_skip[...], NT)

        @pl.when(u == 0)
        def _():
            run_up(1)

        return 0

    lax.fori_loop(0, U, through_qkv, 0)

    def norm_terms(grad, hidden, u, at):
        mean, inv = stat_ref[u, 2 * at : 2 * at + 1, :], stat_ref[u, 2 * at + 1 : 2 * at + 2, :]
        gain, shift = gains[at : at + 1, :], shifts[1 + 3 * at : 2 + 3 * at, :]
        hat = (hidden - mean) * inv
        v = hat * gain + shift
        e, w, r = mish_parts(v)
        slope = w * r + v * (4.0 * e * (1.0 + e)) * (r * r)
        return hat, grad * slope, inv, gain

    def local_sums(hat, grad, gain, sums, got, sems, u, at):
        hat, grad = hat[inner], grad[inner]
        gsmall[8 + at : 9 + at, :] += row_sum(grad * hat)
        gsmall[1 + 3 * at : 2 + 3 * at, :] += row_sum(grad)
        grad = grad * gain
        both = jnp.concatenate([row_sum(grad), row_sum(grad * hat)], axis=0)
        sums[u, 0:2, :] = group_sums(both)
        for copy in share(sums, got, sems, u, me):
            copy.start()

    def whole_sums(sums, got, sems, u):
        for copy in share(sums, got, sems, u, me):
            copy.wait()
        return (sums[u] + got[0, u]) + (got[1, u] + got[2, u])

    def hidden_grad(hat, grad, inv, gain, total, u, mask):
        many = len_ref[u].astype(F32) * (C // GROUPS)
        return inv * (grad * gain - mask * ((total[0:1] + hat * total[1:2]) / many))

    def back_taps(grad, weight):
        wide = grad.astype(F32)
        many = grad.shape[0]
        later = pltpu.roll(wide, many - 1, 0).astype(BF)
        earlier = pltpu.roll(wide, 1, 0).astype(BF)
        return dot(later, weight[0], NT) + dot(grad, weight[1], NT) + dot(earlier, weight[2], NT)

    def wide_mask(u):
        return frame_mask_of(start - EDGE, rows, len_ref[u])

    def second_terms(u, _):
        for kind in range(2):
            halo(kind, u).wait()
        load(4, u).wait()
        gone[u, 0:EDGE, :] = edges[0, u]
        gone[u, F + EDGE :, :] = edges[1, u]
        hat, grad, inv, gain = norm_terms(gone[u] * wide_mask(u), h2_ref[u], u, 1)
        gone[u] = grad
        local_sums(hat, grad, gain, sum_two, got_two, sems_two, u, 1)
        return 0

    lax.fori_loop(0, U, second_terms, 0)

    def second_back(u, _):
        load(5, u).wait()
        load(6, u).wait()
        total = whole_sums(sum_two, got_two, sems_two, u)
        mask = wide_mask(u)
        inv, gain = stat_ref[u, 3:4, :], gains[1:2, :]
        hat = (h2_ref[u] - stat_ref[u, 2:3, :]) * inv
        grad = hidden_grad(hat, gone[u], inv, gain, total, u, mask)
        gsmall[3:4, :] += row_sum(grad[inner])
        low = grad.astype(BF)
        gsecond[...] += tn(taps_of(act_ref[u])[inner], low[inner])
        grad = back_taps(low, conv_second) * mask
        by_time = row_sum(grad[inner])
        gsmall[2:3, :] += by_time
        gsmall[pl.ds(16 + lax.axis_index("dp") * U + u, 1), :] = by_time
        hat, grad, inv, gain = norm_terms(grad, h1_ref[u], u, 0)
        gone[u] = grad
        local_sums(hat, grad, gain, sum_one, got_one, sems_one, u, 0)

        @pl.when(u == 0)
        def _():
            run_up(2)

        return 0

    lax.fori_loop(0, U, second_back, 0)
    pack(sum_refs[1], [gskip, gw_qkv])
    run_mid(0)
    pack(sum_refs[7], [gsecond])
    run_late(0)

    def first_back(u, _):
        total = whole_sums(sum_one, got_one, sems_one, u)
        mask = wide_mask(u)
        inv, gain = stat_ref[u, 1:2, :], gains[0:1, :]
        hat = (h1_ref[u] - stat_ref[u, 0:1, :]) * inv
        grad = hidden_grad(hat, gone[u], inv, gain, total, u, mask)
        gsmall[0:1, :] += row_sum(grad[inner])
        low = grad.astype(BF)
        lows[u] = low
        gfirst[...] += tn(taps_of(x_ref[u])[inner], low[inner])
        return 0

    lax.fori_loop(0, U, first_back, 0)
    run_late(1)
    run_mid(1)
    pack(sum_refs[13], [gfirst])
    steps = 2 * len(stages)
    for n in range(max(steps, len(hops)) + 1):
        for run, ahead, final in (
            (run_last, 0, steps),
            (run_late, 2, steps),
            (run_mid, 2, steps),
            (run_small, 0, len(hops)),
        ):
            if ahead + n <= final:
                run(ahead + n)
        if 0 <= n - 2 <= len(fine) - 3:
            run_up(n + 1)
        if n < U:
            grad = back_taps(lows[n], conv_first)[inner] + gmasked[n]
            gframes[n] = grad * frame_mask_of(start, F, len_ref[n])


def resnet_back(lengths, gqkv, gtwo, res, x, h1, act, h2, stat, conv_first, conv_second, conv_skip, w_qkv, gains, shifts, up_ends, axes):
    U, F, C = gtwo.shape
    count = bits_of(axes)
    shapes = [(3 * C, C), (3 * C, C), (C, C), w_qkv.shape]
    mats = [jax.ShapeDtypeStruct(shape, F32) for shape in shapes]
    up_rows = up_ends.shape[0] << count
    row_counts = [padded_rows(packed_rows(some), axes) for some in (mats[2:], mats[1:2], mats[:1])]
    small_rows = 16 + U * dict(axes)["dp"]
    rows = F + 2 * EDGE
    vmem = pl.BlockSpec(memory_space=pltpu.VMEM)
    sums = pltpu.VMEM((U, 8, C), F32)
    got = pltpu.VMEM((3, U, 8, C), F32)
    return pl.pallas_call(
        functools.partial(resnet_back_kernel, axes),
        out_shape=(
            jax.ShapeDtypeStruct((U, F, C), F32),
            *(jax.ShapeDtypeStruct((many, 128), BF) for many in [up_rows, *row_counts]),
            jax.ShapeDtypeStruct((small_rows, C), F32),
        ),
        in_specs=[pl.BlockSpec(memory_space=pltpu.SMEM)]
        + [pl.BlockSpec(memory_space=pl.ANY)] * 7
        + [vmem] * 8,
        out_specs=[vmem] * 6,
        scratch_shapes=[
            *(pltpu.VMEM(shape, F32) for shape in shapes),
            pltpu.VMEM((U, rows, C), BF),
            *(pltpu.VMEM(x.shape, x.dtype) for x in (gqkv, gtwo, res, x, h1, act, h2)),
            pltpu.SemaphoreType.DMA((7, U)),
            pltpu.VMEM((2, U, EDGE, C), F32),
            pltpu.VMEM((U, rows, C), F32),
            pltpu.VMEM((U, F, C), F32),
            sums,
            got,
            sums,
            got,
            pltpu.SemaphoreType.DMA((2, 2, U)),
            pltpu.SemaphoreType.DMA((2, 3, U)),
            pltpu.SemaphoreType.DMA((2, 3, U)),
            pltpu.VMEM((count, small_rows, C), F32),
            pltpu.SemaphoreType.DMA((2, count)),
            pltpu.SemaphoreType.DMA((2, stage_count(axes, 1), 7)),
            *(ref for many in row_counts for ref in sum_scratch(many, axes)),
        ],
        compiler_params=pltpu.CompilerParams(
            collective_id=4, has_side_effects=True, vmem_limit_bytes=60 * 2**20
        ),
        name="resnet_back",
    )(lengths, gqkv, gtwo, res, x, h1, act, h2, stat, conv_first, conv_second, conv_skip, w_qkv, gains, shifts, up_ends)


def shards(
    frames,
    time_embed,
    lengths,
    out_cotangent,
    conv_first,
    conv_second,
    conv_skip,
    time_proj,
    w_qkv,
    w_out,
    ff_in,
    ff_out,
    conv_down,
    gains,
    shifts,
    ff_bias,
    snake_logs,
):
    channels = frames.shape[2]
    (
        masked_in,
        hidden_one,
        act_in,
        hidden_two,
        resnet_out,
        kv_all,
        probs,
        attended_full,
        queries_aug,
        stats,
        embed_act,
        next_rows,
        factors,
    ) = front(
        lengths,
        frames,
        time_embed,
        out_cotangent,
        conv_first,
        conv_second,
        conv_skip,
        time_proj,
        w_qkv,
        gains,
        shifts,
    )
    (
        layer_out,
        grad_two,
        grad_aug,
        first_rows,
        tail_rows,
        grad_w_out,
        grad_ff_in,
        grad_ff_out,
        grad_conv_down,
        mid_small,
        ff_small,
    ) = middle(
        lengths,
        attended_full,
        resnet_out,
        out_cotangent,
        next_rows,
        w_out,
        ff_in,
        ff_out,
        conv_down,
        gains,
        shifts,
        ff_bias,
        snake_logs,
    )
    axes = (("seq", lax.axis_size("seq")), ("dp", lax.axis_size("dp")))
    grad_qkv, up_ends, small_up, tail_rows = attend_back(
        queries_aug,
        grad_aug,
        kv_all,
        probs,
        factors,
        mid_small,
        ff_small,
        embed_act,
        tail_rows,
        [grad_w_out, grad_ff_in, grad_ff_out, grad_conv_down.reshape(-1, channels)],
        axes,
    )
    grad_frames, up, mid, late, last, small_late = resnet_back(
        lengths,
        grad_qkv,
        grad_two,
        resnet_out,
        masked_in,
        hidden_one,
        act_in,
        hidden_two,
        stats,
        conv_first,
        conv_second,
        conv_skip,
        w_qkv,
        gains,
        shifts,
        up_ends,
        axes,
    )
    weights = (
        conv_first,
        conv_second,
        conv_skip,
        time_proj,
        w_qkv,
        w_out,
        ff_in,
        ff_out,
        conv_down,
        gains,
        shifts,
        ff_bias.reshape(1, -1),
        snake_logs,
    )
    grads = finish(
        lengths,
        first_rows,
        tail_rows,
        layer_out,
        up,
        mid,
        late,
        last,
        small_up,
        small_late,
        [w.shape for w in weights],
    )
    return (grads[13], grad_frames, *grads[:11], grads[11].reshape(-1), grads[12])


def solution(mesh):
    in_specs = (
        P("dp", "seq", None),
        P("dp", None),
        P("dp"),
        P("dp", "seq", None),
        P(),
        P(),
        P(),
        P(),
        P(),
        P(),
        P(),
        P(),
        P(),
        P(),
        P(),
        P(),
        P(),
    )
    out_specs = (
        P("dp", "seq", None),
        P("dp", "seq", None),
        P(),
        P(),
        P(),
        P(),
        P(),
        P(),
        P(),
        P(),
        P(),
        P(),
        P(),
        P(),
        P(),
    )
    return jax.shard_map(shards, mesh=mesh, in_specs=in_specs, out_specs=out_specs, check_vma=False)
```

```python
import functools
import math

import jax
import jax.numpy as jnp
from jax import lax
from jax.experimental import pallas as pl
from jax.experimental.pallas import tpu as pltpu
from jax.sharding import PartitionSpec as P

F32, BF = jnp.float32, jnp.bfloat16
NT = (((1,), (1,)), ((), ()))
NN = (((1,), (0,)), ((), ()))
TN = (((0,), (0,)), ((), ()))
MESH = pl.DeviceIdType.MESH
EDGE = 16


def dot(a, b, dn=NN):
    return lax.dot_general(a, b, dn, preferred_element_type=F32)


HEADS = 2
GROUPS = 8


norm_eps = 1e-05


SIN_PI = (3.141592580060032, -5.167706879868365, 2.55003139258664, -0.598045264752551, 0.0772203056339658)
COS_PI = (0.9999999534804945, -4.934792860766467, 4.05841196261883, -1.3318805129033002, 0.21969758323424166)


def horner(coefficients, x):
    value = coefficients[-1]
    for coefficient in coefficients[-2::-1]:
        value = value * x + coefficient
    return value


def sin_cos_half_turns(turns):
    part = turns - jnp.round(turns)
    square = part * part
    return part * horner(SIN_PI, square), horner(COS_PI, square)


def row_sum(x):
    return jnp.sum(x, axis=0, keepdims=True)


def lane_mean(x):
    return jnp.mean(x, axis=1, keepdims=True)


def tn(a, b):
    return lax.dot_general(a, b, TN, preferred_element_type=F32)


def middle_kernel(
    RB,
    FC,
    len_ref,
    att_ref,
    res_ref,
    cot_ref,
    next_ref,
    w_out,
    ff_in,
    ff_out,
    conv_down,
    gains,
    shifts,
    ff_bias,
    snake_logs,
    out_ref,
    gtwo_ref,
    aug_ref,
    row_ref,
    tail_ref,
    gw_out,
    gff_in,
    gff_out,
    gdown,
    gsmall,
    gff_small,
    pairs,
    before_last,
):
    u, i = pl.program_id(0), pl.program_id(1)
    U, nb = pl.num_programs(0), pl.num_programs(1)
    half = RB // 2
    frames = nb * RB
    length = len_ref[u]
    base = lax.axis_index("seq") * frames
    at = base + i * RB

    @pl.when((u == 0) & (i == 0))
    def _():
        for ref in (gw_out, gff_in, gff_out, gdown, gsmall, gff_small):
            ref[...] = jnp.zeros_like(ref)

    def column_mask(start, rows, step):
        places = start + step * lax.broadcasted_iota(jnp.int32, (rows, 1), 0)
        return jnp.where(places < length, 1.0, 0.0)

    mask = column_mask(at, RB, 1)
    half_mask = column_mask(at, half, 2)
    low_f32 = cot_ref[0, pl.ds(pl.multiple_of(i * half, half), half), :].astype(F32) * half_mask
    gsmall[4:5, :] += row_sum(low_f32)
    low = low_f32.astype(BF)
    follow = jnp.minimum(i * half + half, frames // 2 - 16)
    inner = cot_ref[0, pl.ds(pl.multiple_of(follow, 16), 16), :].astype(F32)[0:1]
    outer = next_ref[0].astype(F32)[0:1]
    after = jnp.where(i == nb - 1, outer, inner) * jnp.where(at + RB < length, 1.0, 0.0)
    row_at = lax.broadcasted_iota(jnp.int32, (half, 1), 0)
    low_next = jnp.where(row_at == half - 1, after, pltpu.roll(low_f32, half - 1, 0)).astype(BF)
    even_grads = dot(low, conv_down[1], NT)
    odd_grads = dot(low, conv_down[2], NT) + dot(low_next, conv_down[0], NT)
    for lanes in (0, 128):
        pairs[lanes // 128, pl.ds(0, half, stride=2), :] = even_grads[:, lanes : lanes + 128]
        pairs[lanes // 128, pl.ds(1, half, stride=2), :] = odd_grads[:, lanes : lanes + 128]
    grad_three = jnp.concatenate([pairs[0], pairs[1]], axis=1) * mask
    gsmall[3:4, :] += row_sum(grad_three)
    grad_low = grad_three.astype(BF)
    attended = att_ref[0]
    att_low = attended.astype(BF)
    resid_two = res_ref[0] + dot(att_low, w_out[...]) + shifts[7:8, :]
    centered = resid_two - lane_mean(resid_two)
    inv = lax.rsqrt(lane_mean(centered * centered) + norm_eps)
    hat = centered * inv
    normed = (hat * gains[3:4, :] + shifts[8:9, :]).astype(BF)
    freq = jnp.exp(snake_logs[0:1, :])
    spread = jnp.exp(snake_logs[1:2, :])
    size = 1.0 / (spread + 1e-09)
    turn = freq * (1.0 / math.pi)
    resid_three = resid_two + shifts[9:10, :]
    grad_normed = jnp.zeros_like(resid_two)
    for c in range(0, ff_bias.shape[1], FC):
        cols = slice(c, c + FC)
        hidden = dot(normed, ff_in[:, cols]) + ff_bias[:, cols]
        sine, cosine = sin_cos_half_turns(hidden * turn[:, cols])
        square = sine * sine
        snaked = (hidden + square * size[:, cols]).astype(BF)
        resid_three = resid_three + dot(snaked, ff_out[cols, :])
        gff_out[cols, :] += tn(snaked, grad_low)
        grad_snaked = dot(grad_low, ff_out[cols, :], NT)
        cross = grad_snaked * (sine * cosine)
        grad_hidden = grad_snaked + cross * (2.0 * size * freq)[:, cols]
        gff_small[0:1, cols] += row_sum(grad_hidden)
        gff_small[1:2, cols] += row_sum(cross * hidden)
        gff_small[2:3, cols] += row_sum(grad_snaked * square)
        hidden_low = grad_hidden.astype(BF)
        gff_in[:, cols] += tn(normed, hidden_low)
        grad_normed = grad_normed + dot(hidden_low, ff_in[:, cols], NT)
    down = (resid_three * mask).astype(BF)
    down_f32 = down.astype(F32)
    for lanes in (0, 128):
        pairs[lanes // 128] = down_f32[:, lanes : lanes + 128]
    even = jnp.concatenate([pairs[j, pl.ds(0, half, stride=2), :] for j in range(2)], axis=1)
    odd = jnp.concatenate([pairs[j, pl.ds(1, half, stride=2), :] for j in range(2)], axis=1)
    first = jnp.where(i == 0, 0.0, before_last[0:1, :])
    before = jnp.where(row_at == 0, first, pltpu.roll(odd, 1, 0)).astype(BF)
    before_last[0:1, :] = odd[half - 1 : half, :]
    tail_ref[0] = dot(down[RB - 16 :, :], conv_down[0])[8:16]
    even, odd = even.astype(BF), odd.astype(BF)
    lowered = dot(before, conv_down[0]) + dot(even, conv_down[1]) + dot(odd, conv_down[2])
    lowered = lowered + shifts[10:11, :]

    @pl.when(i == 0)
    def _():
        row_ref[0] = lowered[0:8]

    out_ref[0] = (lowered * half_mask).astype(BF)
    gdown[0] += tn(odd, low_next)
    gdown[1] += tn(even, low)
    gdown[2] += tn(odd, low)
    gsmall[0:1, :] += row_sum(grad_normed * hat)
    gsmall[2:3, :] += row_sum(grad_normed)
    grad_hat = grad_normed * gains[3:4, :]
    grad_two = grad_three + inv * (
        grad_hat - lane_mean(grad_hat) - hat * lane_mean(grad_hat * hat)
    )
    gtwo_ref[0] = grad_two
    gsmall[1:2, :] += row_sum(grad_two)
    two_low = grad_two.astype(BF)
    gw_out[...] += tn(att_low, two_low)
    grad_att = dot(two_low, w_out[...], NT).astype(BF)
    terms = grad_att.astype(F32) * attended
    lane = lax.broadcasted_iota(jnp.int32, (1, 128), 1)
    zero = jnp.zeros((), F32)
    for h in range(2):
        mine = (lane >= 64 * h) & (lane < 64 * h + 64)
        term = jnp.sum(jnp.where(mine, terms, zero), axis=1, keepdims=True)
        aug_ref[0, h] = with_pieces(jnp.where(mine, grad_att, jnp.zeros((), BF)), term, lane, h)

    @pl.when((u == U - 1) & (i == nb - 1))
    def _():
        gff_small[1:2, :] = gff_small[1:2, :] * (2.0 * size * freq)
        gff_small[2:3, :] = gff_small[2:3, :] * (-(size * size) * spread)


def with_pieces(block, value, lane, h):
    base = 64 * (1 - h)
    for j in range(3):
        piece = value.astype(BF)
        value = value - piece.astype(F32)
        block = jnp.where(lane == base + j, piece, block)
    return block


def middle(lengths, attended, resnet_out, cotangent, next_rows, w_out, ff_in, ff_out, conv_down, gains, shifts, ff_bias, snake_logs, FC=256):
    U, F, C = resnet_out.shape
    RB = min(F, 1024)
    inner = attended.shape[2]
    FF = ff_bias.shape[0]
    whole = lambda shape: pl.BlockSpec(shape, lambda u, i, _: (0,) * len(shape))
    rows = lambda n, c: pl.BlockSpec((1, n, c), lambda u, i, _: (u, i, 0))
    per_utt = lambda n, c: pl.BlockSpec((1, n, c), lambda u, i, _: (u, 0, 0))
    sums = ((inner, C), (C, FF), (FF, C), (3, C, C), (8, C), (8, FF))
    return pl.pallas_call(
        functools.partial(middle_kernel, RB, FC),
        out_shape=(
            jax.ShapeDtypeStruct((U, F // 2, C), BF),
            jax.ShapeDtypeStruct((U, F, C), F32),
            jax.ShapeDtypeStruct((U, 2, F, inner), BF),
            jax.ShapeDtypeStruct((U, 8, C), F32),
            jax.ShapeDtypeStruct((U, 8, C), F32),
            *(jax.ShapeDtypeStruct(shape, F32) for shape in sums),
        ),
        grid_spec=pltpu.PrefetchScalarGridSpec(
            num_scalar_prefetch=1,
            grid=(U, F // RB),
            in_specs=[
                rows(RB, inner),
                rows(RB, C),
                per_utt(F // 2, C),
                per_utt(16, C),
                whole((inner, C)),
                whole((C, FF)),
                whole((FF, C)),
                whole((3, C, C)),
                whole(gains.shape),
                whole(shifts.shape),
                whole((1, FF)),
                whole((2, FF)),
            ],
            out_specs=[
                rows(RB // 2, C),
                rows(RB, C),
                pl.BlockSpec((1, 2, RB, inner), lambda u, i, _: (u, 0, i, 0)),
                per_utt(8, C),
                per_utt(8, C),
                *(whole(shape) for shape in sums),
            ],
            scratch_shapes=[
                pltpu.VMEM((2, RB, 128), F32),
                pltpu.VMEM((8, C), F32),
            ],
        ),
        compiler_params=pltpu.CompilerParams(vmem_limit_bytes=56 * 2**20),
        name="middle",
    )(lengths, attended, resnet_out, cotangent, next_rows, w_out, ff_in, ff_out, conv_down, gains, shifts, ff_bias.reshape(1, -1), snake_logs)


def butterfly(axes):
    hops = []
    for axis, size in axes:
        place = lax.axis_index(axis)
        bit = 1
        while bit < size:
            up = (place // bit) % 2
            hops.append((axis, place + bit - 2 * bit * up, up))
            bit *= 2
    return hops


def bits_of(axes):
    return sum(size.bit_length() - 1 for _, size in axes)


def radices(axis, size, fine):
    while size > 1:
        radix = min(2 if axis == "seq" else 8, size)
        if fine and axis == "dp":
            radix = 2 if fine == 1 else min(4, size)
            fine = 2
        yield radix
        size //= radix


def stages_of(axes, fine=0):
    stages = []
    for axis, size in axes:
        stride = 1
        for radix in radices(axis, size, fine):
            place = lax.axis_index(axis)
            digit = (place // stride) % radix
            peers = [place + ((digit + m) % radix - digit) * stride for m in range(1, radix)]
            stages.append((axis, radix, digit, peers))
            stride *= radix
    return [stages[0], *stages[2:], stages[1]] if fine else stages


def padded_rows(rows, axes):
    unit = EDGE << bits_of(axes)
    return -(-rows // unit) * unit


def packed_rows(mats):
    return sum(m.shape[0] * m.shape[1] // 128 for m in mats)


def greet_stages(stages, extra=()):
    barrier = pltpu.get_barrier_semaphore()
    met = [(axis, peer) for axis, _, _, peers in stages for peer in peers] + list(extra)
    for axis, peer in met:
        pl.semaphore_signal(barrier, inc=1, device_id={axis: peer}, device_id_type=MESH)
    pl.semaphore_wait(barrier, len(met))


def hop_copy(hop, src, dst, sems, place):
    axis, partner, _ = hop
    return pltpu.make_async_remote_copy(
        src, dst, sems.at[(0, *place)], sems.at[(1, *place)], device_id={axis: partner}, device_id_type=MESH
    )


def pack(total, mats):
    row = 0
    for ref in mats:
        rows, columns = ref.shape
        for column in range(0, columns, 128):
            total[pl.ds(row, rows), :] = ref[:, column : column + 128]
            row += rows
    if row < total.shape[0]:
        total[pl.ds(row, total.shape[0] - row), :] = jnp.zeros((total.shape[0] - row, 128), F32)


def shares_of(stages, rows):
    low, length, shares = 0, rows, []
    for _, radix, digit, _ in stages:
        shares.append((low, length, length // radix))
        length //= radix
        low = pl.multiple_of(low + digit * length, EDGE)
    return shares, low


def halving_steps(stages, total, sent, got, ends, sems):
    rows = total.shape[0]
    shares, _ = shares_of(stages, rows)

    def copies(s):
        axis, radix, _, peers = stages[s]
        _, before, length = shares[s]
        for m, peer in enumerate(peers):
            slot = pl.ds(rows - before + m * length, length)
            yield m, slot, hop_copy((axis, peer, 0), sent.at[slot], got.at[slot], sems, (s, m))

    def run(k):
        if k > 0:
            _, radix, digit, _ = stages[k - 1]
            low, _, length = shares[k - 1]
            here = pl.ds(pl.multiple_of(low + digit * length, EDGE), length)
            value = total[here, :]
            for _, slot, copy in copies(k - 1):
                copy.wait()
                value = value + got[slot, :].astype(F32)
            if k < len(stages):
                total[here, :] = value
            else:
                ends[...] = value.astype(BF)
        if k < len(stages):
            _, radix, digit, _ = stages[k]
            low, _, length = shares[k]
            for m, slot, copy in copies(k):
                give = pl.multiple_of(low + (digit + m + 1) % radix * length, EDGE)
                sent[slot, :] = total[pl.ds(give, length), :].astype(BF)
                copy.start()

    return run


def doubling_steps(stages, ends, whole, sems):
    count = len(stages)
    shares, own = shares_of(stages, whole.shape[0])

    def copies(s):
        axis, _, digit, peers = stages[s]
        low, _, length = shares[s]
        here = pl.ds(pl.multiple_of(low + digit * length, EDGE), length)
        for m, peer in enumerate(peers):
            yield hop_copy((axis, peer, 0), whole.at[here], whole.at[here], sems, (s, m))

    def run(k):
        if k == 0:
            whole[pl.ds(own, ends.shape[0]), :] = ends[...]
        if k > 0:
            for copy in copies(count - k):
                copy.wait()
        if k < count:
            for copy in copies(count - 1 - k):
                copy.start()

    return run


def sum_steps(stages, total, sent, got, ends, whole, sems, more_sems):
    count = len(stages)
    halving = halving_steps(stages, total, sent, got, ends, sems)
    doubling = doubling_steps(stages, ends, whole, more_sems)

    def run(k):
        if k <= count:
            halving(k)
        if k >= count:
            doubling(k - count)

    return run


def small_steps(hops, mine, got, sems):
    def run(k):
        if 0 < k <= len(hops):
            hop_copy(hops[k - 1], mine, got.at[k - 1], sems, (k - 1,)).wait()
            mine[...] += got[k - 1]
        if k < len(hops):
            hop_copy(hops[k], mine, got.at[k], sems, (k,)).start()

    return run


def stage_count(axes, fine):
    return sum(len(list(radices(axis, size, fine))) for axis, size in axes)


def halving_scratch(rows, axes, fine):
    return [
        pltpu.VMEM((rows, 128), F32),
        pltpu.VMEM((rows, 128), BF),
        pltpu.VMEM((rows, 128), BF),
        pltpu.SemaphoreType.DMA((2, stage_count(axes, fine), 7)),
    ]


def sum_scratch(rows, axes):
    total, sent, got, sems = halving_scratch(rows, axes, 0)
    return [total, sent, got, pltpu.VMEM((rows >> bits_of(axes), 128), BF), sems, sems]


def finish_kernel(
    len_ref, rows, tails, small_up, small_late, layer, frames_in, up_in, mid_in, late_in, last_in, *refs
):
    outs, patched, frames_out, edge, sems = refs[:13], refs[13], refs[14], refs[15], refs[16]
    big, big_sems = refs[17:26], refs[26]
    up, mid, late, last, in_sems = refs[27:32]
    given = (up_in, mid_in, late_in, last_in)
    bring = [pltpu.make_async_copy(x, y, in_sems.at[n]) for n, (x, y) in enumerate(zip(given, refs[27:31]))]
    for copy in bring:
        copy.start()
    held_frames = refs[32]
    frames_here = pltpu.make_async_copy(frames_in, held_frames, sems.at[2])
    frames_here.start()
    frames_there = pltpu.make_async_copy(held_frames, frames_out, sems.at[3])
    U = rows.shape[0]
    fetch = pltpu.make_async_copy(layer.at[:, pl.ds(0, EDGE)], edge, sems.at[0])
    fetch.start()
    (
        first, second, skip, time_out, qkv, w_out, ff_in, ff_out, down, gains, shifts, bias, logs
    ) = (*big, *outs[9:])

    def send(n):
        return pltpu.make_async_copy(big[n], outs[n], big_sems.at[n])

    def unpack(packed, refs):
        row = 0
        for ref in refs:
            flat = ref.reshape(-1, ref.shape[-1]) if len(ref.shape) == 3 else ref
            rows, columns = flat.shape
            for column in range(0, columns, 128):
                flat[:, column : column + 128] = packed[pl.ds(row, rows), :].astype(F32)
                row += rows

    bring[0].wait()
    unpack(up, [w_out, ff_in, ff_out, down])
    for n in range(5, 9):
        send(n).start()
    frames_here.wait()
    frames_there.start()
    for copy in bring[1:]:
        copy.wait()
    unpack(mid, [skip, qkv])
    unpack(late, [second])
    unpack(last, [first])
    for n in (0, 1, 2, 4):
        send(n).start()
    C = skip.shape[0]
    wide = bias.shape[1] // C
    utts = small_late.shape[0] - 16
    gains[0:3, :] = small_late[8:11, :]
    gains[3:4, :] = small_up[0:1, :]
    shifts[0:7, :] = small_late[0:7, :]
    shifts[7:11, :] = small_up[1:5, :]
    blocks = [small_up[8 * (j + 1) : 8 * (j + 2), :] for j in range(wide)]
    base = packed_rows([w_out, ff_in, ff_out, down.reshape(-1, C)])
    embed = [up[pl.ds(base + utts * j, utts), :].astype(F32) for j in range(time_out.shape[0] // 128)]
    for j in range(wide):
        bias[:, j * C : (j + 1) * C] = blocks[j][0:1]
        logs[:, j * C : (j + 1) * C] = blocks[j][1:3]
    grads = small_late[16:, :]
    for j, part in enumerate(embed):
        time_out[j * 128 : (j + 1) * 128, :] = lax.dot_general(
            part, grads, TN, precision=lax.Precision.HIGHEST, preferred_element_type=F32
        )
    send(3).start()
    fetch.wait()
    me = lax.axis_index("seq")
    frames = 2 * layer.shape[1]
    is_first = lax.broadcasted_iota(jnp.int32, (EDGE, 1), 0) == 0
    for u in range(U):
        value = rows[u, 0:1] + jnp.where(me > 0, tails[u, 7:8], 0.0)
        value = value * jnp.where(me * frames < len_ref[u], 1.0, 0.0)
        edge[u] = jnp.where(is_first, value, edge[u].astype(F32)).astype(BF)
    store = pltpu.make_async_copy(edge, patched.at[:, pl.ds(0, EDGE)], sems.at[1])
    store.start()
    for n in range(9):
        send(n).wait()
    store.wait()
    frames_there.wait()


def finish(lengths, rows, tails, small_up, small_late, layer, frames, sums, shapes):
    vmem = pl.BlockSpec(memory_space=pltpu.VMEM)
    anywhere = pl.BlockSpec(memory_space=pl.ANY)
    return pl.pallas_call(
        finish_kernel,
        out_shape=(
            *(jax.ShapeDtypeStruct(shape, F32) for shape in shapes),
            jax.ShapeDtypeStruct(layer.shape, BF),
            jax.ShapeDtypeStruct(frames.shape, F32),
        ),
        in_specs=[pl.BlockSpec(memory_space=pltpu.SMEM)] + [vmem] * 4 + [anywhere] * 6,
        out_specs=[anywhere] * 9 + [vmem] * 4 + [anywhere] * 2,
        scratch_shapes=[
            pltpu.VMEM((rows.shape[0], EDGE, rows.shape[2]), BF),
            pltpu.SemaphoreType.DMA((4,)),
            *(pltpu.VMEM(shape, F32) for shape in shapes[:9]),
            pltpu.SemaphoreType.DMA((9,)),
            *(pltpu.VMEM(x.shape, BF) for x in sums),
            pltpu.SemaphoreType.DMA((4,)),
            pltpu.VMEM(frames.shape, F32),
        ],
        input_output_aliases={5: len(shapes)},
        compiler_params=pltpu.CompilerParams(vmem_limit_bytes=56 * 2**20),
        name="finish",
    )(lengths, rows, tails, small_up, small_late, layer, frames, *sums)


SCALE = 0.125


def head_lanes(lane, h):
    return (lane >= 64 * h) & (lane < 64 * h + 64)


def greet_seq(me):
    barrier = pltpu.get_barrier_semaphore()
    for flip in (1, 2):
        pl.semaphore_signal(barrier, inc=1, device_id={"seq": flipped(me, flip)}, device_id_type=MESH)
    pl.semaphore_wait(barrier, 2)


def flipped(place, bit):
    return place + bit - 2 * bit * ((place // bit) % 2)


def to_peer(src, dst, sems, place, peer):
    return pltpu.make_async_remote_copy(
        src, dst, sems.at[(0, *place)], sems.at[(1, *place)], device_id={"seq": peer}, device_id_type=MESH
    )


def xor4(place, r):
    low = (place % 2 + r % 2) % 2
    high = (place // 2 + r // 2) % 2
    return 2 * high + low


def backward_kernel(
    axes, qa_ref, da_ref, all_in, probs_ref, factors, mid_small, ff_small, embed_ref, tail_ref, *refs
):
    mats_in, refs = refs[:4], refs[4:]
    grad_ref, ends, small, tail_got, dqt, part, sent, got, sems, small_got, small_sems, tail_sems = refs[:12]
    probs, probs_sems, total, sum_sent, sum_got, sum_sems, all_ref = refs[12:19]
    block_sems, mat_sems, mats = refs[19], refs[20], refs[21:]
    U, _, F, _ = qa_ref.shape
    C = mid_small.shape[1]
    me = lax.axis_index("seq")
    near, far = flipped(me, 1), flipped(me, 2)
    lane = lax.broadcasted_iota(jnp.int32, (1, 128), 1)
    one, zero = jnp.ones((), BF), jnp.zeros((), BF)
    hops, stages = butterfly(axes), stages_of(axes)
    greet_stages(stages, [("seq", xor4(me, 3))])
    tails = pltpu.make_async_remote_copy(
        tail_ref,
        tail_got,
        tail_sems.at[0],
        tail_sems.at[1],
        device_id={"seq": lax.rem(me + 1, lax.axis_size("seq"))},
        device_id_type=MESH,
    )
    tails.start()
    small[...] = jnp.zeros(small.shape, F32)
    small[0:8, :] = mid_small[...]
    wide = ff_small.shape[1] // C
    for j in range(wide):
        small[8 * (j + 1) : 8 * (j + 2), :] = ff_small[:, j * C : (j + 1) * C]

    def bring_mat(n):
        return pltpu.make_async_copy(mats_in[n], mats[n], mat_sems.at[n])

    def fill():
        for n in range(len(mats)):
            bring_mat(n).wait()
        pack(total, mats)
        embed = embed_ref[...].astype(F32) * jnp.where(me == 0, 1.0, 0.0)
        base = packed_rows(mats)
        for j in range(embed.shape[1] // 128):
            for u in range(U):
                row = base + j * U * dict(axes)["dp"] + lax.axis_index("dp") * U + u
                total[pl.ds(row, 1), :] = embed[u : u + 1, j * 128 : (j + 1) * 128]

    fine = stages_of(axes, 1)
    run_sum = halving_steps(fine, total, sum_sent, sum_got, ends, sum_sems)
    run_small = small_steps(hops, small, small_got, small_sems)
    dqt[...] = jnp.zeros(dqt.shape, F32)

    def hop(kind, u):
        peer = far if kind == 1 else near
        return to_peer(sent.at[kind, u], got.at[kind, u], sems, (kind, u), peer)

    def block_of(t):
        late = t // 4
        r = (1 - late) * (3 - t % 2) + late * (1 - (t - 4) // 2)
        return r, (1 - late) * ((t // 2) % 2) + late * (t % 2)

    def fetch(t):
        r, u = block_of(t)
        return pltpu.make_async_copy(probs_ref.at[r, u], probs.at[t % 2], probs_sems.at[t % 2])

    def bring(t):
        r, u = block_of(t)
        return pltpu.make_async_copy(all_in.at[r, u], all_ref.at[r, u], block_sems.at[t])

    bring(0).start()
    fetch(0).start()
    for t in range(1, 8):
        bring(t).start()
    for n in range(len(mats)):
        bring_mat(n).start()
    run_small(0)

    def step(t, _):
        r, u = block_of(t)

        @pl.when(t < 7)
        def _():
            fetch(t + 1).start()

        bring(t).wait()
        fetch(t).wait()
        v = all_ref[r, u, :, 128:256]
        kt = all_ref[r, u, :, 0:128].T
        dks, dvs = [], []
        for h in range(2):
            base = 64 * (1 - h)
            extra = (lane >= base) & (lane < base + 3)
            va = jnp.where(head_lanes(lane, h), v, jnp.where(extra, -one, zero))
            qa = qa_ref[u, h]
            da = da_ref[u, h]
            p = jnp.concatenate(
                [
                    probs[t % 2, h, pl.ds(row * F // 2, F // 2), :].astype(F32)
                    * factors[r, u, 2 * h + row : 2 * h + row + 1, :]
                    for row in range(2)
                ],
                axis=0,
            )
            ds = (p * dot(va, da, NT)).astype(BF)
            dvs.append(dot(p.astype(BF), da))
            dks.append(dot(ds, qa))
            rows = slice(64 * h, 64 * h + 64)
            dqt[u, rows, :] += dot(kt[rows, :], ds)
        part[:, 0:128] = jnp.where(head_lanes(lane, 0), dks[0], dks[1])
        part[:, 128:256] = jnp.where(head_lanes(lane, 0), dvs[0], dvs[1])

        @pl.when(r == 3)
        def _():
            sent[0, u] = part[...].astype(BF)
            hop(0, u).start()

        @pl.when(r == 2)
        def _():
            hop(0, u).wait_recv()
            sent[1, u] = (part[...] + got[0, u].astype(F32)).astype(BF)
            hop(1, u).start()

        @pl.when(r == 1)
        def _():
            sent[2, u] = part[...].astype(BF)
            hop(2, u).start()

        @pl.when(r == 0)
        def _():
            hop(1, u).wait_recv()
            hop(2, u).wait_recv()
            both = part[...] + got[1, u].astype(F32) + got[2, u].astype(F32)
            grad_ref[u, :, 128:384] = both.astype(BF)
            grad_ref[u, :, 0:128] = (dqt[u] * SCALE).T.astype(BF)

        for slot in range(8):
            sums = [n for n in range(len(fine) + 1) if sum_slot(n, len(fine) + 1, 8) == slot]
            smalls = [n for n in range(1, len(hops) + 1) if sum_slot(n - 1, len(hops), 8) == slot]
            if sums or smalls:

                @pl.when(t == slot)
                def _(sums=sums, smalls=smalls):
                    for n in sums:
                        if n == 0:
                            fill()
                        run_sum(n)
                    for n in smalls:
                        run_small(n)

        return 0

    lax.fori_loop(0, 8, step, 0)
    tails.wait()
    for kind in range(3):
        for u in range(U):
            hop(kind, u).wait_send()


def sum_slot(step, count, slots):
    return -(-step * (slots - 1) // (count - 1))


def attend_back(qa, da, kv_all, probs, factors, mid_small, ff_small, embed, tails, mats, axes):
    U, _, F, _ = qa.shape
    C = mid_small.shape[1]
    count = bits_of(axes)
    embed_rows = U * dict(axes)["dp"] * embed.shape[1] // 128
    rows = padded_rows(packed_rows(mats) + embed_rows, axes)
    small_rows = 8 + 8 * (ff_small.shape[1] // C)
    vmem = pl.BlockSpec(memory_space=pltpu.VMEM)
    anywhere = pl.BlockSpec(memory_space=pl.ANY)
    return pl.pallas_call(
        functools.partial(backward_kernel, axes),
        out_shape=(
            jax.ShapeDtypeStruct((U, F, 384), BF),
            jax.ShapeDtypeStruct((rows >> count, 128), BF),
            jax.ShapeDtypeStruct((small_rows, C), F32),
            jax.ShapeDtypeStruct(tails.shape, F32),
        ),
        in_specs=[vmem, vmem, anywhere, anywhere] + [vmem] * 5 + [anywhere] * len(mats),
        out_specs=[vmem] * 4,
        scratch_shapes=[
            pltpu.VMEM((U, 128, F), F32),
            pltpu.VMEM((F, 256), F32),
            pltpu.VMEM((3, U, F, 256), BF),
            pltpu.VMEM((3, U, F, 256), BF),
            pltpu.SemaphoreType.DMA((2, 3, U)),
            pltpu.VMEM((count, small_rows, C), F32),
            pltpu.SemaphoreType.DMA((2, count)),
            pltpu.SemaphoreType.DMA((2,)),
            pltpu.VMEM((2, 2, F, F), BF),
            pltpu.SemaphoreType.DMA((2,)),
            *halving_scratch(rows, axes, 1),
            pltpu.VMEM(kv_all.shape, BF),
            pltpu.SemaphoreType.DMA((8,)),
            pltpu.SemaphoreType.DMA((len(mats),)),
            *(pltpu.VMEM(m.shape, F32) for m in mats),
        ],
        compiler_params=pltpu.CompilerParams(
            collective_id=2, has_side_effects=True, vmem_limit_bytes=60 * 2**20
        ),
        name="attend_back",
    )(qa, da, kv_all, probs, factors, mid_small, ff_small, embed, tails, *mats)


def frame_mask_of(start, rows, length):
    spot = start + lax.broadcasted_iota(jnp.int32, (rows, 1), 0)
    return jnp.where((spot >= 0) & (spot < length), 1.0, 0.0)


def taps_of(x):
    wide = x.astype(F32)
    rows = x.shape[0]
    return jnp.concatenate(
        [pltpu.roll(wide, 1, 0).astype(BF), x, pltpu.roll(wide, rows - 1, 0).astype(BF)], axis=1
    )


def group_sums(rows):
    C = rows.shape[1]
    width = C // GROUPS
    one = lax.broadcasted_iota(jnp.int32, (C, C), 0) // width
    two = lax.broadcasted_iota(jnp.int32, (C, C), 1) // width
    same = jnp.where(one == two, 1.0, 0.0)
    return lax.dot_general(
        rows, same, NN, precision=lax.Precision.HIGHEST, preferred_element_type=F32
    )


def mish_parts(v):
    e = jnp.exp(jnp.minimum(v, 20.0))
    w = e * (e + 2.0)
    r = 1.0 / (w + 2.0)
    return e, w, r


def greet_all(me):
    barrier = pltpu.get_barrier_semaphore()
    for flip in (1, 2, 3):
        pl.semaphore_signal(barrier, inc=1, device_id={"seq": xor4(me, flip)}, device_id_type=MESH)
    pl.semaphore_wait(barrier, 3)


def share(mine, got, sems, u, me):
    return [
        pltpu.make_async_remote_copy(
            mine.at[u],
            got.at[j, u],
            sems.at[0, j, u],
            sems.at[1, j, u],
            device_id={"seq": xor4(me, j + 1)},
            device_id_type=MESH,
        )
        for j in range(3)
    ]


def front_kernel(
    len_ref,
    frames,
    embed,
    cotangent,
    conv_first,
    conv_second,
    conv_skip,
    time_proj,
    w_qkv,
    gains,
    shifts,
    x_out,
    h1_out,
    act_out,
    h2_out,
    res_out,
    all_out,
    probs_out,
    o_ref,
    qa_ref,
    stat_ref,
    embed_ref,
    next_ref,
    factors,
    x_ref,
    h1_ref,
    act_ref,
    h2_ref,
    res_ref,
    all_ref,
    lead,
    stat_one,
    got_one,
    stat_two,
    got_two,
    top,
    acc,
    held_one,
    held_two,
    tops_one,
    tops_two,
    probs,
    tops_used,
    time_rows,
    halo_sems,
    sems_one,
    sems_two,
    kv_sems,
    keep_sems,
    block_sems,
    probs_sems,
):
    U, F, C = frames.shape
    rows = F + 2 * EDGE
    own = pl.ds(EDGE, F)
    me = lax.axis_index("seq")
    count = lax.axis_size("seq")
    after, behind = lax.rem(me + 1, count), lax.rem(me + count - 1, count)
    start = me * F
    near, far = flipped(me, 1), flipped(me, 2)
    lane = lax.broadcasted_iota(jnp.int32, (1, 128), 1)
    one, zero = jnp.ones((), BF), jnp.zeros((), BF)
    greet_all(me)
    made = (x_ref, h1_ref, act_ref, h2_ref, res_ref)
    kept = (x_out, h1_out, act_out, h2_out, res_out)

    def keep(name):
        return pltpu.make_async_copy(made[name], kept[name], keep_sems.at[name])

    def keep_block(r, u):
        return pltpu.make_async_copy(all_ref.at[r, u], all_out.at[r, u], block_sems.at[r, u])

    half = F // 2

    def hop(kind, u, part=None):
        rows = slice(None) if part is None else pl.ds(part * half, half)
        source, slot, peer = ((0, 1, near), (0, 2, far), (2, 3, near))[kind]
        place = (kind, u if part is None else u + part)
        return to_peer(all_ref.at[source, u, rows], all_ref.at[slot, u, rows], kv_sems, place, peer)

    def halo(src, dst, kind, peer):
        return pltpu.make_async_remote_copy(
            src, dst, halo_sems.at[0, kind], halo_sems.at[1, kind], device_id={"seq": peer}, device_id_type=MESH
        )

    halos = [
        halo(frames.at[:, pl.ds(F - EDGE, EDGE)], lead.at[0], 0, after),
        halo(frames.at[:, pl.ds(0, EDGE)], lead.at[1], 1, behind),
        halo(cotangent.at[:, pl.ds(0, EDGE)], next_ref, 2, behind),
    ]
    for copy in halos:
        copy.start()
    active = embed[...].astype(F32)
    e, w, r = mish_parts(active)
    active = (active * w * r).astype(BF)
    embed_ref[...] = active
    time_rows[0:U, :] = dot(active, time_proj[...]) + shifts[2:3, :]
    first_taps = conv_first[...].reshape(3 * C, C)
    second_taps = conv_second[...].reshape(3 * C, C)

    def masked(block, at, u):
        return (block.astype(F32) * frame_mask_of(at, block.shape[0], len_ref[u])).astype(BF)

    for u in range(U):
        x_ref[u, own, :] = masked(frames[u], start, u)
    for copy in halos[:2]:
        copy.wait_recv()
    for u in range(U):
        x_ref[u, 0:EDGE, :] = masked(lead[0, u], start - EDGE, u)
        x_ref[u, F + EDGE :, :] = masked(lead[1, u], start + F, u)
    keep(0).start()

    def valid(i, u):
        return jnp.clip(len_ref[u] - i * F, 0, F).astype(F32)

    def local_stats(hidden, stat, got, sems, u):
        mask = frame_mask_of(start, F, len_ref[u])
        inside = hidden[EDGE : EDGE + F]
        many = jnp.maximum(valid(me, u) * (C // GROUPS), 1.0)
        mean = group_sums(row_sum(inside * mask)) / many
        centered = (inside - mean) * mask
        stat[u, 0:1, :] = mean
        stat[u, 1:2, :] = group_sums(row_sum(centered * centered))
        for copy in share(stat, got, sems, u, me):
            copy.start()

    def whole_stats(stat, got, sems, u):
        for copy in share(stat, got, sems, u, me):
            copy.wait()
        total = len_ref[u].astype(F32)
        parts = [(valid(me, u), stat[u])]
        for j in range(3):
            parts.append((valid(xor4(me, j + 1), u), got[j, u]))
        mean = sum(n * p[0:1] for n, p in parts) / total
        squares = sum(p[1:2] + (n * (C // GROUPS)) * jnp.square(p[0:1] - mean) for n, p in parts)
        inv = lax.rsqrt(squares / (total * (C // GROUPS)) + norm_eps)
        return mean, inv

    def activate(hidden, mean, inv, gain, shift):
        v = (hidden - mean) * inv * gain + shift
        e, w, r = mish_parts(v)
        return v * w * r

    def first_conv(u, _):
        hidden = dot(taps_of(x_ref[u]), first_taps) + shifts[0:1, :]
        h1_ref[u] = hidden
        local_stats(hidden, stat_one, got_one, sems_one, u)
        return 0

    lax.fori_loop(0, U, first_conv, 0)
    keep(1).start()

    def second_conv(u, _):
        mean, inv = whole_stats(stat_one, got_one, sems_one, u)
        stat_ref[u, 0:1, :] = mean
        stat_ref[u, 1:2, :] = inv
        mask = frame_mask_of(start - EDGE, rows, len_ref[u])
        act = activate(h1_ref[u], mean, inv, gains[0:1, :], shifts[1:2, :])
        act_in = ((act + time_rows[pl.ds(u, 1), :]) * mask).astype(BF)
        act_ref[u] = act_in
        hidden = dot(taps_of(act_in), second_taps) + shifts[3:4, :]
        h2_ref[u] = hidden
        local_stats(hidden, stat_two, got_two, sems_two, u)
        return 0

    lax.fori_loop(0, U, second_conv, 0)
    keep(2).start()
    keep(3).start()

    def to_qkv(u, _):
        skip = dot(x_ref[u, own, :], conv_skip[...]) + shifts[5:6, :]
        mean, inv = whole_stats(stat_two, got_two, sems_two, u)
        stat_ref[u, 2:3, :] = mean
        stat_ref[u, 3:4, :] = inv
        mask = frame_mask_of(start, F, len_ref[u])
        act = activate(h2_ref[u, own, :], mean, inv, gains[1:2, :], shifts[4:5, :]) * mask
        res = act + skip
        res_ref[u] = res
        centered = res - lane_mean(res)
        hat = centered * lax.rsqrt(lane_mean(centered * centered) + norm_eps)
        normed = (hat * gains[2:3, :] + shifts[6:7, :]).astype(BF)
        qkv = dot(normed, w_qkv[...]).astype(BF)
        all_ref[0, u] = qkv[:, 128:384]

        @pl.when(u < U - 1)
        def _():
            hop(1, u).start()

        @pl.when(u == U - 1)
        def _():
            for part in (0, 1):
                hop(1, U - 1, part).start()

        hop(0, u).start()
        keep_block(0, u).start()
        for h in range(2):
            other = jnp.where(lane == 64 * (1 - h) + 3, one, zero)
            qa_ref[u, h] = jnp.where(head_lanes(lane, h), qkv[:, 0:128] * SCALE, other)
        return 0

    lax.fori_loop(0, U, to_qkv, 0)
    keep(4).start()
    top[...] = jnp.full(top.shape, -1e30, F32)
    factors[...] = jnp.zeros(factors.shape, F32)
    acc[...] = jnp.zeros(acc.shape, F32)

    def block_of(t):
        late = t // 4
        r = (1 - late) * (t // 2) + late * (2 + t % 2)
        return r, (1 - late) * (t % 2) + late * ((t - 4) // 2)

    def keep_probs(t):
        r, u = block_of(t)
        return pltpu.make_async_copy(probs.at[t % 2], probs_out.at[r, u], probs_sems.at[t % 2])

    def arrive(t):
        @pl.when(t >= 3)
        def _():
            keep_probs(t - 3).wait()

        @pl.when(t >= 2)
        def _():
            keep_probs(t - 2).start()

        @pl.when(t == 2)
        def _():
            hop(0, 0).wait_recv()
            keep_block(1, 0).start()

        @pl.when(t == 3)
        def _():
            hop(0, 1).wait_recv()
            keep_block(1, 1).start()

        @pl.when(t == 4)
        def _():
            hop(1, 0).wait()
            hop(2, 0).start()
            keep_block(2, 0).start()

        @pl.when(t == 5)
        def _():
            hop(2, 0).wait_recv()
            keep_block(3, 0).start()

    def scores(t, held, tops, part=None):
        r, u = block_of(t)
        first, count = (0, F) if part is None else (part * half, half)
        k = all_ref[r, u, pl.ds(first, count), 0:128]
        spot = xor4(me, r) * F + first + lax.broadcasted_iota(jnp.int32, (count, 1), 0)
        bias = jnp.where(spot < len_ref[u], 0.0, -1e9).astype(BF)
        for h in range(2):
            ka = jnp.where(head_lanes(lane, h), k, jnp.where(lane == 64 * (1 - h) + 3, bias, zero))
            s = dot(ka, qa_ref[u, h], NT)
            held[h, 0:count] = s
            tops[h, 0:1, :] = jnp.max(s, axis=0, keepdims=True)

    def weigh(t, slot, held, tops, part=None):
        r, u = block_of(t)
        first, count = (0, F) if part is None else (part * half, half)
        vt = all_ref[r, u, pl.ds(first, count), 128:256].T
        ones = jnp.ones((EDGE, count), BF)
        for h in range(2):
            old = top[u, h, 0:1, :]
            new = jnp.maximum(old, tops[h, 0:1, :])
            p = jnp.exp(held[h, 0:count] - new).astype(BF)
            probs[slot, h, pl.ds(first, count), :] = p
            for row in (0, 1) if part is None else (part,):
                tops_used[r, u, 2 * h + row : 2 * h + row + 1, :] = new
            va = jnp.concatenate([vt[64 * h : 64 * h + 64], ones], axis=0)
            acc[u, h] = acc[u, h] * jnp.exp(old - new) + dot(va, p)
            top[u, h, 0:1, :] = new

    scores(0, held_one, tops_one)

    def two_steps(n, _):
        t = 2 * n
        arrive(t + 1)
        scores(t + 1, held_two, tops_two)
        weigh(t, 0, held_one, tops_one)
        arrive(t + 2)
        scores(t + 2, held_one, tops_one)
        weigh(t + 1, 1, held_two, tops_two)
        return 0

    lax.fori_loop(0, 2, two_steps, 0)
    arrive(5)
    scores(5, held_two, tops_two)
    weigh(4, 0, held_one, tops_one)
    keep_probs(3).wait()
    keep_probs(4).start()
    for part in (0, 1):
        hop(1, 1, part).wait()
        hop(2, 1, part).start()
        scores(6, held_one, tops_one, part)
        if part == 0:
            weigh(5, 1, held_two, tops_two)
            keep_probs(4).wait()
            keep_probs(5).start()
        else:
            keep_block(2, 1).start()
            weigh(7, 1, held_two, tops_two, 0)
        hop(2, 1, part).wait_recv()
        scores(7, held_two, tops_two, part)
        weigh(6, 0, held_one, tops_one, part)
        if part == 0:
            keep_probs(5).wait()
    keep_block(3, 1).start()
    keep_probs(6).start()
    weigh(7, 1, held_two, tops_two, 1)
    keep_probs(7).start()
    for u in range(U):
        outs, logs = [], []
        for h in range(2):
            total = acc[u, h, 64:65, :]
            outs.append(acc[u, h, 0:64, :] / total)
            logs.append(top[u, h, 0:1, :] + jnp.log(total))
        o_ref[u] = jnp.concatenate(outs, axis=0).T
        for r in range(4):
            for row in range(4):
                used = tops_used[r, u, row : row + 1, :]
                factors[r, u, row : row + 1, :] = jnp.exp(used - logs[row // 2])
    for u in range(U):
        hop(0, u).wait_send()
        for part in (None,) if u < U - 1 else (0, 1):
            hop(2, u, part).wait_send()
        for r in range(4):
            keep_block(r, u).wait()
    for name in range(5):
        keep(name).wait()
    keep_probs(6).wait()
    keep_probs(7).wait()
    for copy in halos:
        copy.wait_send()
    halos[2].wait_recv()


def front(lengths, frames, embed, cotangent, conv_first, conv_second, conv_skip, time_proj, w_qkv, gains, shifts):
    U, F, C = frames.shape
    rows = F + 2 * EDGE
    vmem = pl.BlockSpec(memory_space=pltpu.VMEM)
    stat = pltpu.VMEM((U, 8, C), F32)
    got = pltpu.VMEM((3, U, 8, C), F32)
    return pl.pallas_call(
        front_kernel,
        out_shape=(
            jax.ShapeDtypeStruct((U, rows, C), BF),
            jax.ShapeDtypeStruct((U, rows, C), F32),
            jax.ShapeDtypeStruct((U, rows, C), BF),
            jax.ShapeDtypeStruct((U, rows, C), F32),
            jax.ShapeDtypeStruct((U, F, C), F32),
            jax.ShapeDtypeStruct((4, U, F, 256), BF),
            jax.ShapeDtypeStruct((4, U, 2, F, F), BF),
            jax.ShapeDtypeStruct((U, F, 128), F32),
            jax.ShapeDtypeStruct((U, 2, F, 128), BF),
            jax.ShapeDtypeStruct((U, 8, C), F32),
            jax.ShapeDtypeStruct(embed.shape, BF),
            jax.ShapeDtypeStruct((U, EDGE, C), BF),
            jax.ShapeDtypeStruct((4, U, 8, F), F32),
        ),
        in_specs=[pl.BlockSpec(memory_space=pltpu.SMEM), vmem, vmem, pl.BlockSpec(memory_space=pl.ANY)] + [vmem] * 7,
        out_specs=[pl.BlockSpec(memory_space=pl.ANY)] * 7 + [vmem] * 6,
        scratch_shapes=[
            pltpu.VMEM((U, rows, C), BF),
            pltpu.VMEM((U, rows, C), F32),
            pltpu.VMEM((U, rows, C), BF),
            pltpu.VMEM((U, rows, C), F32),
            pltpu.VMEM((U, F, C), F32),
            pltpu.VMEM((4, U, F, 256), BF),
            pltpu.VMEM((2, U, EDGE, C), BF),
            stat,
            got,
            stat,
            got,
            pltpu.VMEM((U, 2, 8, F), F32),
            pltpu.VMEM((U, 2, 64 + EDGE, F), F32),
            pltpu.VMEM((2, F, F), F32),
            pltpu.VMEM((2, F, F), F32),
            pltpu.VMEM((2, 8, F), F32),
            pltpu.VMEM((2, 8, F), F32),
            pltpu.VMEM((2, 2, F, F), BF),
            pltpu.VMEM((4, U, 8, F), F32),
            pltpu.VMEM((8, C), F32),
            pltpu.SemaphoreType.DMA((2, 3)),
            pltpu.SemaphoreType.DMA((2, 3, U)),
            pltpu.SemaphoreType.DMA((2, 3, U)),
            pltpu.SemaphoreType.DMA((2, 3, U + 1)),
            pltpu.SemaphoreType.DMA((5,)),
            pltpu.SemaphoreType.DMA((4, U)),
            pltpu.SemaphoreType.DMA((2,)),
        ],
        compiler_params=pltpu.CompilerParams(
            collective_id=1, has_side_effects=True, vmem_limit_bytes=62 * 2**20
        ),
        name="front",
    )(lengths, frames, embed, cotangent, conv_first, conv_second, conv_skip, time_proj, w_qkv, gains, shifts)


def resnet_back_kernel(
    axes,
    len_ref,
    gqkv_in,
    gtwo_in,
    res_in,
    x_in,
    h1_in,
    act_in,
    h2_in,
    stat_ref,
    conv_first,
    conv_second,
    conv_skip,
    w_qkv,
    gains,
    shifts,
    up_ends,
    gframes,
    up,
    mid,
    late,
    last,
    gsmall,
    gfirst,
    gsecond,
    gskip,
    gw_qkv,
    lows,
    gqkv_ref,
    gtwo_ref,
    res_ref,
    x_ref,
    h1_ref,
    act_ref,
    h2_ref,
    load_sems,
    edges,
    gone,
    gmasked,
    sum_two,
    got_two,
    sum_one,
    got_one,
    halo_sems,
    sems_two,
    sems_one,
    small_got,
    small_sems,
    *sum_refs,
):
    U, F, C = gtwo_ref.shape
    given = (gqkv_in, res_in, gtwo_in, x_in, h2_in, act_in, h1_in)
    held = (gqkv_ref, res_ref, gtwo_ref, x_ref, h2_ref, act_ref, h1_ref)

    def load(name, u):
        return pltpu.make_async_copy(given[name].at[u], held[name].at[u], load_sems.at[name, u])

    for names in ((0, 1, 2, 3), (4, 5, 6)):
        for u in range(U):
            for name in names:
                load(name, u).start()
    rows = F + 2 * EDGE
    own = pl.ds(EDGE, F)
    inner = slice(EDGE, EDGE + F)
    me = lax.axis_index("seq")
    count = lax.axis_size("seq")
    after, behind = lax.rem(me + 1, count), lax.rem(me + count - 1, count)
    start = me * F
    hops, stages = butterfly(axes), stages_of(axes)
    greet_stages(stages, [("seq", xor4(me, 3))])
    fine = stages_of(axes, 1)
    run_up = doubling_steps(fine, up_ends, up, sum_refs[0])
    run_mid = sum_steps(stages, *sum_refs[1:5], mid, *sum_refs[5:7])
    run_late = sum_steps(stages, *sum_refs[7:11], late, *sum_refs[11:13])
    run_last = sum_steps(stages, *sum_refs[13:17], last, *sum_refs[17:19])
    run_small = small_steps(hops, gsmall, small_got, small_sems)
    for ref in (gsmall, sum_two, sum_one, gfirst, gsecond, gskip, gw_qkv):
        ref[...] = jnp.zeros_like(ref)

    run_up(0)

    def halo(kind, u):
        spot = pl.ds(F, EDGE) if kind == 0 else pl.ds(EDGE, EDGE)
        return pltpu.make_async_remote_copy(
            gone.at[u, spot],
            edges.at[kind, u],
            halo_sems.at[0, kind, u],
            halo_sems.at[1, kind, u],
            device_id={"seq": after if kind == 0 else behind},
            device_id_type=MESH,
        )

    def through_qkv(u, _):
        for name in range(4):
            load(name, u).wait()
        res = res_ref[u]
        centered = res - lane_mean(res)
        inv = lax.rsqrt(lane_mean(centered * centered) + norm_eps)
        hat = centered * inv
        normed = (hat * gains[2:3, :] + shifts[6:7, :]).astype(BF)
        gqkv = gqkv_ref[u]
        gw_qkv[...] += tn(normed, gqkv)
        grad = dot(gqkv, w_qkv[...], NT)
        gsmall[10:11, :] += row_sum(grad * hat)
        gsmall[6:7, :] += row_sum(grad)
        grad = grad * gains[2:3, :]
        grad = gtwo_ref[u] + inv * (grad - lane_mean(grad) - hat * lane_mean(grad * hat))
        gone[u, own, :] = grad
        for kind in range(2):
            halo(kind, u).start()
        gsmall[5:6, :] += row_sum(grad)
        low = grad.astype(BF)
        gskip[...] += tn(x_ref[u, own, :], low)
        gmasked[u] = dot(low, conv_skip[...], NT)

        @pl.when(u == 0)
        def _():
            run_up(1)

        return 0

    lax.fori_loop(0, U, through_qkv, 0)

    def norm_terms(grad, hidden, u, at):
        mean, inv = stat_ref[u, 2 * at : 2 * at + 1, :], stat_ref[u, 2 * at + 1 : 2 * at + 2, :]
        gain, shift = gains[at : at + 1, :], shifts[1 + 3 * at : 2 + 3 * at, :]
        hat = (hidden - mean) * inv
        v = hat * gain + shift
        e, w, r = mish_parts(v)
        slope = w * r + v * (4.0 * e * (1.0 + e)) * (r * r)
        return hat, grad * slope, inv, gain

    def local_sums(hat, grad, gain, sums, got, sems, u, at):
        hat, grad = hat[inner], grad[inner]
        gsmall[8 + at : 9 + at, :] += row_sum(grad * hat)
        gsmall[1 + 3 * at : 2 + 3 * at, :] += row_sum(grad)
        grad = grad * gain
        both = jnp.concatenate([row_sum(grad), row_sum(grad * hat)], axis=0)
        sums[u, 0:2, :] = group_sums(both)
        for copy in share(sums, got, sems, u, me):
            copy.start()

    def whole_sums(sums, got, sems, u):
        for copy in share(sums, got, sems, u, me):
            copy.wait()
        return (sums[u] + got[0, u]) + (got[1, u] + got[2, u])

    def hidden_grad(hat, grad, inv, gain, total, u, mask):
        many = len_ref[u].astype(F32) * (C // GROUPS)
        return inv * (grad * gain - mask * ((total[0:1] + hat * total[1:2]) / many))

    def back_taps(grad, weight):
        wide = grad.astype(F32)
        many = grad.shape[0]
        later = pltpu.roll(wide, many - 1, 0).astype(BF)
        earlier = pltpu.roll(wide, 1, 0).astype(BF)
        return dot(later, weight[0], NT) + dot(grad, weight[1], NT) + dot(earlier, weight[2], NT)

    def wide_mask(u):
        return frame_mask_of(start - EDGE, rows, len_ref[u])

    def second_terms(u, _):
        for kind in range(2):
            halo(kind, u).wait()
        load(4, u).wait()
        gone[u, 0:EDGE, :] = edges[0, u]
        gone[u, F + EDGE :, :] = edges[1, u]
        hat, grad, inv, gain = norm_terms(gone[u] * wide_mask(u), h2_ref[u], u, 1)
        gone[u] = grad
        local_sums(hat, grad, gain, sum_two, got_two, sems_two, u, 1)
        return 0

    lax.fori_loop(0, U, second_terms, 0)

    def second_back(u, _):
        load(5, u).wait()
        load(6, u).wait()
        taps = taps_of(act_ref[u])
        total = whole_sums(sum_two, got_two, sems_two, u)
        mask = wide_mask(u)
        inv, gain = stat_ref[u, 3:4, :], gains[1:2, :]
        hat = (h2_ref[u] - stat_ref[u, 2:3, :]) * inv
        grad = hidden_grad(hat, gone[u], inv, gain, total, u, mask)
        gsmall[3:4, :] += row_sum(grad[inner])
        low = grad.astype(BF)
        gsecond[...] += tn(taps[inner], low[inner])
        grad = back_taps(low, conv_second) * mask
        by_time = row_sum(grad[inner])
        gsmall[2:3, :] += by_time
        gsmall[pl.ds(16 + lax.axis_index("dp") * U + u, 1), :] = by_time
        hat, grad, inv, gain = norm_terms(grad, h1_ref[u], u, 0)
        gone[u] = grad
        local_sums(hat, grad, gain, sum_one, got_one, sems_one, u, 0)

        @pl.when(u == 0)
        def _():
            run_up(2)

        return 0

    lax.fori_loop(0, U, second_back, 0)
    pack(sum_refs[1], [gskip, gw_qkv])
    run_mid(0)
    pack(sum_refs[7], [gsecond])
    run_late(0)

    def first_back(u, _):
        taps = taps_of(x_ref[u])
        total = whole_sums(sum_one, got_one, sems_one, u)
        mask = wide_mask(u)
        inv, gain = stat_ref[u, 1:2, :], gains[0:1, :]
        hat = (h1_ref[u] - stat_ref[u, 0:1, :]) * inv
        grad = hidden_grad(hat, gone[u], inv, gain, total, u, mask)
        gsmall[0:1, :] += row_sum(grad[inner])
        low = grad.astype(BF)
        lows[u] = low
        gfirst[...] += tn(taps[inner], low[inner])
        return 0

    lax.fori_loop(0, U, first_back, 0)
    run_late(1)
    run_mid(1)
    pack(sum_refs[13], [gfirst])
    steps = 2 * len(stages)
    for n in range(max(steps, len(hops)) + 1):
        for run, ahead, final in (
            (run_last, 0, steps),
            (run_late, 2, steps),
            (run_mid, 2, steps),
            (run_small, 0, len(hops)),
        ):
            if ahead + n <= final:
                run(ahead + n)
        if 0 <= n - 2 <= len(fine) - 3:
            run_up(n + 1)
        if n < U:
            grad = back_taps(lows[n], conv_first)[inner] + gmasked[n]
            gframes[n] = grad * frame_mask_of(start, F, len_ref[n])


def resnet_back(lengths, gqkv, gtwo, res, x, h1, act, h2, stat, conv_first, conv_second, conv_skip, w_qkv, gains, shifts, up_ends, axes):
    U, F, C = gtwo.shape
    count = bits_of(axes)
    shapes = [(3 * C, C), (3 * C, C), (C, C), w_qkv.shape]
    mats = [jax.ShapeDtypeStruct(shape, F32) for shape in shapes]
    up_rows = up_ends.shape[0] << count
    row_counts = [padded_rows(packed_rows(some), axes) for some in (mats[2:], mats[1:2], mats[:1])]
    small_rows = 16 + U * dict(axes)["dp"]
    rows = F + 2 * EDGE
    vmem = pl.BlockSpec(memory_space=pltpu.VMEM)
    sums = pltpu.VMEM((U, 8, C), F32)
    got = pltpu.VMEM((3, U, 8, C), F32)
    return pl.pallas_call(
        functools.partial(resnet_back_kernel, axes),
        out_shape=(
            jax.ShapeDtypeStruct((U, F, C), F32),
            *(jax.ShapeDtypeStruct((many, 128), BF) for many in [up_rows, *row_counts]),
            jax.ShapeDtypeStruct((small_rows, C), F32),
        ),
        in_specs=[pl.BlockSpec(memory_space=pltpu.SMEM)]
        + [pl.BlockSpec(memory_space=pl.ANY)] * 7
        + [vmem] * 8,
        out_specs=[vmem] * 6,
        scratch_shapes=[
            *(pltpu.VMEM(shape, F32) for shape in shapes),
            pltpu.VMEM((U, rows, C), BF),
            *(pltpu.VMEM(x.shape, x.dtype) for x in (gqkv, gtwo, res, x, h1, act, h2)),
            pltpu.SemaphoreType.DMA((7, U)),
            pltpu.VMEM((2, U, EDGE, C), F32),
            pltpu.VMEM((U, rows, C), F32),
            pltpu.VMEM((U, F, C), F32),
            sums,
            got,
            sums,
            got,
            pltpu.SemaphoreType.DMA((2, 2, U)),
            pltpu.SemaphoreType.DMA((2, 3, U)),
            pltpu.SemaphoreType.DMA((2, 3, U)),
            pltpu.VMEM((count, small_rows, C), F32),
            pltpu.SemaphoreType.DMA((2, count)),
            pltpu.SemaphoreType.DMA((2, stage_count(axes, 1), 7)),
            *(ref for many in row_counts for ref in sum_scratch(many, axes)),
        ],
        compiler_params=pltpu.CompilerParams(
            collective_id=4, has_side_effects=True, vmem_limit_bytes=60 * 2**20
        ),
        name="resnet_back",
    )(lengths, gqkv, gtwo, res, x, h1, act, h2, stat, conv_first, conv_second, conv_skip, w_qkv, gains, shifts, up_ends)


def shards(
    frames,
    time_embed,
    lengths,
    out_cotangent,
    conv_first,
    conv_second,
    conv_skip,
    time_proj,
    w_qkv,
    w_out,
    ff_in,
    ff_out,
    conv_down,
    gains,
    shifts,
    ff_bias,
    snake_logs,
):
    channels = frames.shape[2]
    (
        masked_in,
        hidden_one,
        act_in,
        hidden_two,
        resnet_out,
        kv_all,
        probs,
        attended_full,
        queries_aug,
        stats,
        embed_act,
        next_rows,
        factors,
    ) = front(
        lengths,
        frames,
        time_embed,
        out_cotangent,
        conv_first,
        conv_second,
        conv_skip,
        time_proj,
        w_qkv,
        gains,
        shifts,
    )
    (
        layer_out,
        grad_two,
        grad_aug,
        first_rows,
        tail_rows,
        grad_w_out,
        grad_ff_in,
        grad_ff_out,
        grad_conv_down,
        mid_small,
        ff_small,
    ) = middle(
        lengths,
        attended_full,
        resnet_out,
        out_cotangent,
        next_rows,
        w_out,
        ff_in,
        ff_out,
        conv_down,
        gains,
        shifts,
        ff_bias,
        snake_logs,
    )
    axes = (("seq", lax.axis_size("seq")), ("dp", lax.axis_size("dp")))
    grad_qkv, up_ends, small_up, tail_rows = attend_back(
        queries_aug,
        grad_aug,
        kv_all,
        probs,
        factors,
        mid_small,
        ff_small,
        embed_act,
        tail_rows,
        [grad_w_out, grad_ff_in, grad_ff_out, grad_conv_down.reshape(-1, channels)],
        axes,
    )
    grad_frames, up, mid, late, last, small_late = resnet_back(
        lengths,
        grad_qkv,
        grad_two,
        resnet_out,
        masked_in,
        hidden_one,
        act_in,
        hidden_two,
        stats,
        conv_first,
        conv_second,
        conv_skip,
        w_qkv,
        gains,
        shifts,
        up_ends,
        axes,
    )
    weights = (
        conv_first,
        conv_second,
        conv_skip,
        time_proj,
        w_qkv,
        w_out,
        ff_in,
        ff_out,
        conv_down,
        gains,
        shifts,
        ff_bias.reshape(1, -1),
        snake_logs,
    )
    grads = finish(
        lengths,
        first_rows,
        tail_rows,
        small_up,
        small_late,
        layer_out,
        grad_frames,
        (up, mid, late, last),
        [w.shape for w in weights],
    )
    return (grads[13], grads[14], *grads[:11], grads[11].reshape(-1), grads[12])


def solution(mesh):
    in_specs = (
        P("dp", "seq", None),
        P("dp", None),
        P("dp"),
        P("dp", "seq", None),
        P(),
        P(),
        P(),
        P(),
        P(),
        P(),
        P(),
        P(),
        P(),
        P(),
        P(),
        P(),
        P(),
    )
    out_specs = (
        P("dp", "seq", None),
        P("dp", "seq", None),
        P(),
        P(),
        P(),
        P(),
        P(),
        P(),
        P(),
        P(),
        P(),
        P(),
        P(),
        P(),
        P(),
    )
    return jax.shard_map(shards, mesh=mesh, in_specs=in_specs, out_specs=out_specs, check_vma=False)
```

```python
import functools
import math

import jax
import jax.numpy as jnp
from jax import lax
from jax.experimental import pallas as pl
from jax.experimental.pallas import tpu as pltpu
from jax.sharding import PartitionSpec as P

F32, BF = jnp.float32, jnp.bfloat16
NT = (((1,), (1,)), ((), ()))
NN = (((1,), (0,)), ((), ()))
TN = (((0,), (0,)), ((), ()))
MESH = pl.DeviceIdType.MESH
EDGE = 16


def dot(a, b, dn=NN):
    return lax.dot_general(a, b, dn, preferred_element_type=F32)


HEADS = 2
GROUPS = 8


norm_eps = 1e-05


SIN_PI = (3.141592580060032, -5.167706879868365, 2.55003139258664, -0.598045264752551, 0.0772203056339658)
COS_PI = (0.9999999534804945, -4.934792860766467, 4.05841196261883, -1.3318805129033002, 0.21969758323424166)


def horner(coefficients, x):
    value = coefficients[-1]
    for coefficient in coefficients[-2::-1]:
        value = value * x + coefficient
    return value


def sin_cos_half_turns(turns):
    part = turns - jnp.round(turns)
    square = part * part
    return part * horner(SIN_PI, square), horner(COS_PI, square)


def row_sum(x):
    return jnp.sum(x, axis=0, keepdims=True)


def lane_mean(x):
    return jnp.mean(x, axis=1, keepdims=True)


def tn(a, b):
    return lax.dot_general(a, b, TN, preferred_element_type=F32)


def middle_kernel(
    RB,
    FC,
    len_ref,
    att_ref,
    res_ref,
    cot_ref,
    next_ref,
    w_out,
    ff_in,
    ff_out,
    conv_down,
    gains,
    shifts,
    ff_bias,
    snake_logs,
    out_ref,
    gtwo_ref,
    aug_ref,
    row_ref,
    tail_ref,
    gw_out,
    gff_in,
    gff_out,
    gdown,
    gsmall,
    gff_small,
    pairs,
    before_last,
):
    u, i = pl.program_id(0), pl.program_id(1)
    U, nb = pl.num_programs(0), pl.num_programs(1)
    half = RB // 2
    frames = nb * RB
    length = len_ref[u]
    base = lax.axis_index("seq") * frames
    at = base + i * RB

    @pl.when((u == 0) & (i == 0))
    def _():
        for ref in (gw_out, gff_in, gff_out, gdown, gsmall, gff_small):
            ref[...] = jnp.zeros_like(ref)

    def column_mask(start, rows, step):
        places = start + step * lax.broadcasted_iota(jnp.int32, (rows, 1), 0)
        return jnp.where(places < length, 1.0, 0.0)

    mask = column_mask(at, RB, 1)
    half_mask = column_mask(at, half, 2)
    low_f32 = cot_ref[0, pl.ds(pl.multiple_of(i * half, half), half), :].astype(F32) * half_mask
    gsmall[4:5, :] += row_sum(low_f32)
    low = low_f32.astype(BF)
    follow = jnp.minimum(i * half + half, frames // 2 - 16)
    inner = cot_ref[0, pl.ds(pl.multiple_of(follow, 16), 16), :].astype(F32)[0:1]
    outer = next_ref[0].astype(F32)[0:1]
    after = jnp.where(i == nb - 1, outer, inner) * jnp.where(at + RB < length, 1.0, 0.0)
    row_at = lax.broadcasted_iota(jnp.int32, (half, 1), 0)
    low_next = jnp.where(row_at == half - 1, after, pltpu.roll(low_f32, half - 1, 0)).astype(BF)
    even_grads = dot(low, conv_down[1], NT)
    odd_grads = dot(low, conv_down[2], NT) + dot(low_next, conv_down[0], NT)
    for lanes in (0, 128):
        pairs[lanes // 128, pl.ds(0, half, stride=2), :] = even_grads[:, lanes : lanes + 128]
        pairs[lanes // 128, pl.ds(1, half, stride=2), :] = odd_grads[:, lanes : lanes + 128]
    grad_three = jnp.concatenate([pairs[0], pairs[1]], axis=1) * mask
    gsmall[3:4, :] += row_sum(grad_three)
    grad_low = grad_three.astype(BF)
    attended = att_ref[0]
    att_low = attended.astype(BF)
    resid_two = res_ref[0] + dot(att_low, w_out[...]) + shifts[7:8, :]
    centered = resid_two - lane_mean(resid_two)
    inv = lax.rsqrt(lane_mean(centered * centered) + norm_eps)
    hat = centered * inv
    normed = (hat * gains[3:4, :] + shifts[8:9, :]).astype(BF)
    freq = jnp.exp(snake_logs[0:1, :])
    spread = jnp.exp(snake_logs[1:2, :])
    size = 1.0 / (spread + 1e-09)
    turn = freq * (1.0 / math.pi)
    resid_three = resid_two + shifts[9:10, :]
    grad_normed = jnp.zeros_like(resid_two)
    for c in range(0, ff_bias.shape[1], FC):
        cols = slice(c, c + FC)
        hidden = dot(normed, ff_in[:, cols]) + ff_bias[:, cols]
        sine, cosine = sin_cos_half_turns(hidden * turn[:, cols])
        square = sine * sine
        snaked = (hidden + square * size[:, cols]).astype(BF)
        resid_three = resid_three + dot(snaked, ff_out[cols, :])
        gff_out[cols, :] += tn(snaked, grad_low)
        grad_snaked = dot(grad_low, ff_out[cols, :], NT)
        cross = grad_snaked * (sine * cosine)
        grad_hidden = grad_snaked + cross * (2.0 * size * freq)[:, cols]
        gff_small[0:1, cols] += row_sum(grad_hidden)
        gff_small[1:2, cols] += row_sum(cross * hidden)
        gff_small[2:3, cols] += row_sum(grad_snaked * square)
        hidden_low = grad_hidden.astype(BF)
        gff_in[:, cols] += tn(normed, hidden_low)
        grad_normed = grad_normed + dot(hidden_low, ff_in[:, cols], NT)
    down = (resid_three * mask).astype(BF)
    down_f32 = down.astype(F32)
    for lanes in (0, 128):
        pairs[lanes // 128] = down_f32[:, lanes : lanes + 128]
    even = jnp.concatenate([pairs[j, pl.ds(0, half, stride=2), :] for j in range(2)], axis=1)
    odd = jnp.concatenate([pairs[j, pl.ds(1, half, stride=2), :] for j in range(2)], axis=1)
    first = jnp.where(i == 0, 0.0, before_last[0:1, :])
    before = jnp.where(row_at == 0, first, pltpu.roll(odd, 1, 0)).astype(BF)
    before_last[0:1, :] = odd[half - 1 : half, :]
    tail_ref[0] = dot(down[RB - 16 :, :], conv_down[0])[8:16]
    even, odd = even.astype(BF), odd.astype(BF)
    lowered = dot(before, conv_down[0]) + dot(even, conv_down[1]) + dot(odd, conv_down[2])
    lowered = lowered + shifts[10:11, :]

    @pl.when(i == 0)
    def _():
        row_ref[0] = lowered[0:8]

    out_ref[0] = (lowered * half_mask).astype(BF)
    gdown[0] += tn(odd, low_next)
    gdown[1] += tn(even, low)
    gdown[2] += tn(odd, low)
    gsmall[0:1, :] += row_sum(grad_normed * hat)
    gsmall[2:3, :] += row_sum(grad_normed)
    grad_hat = grad_normed * gains[3:4, :]
    grad_two = grad_three + inv * (
        grad_hat - lane_mean(grad_hat) - hat * lane_mean(grad_hat * hat)
    )
    gtwo_ref[0] = grad_two
    gsmall[1:2, :] += row_sum(grad_two)
    two_low = grad_two.astype(BF)
    gw_out[...] += tn(att_low, two_low)
    grad_att = dot(two_low, w_out[...], NT).astype(BF)
    terms = grad_att.astype(F32) * attended
    lane = lax.broadcasted_iota(jnp.int32, (1, 128), 1)
    zero = jnp.zeros((), F32)
    for h in range(2):
        mine = (lane >= 64 * h) & (lane < 64 * h + 64)
        term = jnp.sum(jnp.where(mine, terms, zero), axis=1, keepdims=True)
        aug_ref[0, h] = with_pieces(jnp.where(mine, grad_att, jnp.zeros((), BF)), term, lane, h)

    @pl.when((u == U - 1) & (i == nb - 1))
    def _():
        gff_small[1:2, :] = gff_small[1:2, :] * (2.0 * size * freq)
        gff_small[2:3, :] = gff_small[2:3, :] * (-(size * size) * spread)


def with_pieces(block, value, lane, h):
    base = 64 * (1 - h)
    for j in range(3):
        piece = value.astype(BF)
        value = value - piece.astype(F32)
        block = jnp.where(lane == base + j, piece, block)
    return block


def middle(lengths, attended, resnet_out, cotangent, next_rows, w_out, ff_in, ff_out, conv_down, gains, shifts, ff_bias, snake_logs, FC=256):
    U, F, C = resnet_out.shape
    RB = min(F, 1024)
    inner = attended.shape[2]
    FF = ff_bias.shape[0]
    whole = lambda shape: pl.BlockSpec(shape, lambda u, i, _: (0,) * len(shape))
    rows = lambda n, c: pl.BlockSpec((1, n, c), lambda u, i, _: (u, i, 0))
    per_utt = lambda n, c: pl.BlockSpec((1, n, c), lambda u, i, _: (u, 0, 0))
    sums = ((inner, C), (C, FF), (FF, C), (3, C, C), (8, C), (8, FF))
    return pl.pallas_call(
        functools.partial(middle_kernel, RB, FC),
        out_shape=(
            jax.ShapeDtypeStruct((U, F // 2, C), BF),
            jax.ShapeDtypeStruct((U, F, C), F32),
            jax.ShapeDtypeStruct((U, 2, F, inner), BF),
            jax.ShapeDtypeStruct((U, 8, C), F32),
            jax.ShapeDtypeStruct((U, 8, C), F32),
            *(jax.ShapeDtypeStruct(shape, F32) for shape in sums),
        ),
        grid_spec=pltpu.PrefetchScalarGridSpec(
            num_scalar_prefetch=1,
            grid=(U, F // RB),
            in_specs=[
                rows(RB, inner),
                rows(RB, C),
                per_utt(F // 2, C),
                per_utt(16, C),
                whole((inner, C)),
                whole((C, FF)),
                whole((FF, C)),
                whole((3, C, C)),
                whole(gains.shape),
                whole(shifts.shape),
                whole((1, FF)),
                whole((2, FF)),
            ],
            out_specs=[
                rows(RB // 2, C),
                rows(RB, C),
                pl.BlockSpec((1, 2, RB, inner), lambda u, i, _: (u, 0, i, 0)),
                per_utt(8, C),
                per_utt(8, C),
                *(whole(shape) for shape in sums),
            ],
            scratch_shapes=[
                pltpu.VMEM((2, RB, 128), F32),
                pltpu.VMEM((8, C), F32),
            ],
        ),
        compiler_params=pltpu.CompilerParams(vmem_limit_bytes=56 * 2**20),
        name="middle",
    )(lengths, attended, resnet_out, cotangent, next_rows, w_out, ff_in, ff_out, conv_down, gains, shifts, ff_bias.reshape(1, -1), snake_logs)


def butterfly(axes):
    hops = []
    for axis, size in axes:
        place = lax.axis_index(axis)
        bit = 1
        while bit < size:
            up = (place // bit) % 2
            hops.append((axis, place + bit - 2 * bit * up, up))
            bit *= 2
    return hops


def bits_of(axes):
    return sum(size.bit_length() - 1 for _, size in axes)


def radices(axis, size, fine):
    while size > 1:
        radix = min(2 if axis == "seq" else 8, size)
        if fine and axis == "dp":
            radix = 2 if fine == 1 else min(4, size)
            fine = 2
        yield radix
        size //= radix


def stages_of(axes, fine=0):
    stages = []
    for axis, size in axes:
        stride = 1
        for radix in radices(axis, size, fine):
            place = lax.axis_index(axis)
            digit = (place // stride) % radix
            peers = [place + ((digit + m) % radix - digit) * stride for m in range(1, radix)]
            stages.append((axis, radix, digit, peers))
            stride *= radix
    return [stages[0], *stages[2:], stages[1]] if fine else stages


def padded_rows(rows, axes):
    unit = EDGE << bits_of(axes)
    return -(-rows // unit) * unit


def packed_rows(mats):
    return sum(m.shape[0] * m.shape[1] // 128 for m in mats)


def greet_stages(stages, extra=()):
    barrier = pltpu.get_barrier_semaphore()
    met = [(axis, peer) for axis, _, _, peers in stages for peer in peers] + list(extra)
    for axis, peer in met:
        pl.semaphore_signal(barrier, inc=1, device_id={axis: peer}, device_id_type=MESH)
    pl.semaphore_wait(barrier, len(met))


def hop_copy(hop, src, dst, sems, place):
    axis, partner, _ = hop
    return pltpu.make_async_remote_copy(
        src, dst, sems.at[(0, *place)], sems.at[(1, *place)], device_id={axis: partner}, device_id_type=MESH
    )


def pack(total, mats):
    row = 0
    for ref in mats:
        rows, columns = ref.shape
        for column in range(0, columns, 128):
            total[pl.ds(row, rows), :] = ref[:, column : column + 128]
            row += rows
    if row < total.shape[0]:
        total[pl.ds(row, total.shape[0] - row), :] = jnp.zeros((total.shape[0] - row, 128), F32)


def shares_of(stages, rows):
    low, length, shares = 0, rows, []
    for _, radix, digit, _ in stages:
        shares.append((low, length, length // radix))
        length //= radix
        low = pl.multiple_of(low + digit * length, EDGE)
    return shares, low


def halving_steps(stages, total, sent, got, ends, sems):
    rows = total.shape[0]
    shares, _ = shares_of(stages, rows)

    def copies(s):
        axis, radix, _, peers = stages[s]
        _, before, length = shares[s]
        for m, peer in enumerate(peers):
            slot = pl.ds(rows - before + m * length, length)
            yield m, slot, hop_copy((axis, peer, 0), sent.at[slot], got.at[slot], sems, (s, m))

    def run(k):
        if k > 0:
            _, radix, digit, _ = stages[k - 1]
            low, _, length = shares[k - 1]
            here = pl.ds(pl.multiple_of(low + digit * length, EDGE), length)
            value = total[here, :]
            for _, slot, copy in copies(k - 1):
                copy.wait()
                value = value + got[slot, :].astype(F32)
            if k < len(stages):
                total[here, :] = value
            else:
                ends[...] = value.astype(BF)
        if k < len(stages):
            _, radix, digit, _ = stages[k]
            low, _, length = shares[k]
            for m, slot, copy in copies(k):
                give = pl.multiple_of(low + (digit + m + 1) % radix * length, EDGE)
                sent[slot, :] = total[pl.ds(give, length), :].astype(BF)
                copy.start()

    return run


def doubling_steps(stages, ends, whole, sems):
    count = len(stages)
    shares, own = shares_of(stages, whole.shape[0])

    def copies(s):
        axis, _, digit, peers = stages[s]
        low, _, length = shares[s]
        here = pl.ds(pl.multiple_of(low + digit * length, EDGE), length)
        for m, peer in enumerate(peers):
            yield hop_copy((axis, peer, 0), whole.at[here], whole.at[here], sems, (s, m))

    def run(k):
        if k == 0:
            whole[pl.ds(own, ends.shape[0]), :] = ends[...]
        if k > 0:
            for copy in copies(count - k):
                copy.wait()
        if k < count:
            for copy in copies(count - 1 - k):
                copy.start()

    return run


def sum_steps(stages, total, sent, got, ends, whole, sems, more_sems):
    count = len(stages)
    halving = halving_steps(stages, total, sent, got, ends, sems)
    doubling = doubling_steps(stages, ends, whole, more_sems)

    def run(k):
        if k <= count:
            halving(k)
        if k >= count:
            doubling(k - count)

    return run


def small_steps(hops, mine, got, sems):
    def run(k):
        if 0 < k <= len(hops):
            hop_copy(hops[k - 1], mine, got.at[k - 1], sems, (k - 1,)).wait()
            mine[...] += got[k - 1]
        if k < len(hops):
            hop_copy(hops[k], mine, got.at[k], sems, (k,)).start()

    return run


def stage_count(axes, fine):
    return sum(len(list(radices(axis, size, fine))) for axis, size in axes)


def halving_scratch(rows, axes, fine):
    return [
        pltpu.VMEM((rows, 128), F32),
        pltpu.VMEM((rows, 128), BF),
        pltpu.VMEM((rows, 128), BF),
        pltpu.SemaphoreType.DMA((2, stage_count(axes, fine), 7)),
    ]


def sum_scratch(rows, axes):
    total, sent, got, sems = halving_scratch(rows, axes, 0)
    return [total, sent, got, pltpu.VMEM((rows >> bits_of(axes), 128), BF), sems, sems]


def finish_kernel(
    len_ref, rows, tails, small_up, small_late, layer, frames_in, up_in, mid_in, late_in, last_in, *refs
):
    outs, patched, frames_out, edge, sems = refs[:13], refs[13], refs[14], refs[15], refs[16]
    big, big_sems = refs[17:26], refs[26]
    up, mid, late, last, in_sems = refs[27:32]
    given = (up_in, mid_in, late_in, last_in)
    bring = [pltpu.make_async_copy(x, y, in_sems.at[n]) for n, (x, y) in enumerate(zip(given, refs[27:31]))]
    for copy in bring:
        copy.start()
    held_frames = refs[32]
    frames_here = pltpu.make_async_copy(frames_in, held_frames, sems.at[2])
    frames_here.start()
    frames_there = pltpu.make_async_copy(held_frames, frames_out, sems.at[3])
    U = rows.shape[0]
    fetch = pltpu.make_async_copy(layer.at[:, pl.ds(0, EDGE)], edge, sems.at[0])
    fetch.start()
    (
        first, second, skip, time_out, qkv, w_out, ff_in, ff_out, down, gains, shifts, bias, logs
    ) = (*big, *outs[9:])

    def send(n):
        return pltpu.make_async_copy(big[n], outs[n], big_sems.at[n])

    def unpack(packed, refs):
        row = 0
        for ref in refs:
            flat = ref.reshape(-1, ref.shape[-1]) if len(ref.shape) == 3 else ref
            rows, columns = flat.shape
            for column in range(0, columns, 128):
                flat[:, column : column + 128] = packed[pl.ds(row, rows), :].astype(F32)
                row += rows

    bring[0].wait()
    unpack(up, [w_out, ff_in, ff_out, down])
    for n in range(5, 9):
        send(n).start()
    frames_here.wait()
    frames_there.start()
    for copy in bring[1:]:
        copy.wait()
    unpack(mid, [skip, qkv])
    unpack(late, [second])
    unpack(last, [first])
    for n in (0, 1, 2, 4):
        send(n).start()
    C = skip.shape[0]
    wide = bias.shape[1] // C
    utts = small_late.shape[0] - 16
    gains[0:3, :] = small_late[8:11, :]
    gains[3:4, :] = small_up[0:1, :]
    shifts[0:7, :] = small_late[0:7, :]
    shifts[7:11, :] = small_up[1:5, :]
    blocks = [small_up[8 * (j + 1) : 8 * (j + 2), :] for j in range(wide)]
    base = packed_rows([w_out, ff_in, ff_out, down.reshape(-1, C)])
    embed = [up[pl.ds(base + utts * j, utts), :].astype(F32) for j in range(time_out.shape[0] // 128)]
    for j in range(wide):
        bias[:, j * C : (j + 1) * C] = blocks[j][0:1]
        logs[:, j * C : (j + 1) * C] = blocks[j][1:3]
    grads = small_late[16:, :]
    for j, part in enumerate(embed):
        time_out[j * 128 : (j + 1) * 128, :] = lax.dot_general(
            part, grads, TN, precision=lax.Precision.HIGHEST, preferred_element_type=F32
        )
    send(3).start()
    fetch.wait()
    me = lax.axis_index("seq")
    frames = 2 * layer.shape[1]
    is_first = lax.broadcasted_iota(jnp.int32, (EDGE, 1), 0) == 0
    for u in range(U):
        value = rows[u, 0:1] + jnp.where(me > 0, tails[u, 7:8], 0.0)
        value = value * jnp.where(me * frames < len_ref[u], 1.0, 0.0)
        edge[u] = jnp.where(is_first, value, edge[u].astype(F32)).astype(BF)
    store = pltpu.make_async_copy(edge, patched.at[:, pl.ds(0, EDGE)], sems.at[1])
    store.start()
    for n in range(9):
        send(n).wait()
    store.wait()
    frames_there.wait()


def finish(lengths, rows, tails, small_up, small_late, layer, frames, sums, shapes):
    vmem = pl.BlockSpec(memory_space=pltpu.VMEM)
    anywhere = pl.BlockSpec(memory_space=pl.ANY)
    return pl.pallas_call(
        finish_kernel,
        out_shape=(
            *(jax.ShapeDtypeStruct(shape, F32) for shape in shapes),
            jax.ShapeDtypeStruct(layer.shape, BF),
            jax.ShapeDtypeStruct(frames.shape, F32),
        ),
        in_specs=[pl.BlockSpec(memory_space=pltpu.SMEM)] + [vmem] * 4 + [anywhere] * 6,
        out_specs=[anywhere] * 9 + [vmem] * 4 + [anywhere] * 2,
        scratch_shapes=[
            pltpu.VMEM((rows.shape[0], EDGE, rows.shape[2]), BF),
            pltpu.SemaphoreType.DMA((4,)),
            *(pltpu.VMEM(shape, F32) for shape in shapes[:9]),
            pltpu.SemaphoreType.DMA((9,)),
            *(pltpu.VMEM(x.shape, BF) for x in sums),
            pltpu.SemaphoreType.DMA((4,)),
            pltpu.VMEM(frames.shape, F32),
        ],
        input_output_aliases={5: len(shapes)},
        compiler_params=pltpu.CompilerParams(vmem_limit_bytes=56 * 2**20),
        name="finish",
    )(lengths, rows, tails, small_up, small_late, layer, frames, *sums)


SCALE = 0.125


def head_lanes(lane, h):
    return (lane >= 64 * h) & (lane < 64 * h + 64)


def greet_seq(me):
    barrier = pltpu.get_barrier_semaphore()
    for flip in (1, 2):
        pl.semaphore_signal(barrier, inc=1, device_id={"seq": flipped(me, flip)}, device_id_type=MESH)
    pl.semaphore_wait(barrier, 2)


def flipped(place, bit):
    return place + bit - 2 * bit * ((place // bit) % 2)


def to_peer(src, dst, sems, place, peer):
    return pltpu.make_async_remote_copy(
        src, dst, sems.at[(0, *place)], sems.at[(1, *place)], device_id={"seq": peer}, device_id_type=MESH
    )


def xor4(place, r):
    low = (place % 2 + r % 2) % 2
    high = (place // 2 + r // 2) % 2
    return 2 * high + low


def backward_kernel(
    axes, qa_ref, da_ref, all_in, probs_ref, factors, mid_small, ff_small, embed_ref, tail_ref, *refs
):
    mats_in, refs = refs[:4], refs[4:]
    grad_ref, ends, small, tail_got, dqt, part, sent, got, sems, small_got, small_sems, tail_sems = refs[:12]
    probs, probs_sems, total, sum_sent, sum_got, sum_sems, all_ref = refs[12:19]
    block_sems, mat_sems, mats = refs[19], refs[20], refs[21:]
    U, _, F, _ = qa_ref.shape
    C = mid_small.shape[1]
    me = lax.axis_index("seq")
    near, far = flipped(me, 1), flipped(me, 2)
    lane = lax.broadcasted_iota(jnp.int32, (1, 128), 1)
    one, zero = jnp.ones((), BF), jnp.zeros((), BF)
    hops, stages = butterfly(axes), stages_of(axes)
    greet_stages(stages, [("seq", xor4(me, 3))])
    tails = pltpu.make_async_remote_copy(
        tail_ref,
        tail_got,
        tail_sems.at[0],
        tail_sems.at[1],
        device_id={"seq": lax.rem(me + 1, lax.axis_size("seq"))},
        device_id_type=MESH,
    )
    tails.start()
    small[...] = jnp.zeros(small.shape, F32)
    small[0:8, :] = mid_small[...]
    wide = ff_small.shape[1] // C
    for j in range(wide):
        small[8 * (j + 1) : 8 * (j + 2), :] = ff_small[:, j * C : (j + 1) * C]

    def bring_mat(n):
        return pltpu.make_async_copy(mats_in[n], mats[n], mat_sems.at[n])

    def fill():
        for n in range(len(mats)):
            bring_mat(n).wait()
        pack(total, mats)
        embed = embed_ref[...].astype(F32) * jnp.where(me == 0, 1.0, 0.0)
        base = packed_rows(mats)
        for j in range(embed.shape[1] // 128):
            for u in range(U):
                row = base + j * U * dict(axes)["dp"] + lax.axis_index("dp") * U + u
                total[pl.ds(row, 1), :] = embed[u : u + 1, j * 128 : (j + 1) * 128]

    fine = stages_of(axes, 1)
    run_sum = halving_steps(fine, total, sum_sent, sum_got, ends, sum_sems)
    run_small = small_steps(hops, small, small_got, small_sems)
    dqt[...] = jnp.zeros(dqt.shape, F32)

    def hop(kind, u):
        peer = far if kind == 1 else near
        return to_peer(sent.at[kind, u], got.at[kind, u], sems, (kind, u), peer)

    def block_of(t):
        late = t // 4
        r = (1 - late) * (3 - t % 2) + late * (1 - (t - 4) // 2)
        return r, (1 - late) * ((t // 2) % 2) + late * (t % 2)

    def fetch(t):
        r, u = block_of(t)
        return pltpu.make_async_copy(probs_ref.at[r, u], probs.at[t % 2], probs_sems.at[t % 2])

    def bring(t):
        r, u = block_of(t)
        return pltpu.make_async_copy(all_in.at[r, u], all_ref.at[r, u], block_sems.at[t])

    bring(0).start()
    fetch(0).start()
    for t in range(1, 8):
        bring(t).start()
    for n in range(len(mats)):
        bring_mat(n).start()
    run_small(0)

    def step(t, _):
        r, u = block_of(t)

        @pl.when(t < 7)
        def _():
            fetch(t + 1).start()

        bring(t).wait()
        fetch(t).wait()
        v = all_ref[r, u, :, 128:256]
        kt = all_ref[r, u, :, 0:128].T
        dks, dvs = [], []
        for h in range(2):
            base = 64 * (1 - h)
            extra = (lane >= base) & (lane < base + 3)
            va = jnp.where(head_lanes(lane, h), v, jnp.where(extra, -one, zero))
            qa = qa_ref[u, h]
            da = da_ref[u, h]
            p = jnp.concatenate(
                [
                    probs[t % 2, h, pl.ds(row * F // 2, F // 2), :].astype(F32)
                    * factors[r, u, 2 * h + row : 2 * h + row + 1, :]
                    for row in range(2)
                ],
                axis=0,
            )
            ds = (p * dot(va, da, NT)).astype(BF)
            dvs.append(dot(p.astype(BF), da))
            dks.append(dot(ds, qa))
            rows = slice(64 * h, 64 * h + 64)
            dqt[u, rows, :] += dot(kt[rows, :], ds)
        part[:, 0:128] = jnp.where(head_lanes(lane, 0), dks[0], dks[1])
        part[:, 128:256] = jnp.where(head_lanes(lane, 0), dvs[0], dvs[1])

        @pl.when(r == 3)
        def _():
            sent[0, u] = part[...].astype(BF)
            hop(0, u).start()

        @pl.when(r == 2)
        def _():
            hop(0, u).wait_recv()
            sent[1, u] = (part[...] + got[0, u].astype(F32)).astype(BF)
            hop(1, u).start()

        @pl.when(r == 1)
        def _():
            sent[2, u] = part[...].astype(BF)
            hop(2, u).start()

        @pl.when(r == 0)
        def _():
            hop(1, u).wait_recv()
            hop(2, u).wait_recv()
            both = part[...] + got[1, u].astype(F32) + got[2, u].astype(F32)
            grad_ref[u, :, 128:384] = both.astype(BF)
            grad_ref[u, :, 0:128] = (dqt[u] * SCALE).T.astype(BF)

        for slot in range(8):
            sums = [n for n in range(len(fine) + 1) if sum_slot(n, len(fine) + 1, 8) == slot]
            smalls = [n for n in range(1, len(hops) + 1) if sum_slot(n - 1, len(hops), 8) == slot]
            if sums or smalls:

                @pl.when(t == slot)
                def _(sums=sums, smalls=smalls):
                    for n in sums:
                        if n == 0:
                            fill()
                        run_sum(n)
                    for n in smalls:
                        run_small(n)

        return 0

    lax.fori_loop(0, 8, step, 0)
    tails.wait()
    for kind in range(3):
        for u in range(U):
            hop(kind, u).wait_send()


def sum_slot(step, count, slots):
    if (count, slots) == (5, 8):
        return (0, 1, 4, 6, 7)[step]
    return step * (slots - 1) // (count - 1)


def attend_back(qa, da, kv_all, probs, factors, mid_small, ff_small, embed, tails, mats, axes):
    U, _, F, _ = qa.shape
    C = mid_small.shape[1]
    count = bits_of(axes)
    embed_rows = U * dict(axes)["dp"] * embed.shape[1] // 128
    rows = padded_rows(packed_rows(mats) + embed_rows, axes)
    small_rows = 8 + 8 * (ff_small.shape[1] // C)
    vmem = pl.BlockSpec(memory_space=pltpu.VMEM)
    anywhere = pl.BlockSpec(memory_space=pl.ANY)
    return pl.pallas_call(
        functools.partial(backward_kernel, axes),
        out_shape=(
            jax.ShapeDtypeStruct((U, F, 384), BF),
            jax.ShapeDtypeStruct((rows >> count, 128), BF),
            jax.ShapeDtypeStruct((small_rows, C), F32),
            jax.ShapeDtypeStruct(tails.shape, F32),
        ),
        in_specs=[vmem, vmem, anywhere, anywhere] + [vmem] * 5 + [anywhere] * len(mats),
        out_specs=[vmem] * 4,
        scratch_shapes=[
            pltpu.VMEM((U, 128, F), F32),
            pltpu.VMEM((F, 256), F32),
            pltpu.VMEM((3, U, F, 256), BF),
            pltpu.VMEM((3, U, F, 256), BF),
            pltpu.SemaphoreType.DMA((2, 3, U)),
            pltpu.VMEM((count, small_rows, C), F32),
            pltpu.SemaphoreType.DMA((2, count)),
            pltpu.SemaphoreType.DMA((2,)),
            pltpu.VMEM((2, 2, F, F), BF),
            pltpu.SemaphoreType.DMA((2,)),
            *halving_scratch(rows, axes, 1),
            pltpu.VMEM(kv_all.shape, BF),
            pltpu.SemaphoreType.DMA((8,)),
            pltpu.SemaphoreType.DMA((len(mats),)),
            *(pltpu.VMEM(m.shape, F32) for m in mats),
        ],
        compiler_params=pltpu.CompilerParams(
            collective_id=2, has_side_effects=True, vmem_limit_bytes=60 * 2**20
        ),
        name="attend_back",
    )(qa, da, kv_all, probs, factors, mid_small, ff_small, embed, tails, *mats)


def frame_mask_of(start, rows, length):
    spot = start + lax.broadcasted_iota(jnp.int32, (rows, 1), 0)
    return jnp.where((spot >= 0) & (spot < length), 1.0, 0.0)


def taps_of(x):
    wide = x.astype(F32)
    rows = x.shape[0]
    return jnp.concatenate(
        [pltpu.roll(wide, 1, 0).astype(BF), x, pltpu.roll(wide, rows - 1, 0).astype(BF)], axis=1
    )


def group_sums(rows):
    C = rows.shape[1]
    width = C // GROUPS
    one = lax.broadcasted_iota(jnp.int32, (C, C), 0) // width
    two = lax.broadcasted_iota(jnp.int32, (C, C), 1) // width
    same = jnp.where(one == two, 1.0, 0.0)
    return lax.dot_general(
        rows, same, NN, precision=lax.Precision.HIGHEST, preferred_element_type=F32
    )


def mish_parts(v):
    e = jnp.exp(jnp.minimum(v, 20.0))
    w = e * (e + 2.0)
    r = 1.0 / (w + 2.0)
    return e, w, r


def greet_all(me):
    barrier = pltpu.get_barrier_semaphore()
    for flip in (1, 2, 3):
        pl.semaphore_signal(barrier, inc=1, device_id={"seq": xor4(me, flip)}, device_id_type=MESH)
    pl.semaphore_wait(barrier, 3)


def share(mine, got, sems, u, me):
    return [
        pltpu.make_async_remote_copy(
            mine.at[u],
            got.at[j, u],
            sems.at[0, j, u],
            sems.at[1, j, u],
            device_id={"seq": xor4(me, j + 1)},
            device_id_type=MESH,
        )
        for j in range(3)
    ]


def front_kernel(
    len_ref,
    frames,
    embed,
    cotangent,
    conv_first,
    conv_second,
    conv_skip,
    time_proj,
    w_qkv,
    gains,
    shifts,
    x_out,
    h1_out,
    act_out,
    h2_out,
    res_out,
    all_out,
    probs_out,
    o_ref,
    qa_ref,
    stat_ref,
    embed_ref,
    next_ref,
    factors,
    x_ref,
    h1_ref,
    act_ref,
    h2_ref,
    res_ref,
    all_ref,
    lead,
    stat_one,
    got_one,
    stat_two,
    got_two,
    top,
    acc,
    held_one,
    held_two,
    tops_one,
    tops_two,
    probs,
    tops_used,
    time_rows,
    halo_sems,
    sems_one,
    sems_two,
    kv_sems,
    keep_sems,
    block_sems,
    probs_sems,
):
    U, F, C = frames.shape
    rows = F + 2 * EDGE
    own = pl.ds(EDGE, F)
    me = lax.axis_index("seq")
    count = lax.axis_size("seq")
    after, behind = lax.rem(me + 1, count), lax.rem(me + count - 1, count)
    start = me * F
    near, far = flipped(me, 1), flipped(me, 2)
    lane = lax.broadcasted_iota(jnp.int32, (1, 128), 1)
    one, zero = jnp.ones((), BF), jnp.zeros((), BF)
    greet_all(me)
    made = (x_ref, h1_ref, act_ref, h2_ref, res_ref)
    kept = (x_out, h1_out, act_out, h2_out, res_out)

    def keep(name):
        return pltpu.make_async_copy(made[name], kept[name], keep_sems.at[name])

    def keep_block(r, u):
        return pltpu.make_async_copy(all_ref.at[r, u], all_out.at[r, u], block_sems.at[r, u])

    half = F // 2

    def hop(kind, u, part=None):
        rows = slice(None) if part is None else pl.ds(part * half, half)
        source, slot, peer = ((0, 1, near), (0, 2, far), (2, 3, near))[kind]
        place = (kind, u if part is None else u + part)
        return to_peer(all_ref.at[source, u, rows], all_ref.at[slot, u, rows], kv_sems, place, peer)

    def halo(src, dst, kind, peer):
        return pltpu.make_async_remote_copy(
            src, dst, halo_sems.at[0, kind], halo_sems.at[1, kind], device_id={"seq": peer}, device_id_type=MESH
        )

    halos = [
        halo(frames.at[:, pl.ds(F - EDGE, EDGE)], lead.at[0], 0, after),
        halo(frames.at[:, pl.ds(0, EDGE)], lead.at[1], 1, behind),
        halo(cotangent.at[:, pl.ds(0, EDGE)], next_ref, 2, behind),
    ]
    for copy in halos:
        copy.start()
    active = embed[...].astype(F32)
    e, w, r = mish_parts(active)
    active = (active * w * r).astype(BF)
    embed_ref[...] = active
    time_rows[0:U, :] = dot(active, time_proj[...]) + shifts[2:3, :]
    first_taps = conv_first[...].reshape(3 * C, C)
    second_taps = conv_second[...].reshape(3 * C, C)

    def masked(block, at, u):
        return (block.astype(F32) * frame_mask_of(at, block.shape[0], len_ref[u])).astype(BF)

    for u in range(U):
        x_ref[u, own, :] = masked(frames[u], start, u)
    for copy in halos[:2]:
        copy.wait_recv()
    for u in range(U):
        x_ref[u, 0:EDGE, :] = masked(lead[0, u], start - EDGE, u)
        x_ref[u, F + EDGE :, :] = masked(lead[1, u], start + F, u)
    keep(0).start()

    def valid(i, u):
        return jnp.clip(len_ref[u] - i * F, 0, F).astype(F32)

    def local_stats(hidden, stat, got, sems, u):
        mask = frame_mask_of(start, F, len_ref[u])
        inside = hidden[EDGE : EDGE + F]
        many = jnp.maximum(valid(me, u) * (C // GROUPS), 1.0)
        mean = group_sums(row_sum(inside * mask)) / many
        centered = (inside - mean) * mask
        stat[u, 0:1, :] = mean
        stat[u, 1:2, :] = group_sums(row_sum(centered * centered))
        for copy in share(stat, got, sems, u, me):
            copy.start()

    def whole_stats(stat, got, sems, u):
        for copy in share(stat, got, sems, u, me):
            copy.wait()
        total = len_ref[u].astype(F32)
        parts = [(valid(me, u), stat[u])]
        for j in range(3):
            parts.append((valid(xor4(me, j + 1), u), got[j, u]))
        mean = sum(n * p[0:1] for n, p in parts) / total
        squares = sum(p[1:2] + (n * (C // GROUPS)) * jnp.square(p[0:1] - mean) for n, p in parts)
        inv = lax.rsqrt(squares / (total * (C // GROUPS)) + norm_eps)
        return mean, inv

    def activate(hidden, mean, inv, gain, shift):
        v = (hidden - mean) * inv * gain + shift
        e, w, r = mish_parts(v)
        return v * w * r

    def first_conv(u, _):
        hidden = dot(taps_of(x_ref[u]), first_taps) + shifts[0:1, :]
        h1_ref[u] = hidden
        local_stats(hidden, stat_one, got_one, sems_one, u)
        return 0

    lax.fori_loop(0, U, first_conv, 0)
    keep(1).start()

    def second_conv(u, _):
        mean, inv = whole_stats(stat_one, got_one, sems_one, u)
        stat_ref[u, 0:1, :] = mean
        stat_ref[u, 1:2, :] = inv
        mask = frame_mask_of(start - EDGE, rows, len_ref[u])
        act = activate(h1_ref[u], mean, inv, gains[0:1, :], shifts[1:2, :])
        act_in = ((act + time_rows[pl.ds(u, 1), :]) * mask).astype(BF)
        act_ref[u] = act_in
        hidden = dot(taps_of(act_in), second_taps) + shifts[3:4, :]
        h2_ref[u] = hidden
        local_stats(hidden, stat_two, got_two, sems_two, u)
        return 0

    lax.fori_loop(0, U, second_conv, 0)
    keep(2).start()
    keep(3).start()

    def to_qkv(u, _):
        skip = dot(x_ref[u, own, :], conv_skip[...]) + shifts[5:6, :]
        mean, inv = whole_stats(stat_two, got_two, sems_two, u)
        stat_ref[u, 2:3, :] = mean
        stat_ref[u, 3:4, :] = inv
        mask = frame_mask_of(start, F, len_ref[u])
        act = activate(h2_ref[u, own, :], mean, inv, gains[1:2, :], shifts[4:5, :]) * mask
        res = act + skip
        res_ref[u] = res
        centered = res - lane_mean(res)
        hat = centered * lax.rsqrt(lane_mean(centered * centered) + norm_eps)
        normed = (hat * gains[2:3, :] + shifts[6:7, :]).astype(BF)
        qkv = dot(normed, w_qkv[...]).astype(BF)
        all_ref[0, u] = qkv[:, 128:384]

        @pl.when(u < U - 1)
        def _():
            hop(1, u).start()

        @pl.when(u == U - 1)
        def _():
            for part in (0, 1):
                hop(1, U - 1, part).start()

        hop(0, u).start()
        keep_block(0, u).start()
        for h in range(2):
            other = jnp.where(lane == 64 * (1 - h) + 3, one, zero)
            qa_ref[u, h] = jnp.where(head_lanes(lane, h), qkv[:, 0:128] * SCALE, other)
        return 0

    lax.fori_loop(0, U, to_qkv, 0)
    keep(4).start()
    top[...] = jnp.full(top.shape, -1e30, F32)
    factors[...] = jnp.zeros(factors.shape, F32)
    acc[...] = jnp.zeros(acc.shape, F32)

    def block_of(t):
        late = t // 4
        r = (1 - late) * (t // 2) + late * (2 + t % 2)
        return r, (1 - late) * (t % 2) + late * ((t - 4) // 2)

    def keep_probs(t):
        r, u = block_of(t)
        return pltpu.make_async_copy(probs.at[t % 2], probs_out.at[r, u], probs_sems.at[t % 2])

    def arrive(t):
        @pl.when(t >= 3)
        def _():
            keep_probs(t - 3).wait()

        @pl.when(t >= 2)
        def _():
            keep_probs(t - 2).start()

        @pl.when(t == 2)
        def _():
            hop(0, 0).wait_recv()
            keep_block(1, 0).start()

        @pl.when(t == 3)
        def _():
            hop(0, 1).wait_recv()
            keep_block(1, 1).start()

        @pl.when(t == 4)
        def _():
            hop(1, 0).wait()
            hop(2, 0).start()
            keep_block(2, 0).start()

        @pl.when(t == 5)
        def _():
            hop(2, 0).wait_recv()
            keep_block(3, 0).start()

    def scores(t, held, tops, part=None):
        r, u = block_of(t)
        first, count = (0, F) if part is None else (part * half, half)
        k = all_ref[r, u, pl.ds(first, count), 0:128]
        spot = xor4(me, r) * F + first + lax.broadcasted_iota(jnp.int32, (count, 1), 0)
        bias = jnp.where(spot < len_ref[u], 0.0, -1e9).astype(BF)
        for h in range(2):
            ka = jnp.where(head_lanes(lane, h), k, jnp.where(lane == 64 * (1 - h) + 3, bias, zero))
            s = dot(ka, qa_ref[u, h], NT)
            held[h, 0:count] = s
            tops[h, 0:1, :] = jnp.max(s, axis=0, keepdims=True)

    def weigh(t, slot, held, tops, part=None):
        r, u = block_of(t)
        first, count = (0, F) if part is None else (part * half, half)
        vt = all_ref[r, u, pl.ds(first, count), 128:256].T
        ones = jnp.ones((EDGE, count), BF)
        for h in range(2):
            old = top[u, h, 0:1, :]
            new = jnp.maximum(old, tops[h, 0:1, :])
            p = jnp.exp(held[h, 0:count] - new).astype(BF)
            probs[slot, h, pl.ds(first, count), :] = p
            for row in (0, 1) if part is None else (part,):
                tops_used[r, u, 2 * h + row : 2 * h + row + 1, :] = new
            va = jnp.concatenate([vt[64 * h : 64 * h + 64], ones], axis=0)
            acc[u, h] = acc[u, h] * jnp.exp(old - new) + dot(va, p)
            top[u, h, 0:1, :] = new

    scores(0, held_one, tops_one)

    def two_steps(n, _):
        t = 2 * n
        arrive(t + 1)
        scores(t + 1, held_two, tops_two)
        weigh(t, 0, held_one, tops_one)
        arrive(t + 2)
        scores(t + 2, held_one, tops_one)
        weigh(t + 1, 1, held_two, tops_two)
        return 0

    lax.fori_loop(0, 2, two_steps, 0)
    arrive(5)
    scores(5, held_two, tops_two)
    weigh(4, 0, held_one, tops_one)
    keep_probs(3).wait()
    keep_probs(4).start()
    for part in (0, 1):
        hop(1, 1, part).wait()
        hop(2, 1, part).start()
        scores(6, held_one, tops_one, part)
        if part == 0:
            weigh(5, 1, held_two, tops_two)
            keep_probs(4).wait()
            keep_probs(5).start()
        else:
            keep_block(2, 1).start()
            weigh(7, 1, held_two, tops_two, 0)
        hop(2, 1, part).wait_recv()
        scores(7, held_two, tops_two, part)
        weigh(6, 0, held_one, tops_one, part)
        if part == 0:
            keep_probs(5).wait()
    keep_block(3, 1).start()
    keep_probs(6).start()
    weigh(7, 1, held_two, tops_two, 1)
    keep_probs(7).start()
    for u in range(U):
        outs, logs = [], []
        for h in range(2):
            total = acc[u, h, 64:65, :]
            outs.append(acc[u, h, 0:64, :] / total)
            logs.append(top[u, h, 0:1, :] + jnp.log(total))
        o_ref[u] = jnp.concatenate(outs, axis=0).T
        for r in range(4):
            for row in range(4):
                used = tops_used[r, u, row : row + 1, :]
                factors[r, u, row : row + 1, :] = jnp.exp(used - logs[row // 2])
    for u in range(U):
        hop(0, u).wait_send()
        for part in (None,) if u < U - 1 else (0, 1):
            hop(2, u, part).wait_send()
        for r in range(4):
            keep_block(r, u).wait()
    for name in range(5):
        keep(name).wait()
    keep_probs(6).wait()
    keep_probs(7).wait()
    for copy in halos:
        copy.wait_send()
    halos[2].wait_recv()


def front(lengths, frames, embed, cotangent, conv_first, conv_second, conv_skip, time_proj, w_qkv, gains, shifts):
    U, F, C = frames.shape
    rows = F + 2 * EDGE
    vmem = pl.BlockSpec(memory_space=pltpu.VMEM)
    stat = pltpu.VMEM((U, 8, C), F32)
    got = pltpu.VMEM((3, U, 8, C), F32)
    return pl.pallas_call(
        front_kernel,
        out_shape=(
            jax.ShapeDtypeStruct((U, rows, C), BF),
            jax.ShapeDtypeStruct((U, rows, C), F32),
            jax.ShapeDtypeStruct((U, rows, C), BF),
            jax.ShapeDtypeStruct((U, rows, C), F32),
            jax.ShapeDtypeStruct((U, F, C), F32),
            jax.ShapeDtypeStruct((4, U, F, 256), BF),
            jax.ShapeDtypeStruct((4, U, 2, F, F), BF),
            jax.ShapeDtypeStruct((U, F, 128), F32),
            jax.ShapeDtypeStruct((U, 2, F, 128), BF),
            jax.ShapeDtypeStruct((U, 8, C), F32),
            jax.ShapeDtypeStruct(embed.shape, BF),
            jax.ShapeDtypeStruct((U, EDGE, C), BF),
            jax.ShapeDtypeStruct((4, U, 8, F), F32),
        ),
        in_specs=[pl.BlockSpec(memory_space=pltpu.SMEM), vmem, vmem, pl.BlockSpec(memory_space=pl.ANY)] + [vmem] * 7,
        out_specs=[pl.BlockSpec(memory_space=pl.ANY)] * 7 + [vmem] * 6,
        scratch_shapes=[
            pltpu.VMEM((U, rows, C), BF),
            pltpu.VMEM((U, rows, C), F32),
            pltpu.VMEM((U, rows, C), BF),
            pltpu.VMEM((U, rows, C), F32),
            pltpu.VMEM((U, F, C), F32),
            pltpu.VMEM((4, U, F, 256), BF),
            pltpu.VMEM((2, U, EDGE, C), BF),
            stat,
            got,
            stat,
            got,
            pltpu.VMEM((U, 2, 8, F), F32),
            pltpu.VMEM((U, 2, 64 + EDGE, F), F32),
            pltpu.VMEM((2, F, F), F32),
            pltpu.VMEM((2, F, F), F32),
            pltpu.VMEM((2, 8, F), F32),
            pltpu.VMEM((2, 8, F), F32),
            pltpu.VMEM((2, 2, F, F), BF),
            pltpu.VMEM((4, U, 8, F), F32),
            pltpu.VMEM((8, C), F32),
            pltpu.SemaphoreType.DMA((2, 3)),
            pltpu.SemaphoreType.DMA((2, 3, U)),
            pltpu.SemaphoreType.DMA((2, 3, U)),
            pltpu.SemaphoreType.DMA((2, 3, U + 1)),
            pltpu.SemaphoreType.DMA((5,)),
            pltpu.SemaphoreType.DMA((4, U)),
            pltpu.SemaphoreType.DMA((2,)),
        ],
        compiler_params=pltpu.CompilerParams(
            collective_id=1, has_side_effects=True, vmem_limit_bytes=62 * 2**20
        ),
        name="front",
    )(lengths, frames, embed, cotangent, conv_first, conv_second, conv_skip, time_proj, w_qkv, gains, shifts)


def resnet_back_kernel(
    axes,
    len_ref,
    gqkv_in,
    gtwo_in,
    res_in,
    x_in,
    h1_in,
    act_in,
    h2_in,
    stat_ref,
    conv_first,
    conv_second,
    conv_skip,
    w_qkv,
    gains,
    shifts,
    up_ends,
    gframes,
    up,
    mid,
    late,
    last,
    gsmall,
    gfirst,
    gsecond,
    gskip,
    gw_qkv,
    lows,
    gqkv_ref,
    gtwo_ref,
    res_ref,
    x_ref,
    h1_ref,
    act_ref,
    h2_ref,
    load_sems,
    edges,
    gone,
    gmasked,
    sum_two,
    got_two,
    sum_one,
    got_one,
    halo_sems,
    sems_two,
    sems_one,
    small_got,
    small_sems,
    *sum_refs,
):
    U, F, C = gtwo_ref.shape
    given = (gqkv_in, res_in, gtwo_in, x_in, h2_in, act_in, h1_in)
    held = (gqkv_ref, res_ref, gtwo_ref, x_ref, h2_ref, act_ref, h1_ref)

    def load(name, u):
        return pltpu.make_async_copy(given[name].at[u], held[name].at[u], load_sems.at[name, u])

    for names in ((0, 1, 2, 3), (4, 5, 6)):
        for u in range(U):
            for name in names:
                load(name, u).start()
    rows = F + 2 * EDGE
    own = pl.ds(EDGE, F)
    inner = slice(EDGE, EDGE + F)
    me = lax.axis_index("seq")
    count = lax.axis_size("seq")
    after, behind = lax.rem(me + 1, count), lax.rem(me + count - 1, count)
    start = me * F
    hops, stages = butterfly(axes), stages_of(axes)
    greet_stages(stages, [("seq", xor4(me, 3))])
    fine = stages_of(axes, 1)
    run_up = doubling_steps(fine, up_ends, up, sum_refs[0])
    run_mid = sum_steps(stages, *sum_refs[1:5], mid, *sum_refs[5:7])
    run_late = sum_steps(stages, *sum_refs[7:11], late, *sum_refs[11:13])
    run_last = sum_steps(stages, *sum_refs[13:17], last, *sum_refs[17:19])
    run_small = small_steps(hops, gsmall, small_got, small_sems)
    for ref in (gsmall, sum_two, sum_one, gfirst, gsecond, gskip, gw_qkv):
        ref[...] = jnp.zeros_like(ref)

    run_up(0)

    def halo(kind, u):
        spot = pl.ds(F, EDGE) if kind == 0 else pl.ds(EDGE, EDGE)
        return pltpu.make_async_remote_copy(
            gone.at[u, spot],
            edges.at[kind, u],
            halo_sems.at[0, kind, u],
            halo_sems.at[1, kind, u],
            device_id={"seq": after if kind == 0 else behind},
            device_id_type=MESH,
        )

    def through_qkv(u, _):
        for name in range(4):
            load(name, u).wait()
        res = res_ref[u]
        centered = res - lane_mean(res)
        inv = lax.rsqrt(lane_mean(centered * centered) + norm_eps)
        hat = centered * inv
        normed = (hat * gains[2:3, :] + shifts[6:7, :]).astype(BF)
        gqkv = gqkv_ref[u]
        gw_qkv[...] += tn(normed, gqkv)
        grad = dot(gqkv, w_qkv[...], NT)
        gsmall[10:11, :] += row_sum(grad * hat)
        gsmall[6:7, :] += row_sum(grad)
        grad = grad * gains[2:3, :]
        grad = gtwo_ref[u] + inv * (grad - lane_mean(grad) - hat * lane_mean(grad * hat))
        gone[u, own, :] = grad
        for kind in range(2):
            halo(kind, u).start()
        gsmall[5:6, :] += row_sum(grad)
        low = grad.astype(BF)
        gskip[...] += tn(x_ref[u, own, :], low)
        gmasked[u] = dot(low, conv_skip[...], NT)

        @pl.when(u == 0)
        def _():
            run_up(1)

        return 0

    lax.fori_loop(0, U, through_qkv, 0)

    def norm_terms(grad, hidden, u, at):
        mean, inv = stat_ref[u, 2 * at : 2 * at + 1, :], stat_ref[u, 2 * at + 1 : 2 * at + 2, :]
        gain, shift = gains[at : at + 1, :], shifts[1 + 3 * at : 2 + 3 * at, :]
        hat = (hidden - mean) * inv
        v = hat * gain + shift
        e, w, r = mish_parts(v)
        slope = w * r + v * (4.0 * e * (1.0 + e)) * (r * r)
        return hat, grad * slope, inv, gain

    def local_sums(hat, grad, gain, sums, got, sems, u, at):
        hat, grad = hat[inner], grad[inner]
        gsmall[8 + at : 9 + at, :] += row_sum(grad * hat)
        gsmall[1 + 3 * at : 2 + 3 * at, :] += row_sum(grad)
        grad = grad * gain
        both = jnp.concatenate([row_sum(grad), row_sum(grad * hat)], axis=0)
        sums[u, 0:2, :] = group_sums(both)
        for copy in share(sums, got, sems, u, me):
            copy.start()

    def whole_sums(sums, got, sems, u):
        for copy in share(sums, got, sems, u, me):
            copy.wait()
        return (sums[u] + got[0, u]) + (got[1, u] + got[2, u])

    def hidden_grad(hat, grad, inv, gain, total, u, mask):
        many = len_ref[u].astype(F32) * (C // GROUPS)
        return inv * (grad * gain - mask * ((total[0:1] + hat * total[1:2]) / many))

    def back_taps(grad, weight):
        wide = grad.astype(F32)
        many = grad.shape[0]
        later = pltpu.roll(wide, many - 1, 0).astype(BF)
        earlier = pltpu.roll(wide, 1, 0).astype(BF)
        return dot(later, weight[0], NT) + dot(grad, weight[1], NT) + dot(earlier, weight[2], NT)

    def wide_mask(u):
        return frame_mask_of(start - EDGE, rows, len_ref[u])

    def second_terms(u, _):
        for kind in range(2):
            halo(kind, u).wait()
        load(4, u).wait()
        gone[u, 0:EDGE, :] = edges[0, u]
        gone[u, F + EDGE :, :] = edges[1, u]
        hat, grad, inv, gain = norm_terms(gone[u] * wide_mask(u), h2_ref[u], u, 1)
        gone[u] = grad
        local_sums(hat, grad, gain, sum_two, got_two, sems_two, u, 1)
        return 0

    lax.fori_loop(0, U, second_terms, 0)

    def second_back(u, _):
        load(5, u).wait()
        load(6, u).wait()
        taps = taps_of(act_ref[u])
        total = whole_sums(sum_two, got_two, sems_two, u)
        mask = wide_mask(u)
        inv, gain = stat_ref[u, 3:4, :], gains[1:2, :]
        hat = (h2_ref[u] - stat_ref[u, 2:3, :]) * inv
        grad = hidden_grad(hat, gone[u], inv, gain, total, u, mask)
        gsmall[3:4, :] += row_sum(grad[inner])
        low = grad.astype(BF)
        gsecond[...] += tn(taps[inner], low[inner])
        grad = back_taps(low, conv_second) * mask
        by_time = row_sum(grad[inner])
        gsmall[2:3, :] += by_time
        gsmall[pl.ds(16 + lax.axis_index("dp") * U + u, 1), :] = by_time
        hat, grad, inv, gain = norm_terms(grad, h1_ref[u], u, 0)
        gone[u] = grad
        local_sums(hat, grad, gain, sum_one, got_one, sems_one, u, 0)

        @pl.when(u == 0)
        def _():
            run_up(2)

        return 0

    lax.fori_loop(0, U, second_back, 0)
    pack(sum_refs[1], [gskip, gw_qkv])
    run_mid(0)
    pack(sum_refs[7], [gsecond])
    run_late(0)

    def first_back(u, _):
        taps = taps_of(x_ref[u])
        total = whole_sums(sum_one, got_one, sems_one, u)
        mask = wide_mask(u)
        inv, gain = stat_ref[u, 1:2, :], gains[0:1, :]
        hat = (h1_ref[u] - stat_ref[u, 0:1, :]) * inv
        grad = hidden_grad(hat, gone[u], inv, gain, total, u, mask)
        gsmall[0:1, :] += row_sum(grad[inner])
        low = grad.astype(BF)
        lows[u] = low
        gfirst[...] += tn(taps[inner], low[inner])
        return 0

    lax.fori_loop(0, U, first_back, 0)
    run_late(1)
    run_mid(1)
    pack(sum_refs[13], [gfirst])
    steps = 2 * len(stages)
    for n in range(max(steps, len(hops)) + 1):
        for run, ahead, final in (
            (run_last, 0, steps),
            (run_late, 2, steps),
            (run_mid, 2, steps),
            (run_small, 0, len(hops)),
        ):
            if ahead + n <= final:
                run(ahead + n)
        if 0 <= n - 2 <= len(fine) - 3:
            run_up(n + 1)
        if n < U:
            grad = back_taps(lows[n], conv_first)[inner] + gmasked[n]
            gframes[n] = grad * frame_mask_of(start, F, len_ref[n])


def resnet_back(lengths, gqkv, gtwo, res, x, h1, act, h2, stat, conv_first, conv_second, conv_skip, w_qkv, gains, shifts, up_ends, axes):
    U, F, C = gtwo.shape
    count = bits_of(axes)
    shapes = [(3 * C, C), (3 * C, C), (C, C), w_qkv.shape]
    mats = [jax.ShapeDtypeStruct(shape, F32) for shape in shapes]
    up_rows = up_ends.shape[0] << count
    row_counts = [padded_rows(packed_rows(some), axes) for some in (mats[2:], mats[1:2], mats[:1])]
    small_rows = 16 + U * dict(axes)["dp"]
    rows = F + 2 * EDGE
    vmem = pl.BlockSpec(memory_space=pltpu.VMEM)
    sums = pltpu.VMEM((U, 8, C), F32)
    got = pltpu.VMEM((3, U, 8, C), F32)
    return pl.pallas_call(
        functools.partial(resnet_back_kernel, axes),
        out_shape=(
            jax.ShapeDtypeStruct((U, F, C), F32),
            *(jax.ShapeDtypeStruct((many, 128), BF) for many in [up_rows, *row_counts]),
            jax.ShapeDtypeStruct((small_rows, C), F32),
        ),
        in_specs=[pl.BlockSpec(memory_space=pltpu.SMEM)]
        + [pl.BlockSpec(memory_space=pl.ANY)] * 7
        + [vmem] * 8,
        out_specs=[vmem] * 6,
        scratch_shapes=[
            *(pltpu.VMEM(shape, F32) for shape in shapes),
            pltpu.VMEM((U, rows, C), BF),
            *(pltpu.VMEM(x.shape, x.dtype) for x in (gqkv, gtwo, res, x, h1, act, h2)),
            pltpu.SemaphoreType.DMA((7, U)),
            pltpu.VMEM((2, U, EDGE, C), F32),
            pltpu.VMEM((U, rows, C), F32),
            pltpu.VMEM((U, F, C), F32),
            sums,
            got,
            sums,
            got,
            pltpu.SemaphoreType.DMA((2, 2, U)),
            pltpu.SemaphoreType.DMA((2, 3, U)),
            pltpu.SemaphoreType.DMA((2, 3, U)),
            pltpu.VMEM((count, small_rows, C), F32),
            pltpu.SemaphoreType.DMA((2, count)),
            pltpu.SemaphoreType.DMA((2, stage_count(axes, 1), 7)),
            *(ref for many in row_counts for ref in sum_scratch(many, axes)),
        ],
        compiler_params=pltpu.CompilerParams(
            collective_id=4, has_side_effects=True, vmem_limit_bytes=60 * 2**20
        ),
        name="resnet_back",
    )(lengths, gqkv, gtwo, res, x, h1, act, h2, stat, conv_first, conv_second, conv_skip, w_qkv, gains, shifts, up_ends)


def shards(
    frames,
    time_embed,
    lengths,
    out_cotangent,
    conv_first,
    conv_second,
    conv_skip,
    time_proj,
    w_qkv,
    w_out,
    ff_in,
    ff_out,
    conv_down,
    gains,
    shifts,
    ff_bias,
    snake_logs,
):
    channels = frames.shape[2]
    (
        masked_in,
        hidden_one,
        act_in,
        hidden_two,
        resnet_out,
        kv_all,
        probs,
        attended_full,
        queries_aug,
        stats,
        embed_act,
        next_rows,
        factors,
    ) = front(
        lengths,
        frames,
        time_embed,
        out_cotangent,
        conv_first,
        conv_second,
        conv_skip,
        time_proj,
        w_qkv,
        gains,
        shifts,
    )
    (
        layer_out,
        grad_two,
        grad_aug,
        first_rows,
        tail_rows,
        grad_w_out,
        grad_ff_in,
        grad_ff_out,
        grad_conv_down,
        mid_small,
        ff_small,
    ) = middle(
        lengths,
        attended_full,
        resnet_out,
        out_cotangent,
        next_rows,
        w_out,
        ff_in,
        ff_out,
        conv_down,
        gains,
        shifts,
        ff_bias,
        snake_logs,
    )
    axes = (("seq", lax.axis_size("seq")), ("dp", lax.axis_size("dp")))
    grad_qkv, up_ends, small_up, tail_rows = attend_back(
        queries_aug,
        grad_aug,
        kv_all,
        probs,
        factors,
        mid_small,
        ff_small,
        embed_act,
        tail_rows,
        [grad_w_out, grad_ff_in, grad_ff_out, grad_conv_down.reshape(-1, channels)],
        axes,
    )
    grad_frames, up, mid, late, last, small_late = resnet_back(
        lengths,
        grad_qkv,
        grad_two,
        resnet_out,
        masked_in,
        hidden_one,
        act_in,
        hidden_two,
        stats,
        conv_first,
        conv_second,
        conv_skip,
        w_qkv,
        gains,
        shifts,
        up_ends,
        axes,
    )
    weights = (
        conv_first,
        conv_second,
        conv_skip,
        time_proj,
        w_qkv,
        w_out,
        ff_in,
        ff_out,
        conv_down,
        gains,
        shifts,
        ff_bias.reshape(1, -1),
        snake_logs,
    )
    grads = finish(
        lengths,
        first_rows,
        tail_rows,
        small_up,
        small_late,
        layer_out,
        grad_frames,
        (up, mid, late, last),
        [w.shape for w in weights],
    )
    return (grads[13], grads[14], *grads[:11], grads[11].reshape(-1), grads[12])


def solution(mesh):
    in_specs = (
        P("dp", "seq", None),
        P("dp", None),
        P("dp"),
        P("dp", "seq", None),
        P(),
        P(),
        P(),
        P(),
        P(),
        P(),
        P(),
        P(),
        P(),
        P(),
        P(),
        P(),
        P(),
    )
    out_specs = (
        P("dp", "seq", None),
        P("dp", "seq", None),
        P(),
        P(),
        P(),
        P(),
        P(),
        P(),
        P(),
        P(),
        P(),
        P(),
        P(),
        P(),
        P(),
    )
    return jax.shard_map(shards, mesh=mesh, in_specs=in_specs, out_specs=out_specs, check_vma=False)
```
